128 devices in a mesh: fsdp: 4 (over z), ctx: 16 (over x, y_lo, core), tp: 2 (over y_hi).
Axes of the slice: x: 4, y: 4 (y_hi: 2, y_lo: 2; y = y_hi * 2 + y_lo), z: 4, core: 2. Of those that a mesh axis runs over, the one named last changes fastest.
Arguments:
- tokens: bfloat16 [4, 2048, 2048], P('fsdp', 'ctx'), may hold values from -6 to 6
- segments: int32 [4, 2048], P('fsdp'), may hold values from 0 to 30, as said below
- w_qkv: bfloat16 [2048, 3, 2048], P('fsdp', None, 'tp'), may hold values from -0.125 to 0.125
- b_qkv: bfloat16 [3, 32, 64], P(None, 'tp', 'fsdp'), may hold values from -3 to 3
- w_out: bfloat16 [2048, 2048], P('tp', 'fsdp'), may hold values from -1 to 1
- w_gate_up: bfloat16 [2048, 2, 5632], P('fsdp', None, 'tp'), may hold values from -0.125 to 0.125
- w_down: bfloat16 [5632, 2048], P('tp', 'fsdp'), may hold values from -0.078125 to 0.078125
- norm_gains: bfloat16 [2, 2048], P(None, 'fsdp'), may hold values from 0.25 to 1.75
- norm_shifts: bfloat16 [2, 2048], P(None, 'fsdp'), may hold values from -3 to 3
- cotangent: bfloat16 [4, 2048, 2048], P('fsdp', 'ctx'), may hold values from -6 to 6
Outputs:
- layer_out: bfloat16 [4, 2048, 2048], P('fsdp', 'ctx')
- grad_tokens: float32 [4, 2048, 2048], P('fsdp', 'ctx')
- grad_qkv: float32 [2048, 3, 2048], P('fsdp', None, 'tp')
- grad_bias: float32 [3, 32, 64], P(None, 'tp', 'fsdp')
- grad_out: float32 [2048, 2048], P('tp', 'fsdp')
- grad_gate_up: float32 [2048, 2, 5632], P('fsdp', None, 'tp')
- grad_down: float32 [5632, 2048], P('tp', 'fsdp')
- grad_gains: float32 [2, 2048], P(None, 'fsdp')
- grad_shifts: float32 [2, 2048], P(None, 'fsdp')
The draws below stay inside these ranges and needn't reach their ends.
Inputs may be any that keep to these rules, and one draw needn't show every extreme that they name: `segments`: segment numbers start at 0 in every sequence and rise by one at each new document, never falling; in every sequence one document covers all positions from 127 to 1920, and every sequence ends at the same largest segment number.
All inputs are finite; a program needn't handle non-finite values.
Results may differ from the reference program's by a relative error of at most 0.022.
Values may be sent and summed in bfloat16 or wider, within the bound.
A program may use at most 256 MiB of HBM per device.

```python
import jax
import jax.numpy as jnp
from jax import lax

D = 2048
HEADS = 32
HEAD_DIM = 64
FF = 5632
ROT = 16
SEQ_LEN = 2048
SEQS = 4
TOK_CTX = 128
QBLOCK = 512


def draw_segments(key, part):
    key = jax.random.fold_in(key, 7)
    zone_len = TOK_CTX - 1
    breaks = max(1, zone_len // 8)
    front_keys = jax.random.split(jax.random.fold_in(key, 1), SEQS)
    rear_keys = jax.random.split(jax.random.fold_in(key, 2), SEQS)
    front_rank = jax.vmap(lambda k: jax.random.permutation(k, zone_len))(front_keys)
    rear_rank = jax.vmap(lambda k: jax.random.permutation(k, zone_len))(rear_keys)
    front_flags = (front_rank < breaks).astype(jnp.int32)
    rear_flags = (rear_rank < breaks).astype(jnp.int32)
    middle_len = SEQ_LEN - 1 - 2 * zone_len
    flags = jnp.concatenate([jnp.zeros((SEQS, 1), jnp.int32), front_flags, jnp.zeros((SEQS, middle_len), jnp.int32), rear_flags], axis=1)
    return jnp.cumsum(flags, axis=1).astype(jnp.int32)


def block_scale(own_key, dims, pieces, low, top_value):
    factor_of, own = 1.0, jax.random.fold_in(own_key, 6)
    for dim, shards_of in pieces:
        draws = jnp.exp(jax.random.uniform(jax.random.fold_in(own, dim), (shards_of,), jnp.float32, low / len(pieces), top_value / len(pieces)))
        factor_of = factor_of * jnp.repeat(draws, dims[dim] // shards_of).reshape([-1 if axis == dim else 1 for axis in range(len(dims))])
    return factor_of


def noise(key, dims, spread, reach, cuts=(), dtype=jnp.bfloat16):
    entries = jax.random.normal(key, dims, jnp.float32) * spread
    if len(cuts) > 0:
        entries = block_scale(key, dims, cuts, -0.22, 0.18) * entries
    return jnp.clip(entries, min=-reach, max=reach).astype(dtype)


def setup_inputs(seed: int = 0) -> dict:
    streams_of = jax.random.split(jax.random.key(seed), 11)
    tokens = noise(streams_of[0], (SEQS, SEQ_LEN, D), 1.0, 6.0, ((0, 4), (1, 16)))
    segments = draw_segments(jax.random.fold_in(streams_of[10], 71), 0)
    w_qkv = noise(streams_of[2], (D, 3, D), D ** -0.5, 0.125, ((0, 4), (2, 2)))
    b_qkv = noise(streams_of[3], (3, HEADS, HEAD_DIM), 0.5, 3.0, ((1, 2), (2, 4)))
    w_out = noise(streams_of[4], (D, D), (D // 64) ** -0.5, 1.0, ((0, 2), (1, 4)))
    w_gate_up = noise(streams_of[5], (D, 2, FF), D ** -0.5, 0.125, ((0, 4), (2, 2)))
    w_down = noise(streams_of[6], (FF, D), FF ** -0.5, 0.078125, ((0, 2), (1, 4)))
    norm_gains = jnp.clip(1.0 + 0.15 * jax.random.normal(streams_of[7], (2, D), jnp.float32), 0.25, 1.75).astype(jnp.bfloat16)
    norm_shifts = noise(streams_of[8], (2, D), 0.5, 3.0, ((1, 4),))
    cotangent = noise(streams_of[9], (SEQS, SEQ_LEN, D), 1.0, 6.0, ((0, 4), (1, 16)))
    return dict(tokens=tokens, segments=segments, w_qkv=w_qkv, b_qkv=b_qkv, w_out=w_out, w_gate_up=w_gate_up, w_down=w_down, norm_gains=norm_gains, norm_shifts=norm_shifts, cotangent=cotangent)


EPS = 1e-05
NEG = -1e+30
HIGHEST = lax.Precision.HIGHEST

@jax.custom_vjp
def low(v):
    return lax.optimization_barrier(v.astype(jnp.bfloat16)).astype(jnp.float32)

@jax.custom_vjp
def low_back(v):
    return v

def low_keep(v):
    return (low(v), None)

def low_pass(kept, grad):
    return (grad,)

def back_keep(v):
    return (v, None)

def back_low(kept, grad):
    return (low(grad),)
low.defvjp(low_keep, low_pass)
low_back.defvjp(back_keep, back_low)

def layer_norm(values, gain_row, shift_row):
    row_mean = lax.optimization_barrier(jnp.mean(values, axis=-1, keepdims=True))
    centred = values - row_mean
    variance = lax.optimization_barrier(jnp.mean(centred * centred, axis=-1, keepdims=True))
    return centred * lax.rsqrt(variance + EPS) * gain_row + shift_row

def rotation_tables():
    half_rot = ROT // 2
    positions = jnp.arange(SEQ_LEN).astype(jnp.float32)
    inverse = 10000.0 ** (-(jnp.arange(half_rot).astype(jnp.float32) * 2.0 / ROT))
    angles = positions[:, None] * inverse[None, :]
    return (jnp.cos(angles)[:, None, :], jnp.sin(angles)[:, None, :])

def rotate(values, cosine_table, sine_table):
    half_rot = ROT // 2
    front_half = values[..., :half_rot]
    back_half = values[..., half_rot:ROT]
    return jnp.concatenate([front_half * cosine_table - back_half * sine_table, back_half * cosine_table + front_half * sine_table, values[..., ROT:]], axis=-1)

def head_attention(queries, key_rows, value_rows, segment):
    columns = jnp.arange(SEQ_LEN)

    def one_block(offset):
        rows_q = lax.dynamic_slice_in_dim(queries, offset, QBLOCK, 0)
        rows_seg = lax.dynamic_slice_in_dim(segment, offset, QBLOCK, 0)
        scores = low_back(jnp.dot(rows_q, key_rows.T, precision=HIGHEST) * HEAD_DIM ** (-0.5))
        places = offset + jnp.arange(QBLOCK)
        allowed = (rows_seg[:, None] == segment[None, :]) & (columns[None, :] <= places[:, None])
        weights_p = low(jax.nn.softmax(jnp.where(allowed, scores, NEG), axis=-1))
        return jnp.dot(weights_p, value_rows, precision=HIGHEST)
    offsets = (jnp.arange(SEQ_LEN // QBLOCK) * QBLOCK).astype(jnp.int32)
    return lax.map(one_block, offsets).reshape(SEQ_LEN, HEAD_DIM)

def forward(tokens, w_qkv, b_qkv, w_out, w_gate_up, w_down, norm_gains, norm_shifts, segments):
    cosine_table, sine_table = rotation_tables()

    def one_sequence(pair_item):
        values_in, segment = pair_item
        normed_a = low(layer_norm(values_in, norm_gains[0], norm_shifts[0]))
        projected = jnp.dot(normed_a, w_qkv.reshape(D, 3 * D), precision=HIGHEST)
        projected = projected.reshape(SEQ_LEN, 3, HEADS, HEAD_DIM) + b_qkv
        projected = low(low_back(projected))
        queries = low(rotate(projected[:, 0], cosine_table, sine_table))
        key_rows = low(rotate(projected[:, 1], cosine_table, sine_table))
        value_rows = projected[:, 2]
        head_fn = jax.checkpoint(lambda triple: head_attention(triple[0], triple[1], triple[2], segment))
        outputs = lax.map(head_fn, (queries.transpose(1, 0, 2), key_rows.transpose(1, 0, 2), value_rows.transpose(1, 0, 2)))
        attended = low_back(low(outputs.transpose(1, 0, 2).reshape(SEQ_LEN, D)))
        middle = values_in + low_back(jnp.dot(attended, w_out, precision=HIGHEST))
        normed_b = low(layer_norm(middle, norm_gains[1], norm_shifts[1]))
        gate_up = low_back(jnp.dot(normed_b, w_gate_up.reshape(D, 2 * FF), precision=HIGHEST))
        gate_up = gate_up.reshape(SEQ_LEN, 2, FF)
        activated = low(jax.nn.silu(gate_up[:, 0]) * gate_up[:, 1])
        return middle + low_back(jnp.dot(activated, w_down, precision=HIGHEST))
    return lax.map(one_sequence, (tokens, segments))

def reference(tokens, segments, w_qkv, b_qkv, w_out, w_gate_up, w_down, norm_gains, norm_shifts, cotangent):
    inputs = [a.astype(jnp.float32) for a in (tokens, w_qkv, b_qkv, w_out, w_gate_up, w_down, norm_gains, norm_shifts)]

    def closed(x_in, wq, bq, wo, wgu, wd, gain_rows, shift_rows):
        return forward(x_in, wq, bq, wo, wgu, wd, gain_rows, shift_rows, segments)
    result, vjp_fn = jax.vjp(closed, *inputs)
    grads = vjp_fn(cotangent.astype(jnp.float32))
    return (result.astype(jnp.bfloat16), grads[0], grads[1], grads[2], grads[3], grads[4], grads[5], grads[6], grads[7])
```

```python
import functools

import jax
import jax.numpy as jnp
from jax import lax
from jax.experimental import pallas as pl
from jax.experimental.pallas import tpu as pltpu
from jax.sharding import Mesh
from jax.sharding import PartitionSpec as P

EPS = 1e-05
NEG = -1e30
ROT = 16
HEAD = 64
SEQ = 2048
WIDTH = 2048
OWN = 64
ROWS = 512
QB = 256
F32 = jnp.float32
BF16 = jnp.bfloat16
MESH_ID = pl.DeviceIdType.MESH
ANY = pl.BlockSpec(memory_space=pl.ANY)
VMEM = pl.BlockSpec(memory_space=pltpu.VMEM)


def place():
    return tuple(lax.axis_index(a) for a in ("z", "x", "yl", "core", "yh"))


def lanes(index, size=128):
    return pl.ds(pl.multiple_of(index * size, size), size)


def rows_at(index, size):
    return pl.ds(pl.multiple_of(index * size, size), size)


def z_peer(d):
    z = lax.axis_index("z")
    return {"z": lax.rem(z + d, 4)}


def x_peer(d):
    x = lax.axis_index("x")
    return {"x": lax.rem(x + d, 4)}


def y_peer(d):
    y = lax.rem(lax.axis_index("yh") * 2 + lax.axis_index("yl") + d, 4)
    return {"yh": y // 2, "yl": lax.rem(y, 2)}


def xy_peer(dx, dy):
    return {**x_peer(dx), **y_peer(dy)}


def sibling():
    return {"core": 1 - lax.axis_index("core")}


Z_PEERS = [functools.partial(z_peer, d) for d in (1, 2, 3)]
X_PEERS = [functools.partial(x_peer, d) for d in (1, 2, 3)]
Y_PEERS = [functools.partial(y_peer, d) for d in (1, 2, 3)]
XY_ALL = [(dx, dy) for dx in range(4) for dy in range(4) if dx or dy]
XY_PEERS = [functools.partial(xy_peer, dx, dy) for dx, dy in XY_ALL]


class Engine:
    def __init__(self, send_sem, recv_sem, local_sem):
        self.sems = (send_sem, recv_sem, local_sem)
        self.remote = 0
        self.locals = 0

    def send(self, src, dst, device):
        i = self.remote
        self.remote += 1
        copy = pltpu.make_async_remote_copy(
            src, dst, self.sems[0].at[i], self.sems[1].at[i], device_id=device, device_id_type=MESH_ID
        )
        copy.start()
        return copy

    def local(self, src, dst):
        i = self.locals
        self.locals += 1
        copy = pltpu.make_async_copy(src, dst, self.sems[2].at[i])
        copy.start()
        return copy


class Op:
    def __init__(self, ins, outs, peers, body, scratch=()):
        self.ins, self.outs, self.peers, self.body, self.scratch = ins, outs, peers, body, scratch


def exchange(name, number, ops, n_remote, n_local):
    peers = []
    for op in ops:
        for peer in op.peers:
            if peer not in peers:
                peers.append(peer)

    def kernel(*refs):
        refs = list(refs)

        def take(count):
            taken = refs[:count]
            del refs[:count]
            return taken

        ins = [take(len(op.ins)) for op in ops]
        outs = [take(len(op.outs)) for op in ops]
        scratch = [take(len(op.scratch)) for op in ops]
        engine = Engine(*refs)
        barrier = pltpu.get_barrier_semaphore()
        for peer in peers:
            pl.semaphore_signal(barrier, 1, device_id=peer(), device_id_type=MESH_ID)
        pl.semaphore_wait(barrier, len(peers))
        running = [op.body(engine, *i, *o, *s) for op, i, o, s in zip(ops, ins, outs, scratch)]
        while running:
            left = []
            for item in running:
                try:
                    next(item)
                    left.append(item)
                except StopIteration:
                    pass
            running = left

    results = pl.pallas_call(
        kernel,
        out_shape=[jax.ShapeDtypeStruct(o[0], o[1]) for op in ops for o in op.outs],
        in_specs=[ANY for op in ops for _ in op.ins],
        out_specs=[o[2] if len(o) > 2 else ANY for op in ops for o in op.outs],
        scratch_shapes=[s for op in ops for s in op.scratch]
        + [
            pltpu.SemaphoreType.DMA((n_remote,)),
            pltpu.SemaphoreType.DMA((n_remote,)),
            pltpu.SemaphoreType.DMA((n_local,)),
        ],
        compiler_params=pltpu.CompilerParams(
            collective_id=number, has_side_effects=True, vmem_limit_bytes=32 * 2**20
        ),
        name=name,
    )(*[i for op in ops for i in op.ins])
    split = []
    for op in ops:
        split.append(tuple(results[: len(op.outs)]))
        results = results[len(op.outs) :]
    return split


def swap_op(values):
    def body(engine, src, dst):
        core = lax.axis_index("core")
        copy = engine.send(src.at[rows_at(1 - core, OWN)], dst, sibling())
        yield
        copy.wait()

    return Op([values], [((OWN, WIDTH), values.dtype)], [sibling], body)


def weight_z_op(piece):
    n = piece.shape[1]

    def body(engine, src, dst):
        z = lax.axis_index("z")
        copies = [engine.local(src.at[z], dst.at[z])]
        for d in (1, 2, 3):
            to = z_peer(d)
            copies.append(engine.send(src.at[to["z"]], dst.at[z], to))
        yield
        for copy in copies:
            copy.wait()

    return Op([piece], [((4, n, 128), piece.dtype)], Z_PEERS, body)


def small_op(packed):
    def body(engine, src, dst):
        z, yh = lax.axis_index("z"), lax.axis_index("yh")
        copies = [engine.local(src, dst.at[z, yh])]
        for d in range(4):
            for e in range(2):
                if d or e:
                    to = {"z": lax.rem(z + d, 4), "yh": lax.rem(yh + e, 2)}
                    copies.append(engine.send(src, dst.at[z, yh], to))
        yield
        for copy in copies:
            copy.wait()

    def partner(d, e):
        return {
            "z": lax.rem(lax.axis_index("z") + d, 4),
            "yh": lax.rem(lax.axis_index("yh") + e, 2),
        }

    peers = [functools.partial(partner, d, e) for d in range(4) for e in range(2) if d or e]
    return Op([packed], [((4, 2) + packed.shape, packed.dtype)], peers, body)


def z_gather_op(block):
    def body(engine, src, dst):
        z = lax.axis_index("z")
        copies = [engine.local(src, dst.at[z])]
        for d in (1, 2, 3):
            copies.append(engine.send(src, dst.at[z], z_peer(d)))
        yield
        for copy in copies:
            copy.wait()

    return Op([block], [((4,) + block.shape, block.dtype)], Z_PEERS, body)


def token_gather_op(block):
    def body(engine, src, dst):
        z, core = lax.axis_index("z"), lax.axis_index("core")
        mine = dst.at[rows_at(z * 2 + core, OWN)]
        first = [engine.send(src, mine, z_peer(d)) for d in (1, 2, 3)]
        rest = [engine.send(src, mine, sibling()), engine.local(src, mine)]
        yield
        for d in (1, 2, 3):
            first[d - 1].wait_recv()
            here = dst.at[rows_at(lax.rem(z + 4 - d, 4) * 2 + core, OWN)]
            rest.append(engine.send(here, here, sibling()))
        yield
        for copy in first:
            copy.wait_send()
        for copy in rest:
            copy.wait()

    return Op([block], [((ROWS, WIDTH), block.dtype)], Z_PEERS + [sibling], body)


def token_scatter_op(partial):
    def body(engine, src, dst, own, other, arrived):
        z, core = lax.axis_index("z"), lax.axis_index("core")
        pairs = []
        for i in range(4):
            base = lax.rem(z + 1 + i, 4) * 2
            there = engine.send(src.at[rows_at(base + 1 - core, OWN)], other.at[i], sibling())
            here = engine.local(src.at[rows_at(base + core, OWN)], own.at[i])
            pairs.append((there, here))
        yield
        sent = []
        for i in range(3):
            pairs[i][0].wait_recv()
            pairs[i][1].wait()
            own[i] = (own[i].astype(F32) + other[i].astype(F32)).astype(BF16)
            sent.append(engine.send(own.at[i], arrived.at[i], z_peer(i + 1)))
        yield
        pairs[3][0].wait_recv()
        pairs[3][1].wait()
        dst[...] = own[3].astype(F32) + other[3].astype(F32)
        for i in range(3):
            sent[i].wait_recv()
            dst[...] += arrived[i].astype(F32)
        for i in range(3):
            sent[i].wait_send()
        for there, _ in pairs:
            there.wait_send()

    scratch = (
        pltpu.VMEM((4, OWN, WIDTH), BF16),
        pltpu.VMEM((4, OWN, WIDTH), BF16),
        pltpu.VMEM((3, OWN, WIDTH), BF16),
    )
    return Op([partial], [((OWN, WIDTH), F32, VMEM)], Z_PEERS + [sibling], body, scratch)


def first_part(n):
    return (n // 2 + 15) // 16 * 16


def weight_xy_op(piece):
    n = piece.shape[1]
    cut = first_part(n)
    head, tail = pl.ds(0, cut), pl.ds(cut, n - cut)

    def body(engine, src, dst):
        x = lax.axis_index("x")
        y = lax.axis_index("yh") * 2 + lax.axis_index("yl")
        local = [engine.local(src.at[zz], dst.at[y, :, lanes(zz * 4 + x)]) for zz in range(4)]
        along_x, along_y = [], []
        for d in (1, 2, 3):
            for zz in range(4):
                along_x.append(engine.send(src.at[zz, head], dst.at[y, head, lanes(zz * 4 + x)], x_peer(d)))
                along_y.append(engine.send(src.at[zz, tail], dst.at[y, tail, lanes(zz * 4 + x)], y_peer(d)))
        yield
        for copy in local:
            copy.wait()
        for copy in along_x:
            copy.wait_recv()
        second = [engine.send(dst.at[y, head], dst.at[y, head], y_peer(d)) for d in (1, 2, 3)]
        for copy in along_y:
            copy.wait_recv()
        for d in (1, 2, 3):
            for zz in range(4):
                block = dst.at[:, tail, lanes(zz * 4 + x)]
                second.append(engine.send(block, block, x_peer(d)))
        yield
        for copy in along_x + along_y:
            copy.wait_send()
        for copy in second:
            copy.wait()

    return Op([piece], [((4, n, WIDTH), piece.dtype)], X_PEERS + Y_PEERS, body)


def items_out_op(values, n):
    def body(engine, src, dst):
        x, yl, yh = lax.axis_index("x"), lax.axis_index("yl"), lax.axis_index("yh")
        y = yh * 2 + yl
        mine = dst.at[:, lanes(x * 4 + yl * 2 + yh)]
        copies = []
        for dx, dy in XY_ALL:
            tx, ty = lax.rem(x + dx, 4), lax.rem(y + dy, 4)
            copies.append(engine.send(src.at[rows_at(ty, n), lanes(tx)], mine, xy_peer(dx, dy)))
        copies.append(engine.local(src.at[rows_at(y, n), lanes(x)], mine))
        yield
        for copy in copies:
            copy.wait()

    return Op([values], [((n, SEQ), values.dtype)], XY_PEERS, body)


def items_back_op(values):
    n = values.shape[0]

    def body(engine, src, dst):
        x, yl, yh = lax.axis_index("x"), lax.axis_index("yl"), lax.axis_index("yh")
        y = yh * 2 + yl
        mine = dst.at[rows_at(y, n), lanes(x)]
        copies = []
        for dx, dy in XY_ALL:
            to = xy_peer(dx, dy)
            copies.append(engine.send(src.at[:, lanes(to["x"] * 4 + to["yl"] * 2 + to["yh"])], mine, to))
        copies.append(engine.local(src.at[:, lanes(x * 4 + yl * 2 + yh)], mine))
        yield
        for copy in copies:
            copy.wait()

    return Op([values], [((4 * n, ROWS), values.dtype)], XY_PEERS, body)


def grad_first_op(grad):
    n = grad.shape[1]
    cut = first_part(n)
    head, tail = pl.ds(0, cut), pl.ds(cut, n - cut)

    def body(engine, src, by_y, by_x):
        copies = []
        for d in (1, 2, 3):
            ty, tx = y_peer(d), x_peer(d)
            copies.append(engine.send(src.at[ty["yh"] * 2 + ty["yl"], head], by_y.at[d - 1], ty))
            for zz in range(4):
                block = src.at[:, tail, lanes(zz * 4 + tx["x"])]
                copies.append(engine.send(block, by_x.at[d - 1, :, :, lanes(zz)], tx))
        yield
        for copy in copies:
            copy.wait()

    outs = [((3, cut, WIDTH), grad.dtype), ((3, 4, n - cut, 512), grad.dtype)]
    return Op([grad], outs, X_PEERS + Y_PEERS, body)


def sum_first(grad, by_y, by_x):
    n = grad.shape[1]
    cut = first_part(n)
    x = lax.axis_index("x")
    y = lax.axis_index("yh") * 2 + lax.axis_index("yl")
    own_y = lax.dynamic_index_in_dim(grad[:, :cut], y, 0, keepdims=False).astype(F32)
    tail = grad[:, cut:].reshape(4, n - cut, 4, 4, 128)
    own_x = lax.dynamic_index_in_dim(tail, x, 3, keepdims=False).reshape(4, n - cut, 512).astype(F32)
    summed_y = own_y + jnp.sum(by_y.astype(F32), axis=0)
    summed_x = own_x + jnp.sum(by_x.astype(F32), axis=0)
    return summed_y.astype(BF16), summed_x.astype(BF16)


def grad_second_op(head_sum, tail_sum):
    cut, rest = head_sum.shape[0], tail_sum.shape[1]

    def body(engine, heads, tails, by_x, by_y):
        copies = []
        for d in (1, 2, 3):
            ty, tx = y_peer(d), x_peer(d)
            copies.append(engine.send(tails.at[ty["yh"] * 2 + ty["yl"]], by_y.at[d - 1], ty))
            for zz in range(4):
                block = heads.at[:, lanes(zz * 4 + tx["x"])]
                copies.append(engine.send(block, by_x.at[d - 1, :, lanes(zz)], tx))
        yield
        for copy in copies:
            copy.wait()

    outs = [((3, cut, 512), BF16), ((3, rest, 512), BF16)]
    return Op([head_sum, tail_sum], outs, X_PEERS + Y_PEERS, body)


def sum_second(head_sum, tail_sum, by_x, by_y):
    cut = head_sum.shape[0]
    x = lax.axis_index("x")
    y = lax.axis_index("yh") * 2 + lax.axis_index("yl")
    own_x = lax.dynamic_index_in_dim(head_sum.reshape(cut, 4, 4, 128), x, 2, keepdims=False)
    own_y = lax.dynamic_index_in_dim(tail_sum, y, 0, keepdims=False)
    heads = own_x.reshape(cut, 512).astype(F32) + jnp.sum(by_x.astype(F32), axis=0)
    tails = own_y.astype(F32) + jnp.sum(by_y.astype(F32), axis=0)
    return jnp.concatenate([heads, tails], axis=0).astype(BF16)


def grad_z_op(summed):
    n = summed.shape[0]

    def body(engine, src, dst):
        z = lax.axis_index("z")
        copies = [engine.local(src.at[:, lanes(z)], dst.at[z])]
        for d in (1, 2, 3):
            to = z_peer(d)
            copies.append(engine.send(src.at[:, lanes(to["z"])], dst.at[z], to))
        yield
        for copy in copies:
            copy.wait()

    return Op([summed], [((4, n, 128), summed.dtype)], Z_PEERS, body)


def hand_back_op(block):
    def body(engine, src, dst):
        core, yh = lax.axis_index("core"), lax.axis_index("yh")
        far = {"core": yh, "yh": 1 - yh}
        near = {"core": yh}
        stays = core == yh
        mine = dst.at[rows_at(core, OWN)]
        i, j = engine.remote, engine.locals
        engine.remote += 4
        engine.locals += 1
        send_sem, recv_sem, local_sem = engine.sems

        def make(to, slot):
            return pltpu.make_async_remote_copy(
                src,
                mine,
                send_sem.at[i + slot],
                recv_sem.at[i + 2 + core],
                device_id=to,
                device_id_type=MESH_ID,
            )

        def arrival(half):
            part = dst.at[rows_at(half, OWN)]
            return pltpu.make_async_remote_copy(
                part, part, send_sem.at[i], recv_sem.at[i + 2 + half], device_id=far, device_id_type=MESH_ID
            )

        make(far, 0).start()

        @pl.when(stays)
        def _():
            pltpu.make_async_copy(src, mine, local_sem.at[j]).start()

        @pl.when(jnp.logical_not(stays))
        def _():
            make(near, 1).start()

        yield
        make(far, 0).wait_send()

        @pl.when(stays)
        def _():
            pltpu.make_async_copy(src, mine, local_sem.at[j]).wait()
            arrival(1 - core).wait_recv()

        @pl.when(jnp.logical_not(stays))
        def _():
            make(near, 1).wait_send()
            arrival(core).wait_recv()
            arrival(1 - core).wait_recv()

    def partner(dc, dh):
        return {
            "core": lax.rem(lax.axis_index("core") + dc, 2),
            "yh": lax.rem(lax.axis_index("yh") + dh, 2),
        }

    peers = [functools.partial(partner, dc, dh) for dc, dh in ((0, 1), (1, 0), (1, 1))]
    return Op([block], [((2 * OWN, WIDTH), block.dtype)], peers, body)


def dot(a, b, dims):
    return lax.dot_general(a, b, ((dims[:1], dims[1:]), ((), ())), preferred_element_type=F32)


def rope(block, cosine, sine):
    front, back = block[:8], block[8:16]
    return jnp.concatenate(
        [front * cosine - back * sine, back * cosine + front * sine, block[16:]], axis=0
    )


def rope_back(block, cosine, sine):
    front, back = block[:8], block[8:16]
    return jnp.concatenate(
        [front * cosine + back * sine, back * cosine - front * sine, block[16:]], axis=0
    )


def masked_scores(scores, start, seg_row, seg_col):
    stop = start + QB

    def hide(first, last, by_segment, causal):
        part = scores[first:last]
        keep = None
        if by_segment:
            keep = seg_col[first:last] == seg_row[:, start:stop]
        if causal:
            key_at = first + lax.broadcasted_iota(jnp.int32, part.shape, 0)
            query_at = start + lax.broadcasted_iota(jnp.int32, part.shape, 1)
            order = key_at <= query_at
            keep = order if keep is None else keep & order
        return jnp.where(keep, part, NEG)

    if start == 0:
        return hide(0, stop, True, True)
    if stop + 127 <= SEQ:
        parts = [hide(0, 128, True, False)]
        if start > 128:
            parts.append(scores[128:start])
        parts.append(hide(start, stop, False, True))
        return jnp.concatenate(parts, axis=0)
    return jnp.concatenate([hide(0, start, True, False), hide(start, stop, True, True)], axis=0)


def attend_kernel(qkv_ref, row_ref, col_ref, cos_ref, sin_ref, o_ref, wide_ref, lse_ref, qk_ref):
    cosine, sine = cos_ref[...], sin_ref[...]
    q_t = rope(qkv_ref[:HEAD].astype(F32), cosine, sine).astype(BF16) * jnp.asarray(0.125, BF16)
    k_t = rope(qkv_ref[HEAD : 2 * HEAD].astype(F32), cosine, sine).astype(BF16)
    v_t = qkv_ref[2 * HEAD :]
    qk_ref[:HEAD] = q_t
    qk_ref[HEAD:] = k_t
    keys = k_t.astype(F32).T.astype(BF16)
    seg_row, seg_col = row_ref[...], col_ref[...]
    for start in range(0, SEQ, QB):
        stop = start + QB
        scores = dot(keys[:stop], q_t[:, start:stop], (1, 0))
        scores = masked_scores(scores, start, seg_row, seg_col)
        top = jnp.max(scores, axis=0, keepdims=True)
        terms = jnp.exp(scores - top)
        total = jnp.sum(terms, axis=0, keepdims=True)
        out = dot(v_t[:, :stop], terms.astype(BF16), (1, 0)) / total
        wide_ref[:, start:stop] = out
        o_ref[:, start:stop] = out.astype(BF16)
        lse_ref[:, start:stop] = top + jnp.log(total)


def attend_back_kernel(
    qk_ref, qkv_ref, do_ref, wide_ref, lse_ref, row_ref, col_ref, cos_ref, sin_ref, out_ref, dk_ref, dv_ref
):
    cosine, sine = cos_ref[...], sin_ref[...]
    q_t, k_t, do_t = qk_ref[:HEAD], qk_ref[HEAD:], do_ref[...]
    queries = q_t.astype(F32).T.astype(BF16)
    keys = k_t.astype(F32).T.astype(BF16)
    values = qkv_ref[2 * HEAD :].astype(F32).T.astype(BF16)
    grads = do_t.astype(F32).T.astype(BF16)
    centre = jnp.sum(do_t.astype(F32) * wide_ref[...], axis=0, keepdims=True)
    lse = lse_ref[...]
    seg_row, seg_col = row_ref[...], col_ref[...]
    dk_ref[...] = jnp.zeros_like(dk_ref)
    dv_ref[...] = jnp.zeros_like(dv_ref)
    dq_parts = []
    for start in range(0, SEQ, QB):
        stop = start + QB
        scores = dot(keys[:stop], q_t[:, start:stop], (1, 0))
        scores = masked_scores(scores, start, seg_row, seg_col)
        probs = jnp.exp(scores - lse[:, start:stop])
        d_probs = dot(values[:stop], do_t[:, start:stop], (1, 0))
        d_scores = (probs * (d_probs - centre[:, start:stop])).astype(BF16)
        dv_ref[:stop] += dot(probs.astype(BF16), grads[start:stop], (1, 0))
        dk_ref[:stop] += dot(d_scores, queries[start:stop], (1, 0))
        dq_parts.append(dot(k_t[:, :stop], d_scores, (1, 0)) * 0.125)
    out_ref[:HEAD] = rope_back(jnp.concatenate(dq_parts, axis=1), cosine, sine).astype(BF16)
    out_ref[HEAD : 2 * HEAD] = rope_back(dk_ref[...].T, cosine, sine).astype(BF16)
    out_ref[2 * HEAD :] = dv_ref[...].T.astype(BF16)


def kernel_here(kernel, name, out_shape, scratch=()):
    return pl.pallas_call(
        kernel,
        out_shape=out_shape,
        scratch_shapes=scratch,
        compiler_params=pltpu.CompilerParams(vmem_limit_bytes=48 * 2**20),
        name=name,
    )


def rotation_tables():
    half = ROT // 2
    positions = jnp.arange(SEQ).astype(F32)
    inverse = 10000.0 ** (-(jnp.arange(half).astype(F32) * 2.0 / ROT))
    angles = inverse[:, None] * positions[None, :]
    return jnp.cos(angles), jnp.sin(angles)


def layer_norm(values, gain_row, shift_row):
    row_mean = jnp.mean(values, axis=-1, keepdims=True)
    centred = values - row_mean
    variance = jnp.mean(centred * centred, axis=-1, keepdims=True)
    rstd = lax.rsqrt(variance + EPS)
    normed = centred * rstd
    return normed * gain_row + shift_row, normed, rstd


def norm_back(gradient, normed, rstd, gain_row):
    shaped = gradient * gain_row
    centre = (
        shaped
        - jnp.mean(shaped, axis=-1, keepdims=True)
        - normed * jnp.mean(shaped * normed, axis=-1, keepdims=True)
    )
    return centre * rstd, jnp.sum(gradient * normed, axis=0), jnp.sum(gradient, axis=0)


def local(tokens, segments, w_qkv, b_qkv, w_out, w_gate_up, w_down, norm_gains, norm_shifts, cotangent):
    z, x, yl, core, yh = place()

    def pick(values, axis, index):
        return lax.dynamic_index_in_dim(values, index, axis, keepdims=False)

    piece = lax.dynamic_slice_in_dim(w_qkv, x * 128, 128, 0).reshape(128, 3, 4, 2, 2, HEAD)
    piece = pick(pick(piece, 3, core), 3, yl)
    piece_qkv = piece.transpose(2, 1, 3, 0).reshape(4, 192, 128)
    piece = w_out.reshape(4, 2, 2, 64, 4, 128)
    piece_out = pick(pick(pick(piece, 1, core), 1, yl), 2, x)
    piece = lax.dynamic_slice_in_dim(w_gate_up, x * 128, 128, 0).reshape(128, 2, 4, 2, 2, 176)
    piece = pick(pick(piece, 3, core), 3, yl)
    piece_gu = piece.transpose(2, 1, 3, 0).reshape(4, 352, 128)
    piece = w_down.reshape(4, 2, 2, 176, 4, 128)
    piece_down = pick(pick(pick(piece, 1, core), 1, yl), 2, x)

    packed = jnp.concatenate(
        [
            norm_gains,
            norm_shifts,
            jnp.pad(b_qkv.reshape(-1), (0, 256)).reshape(2, 512),
            jnp.zeros((10, 512), BF16),
        ],
        axis=0,
    )
    token_block, grad_block = tokens[0], cotangent[0]
    got = exchange(
        "start",
        1,
        [
            swap_op(token_block),
            swap_op(grad_block),
            small_op(packed),
            z_gather_op(segments.reshape(16, 128)),
            weight_z_op(piece_qkv),
            weight_z_op(piece_out),
            weight_z_op(piece_gu),
            weight_z_op(piece_down),
        ],
        32,
        8,
    )
    (swapped_x,), (swapped_dy,), (small,), (all_segments,) = got[:4]
    (z_qkv,), (z_out,), (z_gu,), (z_down,) = got[4:]

    stays = core == yh
    x_own = jnp.where(stays, lax.dynamic_slice_in_dim(token_block, core * OWN, OWN, 0), swapped_x).astype(F32)
    dy_own = jnp.where(stays, lax.dynamic_slice_in_dim(grad_block, core * OWN, OWN, 0), swapped_dy)
    wide = small[:, 0, :4].transpose(1, 0, 2).reshape(4, WIDTH).astype(F32)
    gains, shifts = wide[:2], wide[2:]
    bias = small[:, :, 4:6].reshape(4, 2, 1024)[:, :, :768].reshape(4, 2, 3, 4, 2, 2, 16)
    bias = pick(pick(bias, 3, z), 3, core)
    bias = bias.transpose(1, 3, 2, 0, 4).reshape(768, 1).astype(F32)
    item_segments = pick(all_segments, 0, x).reshape(1, SEQ)
    segment_column = item_segments.reshape(SEQ, 1)
    cosine, sine = rotation_tables()

    h1_full, normed_a, rstd_a = layer_norm(x_own, gains[:1], shifts[:1])
    (h1,), (m_qkv,) = exchange(
        "gather_h1", 2, [token_gather_op(h1_full.astype(BF16)), weight_xy_op(z_qkv)], 64, 8
    )
    m_qkv = m_qkv.reshape(768, WIDTH)
    qkv_t = (dot(m_qkv, h1, (1, 1)) + bias).astype(BF16)

    (item_qkv,), (dy,), (m_out,) = exchange(
        "to_items", 3, [items_out_op(qkv_t, 192), token_gather_op(dy_own), weight_xy_op(z_out)], 72, 8
    )
    m_out = m_out.reshape(256, WIDTH)
    o_item, o_wide, lse, qk_item = kernel_here(
        attend_kernel,
        "attend",
        [
            jax.ShapeDtypeStruct((HEAD, SEQ), BF16),
            jax.ShapeDtypeStruct((HEAD, SEQ), F32),
            jax.ShapeDtypeStruct((1, SEQ), F32),
            jax.ShapeDtypeStruct((2 * HEAD, SEQ), BF16),
        ],
    )(item_qkv, item_segments, segment_column, cosine, sine)
    ((o_t,),) = exchange("from_items", 4, [items_back_op(o_item)], 16, 2)

    part = dot(o_t, m_out, (0, 0)).astype(BF16)
    (attn_own,), (m_down,) = exchange(
        "sum_out", 5, [token_scatter_op(part), weight_xy_op(z_down)], 64, 12
    )
    middle = x_own + attn_own
    h2_full, normed_b, rstd_b = layer_norm(middle, gains[1:], shifts[1:])
    (h2,), (m_gu,) = exchange(
        "gather_h2", 6, [token_gather_op(h2_full.astype(BF16)), weight_xy_op(z_gu)], 64, 8
    )
    m_gu = m_gu.reshape(1408, WIDTH)
    m_down = m_down.reshape(704, WIDTH)

    gate_up = dot(m_gu, h2, (1, 1)).reshape(4, 2, 176, ROWS)
    gate, up = gate_up[:, 0], gate_up[:, 1]
    sigmoid = jax.nn.sigmoid(gate)
    silu = gate * sigmoid
    act = (silu * up).astype(BF16).reshape(704, ROWS)
    d_act = dot(m_down, dy, (1, 1)).reshape(4, 176, ROWS)
    d_gate = d_act * up * sigmoid * (1.0 + gate * (1.0 - sigmoid))
    d_gu = jnp.stack([d_gate, d_act * silu], axis=1).astype(BF16).reshape(1408, ROWS)
    mlp_part = dot(act, m_down, (0, 0)).astype(BF16)
    back_part = dot(d_gu, m_gu, (0, 0)).astype(BF16)
    (mlp_own,), (dh2_own,) = exchange(
        "sum_mlp", 7, [token_scatter_op(back_part), token_scatter_op(mlp_part)][::-1], 16, 8
    )
    g_gu = dot(d_gu, h2, (1, 0)).astype(BF16).reshape(4, 352, WIDTH)
    g_down = dot(act, dy, (1, 0)).astype(BF16).reshape(4, 176, WIDTH)

    out_own = (middle + mlp_own).astype(BF16)
    back_b, gain_b, shift_b = norm_back(dh2_own, normed_b, rstd_b, gains[1:])
    d_middle = dy_own.astype(F32) + back_b
    (dz,), first_gu, first_down = exchange(
        "gather_dz",
        8,
        [token_gather_op(d_middle.astype(BF16)), grad_first_op(g_gu), grad_first_op(g_down)],
        48,
        2,
    )
    d_o = dot(m_out, dz, (1, 1)).astype(BF16)
    g_out = dot(o_t, dz, (1, 0)).astype(BF16).reshape(4, 64, WIDTH)
    sums_gu = sum_first(g_gu, *first_gu)
    sums_down = sum_first(g_down, *first_down)
    (do_item,), second_gu, second_down = exchange(
        "do_items",
        9,
        [items_out_op(d_o, HEAD), grad_second_op(*sums_gu), grad_second_op(*sums_down)],
        64,
        2,
    )
    d_item = kernel_here(
        attend_back_kernel,
        "attend_back",
        jax.ShapeDtypeStruct((192, SEQ), BF16),
        [pltpu.VMEM((SEQ, HEAD), F32), pltpu.VMEM((SEQ, HEAD), F32)],
    )(qk_item, item_qkv, do_item, o_wide, lse, item_segments, segment_column, cosine, sine)
    mlp_sum = jnp.concatenate([sum_second(*sums_gu, *second_gu), sum_second(*sums_down, *second_down)], axis=0)
    (d_qkv,), (mlp_z,) = exchange("d_items", 10, [items_back_op(d_item), grad_z_op(mlp_sum)], 24, 2)
    mlp_all = lax.all_gather(mlp_z, ("x", "yl", "core"), axis=0)

    back_part = dot(d_qkv, m_qkv, (0, 0)).astype(BF16)
    g_qkv = dot(d_qkv, h1, (1, 0)).astype(BF16).reshape(4, 192, WIDTH)
    g_bias = jnp.sum(d_qkv.astype(F32), axis=1)
    (dh1_own,), first_qkv, first_out = exchange(
        "sum_dh1", 11, [token_scatter_op(back_part), grad_first_op(g_qkv), grad_first_op(g_out)], 48, 8
    )
    back_a, gain_a, shift_a = norm_back(dh1_own, normed_a, rstd_a, gains[:1])
    grad_own = (d_middle + back_a).astype(BF16)
    sums_qkv = sum_first(g_qkv, *first_qkv)
    sums_out = sum_first(g_out, *first_out)
    (layer_out,), (grad_tokens,), second_qkv, second_out = exchange(
        "hand_back",
        12,
        [hand_back_op(out_own), hand_back_op(grad_own), grad_second_op(*sums_qkv), grad_second_op(*sums_out)],
        48,
        2,
    )
    attn_sum = jnp.concatenate([sum_second(*sums_qkv, *second_qkv), sum_second(*sums_out, *second_out)], axis=0)
    ((attn_z,),) = exchange("grad_z", 13, [grad_z_op(attn_sum)], 4, 2)
    attn_all = lax.all_gather(attn_z, ("x", "yl", "core"), axis=0)

    bias_slots = jnp.arange(8)[:, None] == z * 2 + core
    norms = jnp.stack([gain_a, gain_b, shift_a, shift_b])
    vector = jnp.concatenate([norms.reshape(-1), jnp.where(bias_slots, g_bias[None], 0.0).reshape(-1)])
    vector = lax.psum(vector, ("z", "x", "yl", "core", "yh"))
    norms = lax.dynamic_slice_in_dim(vector[: 4 * WIDTH].reshape(4, WIDTH), z * 512, 512, 1)
    bias_all = vector[4 * WIDTH :].reshape(4, 2, 2, 2, 3, 4, 16)
    bias_all = pick(pick(bias_all, 2, yh), 4, z)
    grad_bias = bias_all.transpose(3, 0, 1, 2, 4).reshape(3, 16, 16)

    mlp_all = mlp_all.reshape(4, 2, 2, 4, 528, 128).astype(F32)
    attn_all = attn_all.reshape(4, 2, 2, 4, 256, 128).astype(F32)
    out_qkv = attn_all[..., :192, :].reshape(4, 2, 2, 4, 3, 64, 128)
    out_qkv = out_qkv.transpose(0, 6, 4, 3, 2, 1, 5).reshape(512, 3, 1024)
    out_out = attn_all[..., 192:, :].transpose(3, 2, 1, 4, 0, 5).reshape(1024, 512)
    out_gu = mlp_all[..., :352, :].reshape(4, 2, 2, 4, 2, 176, 128)
    out_gu = out_gu.transpose(0, 6, 4, 3, 2, 1, 5).reshape(512, 2, 2816)
    out_down = mlp_all[..., 352:, :].transpose(3, 2, 1, 4, 0, 5).reshape(2816, 512)
    return (
        layer_out[None],
        grad_tokens.astype(F32)[None],
        out_qkv,
        grad_bias,
        out_out,
        out_gu,
        out_down,
        norms[:2],
        norms[2:],
    )


def solution(mesh):
    fine = Mesh(mesh.devices.reshape(4, 4, 2, 2, 2), ("z", "x", "yl", "core", "yh"))
    ctx = ("x", "yl", "core")
    return jax.shard_map(
        local,
        mesh=fine,
        in_specs=(
            P("z", ctx, None),
            P("z", None),
            P("z", None, "yh"),
            P(None, "yh", "z"),
            P("yh", "z"),
            P("z", None, "yh"),
            P("yh", "z"),
            P(None, "z"),
            P(None, "z"),
            P("z", ctx, None),
        ),
        out_specs=(
            P("z", ctx, None),
            P("z", ctx, None),
            P("z", None, "yh"),
            P(None, "yh", "z"),
            P("yh", "z"),
            P("z", None, "yh"),
            P("yh", "z"),
            P(None, "z"),
            P(None, "z"),
        ),
        check_vma=False,
    )
```

```python
import functools

import jax
import jax.numpy as jnp
from jax import lax
from jax.experimental import pallas as pl
from jax.experimental.pallas import tpu as pltpu
from jax.sharding import Mesh
from jax.sharding import PartitionSpec as P

EPS = 1e-05
NEG = -1e30
ROT = 16
HEAD = 64
SEQ = 2048
WIDTH = 2048
OWN = 64
ROWS = 512
QB = 256
F32 = jnp.float32
BF16 = jnp.bfloat16
MESH_ID = pl.DeviceIdType.MESH
ANY = pl.BlockSpec(memory_space=pl.ANY)
VMEM = pl.BlockSpec(memory_space=pltpu.VMEM)


def place():
    return tuple(lax.axis_index(a) for a in ("z", "x", "yl", "core", "yh"))


def lanes(index, size=128):
    return pl.ds(pl.multiple_of(index * size, size), size)


def rows_at(index, size):
    return pl.ds(pl.multiple_of(index * size, size), size)


def z_peer(d):
    z = lax.axis_index("z")
    return {"z": lax.rem(z + d, 4)}


def x_peer(d):
    x = lax.axis_index("x")
    return {"x": lax.rem(x + d, 4)}


def y_peer(d):
    y = lax.rem(lax.axis_index("yh") * 2 + lax.axis_index("yl") + d, 4)
    return {"yh": y // 2, "yl": lax.rem(y, 2)}


def xy_peer(dx, dy):
    return {**x_peer(dx), **y_peer(dy)}


def sibling():
    return {"core": 1 - lax.axis_index("core")}


Z_PEERS = [functools.partial(z_peer, d) for d in (1, 2, 3)]
X_PEERS = [functools.partial(x_peer, d) for d in (1, 2, 3)]
Y_PEERS = [functools.partial(y_peer, d) for d in (1, 2, 3)]
XY_ALL = [(dx, dy) for dx in range(4) for dy in range(4) if dx or dy]
XY_PEERS = [functools.partial(xy_peer, dx, dy) for dx, dy in XY_ALL]


class Engine:
    def __init__(self, send_sem, recv_sem, local_sem):
        self.sems = (send_sem, recv_sem, local_sem)
        self.remote = 0
        self.locals = 0

    def send(self, src, dst, device):
        i = self.remote
        self.remote += 1
        copy = pltpu.make_async_remote_copy(
            src, dst, self.sems[0].at[i], self.sems[1].at[i], device_id=device, device_id_type=MESH_ID
        )
        copy.start()
        return copy

    def local(self, src, dst):
        i = self.locals
        self.locals += 1
        copy = pltpu.make_async_copy(src, dst, self.sems[2].at[i])
        copy.start()
        return copy


class Op:
    def __init__(self, ins, outs, peers, body, scratch=()):
        self.ins, self.outs, self.peers, self.body, self.scratch = ins, outs, peers, body, scratch


def exchange(name, number, ops, n_remote, n_local):
    peers = []
    for op in ops:
        for peer in op.peers:
            if peer not in peers:
                peers.append(peer)

    def kernel(*refs):
        refs = list(refs)

        def take(count):
            taken = refs[:count]
            del refs[:count]
            return taken

        ins = [take(len(op.ins)) for op in ops]
        outs = [take(len(op.outs)) for op in ops]
        scratch = [take(len(op.scratch)) for op in ops]
        engine = Engine(*refs)
        barrier = pltpu.get_barrier_semaphore()
        for peer in peers:
            pl.semaphore_signal(barrier, 1, device_id=peer(), device_id_type=MESH_ID)
        pl.semaphore_wait(barrier, len(peers))
        running = [op.body(engine, *i, *o, *s) for op, i, o, s in zip(ops, ins, outs, scratch)]
        while running:
            left = []
            for item in running:
                try:
                    next(item)
                    left.append(item)
                except StopIteration:
                    pass
            running = left

    given = [i if isinstance(i, tuple) else (i, ANY) for op in ops for i in op.ins]
    results = pl.pallas_call(
        kernel,
        out_shape=[jax.ShapeDtypeStruct(o[0], o[1]) for op in ops for o in op.outs],
        in_specs=[spec for _, spec in given],
        out_specs=[o[2] if len(o) > 2 else ANY for op in ops for o in op.outs],
        scratch_shapes=[s for op in ops for s in op.scratch]
        + [
            pltpu.SemaphoreType.DMA((n_remote,)),
            pltpu.SemaphoreType.DMA((n_remote,)),
            pltpu.SemaphoreType.DMA((n_local,)),
        ],
        compiler_params=pltpu.CompilerParams(
            collective_id=number, has_side_effects=True, vmem_limit_bytes=48 * 2**20
        ),
        name=name,
    )(*[value for value, _ in given])
    split = []
    for op in ops:
        split.append(tuple(results[: len(op.outs)]))
        results = results[len(op.outs) :]
    return split


def swap_op(values):
    def body(engine, src, dst):
        core = lax.axis_index("core")
        copy = engine.send(src.at[rows_at(1 - core, OWN)], dst, sibling())
        yield
        copy.wait()

    return Op([values], [((OWN, WIDTH), values.dtype)], [sibling], body)


def send_pieces(engine, pieces, dst):
    z = lax.axis_index("z")
    copies = [engine.local(pieces(z), dst.at[z])]
    for d in (1, 2, 3):
        to = z_peer(d)
        copies.append(engine.send(pieces(to["z"]), dst.at[z], to))
    return copies


def weight_rows_op(weight, n):
    def body(engine, src, dst):
        x, yl, core = (lax.axis_index(a) for a in ("x", "yl", "core"))

        def pieces(z):
            return src.at[rows_at((z * 2 + core) * 2 + yl, n), lanes(x)]

        copies = send_pieces(engine, pieces, dst)
        yield
        for copy in copies:
            copy.wait()

    return Op([weight], [((4, n, 128), weight.dtype)], Z_PEERS, body)


def weight_columns_op(weight, n, middle):
    groups = weight.shape[1] if middle else weight.shape[0]
    features = weight.shape[2]
    joined = not middle
    block = (128, groups, features) if middle else (groups, 128, features)

    def body(engine, src, *refs):
        dsts = refs[: 1 if joined else groups]
        held, turned, cut = refs[len(dsts) :]
        x, yl, core = (lax.axis_index(a) for a in ("x", "yl", "core"))
        rows = rows_at(x, 128)
        load = engine.local(src.at[rows] if middle else src.at[:, rows], held)
        yield
        load.wait()
        copies = []
        for g in range(groups):
            turned[...] = (held[:, g, :] if middle else held[g]).astype(F32).T
            for z in range(4):
                rows = rows_at((z * 2 + core) * 2 + yl, n)
                cut[g, z] = turned[rows, :].astype(BF16)
        for g in range(groups):
            dst = dsts[0].at[:, pl.ds(g * n, n)] if joined else dsts[g]
            copies += send_pieces(engine, lambda z: cut.at[g, z], dst)
        yield
        for copy in copies:
            copy.wait()

    if joined:
        outs = [((4, groups * n, 128), BF16)]
    else:
        outs = [((4, n, 128), BF16)] * groups
    scratch = (pltpu.VMEM(block, BF16), pltpu.VMEM((features, 128), F32), pltpu.VMEM((groups, 4, n, 128), BF16))
    return Op([weight], outs, Z_PEERS, body, scratch)


def small_op(packed):
    def body(engine, src, dst):
        z, yh = lax.axis_index("z"), lax.axis_index("yh")
        copies = [engine.local(src, dst.at[z, yh])]
        for d in range(4):
            for e in range(2):
                if d or e:
                    to = {"z": lax.rem(z + d, 4), "yh": lax.rem(yh + e, 2)}
                    copies.append(engine.send(src, dst.at[z, yh], to))
        yield
        for copy in copies:
            copy.wait()

    def partner(d, e):
        return {
            "z": lax.rem(lax.axis_index("z") + d, 4),
            "yh": lax.rem(lax.axis_index("yh") + e, 2),
        }

    peers = [functools.partial(partner, d, e) for d in range(4) for e in range(2) if d or e]
    return Op([packed], [((4, 2) + packed.shape, packed.dtype)], peers, body)


def z_gather_op(block):
    def body(engine, src, dst):
        z = lax.axis_index("z")
        copies = [engine.local(src, dst.at[z])]
        for d in (1, 2, 3):
            copies.append(engine.send(src, dst.at[z], z_peer(d)))
        yield
        for copy in copies:
            copy.wait()

    return Op([block], [((4,) + block.shape, block.dtype)], Z_PEERS, body)


def token_gather_op(block):
    def body(engine, src, dst):
        z, core = lax.axis_index("z"), lax.axis_index("core")
        mine = dst.at[rows_at(z * 2 + core, OWN)]
        first = [engine.send(src, mine, z_peer(d)) for d in (1, 2, 3)]
        rest = [engine.send(src, mine, sibling()), engine.local(src, mine)]
        yield
        for d in (1, 2, 3):
            first[d - 1].wait_recv()
            here = dst.at[rows_at(lax.rem(z + 4 - d, 4) * 2 + core, OWN)]
            rest.append(engine.send(here, here, sibling()))
        yield
        for copy in first:
            copy.wait_send()
        for copy in rest:
            copy.wait()

    return Op([block], [((ROWS, WIDTH), block.dtype)], Z_PEERS + [sibling], body)


def token_scatter_op(partial):
    def body(engine, src, dst, own, other, arrived):
        z, core = lax.axis_index("z"), lax.axis_index("core")
        pairs = []
        for i in range(4):
            base = lax.rem(z + 1 + i, 4) * 2
            there = engine.send(src.at[rows_at(base + 1 - core, OWN)], other.at[i], sibling())
            here = engine.local(src.at[rows_at(base + core, OWN)], own.at[i])
            pairs.append((there, here))
        yield
        sent = []
        for i in range(3):
            pairs[i][0].wait_recv()
            pairs[i][1].wait()
            own[i] = (own[i].astype(F32) + other[i].astype(F32)).astype(BF16)
            sent.append(engine.send(own.at[i], arrived.at[i], z_peer(i + 1)))
        yield
        pairs[3][0].wait_recv()
        pairs[3][1].wait()
        dst[...] = own[3].astype(F32) + other[3].astype(F32)
        for i in range(3):
            sent[i].wait_recv()
            dst[...] += arrived[i].astype(F32)
        for i in range(3):
            sent[i].wait_send()
        for there, _ in pairs:
            there.wait_send()

    scratch = (
        pltpu.VMEM((4, OWN, WIDTH), BF16),
        pltpu.VMEM((4, OWN, WIDTH), BF16),
        pltpu.VMEM((3, OWN, WIDTH), BF16),
    )
    return Op([partial], [((OWN, WIDTH), F32, VMEM)], Z_PEERS + [sibling], body, scratch)


def first_part(n):
    return (n // 2 + 15) // 16 * 16


def weight_xy_op(piece):
    n = piece.shape[1]
    cut = first_part(n)
    head, tail = pl.ds(0, cut), pl.ds(cut, n - cut)

    def body(engine, src, dst):
        x = lax.axis_index("x")
        y = lax.axis_index("yh") * 2 + lax.axis_index("yl")
        local = [engine.local(src.at[zz], dst.at[y, :, lanes(zz * 4 + x)]) for zz in range(4)]
        along_x, along_y = [], []
        for d in (1, 2, 3):
            for zz in range(4):
                along_x.append(engine.send(src.at[zz, head], dst.at[y, head, lanes(zz * 4 + x)], x_peer(d)))
                along_y.append(engine.send(src.at[zz, tail], dst.at[y, tail, lanes(zz * 4 + x)], y_peer(d)))
        yield
        for copy in local:
            copy.wait()
        for copy in along_x:
            copy.wait_recv()
        left_y, left_x = lax.rem(y + 3, 4), lax.rem(x + 3, 4)
        right_y, right_x = lax.rem(y + 1, 4), lax.rem(x + 1, 4)
        ring_y = [engine.send(dst.at[y, head], dst.at[y, head], y_peer(d)) for d in (1, 3)]
        for copy in along_y:
            copy.wait_recv()

        def column(zz, xx):
            return dst.at[:, tail, lanes(zz * 4 + xx)]

        ring_x = [[engine.send(column(zz, x), column(zz, x), x_peer(d)) for zz in range(4)] for d in (1, 3)]
        yield
        rest = []
        half = first_part(cut)
        early, late = pl.ds(0, half), pl.ds(half, cut - half)
        ring_y[0].wait_recv()
        rest.append(engine.send(dst.at[left_y, early], dst.at[left_y, early], y_peer(1)))
        ring_y[1].wait_recv()
        rest.append(engine.send(dst.at[right_y, late], dst.at[right_y, late], y_peer(3)))
        for zz in range(2):
            ring_x[0][zz].wait_recv()
            rest.append(engine.send(column(zz, left_x), column(zz, left_x), x_peer(1)))
            ring_x[1][zz + 2].wait_recv()
            rest.append(engine.send(column(zz + 2, right_x), column(zz + 2, right_x), x_peer(3)))
        yield
        for zz in range(2):
            ring_x[0][zz + 2].wait_recv()
            ring_x[1][zz].wait_recv()
        for copy in along_x + along_y + ring_y + ring_x[0] + ring_x[1]:
            copy.wait_send()
        for copy in rest:
            copy.wait()

    return Op([piece], [((4, n, WIDTH), piece.dtype)], X_PEERS + Y_PEERS, body)


def send_items(engine, src, dst, n):
    x, yl, yh = (lax.axis_index(a) for a in ("x", "yl", "yh"))
    y = yh * 2 + yl
    mine = dst.at[:, lanes(x * 4 + yl * 2 + yh)]
    copies = []
    for dx, dy in XY_ALL:
        tx, ty = lax.rem(x + dx, 4), lax.rem(y + dy, 4)
        copies.append(engine.send(src.at[rows_at(ty, n), lanes(tx)], mine, xy_peer(dx, dy)))
    copies.append(engine.local(src.at[rows_at(y, n), lanes(x)], mine))
    return copies


def return_items(engine, src, dst, n):
    x, yl, yh = (lax.axis_index(a) for a in ("x", "yl", "yh"))
    mine = dst.at[rows_at(yh * 2 + yl, n), lanes(x)]
    copies = []
    for dx, dy in XY_ALL:
        to = xy_peer(dx, dy)
        copies.append(engine.send(src.at[:, lanes(to["x"] * 4 + to["yl"] * 2 + to["yh"])], mine, to))
    copies.append(engine.local(src.at[:, lanes(x * 4 + yl * 2 + yh)], mine))
    return copies


def attention_op(qkv_t, seg_row, seg_col, cosine, sine):
    def body(engine, src, row, col, cos, sin, dst, kept, wide, lse, item, out):
        copies = send_items(engine, src, item, 3 * HEAD)
        yield
        for copy in copies[:-1]:
            copy.wait_recv()
        copies[-1].wait()
        yield
        attend(item, row, col, cos, sin, out, wide, lse, kept)
        for copy in copies[:-1]:
            copy.wait_send()
        back = return_items(engine, out, dst, HEAD)
        yield
        yield
        for copy in back:
            copy.wait()

    outs = [
        ((4 * HEAD, ROWS), BF16),
        ((3 * HEAD, SEQ), BF16, VMEM),
        ((HEAD, SEQ), F32, VMEM),
        ((1, SEQ), F32, VMEM),
    ]
    scratch = (pltpu.VMEM((3 * HEAD, SEQ), BF16), pltpu.VMEM((HEAD, SEQ), BF16))
    ins = [qkv_t] + [(value, VMEM) for value in (seg_row, seg_col, cosine, sine)]
    return Op(ins, outs, XY_PEERS, body, scratch)


def attention_back_op(d_o, kept, wide, lse, seg_row, seg_col, cosine, sine):
    def body(engine, src, kept, wide, lse, row, col, cos, sin, dst, item, out, dk, dv):
        copies = send_items(engine, src, item, HEAD)
        yield
        for copy in copies[:-1]:
            copy.wait_recv()
        copies[-1].wait()
        yield
        attend_back(kept, item, wide, lse, row, col, cos, sin, out, dk, dv)
        for copy in copies[:-1]:
            copy.wait_send()
        back = return_items(engine, out, dst, 3 * HEAD)
        yield
        yield
        for copy in back:
            copy.wait()

    scratch = (
        pltpu.VMEM((HEAD, SEQ), BF16),
        pltpu.VMEM((3 * HEAD, SEQ), BF16),
        pltpu.VMEM((SEQ, HEAD), F32),
        pltpu.VMEM((SEQ, HEAD), F32),
    )
    ins = [d_o] + [(value, VMEM) for value in (kept, wide, lse, seg_row, seg_col, cosine, sine)]
    return Op(ins, [((12 * HEAD, ROWS), BF16)], XY_PEERS, body, scratch)


def add_up(total, own, others, index, rows, width):
    def step(i, carry):
        here = (*index, rows_at(i, 16), slice(0, width))
        value = own[here].astype(F32)
        for k in range(3):
            value += others[(k, *here)].astype(F32)
        total[here] = value.astype(total.dtype)
        return carry

    lax.fori_loop(0, rows // 16, step, 0)


def grad_first_op(grad):
    n = grad.shape[1]
    cut = first_part(n)
    rest = n - cut
    head, tail = pl.ds(0, cut), pl.ds(cut, rest)

    def body(engine, src, sum_y, sum_x, by_y, by_x, own_y, own_x):
        x = lax.axis_index("x")
        y = lax.axis_index("yh") * 2 + lax.axis_index("yl")
        copies, local = [], [engine.local(src.at[y, head], own_y)]
        for zz in range(4):
            local.append(engine.local(src.at[:, tail, lanes(zz * 4 + x)], own_x.at[:, :, lanes(zz)]))
        for d in (1, 2, 3):
            ty, tx = y_peer(d), x_peer(d)
            copies.append(engine.send(src.at[ty["yh"] * 2 + ty["yl"], head], by_y.at[d - 1], ty))
            for zz in range(4):
                block = src.at[:, tail, lanes(zz * 4 + tx["x"])]
                copies.append(engine.send(block, by_x.at[d - 1, :, :, lanes(zz)], tx))
        yield
        for copy in local:
            copy.wait()
        yield
        for copy in copies:
            copy.wait_recv()
        add_up(sum_y, own_y, by_y, (), cut, WIDTH)
        for q in range(4):
            add_up(sum_x, own_x, by_x, (q,), rest, 512)
        for copy in copies:
            copy.wait_send()

    outs = [((cut, WIDTH), BF16, VMEM), ((4, rest, 512), BF16, VMEM)]
    scratch = (
        pltpu.VMEM((3, cut, WIDTH), BF16),
        pltpu.VMEM((3, 4, rest, 512), BF16),
        pltpu.VMEM((cut, WIDTH), BF16),
        pltpu.VMEM((4, rest, 512), BF16),
    )
    return Op([grad], outs, X_PEERS + Y_PEERS, body, scratch)


def grad_rest_op(sum_y, sum_x, gather=False):
    cut, rest = sum_y.shape[0], sum_x.shape[1]
    n = cut + rest

    def body(engine, heads, tails, dst, by_x, by_y, own, total, *held):
        x, yl, core = (lax.axis_index(a) for a in ("x", "yl", "core"))
        y = lax.axis_index("yh") * 2 + yl
        copies, local = [], [engine.local(tails.at[y], own.at[pl.ds(cut, rest)])]
        for zz in range(4):
            local.append(engine.local(heads.at[:, lanes(zz * 4 + x)], own.at[pl.ds(0, cut), lanes(zz)]))
        for d in (1, 2, 3):
            ty, tx = y_peer(d), x_peer(d)
            copies.append(engine.send(tails.at[ty["yh"] * 2 + ty["yl"]], by_y.at[d - 1], ty))
            for zz in range(4):
                block = heads.at[:, lanes(zz * 4 + tx["x"])]
                copies.append(engine.send(block, by_x.at[d - 1, :, lanes(zz)], tx))
        yield
        for copy in local:
            copy.wait()
        for copy in copies:
            copy.wait_recv()
        add_up(total.at[pl.ds(0, cut)], own.at[pl.ds(0, cut)], by_x, (), cut, 512)
        add_up(total.at[pl.ds(cut, rest)], own.at[pl.ds(cut, rest)], by_y, (), rest, 512)
        landing = held[0] if gather else dst
        moved = send_pieces(engine, lambda z: total.at[:, lanes(z)], landing)
        for copy in copies:
            copy.wait_send()
        yield
        for copy in moved:
            copy.wait()
        if not gather:
            return

        def slot(xx, ll, cc):
            return (xx * 2 + ll) * 2 + cc

        first, second = pl.ds(0, 2), pl.ds(2, 2)
        me = slot(x, yl, core)
        partner = {"yl": 1 - yl}
        there = sibling()
        done = [engine.local(landing, dst.at[me]), engine.send(landing, dst.at[me], there)]
        to_y = engine.send(landing.at[first], dst.at[me, first], partner)
        to_x = [engine.send(landing.at[second], dst.at[me, second], x_peer(d)) for d in (1, 2, 3)]
        yield
        done[0].wait()
        final = []

        def pass_on(index, part):
            block = dst.at[index, part]
            done.append(engine.send(block, block, there))

        for d in (1, 2, 3):
            block = dst.at[me, first]
            final.append((slot(lax.rem(x + 4 - d, 4), yl, core), first, engine.send(block, block, x_peer(d))))
        block = dst.at[me, second]
        final.append((slot(x, 1 - yl, core), second, engine.send(block, block, partner)))
        to_y.wait_recv()
        other = slot(x, 1 - yl, core)
        for d in (1, 2, 3):
            block = dst.at[other, first]
            final.append((slot(lax.rem(x + 4 - d, 4), 1 - yl, core), first, engine.send(block, block, x_peer(d))))
        pass_on(other, first)
        for d in (1, 2, 3):
            to_x[d - 1].wait_recv()
            source = lax.rem(x + 4 - d, 4)
            block = dst.at[slot(source, yl, core), second]
            final.append((slot(source, 1 - yl, core), second, engine.send(block, block, partner)))
            pass_on(slot(source, yl, core), second)
        yield
        for index, part, copy in final:
            copy.wait_recv()
            pass_on(index, part)
        yield
        for copy in [to_y] + to_x + [c for _, _, c in final]:
            copy.wait_send()
        for copy in done[1:]:
            copy.wait()

    shape = (4, n, 128)
    scratch = [
        pltpu.VMEM((3, cut, 512), BF16),
        pltpu.VMEM((3, rest, 512), BF16),
        pltpu.VMEM((n, 512), BF16),
        pltpu.VMEM((n, 512), BF16),
    ]
    peers = X_PEERS + Y_PEERS + Z_PEERS
    if gather:
        scratch.append(pltpu.VMEM(shape, BF16))
        shape = (16,) + shape
        peers = peers + [sibling, other_yl]
    return Op([sum_y, sum_x], [(shape, BF16)], peers, body, tuple(scratch))


def other_yl():
    return {"yl": 1 - lax.axis_index("yl")}


def group_peer(dz, dc):
    return {
        "z": lax.rem(lax.axis_index("z") + dz, 4),
        "core": lax.rem(lax.axis_index("core") + dc, 2),
    }


GROUP_ALL = [(dz, dc) for dz in range(4) for dc in range(2) if dz or dc]
GROUP_PEERS = [functools.partial(group_peer, dz, dc) for dz, dc in GROUP_ALL]


def small_sum_op(norms, bias):
    def body(engine, norms, bias, norm_sum, bias_all, by_group, by_x, by_y):
        z, x, yl, core, yh = place()
        y = yh * 2 + yl
        me = z * 2 + core
        first = []
        for dz, dc in GROUP_ALL:
            to = group_peer(dz, dc)
            first.append(engine.send(norms.at[:, lanes(to["z"], 512)], by_group.at[me], to))
        mine = engine.local(norms.at[:, lanes(z, 512)], by_group.at[me])
        yield
        mine.wait()
        for copy in first:
            copy.wait()
        by_x[x, :, :512] = sum(by_group[k] for k in range(8))
        by_x[x, :, 512:] = bias[...]
        second = [engine.send(by_x.at[x], by_x.at[x], x_peer(d)) for d in (1, 2, 3)]
        yield
        for copy in second:
            copy.wait()
        by_y[y] = sum(by_x[k] for k in range(4))
        third = [engine.send(by_y.at[y], by_y.at[y], y_peer(d)) for d in (1, 2, 3)]
        yield
        for copy in third:
            copy.wait()
        total = sum(by_y[k] for k in range(4))
        norm_sum[...] = total[:, :512]
        bias_all[me] = total[:, 512:]
        last = [engine.send(bias_all.at[me], bias_all.at[me], group_peer(dz, dc)) for dz, dc in GROUP_ALL]
        yield
        for copy in last:
            copy.wait()

    outs = [((8, 512), F32, VMEM), ((8, 8, 128), F32, VMEM)]
    scratch = (
        pltpu.VMEM((8, 8, 512), F32),
        pltpu.VMEM((4, 8, 640), F32),
        pltpu.VMEM((4, 8, 640), F32),
    )
    return Op([(norms, VMEM), (bias, VMEM)], outs, GROUP_PEERS + X_PEERS + Y_PEERS, body, scratch)


def hand_back_op(block):
    def body(engine, src, dst):
        core, yh = lax.axis_index("core"), lax.axis_index("yh")
        far = {"core": yh, "yh": 1 - yh}
        near = {"core": yh}
        stays = core == yh
        mine = dst.at[rows_at(core, OWN)]
        i, j = engine.remote, engine.locals
        engine.remote += 4
        engine.locals += 1
        send_sem, recv_sem, local_sem = engine.sems

        def make(to, slot):
            return pltpu.make_async_remote_copy(
                src,
                mine,
                send_sem.at[i + slot],
                recv_sem.at[i + 2 + core],
                device_id=to,
                device_id_type=MESH_ID,
            )

        def arrival(half):
            part = dst.at[rows_at(half, OWN)]
            return pltpu.make_async_remote_copy(
                part, part, send_sem.at[i], recv_sem.at[i + 2 + half], device_id=far, device_id_type=MESH_ID
            )

        make(far, 0).start()

        @pl.when(stays)
        def _():
            pltpu.make_async_copy(src, mine, local_sem.at[j]).start()

        @pl.when(jnp.logical_not(stays))
        def _():
            make(near, 1).start()

        yield
        make(far, 0).wait_send()

        @pl.when(stays)
        def _():
            pltpu.make_async_copy(src, mine, local_sem.at[j]).wait()
            arrival(1 - core).wait_recv()

        @pl.when(jnp.logical_not(stays))
        def _():
            make(near, 1).wait_send()
            arrival(core).wait_recv()
            arrival(1 - core).wait_recv()

    def partner(dc, dh):
        return {
            "core": lax.rem(lax.axis_index("core") + dc, 2),
            "yh": lax.rem(lax.axis_index("yh") + dh, 2),
        }

    peers = [functools.partial(partner, dc, dh) for dc, dh in ((0, 1), (1, 0), (1, 1))]
    return Op([block], [((2 * OWN, WIDTH), block.dtype)], peers, body)


def dot(a, b, dims):
    return lax.dot_general(a, b, ((dims[:1], dims[1:]), ((), ())), preferred_element_type=F32)


def rope(block, cosine, sine):
    front, back = block[:8], block[8:16]
    return jnp.concatenate(
        [front * cosine - back * sine, back * cosine + front * sine, block[16:]], axis=0
    )


def rope_back(block, cosine, sine):
    front, back = block[:8], block[8:16]
    return jnp.concatenate(
        [front * cosine + back * sine, back * cosine - front * sine, block[16:]], axis=0
    )


def masked_scores(scores, start, seg_row, seg_col):
    stop = start + QB

    def hide(first, last, by_segment, causal):
        part = scores[first:last]
        keep = None
        if by_segment:
            keep = seg_col[first:last] == seg_row[:, start:stop]
        if causal:
            key_at = first + lax.broadcasted_iota(jnp.int32, part.shape, 0)
            query_at = start + lax.broadcasted_iota(jnp.int32, part.shape, 1)
            order = key_at <= query_at
            keep = order if keep is None else keep & order
        return jnp.where(keep, part, NEG)

    if start == 0:
        return hide(0, stop, True, True)
    if stop + 127 <= SEQ:
        parts = [hide(0, 128, True, False)]
        if start > 128:
            parts.append(scores[128:start])
        parts.append(hide(start, stop, False, True))
        return jnp.concatenate(parts, axis=0)
    return jnp.concatenate([hide(0, start, True, False), hide(start, stop, True, True)], axis=0)


def attend(qkv_ref, row_ref, col_ref, cos_ref, sin_ref, o_ref, wide_ref, lse_ref, kept_ref):
    cosine, sine = cos_ref[...], sin_ref[...]
    q_t = rope(qkv_ref[:HEAD].astype(F32), cosine, sine).astype(BF16) * jnp.asarray(0.125, BF16)
    k_t = rope(qkv_ref[HEAD : 2 * HEAD].astype(F32), cosine, sine).astype(BF16)
    v_t = qkv_ref[2 * HEAD :]
    kept_ref[:HEAD] = q_t
    kept_ref[HEAD : 2 * HEAD] = k_t
    kept_ref[2 * HEAD :] = v_t
    keys = k_t.astype(F32).T.astype(BF16)
    seg_row, seg_col = row_ref[...], col_ref[...]
    for start in range(0, SEQ, QB):
        stop = start + QB
        scores = dot(keys[:stop], q_t[:, start:stop], (1, 0))
        scores = masked_scores(scores, start, seg_row, seg_col)
        top = jnp.max(scores, axis=0, keepdims=True)
        terms = jnp.exp(scores - top)
        total = jnp.sum(terms, axis=0, keepdims=True)
        out = dot(v_t[:, :stop], terms.astype(BF16), (1, 0)) / total
        wide_ref[:, start:stop] = out
        o_ref[:, start:stop] = out.astype(BF16)
        lse_ref[:, start:stop] = top + jnp.log(total)


def attend_back(kept_ref, do_ref, wide_ref, lse_ref, row_ref, col_ref, cos_ref, sin_ref, out_ref, dk_ref, dv_ref):
    cosine, sine = cos_ref[...], sin_ref[...]
    q_t, k_t, do_t = kept_ref[:HEAD], kept_ref[HEAD : 2 * HEAD], do_ref[...]
    queries = q_t.astype(F32).T.astype(BF16)
    keys = k_t.astype(F32).T.astype(BF16)
    values = kept_ref[2 * HEAD :].astype(F32).T.astype(BF16)
    grads = do_t.astype(F32).T.astype(BF16)
    centre = jnp.sum(do_t.astype(F32) * wide_ref[...], axis=0, keepdims=True)
    lse = lse_ref[...]
    seg_row, seg_col = row_ref[...], col_ref[...]
    dk_ref[...] = jnp.zeros_like(dk_ref)
    dv_ref[...] = jnp.zeros_like(dv_ref)
    dq_parts = []
    for start in range(0, SEQ, QB):
        stop = start + QB
        scores = dot(keys[:stop], q_t[:, start:stop], (1, 0))
        scores = masked_scores(scores, start, seg_row, seg_col)
        probs = jnp.exp(scores - lse[:, start:stop])
        d_probs = dot(values[:stop], do_t[:, start:stop], (1, 0))
        d_scores = (probs * (d_probs - centre[:, start:stop])).astype(BF16)
        dv_ref[:stop] += dot(probs.astype(BF16), grads[start:stop], (1, 0))
        dk_ref[:stop] += dot(d_scores, queries[start:stop], (1, 0))
        dq_parts.append(dot(k_t[:, :stop], d_scores, (1, 0)) * 0.125)
    out_ref[:HEAD] = rope_back(jnp.concatenate(dq_parts, axis=1), cosine, sine).astype(BF16)
    out_ref[HEAD : 2 * HEAD] = rope_back(dk_ref[...].T, cosine, sine).astype(BF16)
    out_ref[2 * HEAD :] = dv_ref[...].T.astype(BF16)


def assemble_kernel(mlp_ref, attn_ref, gu_ref, down_ref, qkv_ref, out_ref, turned):
    for g in range(2):
        for zz in range(4):
            for core in range(2):
                for yl in range(2):
                    row = zz * 704 + core * 352 + yl * 176
                    block = mlp_ref[0, yl * 2 + core, zz, g * 176 : (g + 1) * 176]
                    turned[row : row + 176, :] = block.astype(F32)
        for t in range(22):
            gu_ref[:, g, t * 128 : (t + 1) * 128] = turned[t * 128 : (t + 1) * 128, :].T
    for zz in range(4):
        for core in range(2):
            for yl in range(2):
                row = zz * 704 + core * 352 + yl * 176
                down_ref[row : row + 176, :] = mlp_ref[0, yl * 2 + core, zz, 352:].astype(F32)
                row = zz * 256 + core * 128 + yl * 64
                out_ref[row : row + 32, :] = attn_ref[0, yl * 2 + core, zz, 96:128].astype(F32)
                out_ref[row + 32 : row + 64, :] = attn_ref[0, yl * 2 + core, zz, 224:].astype(F32)
            for part in range(3):
                pieces = []
                for yl in range(2):
                    for row in (part * 64, part * 64 + 32):
                        row = row if row < 96 else row + 32
                        pieces.append(attn_ref[0, yl * 2 + core, zz, row : row + 32])
                block = jnp.concatenate(pieces, axis=0)
                column = zz * 256 + core * 128
                qkv_ref[part, :, column : column + 128] = block.astype(F32).T


def assemble(mlp_all, attn_all):
    mlp_all = mlp_all.reshape(4, 4, 4, 528, 128)
    attn_all = attn_all.reshape(4, 4, 4, 256, 128)
    return pl.pallas_call(
        assemble_kernel,
        grid=(4,),
        in_specs=[
            pl.BlockSpec((1, 4, 4, 528, 128), lambda i: (i, 0, 0, 0, 0)),
            pl.BlockSpec((1, 4, 4, 256, 128), lambda i: (i, 0, 0, 0, 0)),
        ],
        out_specs=[
            pl.BlockSpec((128, 2, 2816), lambda i: (i, 0, 0)),
            pl.BlockSpec((2816, 128), lambda i: (0, i)),
            pl.BlockSpec((3, 128, 1024), lambda i: (0, i, 0)),
            pl.BlockSpec((1024, 128), lambda i: (0, i)),
        ],
        out_shape=[
            jax.ShapeDtypeStruct((512, 2, 2816), F32),
            jax.ShapeDtypeStruct((2816, 512), F32),
            jax.ShapeDtypeStruct((3, 512, 1024), F32),
            jax.ShapeDtypeStruct((1024, 512), F32),
        ],
        scratch_shapes=[pltpu.VMEM((2816, 128), F32)],
        compiler_params=pltpu.CompilerParams(vmem_limit_bytes=48 * 2**20),
        name="assemble",
    )(mlp_all, attn_all)


def rotation_tables():
    half = ROT // 2
    positions = jnp.arange(SEQ).astype(F32)
    inverse = 10000.0 ** (-(jnp.arange(half).astype(F32) * 2.0 / ROT))
    angles = inverse[:, None] * positions[None, :]
    return jnp.cos(angles), jnp.sin(angles)


def layer_norm(values, gain_row, shift_row):
    row_mean = jnp.mean(values, axis=-1, keepdims=True)
    centred = values - row_mean
    variance = jnp.mean(centred * centred, axis=-1, keepdims=True)
    rstd = lax.rsqrt(variance + EPS)
    normed = centred * rstd
    return normed * gain_row + shift_row, normed, rstd


def norm_back(gradient, normed, rstd, gain_row):
    shaped = gradient * gain_row
    centre = (
        shaped
        - jnp.mean(shaped, axis=-1, keepdims=True)
        - normed * jnp.mean(shaped * normed, axis=-1, keepdims=True)
    )
    return centre * rstd, jnp.sum(gradient * normed, axis=0), jnp.sum(gradient, axis=0)


def local(tokens, segments, w_qkv, b_qkv, w_out, w_gate_up, w_down, norm_gains, norm_shifts, cotangent):
    z, x, yl, core, yh = place()

    def pick(values, axis, index):
        return lax.dynamic_index_in_dim(values, index, axis, keepdims=False)

    packed = jnp.concatenate(
        [
            norm_gains,
            norm_shifts,
            jnp.pad(b_qkv.reshape(-1), (0, 256)).reshape(2, 512),
            jnp.zeros((10, 512), BF16),
        ],
        axis=0,
    )
    token_block, grad_block = tokens[0], cotangent[0]
    got = exchange(
        "start",
        1,
        [
            swap_op(token_block),
            swap_op(grad_block),
            small_op(packed),
            z_gather_op(segments.reshape(16, 128)),
            weight_columns_op(w_qkv.transpose(1, 0, 2), HEAD, False),
            weight_rows_op(w_out, 64),
            weight_rows_op(w_down, 176),
            weight_columns_op(w_gate_up, 176, True),
        ],
        48,
        16,
    )
    (swapped_x,), (swapped_dy,), (small,), (all_segments,) = got[:4]
    (z_qkv,), (z_out,), (z_down,), (z_gate, z_up) = got[4:]

    stays = core == yh
    x_own = jnp.where(stays, lax.dynamic_slice_in_dim(token_block, core * OWN, OWN, 0), swapped_x).astype(F32)
    dy_own = jnp.where(stays, lax.dynamic_slice_in_dim(grad_block, core * OWN, OWN, 0), swapped_dy)
    wide = small[:, 0, :4].transpose(1, 0, 2).reshape(4, WIDTH).astype(F32)
    gains, shifts = wide[:2], wide[2:]
    bias = small[:, :, 4:6].reshape(4, 2, 1024)[:, :, :768].reshape(4, 2, 3, 4, 2, 2, 16)
    bias = pick(pick(bias, 3, z), 3, core)
    bias = bias.transpose(1, 3, 2, 0, 4).reshape(768, 1).astype(F32)
    item_segments = pick(all_segments, 0, x).reshape(1, SEQ)
    segment_column = item_segments.reshape(SEQ, 1)
    cosine, sine = rotation_tables()

    h1_full, normed_a, rstd_a = layer_norm(x_own, gains[:1], shifts[:1])
    (m_qkv,), (h1,) = exchange(
        "gather_h1", 2, [weight_xy_op(z_qkv), token_gather_op(h1_full.astype(BF16))], 64, 8
    )
    m_qkv = m_qkv.reshape(768, WIDTH)
    qkv_t = (dot(m_qkv, h1, (1, 1)) + bias).astype(BF16)

    attention, (dy,), (m_out,), (m_down,) = exchange(
        "attention",
        3,
        [
            attention_op(qkv_t, item_segments, segment_column, cosine, sine),
            token_gather_op(dy_own),
            weight_xy_op(z_out),
            weight_xy_op(z_down),
        ],
        144,
        16,
    )
    o_t, kept, o_wide, lse = attention
    m_out = m_out.reshape(256, WIDTH)
    m_down = m_down.reshape(704, WIDTH)

    part = dot(o_t, m_out, (0, 0)).astype(BF16)
    (m_gate,), (attn_own,) = exchange("sum_out", 4, [weight_xy_op(z_gate), token_scatter_op(part)], 64, 12)
    middle = x_own + attn_own
    h2_full, normed_b, rstd_b = layer_norm(middle, gains[1:], shifts[1:])
    (m_up,), (h2,) = exchange(
        "gather_h2", 5, [weight_xy_op(z_up), token_gather_op(h2_full.astype(BF16))], 64, 8
    )
    m_gate = m_gate.reshape(704, WIDTH)
    m_up = m_up.reshape(704, WIDTH)

    gate, up = dot(m_gate, h2, (1, 1)), dot(m_up, h2, (1, 1))
    sigmoid = jax.nn.sigmoid(gate)
    silu = gate * sigmoid
    act = (silu * up).astype(BF16)
    d_act = dot(m_down, dy, (1, 1))
    d_gate = (d_act * up * sigmoid * (1.0 + gate * (1.0 - sigmoid))).astype(BF16)
    d_up = (d_act * silu).astype(BF16)
    mlp_part = dot(act, m_down, (0, 0)).astype(BF16)
    back_part = (dot(d_gate, m_gate, (0, 0)) + dot(d_up, m_up, (0, 0))).astype(BF16)

    def weight_grad(a, b):
        return dot(a, b, (1, 0)).astype(BF16).reshape(4, a.shape[0] // 4, WIDTH)

    g_gate, g_up, g_down = weight_grad(d_gate, h2), weight_grad(d_up, h2), weight_grad(act, dy)
    (dh2_own,), (mlp_own,), first_gate, first_down = exchange(
        "sum_mlp",
        6,
        [token_scatter_op(back_part), token_scatter_op(mlp_part), grad_first_op(g_gate), grad_first_op(g_down)],
        48,
        24,
    )

    out_own = (middle + mlp_own).astype(BF16)
    back_b, gain_b, shift_b = norm_back(dh2_own, normed_b, rstd_b, gains[1:])
    d_middle = dy_own.astype(F32) + back_b
    (dz,), first_up, (z_down,) = exchange(
        "gather_dz",
        7,
        [token_gather_op(d_middle.astype(BF16)), grad_first_op(g_up), grad_rest_op(*first_down)],
        48,
        24,
    )
    d_o = dot(m_out, dz, (1, 1)).astype(BF16)
    g_out = weight_grad(o_t, dz)
    (d_qkv,), (z_gate,), (z_up,), (layer_out,) = exchange(
        "attention_back",
        8,
        [
            attention_back_op(d_o, kept, o_wide, lse, item_segments, segment_column, cosine, sine),
            grad_rest_op(*first_gate),
            grad_rest_op(*first_up),
            hand_back_op(out_own),
        ],
        96,
        24,
    )
    mlp_z = jnp.concatenate([z_gate, z_up, z_down], axis=1)
    mlp_all = lax.all_gather(mlp_z, ("x", "yl", "core"), axis=0)

    back_part = dot(d_qkv, m_qkv, (0, 0)).astype(BF16)
    g_qkv = weight_grad(d_qkv, h1)
    g_bias = jnp.sum(d_qkv.astype(F32), axis=1)
    (dh1_own,), first_qkv, first_out = exchange(
        "sum_dh1", 9, [token_scatter_op(back_part), grad_first_op(g_qkv), grad_first_op(g_out)], 48, 24
    )
    back_a, gain_a, shift_a = norm_back(dh1_own, normed_a, rstd_a, gains[:1])
    grad_own = (d_middle + back_a).astype(BF16)
    norms = jnp.pad(jnp.stack([gain_a, gain_b, shift_a, shift_b]), ((0, 4), (0, 0)))
    first_attn = [jnp.concatenate([a, b], axis=-2) for a, b in zip(first_qkv, first_out)]
    (attn_all,), (norm_sum, bias_all), (grad_tokens,) = exchange(
        "finish",
        10,
        [
            grad_rest_op(*first_attn, gather=True),
            small_sum_op(norms, jnp.pad(g_bias, (0, 256)).reshape(8, 128)),
            hand_back_op(grad_own),
        ],
        80,
        24,
    )
    attn_all = attn_all.reshape(16, 4, 256, 128)
    bias_all = bias_all.reshape(8, 1024)[:, :768].reshape(4, 2, 2, 2, 3, 4, 16)
    bias_all = pick(pick(bias_all, 2, yh), 4, z)
    grad_bias = bias_all.transpose(3, 0, 1, 2, 4).reshape(3, 16, 16)
    out_gu, out_down, out_qkv, out_out = assemble(mlp_all, attn_all)
    return (
        layer_out[None],
        grad_tokens.astype(F32)[None],
        out_qkv.transpose(1, 0, 2),
        grad_bias,
        out_out,
        out_gu,
        out_down,
        norm_sum[:2],
        norm_sum[2:4],
    )


def solution(mesh):
    fine = Mesh(mesh.devices.reshape(4, 4, 2, 2, 2), ("z", "x", "yl", "core", "yh"))
    ctx = ("x", "yl", "core")
    return jax.shard_map(
        local,
        mesh=fine,
        in_specs=(
            P("z", ctx, None),
            P("z", None),
            P("z", None, "yh"),
            P(None, "yh", "z"),
            P("yh", "z"),
            P("z", None, "yh"),
            P("yh", "z"),
            P(None, "z"),
            P(None, "z"),
            P("z", ctx, None),
        ),
        out_specs=(
            P("z", ctx, None),
            P("z", ctx, None),
            P("z", None, "yh"),
            P(None, "yh", "z"),
            P("yh", "z"),
            P("z", None, "yh"),
            P("yh", "z"),
            P(None, "z"),
            P(None, "z"),
        ),
        check_vma=False,
    )
```

```python
import functools

import jax
import jax.numpy as jnp
from jax import lax
from jax.experimental import pallas as pl
from jax.experimental.pallas import tpu as pltpu
from jax.sharding import Mesh
from jax.sharding import PartitionSpec as P

EPS = 1e-05
NEG = -1e30
ROT = 16
HEAD = 64
SEQ = 2048
WIDTH = 2048
OWN = 64
ROWS = 512
QB = 256
F32 = jnp.float32
BF16 = jnp.bfloat16
MESH_ID = pl.DeviceIdType.MESH
ANY = pl.BlockSpec(memory_space=pl.ANY)
VMEM = pl.BlockSpec(memory_space=pltpu.VMEM)


def place():
    return tuple(lax.axis_index(a) for a in ("z", "x", "yl", "core", "yh"))


def lanes(index, size=128):
    return pl.ds(pl.multiple_of(index * size, size), size)


def rows_at(index, size):
    return pl.ds(pl.multiple_of(index * size, size), size)


def z_peer(d):
    z = lax.axis_index("z")
    return {"z": lax.rem(z + d, 4)}


def x_peer(d):
    x = lax.axis_index("x")
    return {"x": lax.rem(x + d, 4)}


def y_peer(d):
    y = lax.rem(lax.axis_index("yh") * 2 + lax.axis_index("yl") + d, 4)
    return {"yh": y // 2, "yl": lax.rem(y, 2)}


def xy_peer(dx, dy):
    return {**x_peer(dx), **y_peer(dy)}


def sibling():
    return {"core": 1 - lax.axis_index("core")}


Z_PEERS = [functools.partial(z_peer, d) for d in (1, 2, 3)]
X_PEERS = [functools.partial(x_peer, d) for d in (1, 2, 3)]
Y_PEERS = [functools.partial(y_peer, d) for d in (1, 2, 3)]
XY_ALL = [(dx, dy) for dx in range(4) for dy in range(4) if dx or dy]
XY_PEERS = [functools.partial(xy_peer, dx, dy) for dx, dy in XY_ALL]


class Engine:
    def __init__(self, send_sem, recv_sem, local_sem):
        self.sems = (send_sem, recv_sem, local_sem)
        self.remote = 0
        self.locals = 0

    def send(self, src, dst, device):
        i = self.remote
        self.remote += 1
        copy = pltpu.make_async_remote_copy(
            src, dst, self.sems[0].at[i], self.sems[1].at[i], device_id=device, device_id_type=MESH_ID
        )
        copy.start()
        return copy

    def local(self, src, dst):
        i = self.locals
        self.locals += 1
        copy = pltpu.make_async_copy(src, dst, self.sems[2].at[i])
        copy.start()
        return copy


class Op:
    def __init__(self, ins, outs, peers, body, scratch=()):
        self.ins, self.outs, self.peers, self.body, self.scratch = ins, outs, peers, body, scratch


def greet(peers):
    barrier = pltpu.get_barrier_semaphore()
    for peer in peers:
        pl.semaphore_signal(barrier, 1, device_id=peer(), device_id_type=MESH_ID)
    pl.semaphore_wait(barrier, len(peers))


def semaphores(n_remote, n_local):
    return [
        pltpu.SemaphoreType.DMA((n_remote,)),
        pltpu.SemaphoreType.DMA((n_remote,)),
        pltpu.SemaphoreType.DMA((n_local,)),
    ]


def exchange(name, number, ops, n_remote, n_local):
    peers = []
    for op in ops:
        for peer in op.peers:
            if peer not in peers:
                peers.append(peer)

    def kernel(*refs):
        refs = list(refs)

        def take(count):
            taken = refs[:count]
            del refs[:count]
            return taken

        ins = [take(len(op.ins)) for op in ops]
        outs = [take(len(op.outs)) for op in ops]
        scratch = [take(len(op.scratch)) for op in ops]
        engine = Engine(*refs)
        greet(peers)
        running = [op.body(engine, *i, *o, *s) for op, i, o, s in zip(ops, ins, outs, scratch)]
        while running:
            left = []
            for item in running:
                try:
                    next(item)
                    left.append(item)
                except StopIteration:
                    pass
            running = left

    given = [i if isinstance(i, tuple) else (i, ANY) for op in ops for i in op.ins]
    results = pl.pallas_call(
        kernel,
        out_shape=[jax.ShapeDtypeStruct(o[0], o[1]) for op in ops for o in op.outs],
        in_specs=[spec for _, spec in given],
        out_specs=[o[2] if len(o) > 2 else ANY for op in ops for o in op.outs],
        scratch_shapes=[s for op in ops for s in op.scratch]
        + semaphores(n_remote, n_local),
        compiler_params=pltpu.CompilerParams(
            collective_id=number, has_side_effects=True, vmem_limit_bytes=48 * 2**20
        ),
        name=name,
    )(*[value for value, _ in given])
    split = []
    for op in ops:
        split.append(tuple(results[: len(op.outs)]))
        results = results[len(op.outs) :]
    return split


def spread(values):
    return jnp.concatenate(
        [values[:, (a * 4 + b) * 128 : (a * 4 + b + 1) * 128] for b in range(4) for a in range(4)], axis=1
    )


def finish(thread):
    for _ in thread:
        pass


def send_pieces(engine, pieces, slots):
    z = lax.axis_index("z")
    copies = [engine.local(pieces(z), slots(z))]
    for d in (1, 2, 3):
        to = z_peer(d)
        copies.append(engine.send(pieces(to["z"]), slots(z), to))
    return copies


def gather_tokens(engine, src, dst):
    z, core = lax.axis_index("z"), lax.axis_index("core")
    mine = dst.at[rows_at(z * 2 + core, OWN)]
    first = [engine.send(src, mine, z_peer(d)) for d in (1, 2, 3)]
    rest = [engine.send(src, mine, sibling()), engine.local(src, mine)]
    yield
    for d in (1, 2, 3):
        first[d - 1].wait_recv()
        here = dst.at[rows_at(lax.rem(z + 4 - d, 4) * 2 + core, OWN)]
        rest.append(engine.send(here, here, sibling()))
    yield
    for copy in first:
        copy.wait_send()
    for copy in rest:
        copy.wait()


def gather_weight(engine, src, dst):
    n = src.shape[0]
    top = first_part(n)
    head, tail = pl.ds(0, top), pl.ds(top, n - top)
    x = lax.axis_index("x")
    y = lax.axis_index("yh") * 2 + lax.axis_index("yl")
    left_y, left_x = lax.rem(y + 3, 4), lax.rem(x + 3, 4)
    right_y, right_x = lax.rem(y + 1, 4), lax.rem(x + 1, 4)
    mine = lanes(x, 512)
    local = engine.local(src, dst.at[y, :, mine])
    along_x = [engine.send(src.at[head], dst.at[y, head, mine], x_peer(d)) for d in (1, 2, 3)]
    along_y = [engine.send(src.at[tail], dst.at[y, tail, mine], y_peer(d)) for d in (1, 2, 3)]
    yield
    local.wait()
    for copy in along_x:
        copy.wait_recv()
    ring_y = [engine.send(dst.at[y, head], dst.at[y, head], y_peer(d)) for d in (1, 3)]
    for copy in along_y:
        copy.wait_recv()
    ring_x = [engine.send(dst.at[:, tail, mine], dst.at[:, tail, mine], x_peer(d)) for d in (1, 3)]
    yield
    rest = []
    half = first_part(top)
    early, late = pl.ds(0, half), pl.ds(half, top - half)
    ring_y[0].wait_recv()
    rest.append(engine.send(dst.at[left_y, early], dst.at[left_y, early], y_peer(1)))
    ring_y[1].wait_recv()
    rest.append(engine.send(dst.at[right_y, late], dst.at[right_y, late], y_peer(3)))
    ring_x[0].wait_recv()
    block = dst.at[:, tail, lanes(left_x * 2, 256)]
    rest.append(engine.send(block, block, x_peer(1)))
    ring_x[1].wait_recv()
    block = dst.at[:, tail, lanes(right_x * 2 + 1, 256)]
    rest.append(engine.send(block, block, x_peer(3)))
    yield
    for copy in along_x + along_y + ring_y + ring_x:
        copy.wait_send()
    for copy in rest:
        copy.wait()


def token_gather_op(block):
    return Op([block], [((ROWS, WIDTH), block.dtype)], Z_PEERS + [sibling], gather_tokens)


def token_scatter_op(partial):
    def body(engine, src, dst, own, other, arrived):
        z, core = lax.axis_index("z"), lax.axis_index("core")
        pairs = []
        for i in range(4):
            base = lax.rem(z + 1 + i, 4) * 2
            there = engine.send(src.at[rows_at(base + 1 - core, OWN)], other.at[i], sibling())
            here = engine.local(src.at[rows_at(base + core, OWN)], own.at[i])
            pairs.append((there, here))
        yield
        sent = []
        for i in range(3):
            pairs[i][0].wait_recv()
            pairs[i][1].wait()
            own[i] = (own[i].astype(F32) + other[i].astype(F32)).astype(BF16)
            sent.append(engine.send(own.at[i], arrived.at[i], z_peer(i + 1)))
        yield
        pairs[3][0].wait_recv()
        pairs[3][1].wait()
        dst[...] = own[3].astype(F32) + other[3].astype(F32)
        for i in range(3):
            sent[i].wait_recv()
            dst[...] += arrived[i].astype(F32)
        for i in range(3):
            sent[i].wait_send()
        for there, _ in pairs:
            there.wait_send()

    scratch = (
        pltpu.VMEM((4, OWN, WIDTH), BF16),
        pltpu.VMEM((4, OWN, WIDTH), BF16),
        pltpu.VMEM((3, OWN, WIDTH), BF16),
    )
    return Op([partial], [((OWN, WIDTH), F32, VMEM)], Z_PEERS + [sibling], body, scratch)


def first_part(n):
    return (n // 2 + 15) // 16 * 16


def send_items(engine, src, dst, n):
    x, yl, yh = (lax.axis_index(a) for a in ("x", "yl", "yh"))
    y = yh * 2 + yl
    mine = dst.at[:, lanes(x * 4 + yl * 2 + yh)]
    copies = []
    for dx, dy in XY_ALL:
        tx, ty = lax.rem(x + dx, 4), lax.rem(y + dy, 4)
        copies.append(engine.send(src.at[rows_at(ty, n), lanes(tx)], mine, xy_peer(dx, dy)))
    copies.append(engine.local(src.at[rows_at(y, n), lanes(x)], mine))
    return copies


def return_items(engine, src, dst, n):
    x, yl, yh = (lax.axis_index(a) for a in ("x", "yl", "yh"))
    mine = dst.at[rows_at(yh * 2 + yl, n), lanes(x)]
    copies = []
    for dx, dy in XY_ALL:
        to = xy_peer(dx, dy)
        copies.append(engine.send(src.at[:, lanes(to["x"] * 4 + to["yl"] * 2 + to["yh"])], mine, to))
    copies.append(engine.local(src.at[:, lanes(x * 4 + yl * 2 + yh)], mine))
    return copies


def attention_back_op(d_o, kept, wide, lse, seg_row, seg_col, cosine, sine):
    def body(engine, src, kept, wide, lse, row, col, cos, sin, dst, item, out, dk, dv):
        copies = send_items(engine, src, item, HEAD)
        yield
        for copy in copies[:-1]:
            copy.wait_recv()
        copies[-1].wait()
        yield
        attend_back(kept, item, wide, lse, row, col, cos, sin, out, dk, dv)
        for copy in copies[:-1]:
            copy.wait_send()
        back = return_items(engine, out, dst, 3 * HEAD)
        yield
        yield
        for copy in back:
            copy.wait()

    scratch = (
        pltpu.VMEM((HEAD, SEQ), BF16),
        pltpu.VMEM((3 * HEAD, SEQ), BF16),
        pltpu.VMEM((SEQ, HEAD), F32),
        pltpu.VMEM((SEQ, HEAD), F32),
    )
    ins = [d_o] + [(value, VMEM) for value in (kept, wide, lse, seg_row, seg_col, cosine, sine)]
    return Op(ins, [((12 * HEAD, ROWS), BF16)], XY_PEERS, body, scratch)


def add_up(total, own, others, index, rows, width):
    def step(i, carry):
        here = (*index, rows_at(i, 16), slice(0, width))
        value = own[here].astype(F32)
        for k in range(3):
            value += others[(k, *here)].astype(F32)
        total[here] = value.astype(total.dtype)
        return carry

    lax.fori_loop(0, rows // 16, step, 0)


def grad_first_op(grad):
    n = grad.shape[1]
    cut = first_part(n)
    rest = n - cut
    head, tail = pl.ds(0, cut), pl.ds(cut, rest)

    def body(engine, src, sum_y, sum_x, by_y, by_x, own_y, own_x):
        x = lax.axis_index("x")
        y = lax.axis_index("yh") * 2 + lax.axis_index("yl")
        copies = []
        local = [engine.local(src.at[y, head], own_y), engine.local(src.at[:, tail, lanes(x, 512)], own_x)]
        for d in (1, 2, 3):
            ty, tx = y_peer(d), x_peer(d)
            copies.append(engine.send(src.at[ty["yh"] * 2 + ty["yl"], head], by_y.at[d - 1], ty))
            copies.append(engine.send(src.at[:, tail, lanes(tx["x"], 512)], by_x.at[d - 1], tx))
        yield
        for copy in local:
            copy.wait()
        yield
        for copy in copies:
            copy.wait_recv()
        add_up(sum_y, own_y, by_y, (), cut, WIDTH)
        for q in range(4):
            add_up(sum_x, own_x, by_x, (q,), rest, 512)
        for copy in copies:
            copy.wait_send()

    outs = [((cut, WIDTH), BF16, VMEM), ((4, rest, 512), BF16, VMEM)]
    scratch = (
        pltpu.VMEM((3, cut, WIDTH), BF16),
        pltpu.VMEM((3, 4, rest, 512), BF16),
        pltpu.VMEM((cut, WIDTH), BF16),
        pltpu.VMEM((4, rest, 512), BF16),
    )
    return Op([grad], outs, X_PEERS + Y_PEERS, body, scratch)


def grad_rest_op(sum_y, sum_x, gather=False):
    cut, rest = sum_y.shape[0], sum_x.shape[1]
    n = cut + rest

    def body(engine, heads, tails, dst, by_x, by_y, own, total, *held):
        x, yl, core = (lax.axis_index(a) for a in ("x", "yl", "core"))
        y = lax.axis_index("yh") * 2 + yl
        copies, local = [], [engine.local(tails.at[y], own.at[pl.ds(cut, rest)])]
        local.append(engine.local(heads.at[:, lanes(x, 512)], own.at[pl.ds(0, cut)]))
        for d in (1, 2, 3):
            ty, tx = y_peer(d), x_peer(d)
            copies.append(engine.send(tails.at[ty["yh"] * 2 + ty["yl"]], by_y.at[d - 1], ty))
            copies.append(engine.send(heads.at[:, lanes(tx["x"], 512)], by_x.at[d - 1], tx))
        yield
        for copy in local:
            copy.wait()
        for copy in copies:
            copy.wait_recv()
        add_up(total.at[pl.ds(0, cut)], own.at[pl.ds(0, cut)], by_x, (), cut, 512)
        add_up(total.at[pl.ds(cut, rest)], own.at[pl.ds(cut, rest)], by_y, (), rest, 512)
        landing = held[0] if gather else dst
        moved = send_pieces(engine, lambda z: total.at[:, lanes(z)], lambda z: landing.at[z])
        for copy in copies:
            copy.wait_send()
        yield
        for copy in moved:
            copy.wait()
        if not gather:
            return

        def slot(xx, ll, cc):
            return (xx * 2 + ll) * 2 + cc

        first, second = pl.ds(0, 2), pl.ds(2, 2)
        me = slot(x, yl, core)
        partner = {"yl": 1 - yl}
        there = sibling()
        done = [engine.local(landing, dst.at[me]), engine.send(landing, dst.at[me], there)]
        to_y = engine.send(landing.at[first], dst.at[me, first], partner)
        to_x = [engine.send(landing.at[second], dst.at[me, second], x_peer(d)) for d in (1, 2, 3)]
        yield
        done[0].wait()
        final = []

        def pass_on(index, part):
            block = dst.at[index, part]
            done.append(engine.send(block, block, there))

        for d in (1, 2, 3):
            block = dst.at[me, first]
            final.append((slot(lax.rem(x + 4 - d, 4), yl, core), first, engine.send(block, block, x_peer(d))))
        block = dst.at[me, second]
        final.append((slot(x, 1 - yl, core), second, engine.send(block, block, partner)))
        to_y.wait_recv()
        other = slot(x, 1 - yl, core)
        for d in (1, 2, 3):
            block = dst.at[other, first]
            final.append((slot(lax.rem(x + 4 - d, 4), 1 - yl, core), first, engine.send(block, block, x_peer(d))))
        pass_on(other, first)
        for d in (1, 2, 3):
            to_x[d - 1].wait_recv()
            source = lax.rem(x + 4 - d, 4)
            block = dst.at[slot(source, yl, core), second]
            final.append((slot(source, 1 - yl, core), second, engine.send(block, block, partner)))
            pass_on(slot(source, yl, core), second)
        yield
        for index, part, copy in final:
            copy.wait_recv()
            pass_on(index, part)
        yield
        for copy in [to_y] + to_x + [c for _, _, c in final]:
            copy.wait_send()
        for copy in done[1:]:
            copy.wait()

    shape = (4, n, 128)
    scratch = [
        pltpu.VMEM((3, cut, 512), BF16),
        pltpu.VMEM((3, rest, 512), BF16),
        pltpu.VMEM((n, 512), BF16),
        pltpu.VMEM((n, 512), BF16),
    ]
    peers = X_PEERS + Y_PEERS + Z_PEERS
    if gather:
        scratch.append(pltpu.VMEM(shape, BF16))
        shape = (16,) + shape
        peers = peers + [sibling, other_yl]
    return Op([sum_y, sum_x], [(shape, BF16)], peers, body, tuple(scratch))


def other_yl():
    return {"yl": 1 - lax.axis_index("yl")}


def group_peer(dz, dc):
    return {
        "z": lax.rem(lax.axis_index("z") + dz, 4),
        "core": lax.rem(lax.axis_index("core") + dc, 2),
    }


GROUP_ALL = [(dz, dc) for dz in range(4) for dc in range(2) if dz or dc]
GROUP_PEERS = [functools.partial(group_peer, dz, dc) for dz, dc in GROUP_ALL]


def small_sum_op(norms, bias):
    def body(engine, norms, bias, norm_sum, bias_all, by_group, by_x, by_y):
        z, x, yl, core, yh = place()
        y = yh * 2 + yl
        me = z * 2 + core
        first = []
        for dz, dc in GROUP_ALL:
            to = group_peer(dz, dc)
            first.append(engine.send(norms.at[:, lanes(to["z"], 512)], by_group.at[me], to))
        mine = engine.local(norms.at[:, lanes(z, 512)], by_group.at[me])
        yield
        mine.wait()
        for copy in first:
            copy.wait()
        by_x[x, :, :512] = sum(by_group[k] for k in range(8))
        by_x[x, :, 512:] = bias[...]
        second = [engine.send(by_x.at[x], by_x.at[x], x_peer(d)) for d in (1, 2, 3)]
        yield
        for copy in second:
            copy.wait()
        by_y[y] = sum(by_x[k] for k in range(4))
        third = [engine.send(by_y.at[y], by_y.at[y], y_peer(d)) for d in (1, 2, 3)]
        yield
        for copy in third:
            copy.wait()
        total = sum(by_y[k] for k in range(4))
        norm_sum[...] = total[:, :512]
        bias_all[me] = total[:, 512:]
        last = [engine.send(bias_all.at[me], bias_all.at[me], group_peer(dz, dc)) for dz, dc in GROUP_ALL]
        yield
        for copy in last:
            copy.wait()

    outs = [((8, 512), F32, VMEM), ((8, 8, 128), F32, VMEM)]
    scratch = (
        pltpu.VMEM((8, 8, 512), F32),
        pltpu.VMEM((4, 8, 640), F32),
        pltpu.VMEM((4, 8, 640), F32),
    )
    return Op([(norms, VMEM), (bias, VMEM)], outs, GROUP_PEERS + X_PEERS + Y_PEERS, body, scratch)


def hand_back_op(block):
    def body(engine, src, dst):
        core, yh = lax.axis_index("core"), lax.axis_index("yh")
        far = {"core": yh, "yh": 1 - yh}
        near = {"core": yh}
        stays = core == yh
        mine = dst.at[rows_at(core, OWN)]
        i, j = engine.remote, engine.locals
        engine.remote += 4
        engine.locals += 1
        send_sem, recv_sem, local_sem = engine.sems

        def make(to, slot):
            return pltpu.make_async_remote_copy(
                src,
                mine,
                send_sem.at[i + slot],
                recv_sem.at[i + 2 + core],
                device_id=to,
                device_id_type=MESH_ID,
            )

        def arrival(half):
            part = dst.at[rows_at(half, OWN)]
            return pltpu.make_async_remote_copy(
                part, part, send_sem.at[i], recv_sem.at[i + 2 + half], device_id=far, device_id_type=MESH_ID
            )

        make(far, 0).start()

        @pl.when(stays)
        def _():
            pltpu.make_async_copy(src, mine, local_sem.at[j]).start()

        @pl.when(jnp.logical_not(stays))
        def _():
            make(near, 1).start()

        yield
        make(far, 0).wait_send()

        @pl.when(stays)
        def _():
            pltpu.make_async_copy(src, mine, local_sem.at[j]).wait()
            arrival(1 - core).wait_recv()

        @pl.when(jnp.logical_not(stays))
        def _():
            make(near, 1).wait_send()
            arrival(core).wait_recv()
            arrival(1 - core).wait_recv()

    def partner(dc, dh):
        return {
            "core": lax.rem(lax.axis_index("core") + dc, 2),
            "yh": lax.rem(lax.axis_index("yh") + dh, 2),
        }

    peers = [functools.partial(partner, dc, dh) for dc, dh in ((0, 1), (1, 0), (1, 1))]
    return Op([block], [((2 * OWN, WIDTH), block.dtype)], peers, body)


def dot(a, b, dims):
    return lax.dot_general(a, b, ((dims[:1], dims[1:]), ((), ())), preferred_element_type=F32)


def rope(block, cosine, sine):
    front, back = block[:8], block[8:16]
    return jnp.concatenate(
        [front * cosine - back * sine, back * cosine + front * sine, block[16:]], axis=0
    )


def rope_back(block, cosine, sine):
    front, back = block[:8], block[8:16]
    return jnp.concatenate(
        [front * cosine + back * sine, back * cosine - front * sine, block[16:]], axis=0
    )


def masked_scores(scores, start, seg_row, seg_col):
    stop = start + QB

    def hide(first, last, by_segment, causal):
        part = scores[first:last]
        keep = None
        if by_segment:
            keep = seg_col[first:last] == seg_row[:, start:stop]
        if causal:
            key_at = first + lax.broadcasted_iota(jnp.int32, part.shape, 0)
            query_at = start + lax.broadcasted_iota(jnp.int32, part.shape, 1)
            order = key_at <= query_at
            keep = order if keep is None else keep & order
        return jnp.where(keep, part, NEG)

    if start == 0:
        return hide(0, stop, True, True)
    if stop + 127 <= SEQ:
        parts = [hide(0, 128, True, False)]
        if start > 128:
            parts.append(scores[128:start])
        parts.append(hide(start, stop, False, True))
        return jnp.concatenate(parts, axis=0)
    return jnp.concatenate([hide(0, start, True, False), hide(start, stop, True, True)], axis=0)


def attend(qkv_ref, row_ref, col_ref, cos_ref, sin_ref, o_ref, wide_ref, lse_ref, kept_ref):
    cosine, sine = cos_ref[...], sin_ref[...]
    q_t = rope(qkv_ref[:HEAD].astype(F32), cosine, sine).astype(BF16) * jnp.asarray(0.125, BF16)
    k_t = rope(qkv_ref[HEAD : 2 * HEAD].astype(F32), cosine, sine).astype(BF16)
    v_t = qkv_ref[2 * HEAD :]
    kept_ref[:HEAD] = q_t
    kept_ref[HEAD : 2 * HEAD] = k_t
    kept_ref[2 * HEAD :] = v_t
    keys = k_t.astype(F32).T.astype(BF16)
    seg_row, seg_col = row_ref[...], col_ref[...]
    for start in range(0, SEQ, QB):
        stop = start + QB
        scores = dot(keys[:stop], q_t[:, start:stop], (1, 0))
        scores = masked_scores(scores, start, seg_row, seg_col)
        top = jnp.max(scores, axis=0, keepdims=True)
        terms = jnp.exp(scores - top)
        total = jnp.sum(terms, axis=0, keepdims=True)
        out = dot(v_t[:, :stop], terms.astype(BF16), (1, 0)) / total
        wide_ref[:, start:stop] = out
        o_ref[:, start:stop] = out.astype(BF16)
        lse_ref[:, start:stop] = top + jnp.log(total)


def attend_back(kept_ref, do_ref, wide_ref, lse_ref, row_ref, col_ref, cos_ref, sin_ref, out_ref, dk_ref, dv_ref):
    cosine, sine = cos_ref[...], sin_ref[...]
    q_t, k_t, do_t = kept_ref[:HEAD], kept_ref[HEAD : 2 * HEAD], do_ref[...]
    queries = q_t.astype(F32).T.astype(BF16)
    keys = k_t.astype(F32).T.astype(BF16)
    values = kept_ref[2 * HEAD :].astype(F32).T.astype(BF16)
    grads = do_t.astype(F32).T.astype(BF16)
    centre = jnp.sum(do_t.astype(F32) * wide_ref[...], axis=0, keepdims=True)
    lse = lse_ref[...]
    seg_row, seg_col = row_ref[...], col_ref[...]
    dk_ref[...] = jnp.zeros_like(dk_ref)
    dv_ref[...] = jnp.zeros_like(dv_ref)
    dq_parts = []
    for start in range(0, SEQ, QB):
        stop = start + QB
        scores = dot(keys[:stop], q_t[:, start:stop], (1, 0))
        scores = masked_scores(scores, start, seg_row, seg_col)
        probs = jnp.exp(scores - lse[:, start:stop])
        d_probs = dot(values[:stop], do_t[:, start:stop], (1, 0))
        d_scores = (probs * (d_probs - centre[:, start:stop])).astype(BF16)
        dv_ref[:stop] += dot(probs.astype(BF16), grads[start:stop], (1, 0))
        dk_ref[:stop] += dot(d_scores, queries[start:stop], (1, 0))
        dq_parts.append(dot(k_t[:, :stop], d_scores, (1, 0)) * 0.125)
    out_ref[:HEAD] = rope_back(jnp.concatenate(dq_parts, axis=1), cosine, sine).astype(BF16)
    out_ref[HEAD : 2 * HEAD] = rope_back(dk_ref[...].T, cosine, sine).astype(BF16)
    out_ref[2 * HEAD :] = dv_ref[...].T.astype(BF16)


def small_peer(dz, dh):
    return {
        "z": lax.rem(lax.axis_index("z") + dz, 4),
        "yh": lax.rem(lax.axis_index("yh") + dh, 2),
    }


SMALL_ALL = [(dz, dh) for dz in range(4) for dh in range(2) if dz or dh]
FORWARD_PEERS = XY_PEERS + Z_PEERS + [sibling]
FORWARD_PEERS += [functools.partial(small_peer, dz, 1) for dz in (1, 2, 3)]

FORWARD_OUTS = [
    ("m_qkv", (4, 192, WIDTH), BF16, VMEM),
    ("m_out", (4, 64, WIDTH), BF16, VMEM),
    ("m_down", (4, 176, WIDTH), BF16, ANY),
    ("m_gate", (4, 176, WIDTH), BF16, ANY),
    ("m_up", (4, 176, WIDTH), BF16, ANY),
    ("x_own", (OWN, WIDTH), BF16, VMEM),
    ("dy_own", (OWN, WIDTH), BF16, VMEM),
    ("middle", (OWN, WIDTH), F32, VMEM),
    ("norms", (8, WIDTH), F32, VMEM),
    ("h1", (ROWS, WIDTH), BF16, VMEM),
    ("h2", (ROWS, WIDTH), BF16, VMEM),
    ("dy", (ROWS, WIDTH), BF16, ANY),
    ("o_t", (4 * HEAD, ROWS), BF16, VMEM),
    ("kept", (3 * HEAD, SEQ), BF16, VMEM),
    ("wide", (HEAD, SEQ), F32, VMEM),
    ("lse", (1, SEQ), F32, VMEM),
    ("seg_row", (1, SEQ), F32, VMEM),
    ("seg_col", (SEQ, 1), F32, VMEM),
]
FORWARD_SCRATCH = [
    ("small", (4, 2, 16, 640), BF16),
    ("near_x", (OWN, WIDTH), BF16),
    ("near_dy", (OWN, WIDTH), BF16),
    ("far_x", (OWN, WIDTH), BF16),
    ("far_dy", (OWN, WIDTH), BF16),
    ("h1_own", (OWN, WIDTH), BF16),
    ("h2_own", (OWN, WIDTH), BF16),
    ("held_qkv", (3, 128, 1024), BF16),
    ("held_gu", (128, 2, 2816), BF16),
    ("turned", (2816, 128), F32),
    ("cut_qkv", (4, 192, 128), BF16),
    ("cut_gate", (4, 176, 128), BF16),
    ("cut_up", (4, 176, 128), BF16),
    ("p_qkv", (192, 512), BF16),
    ("p_out", (64, 512), BF16),
    ("p_down", (176, 512), BF16),
    ("p_gate", (176, 512), BF16),
    ("p_up", (176, 512), BF16),
    ("bias", (4, 192, 1), F32),
    ("qkv_t", (12 * HEAD, ROWS), BF16),
    ("item", (3 * HEAD, SEQ), BF16),
    ("out", (HEAD, SEQ), BF16),
    ("o_rows", (ROWS, 4 * HEAD), BF16),
    ("give", (4, OWN, WIDTH), BF16),
    ("other", (4, OWN, WIDTH), BF16),
    ("own", (4, OWN, WIDTH), F32),
    ("total", (3, OWN, WIDTH), BF16),
    ("arrived", (3, OWN, WIDTH), BF16),
]


class Refs:
    pass


def forward_kernel(*refs):
    r = Refs()
    names = ["tokens", "cotangent", "packed", "w_qkv", "w_out", "w_down", "w_gate_up", "cos", "sin"]
    names += [o[0] for o in FORWARD_OUTS] + [o[0] for o in FORWARD_SCRATCH]
    for name, ref in zip(names, refs):
        setattr(r, name, ref)
    engine = Engine(*refs[len(names) :])
    z, x, yl, core, yh = place()
    y = yh * 2 + yl
    greet(FORWARD_PEERS)

    load_qkv = engine.local(r.w_qkv.at[:, rows_at(x, 128)], r.held_qkv)
    load_x = engine.local(r.tokens.at[rows_at(core, OWN)], r.near_x)
    load_dy = engine.local(r.cotangent.at[rows_at(core, OWN)], r.near_dy)
    swap_x = engine.send(r.tokens.at[rows_at(1 - core, OWN)], r.far_x, sibling())
    smalls = [engine.send(r.packed, r.small.at[z, yh], small_peer(dz, dh)) for dz, dh in SMALL_ALL]
    small_here = engine.local(r.packed, r.small.at[z, yh])
    load_gu = engine.local(r.w_gate_up.at[rows_at(x, 128)], r.held_gu)
    swap_dy = engine.send(r.cotangent.at[rows_at(1 - core, OWN)], r.far_dy, sibling())

    def rows_of(n):
        return lambda zz: rows_at((zz * 2 + core) * 2 + yl, n)

    def slots_of(piece):
        return lambda zz: piece.at[:, lanes(zz)]

    load_qkv.wait()
    for part in range(3):
        r.turned[:1024, :] = r.held_qkv[part].astype(F32).T
        for zz in range(4):
            r.cut_qkv[zz, part * HEAD : (part + 1) * HEAD] = r.turned[rows_of(HEAD)(zz), :].astype(BF16)
    pieces_qkv = send_pieces(engine, lambda zz: r.cut_qkv.at[zz], slots_of(r.p_qkv))

    stays = core == yh
    load_x.wait()
    swap_x.wait_recv()
    x_rows = spread(jnp.where(stays, r.near_x[...].astype(F32), r.far_x[...].astype(F32)))
    r.x_own[...] = x_rows.astype(BF16)
    small_here.wait()
    for copy in smalls:
        copy.wait_recv()
    parts = [r.small[zz, 0].astype(F32) for zz in range(4)]
    r.norms[...] = jnp.concatenate(
        [parts[zz][:8, xx * 128 : (xx + 1) * 128] for xx in range(4) for zz in range(4)], axis=1
    )
    h1_full, _, _ = layer_norm(x_rows, r.norms[0:1], r.norms[2:3])
    r.h1_own[...] = h1_full.astype(BF16)
    tokens_h1 = gather_tokens(engine, r.h1_own, r.h1)
    next(tokens_h1)

    for copy in pieces_qkv[1:]:
        copy.wait_recv()
    pieces_qkv[0].wait()
    weight_qkv = gather_weight(engine, r.p_qkv, r.m_qkv)
    next(weight_qkv)
    pieces_out = send_pieces(engine, lambda zz: r.w_out.at[rows_of(64)(zz), lanes(x)], slots_of(r.p_out))

    lane_at = lax.broadcasted_iota(jnp.int32, (64, 128), 1)
    for h in range(2):
        table = jnp.concatenate([r.small[zz, h, :, 512:].astype(F32) for zz in range(4)], axis=0)
        for j in range(2):
            for part in range(3):
                picked = jnp.where(lane_at == (z * 2 + core) * 6 + j * 3 + part, table, 0.0)
                r.bias[h * 2 + j, part * HEAD : (part + 1) * HEAD] = jnp.sum(picked, axis=1, keepdims=True)
    marks = r.small[x, 0, :, :512].astype(F32)
    marks = [marks[4 + i : 5 + i, k * 128 : (k + 1) * 128] for i in range(4) for k in range(4)]
    r.seg_row[...] = jnp.concatenate(marks, axis=1)
    marks = jnp.concatenate(marks, axis=0).T
    r.seg_col[...] = jnp.concatenate([marks[:, k : k + 1] for k in range(16)], axis=0)

    next(weight_qkv)
    load_gu.wait()
    r.turned[...] = r.held_gu[:, 0, :].astype(F32).T
    for zz in range(4):
        r.cut_gate[zz] = r.turned[rows_of(176)(zz), :].astype(BF16)
    next(tokens_h1)
    next(weight_qkv)
    pieces_gate = send_pieces(engine, lambda zz: r.cut_gate.at[zz], slots_of(r.p_gate))
    pieces_down = send_pieces(engine, lambda zz: r.w_down.at[rows_of(176)(zz), lanes(x)], slots_of(r.p_down))
    r.turned[...] = r.held_gu[:, 1, :].astype(F32).T
    for zz in range(4):
        r.cut_up[zz] = r.turned[rows_of(176)(zz), :].astype(BF16)
    pieces_up = send_pieces(engine, lambda zz: r.cut_up.at[zz], slots_of(r.p_up))

    def start_weight(pieces, piece, matrix):
        pieces[0].wait()
        for copy in pieces[1:]:
            copy.wait_recv()
        thread = gather_weight(engine, piece, matrix)
        next(thread)
        return thread

    weight_out = start_weight(pieces_out, r.p_out, r.m_out)
    load_dy.wait()
    swap_dy.wait_recv()
    dy_rows = jnp.where(stays, r.near_dy[...].astype(F32), r.far_dy[...].astype(F32))
    r.dy_own[...] = spread(dy_rows).astype(BF16)
    finish(tokens_h1)
    finish(weight_qkv)

    place_here = lanes(x * 4 + yl * 2 + yh)
    to_items, stay = [], None
    for dy in (2, 1, 3, 0):
        ty = lax.rem(y + dy, 4)
        rows = rows_at(ty, 3 * HEAD)
        r.qkv_t[rows, :] = (dot(r.m_qkv[ty], r.h1[...], (1, 1)) + r.bias[ty]).astype(BF16)
        for dx in (2, 1, 3, 0):
            block = r.qkv_t.at[rows, lanes(lax.rem(x + dx, 4))]
            if dx or dy:
                to_items.append(engine.send(block, r.item.at[:, place_here], xy_peer(dx, dy)))
            else:
                stay = engine.local(block, r.item.at[:, place_here])
    tokens_dy = gather_tokens(engine, r.dy_own, r.dy)
    next(tokens_dy)
    next(weight_out)
    stay.wait()
    for copy in to_items:
        copy.wait_recv()
    next(weight_out)
    weight_down = start_weight(pieces_down, r.p_down, r.m_down)
    weight_gate = start_weight(pieces_gate, r.p_gate, r.m_gate)
    attend(r.item, r.seg_row, r.seg_col, r.cos, r.sin, r.out, r.wide, r.lse, r.kept)
    back = return_items(engine, r.out, r.o_t, HEAD)
    next(weight_down)
    next(tokens_dy)
    finish(weight_out)
    back[-1].wait()
    for copy in back[:-1]:
        copy.wait_recv()

    r.o_rows[...] = r.o_t[...].astype(F32).T.astype(BF16)
    matrix = r.m_out[...].reshape(4 * HEAD, WIDTH)
    to_core = []
    for i in range(4):
        base = lax.rem(z + 1 + i, 4) * 2
        r.give[i] = dot(r.o_rows[rows_at(base + 1 - core, OWN), :], matrix, (1, 0)).astype(BF16)
        to_core.append(engine.send(r.give.at[i], r.other.at[i], sibling()))
        r.own[i] = dot(r.o_rows[rows_at(base + core, OWN), :], matrix, (1, 0))
    to_z = []
    for i in range(3):
        to_core[i].wait_recv()
        r.total[i] = (r.own[i] + r.other[i].astype(F32)).astype(BF16)
        to_z.append(engine.send(r.total.at[i], r.arrived.at[i], z_peer(i + 1)))
    next(weight_gate)
    next(weight_down)
    weight_up = start_weight(pieces_up, r.p_up, r.m_up)
    to_core[3].wait_recv()
    r.middle[...] = x_rows + r.own[3] + r.other[3].astype(F32)
    for copy, arrived in zip(to_z, range(3)):
        copy.wait_recv()
        r.middle[...] += r.arrived[arrived].astype(F32)

    h2_full, _, _ = layer_norm(r.middle[...], r.norms[1:2], r.norms[3:4])
    r.h2_own[...] = h2_full.astype(BF16)
    tokens_h2 = gather_tokens(engine, r.h2_own, r.h2)
    next(tokens_h2)
    next(weight_up)
    next(weight_gate)
    finish(weight_down)
    next(weight_up)
    next(tokens_h2)
    finish(weight_gate)
    finish(tokens_dy)
    finish(weight_up)
    finish(tokens_h2)
    sent = smalls + to_items + back[:-1] + to_core + to_z + [swap_x, swap_dy]
    for pieces in (pieces_qkv, pieces_out, pieces_gate, pieces_down, pieces_up):
        sent += pieces[1:]
    for copy in sent:
        copy.wait_send()


def forward(tokens, cotangent, packed, w_qkv, w_out, w_down, w_gate_up, cosine, sine):
    values = pl.pallas_call(
        forward_kernel,
        out_shape=[jax.ShapeDtypeStruct(o[1], o[2]) for o in FORWARD_OUTS],
        in_specs=[ANY] * 7 + [VMEM] * 2,
        out_specs=[o[3] for o in FORWARD_OUTS],
        scratch_shapes=[pltpu.VMEM(shape, dtype) for _, shape, dtype in FORWARD_SCRATCH] + semaphores(160, 24),
        compiler_params=pltpu.CompilerParams(
            collective_id=1, has_side_effects=True, vmem_limit_bytes=50 * 2**20
        ),
        name="forward",
    )(tokens, cotangent, packed, w_qkv, w_out, w_down, w_gate_up, cosine, sine)
    result = Refs()
    for (name, *_), value in zip(FORWARD_OUTS, values):
        setattr(result, name, value)
    return result


def assemble_kernel(mlp_ref, attn_ref, gu_ref, down_ref, qkv_ref, out_ref, turned):
    for g in range(2):
        for zz in range(4):
            for core in range(2):
                for yl in range(2):
                    row = zz * 704 + core * 352 + yl * 176
                    block = mlp_ref[0, yl * 2 + core, zz, g * 176 : (g + 1) * 176]
                    turned[row : row + 176, :] = block.astype(F32)
        for t in range(22):
            gu_ref[:, g, t * 128 : (t + 1) * 128] = turned[t * 128 : (t + 1) * 128, :].T
    for zz in range(4):
        for core in range(2):
            for yl in range(2):
                row = zz * 704 + core * 352 + yl * 176
                down_ref[row : row + 176, :] = mlp_ref[0, yl * 2 + core, zz, 352:].astype(F32)
                row = zz * 256 + core * 128 + yl * 64
                out_ref[row : row + 32, :] = attn_ref[0, yl * 2 + core, zz, 96:128].astype(F32)
                out_ref[row + 32 : row + 64, :] = attn_ref[0, yl * 2 + core, zz, 224:].astype(F32)
            for part in range(3):
                pieces = []
                for yl in range(2):
                    for row in (part * 64, part * 64 + 32):
                        row = row if row < 96 else row + 32
                        pieces.append(attn_ref[0, yl * 2 + core, zz, row : row + 32])
                block = jnp.concatenate(pieces, axis=0)
                column = zz * 256 + core * 128
                qkv_ref[part, :, column : column + 128] = block.astype(F32).T


def assemble(mlp_all, attn_all):
    mlp_all = mlp_all.reshape(4, 4, 4, 528, 128)
    attn_all = attn_all.reshape(4, 4, 4, 256, 128)
    return pl.pallas_call(
        assemble_kernel,
        grid=(4,),
        in_specs=[
            pl.BlockSpec((1, 4, 4, 528, 128), lambda i: (i, 0, 0, 0, 0)),
            pl.BlockSpec((1, 4, 4, 256, 128), lambda i: (i, 0, 0, 0, 0)),
        ],
        out_specs=[
            pl.BlockSpec((128, 2, 2816), lambda i: (i, 0, 0)),
            pl.BlockSpec((2816, 128), lambda i: (0, i)),
            pl.BlockSpec((3, 128, 1024), lambda i: (0, i, 0)),
            pl.BlockSpec((1024, 128), lambda i: (0, i)),
        ],
        out_shape=[
            jax.ShapeDtypeStruct((512, 2, 2816), F32),
            jax.ShapeDtypeStruct((2816, 512), F32),
            jax.ShapeDtypeStruct((3, 512, 1024), F32),
            jax.ShapeDtypeStruct((1024, 512), F32),
        ],
        scratch_shapes=[pltpu.VMEM((2816, 128), F32)],
        compiler_params=pltpu.CompilerParams(vmem_limit_bytes=48 * 2**20),
        name="assemble",
    )(mlp_all, attn_all)


def rotation_tables():
    half = ROT // 2
    positions = jnp.arange(SEQ).astype(F32)
    inverse = 10000.0 ** (-(jnp.arange(half).astype(F32) * 2.0 / ROT))
    angles = inverse[:, None] * positions[None, :]
    return jnp.cos(angles), jnp.sin(angles)


def layer_norm(values, gain_row, shift_row):
    row_mean = jnp.mean(values, axis=-1, keepdims=True)
    centred = values - row_mean
    variance = jnp.mean(centred * centred, axis=-1, keepdims=True)
    rstd = lax.rsqrt(variance + EPS)
    normed = centred * rstd
    return normed * gain_row + shift_row, normed, rstd


def norm_back(gradient, normed, rstd, gain_row):
    shaped = gradient * gain_row
    centre = (
        shaped
        - jnp.mean(shaped, axis=-1, keepdims=True)
        - normed * jnp.mean(shaped * normed, axis=-1, keepdims=True)
    )
    return centre * rstd, jnp.sum(gradient * normed, axis=0), jnp.sum(gradient, axis=0)


def local(tokens, segments, w_qkv, b_qkv, w_out, w_gate_up, w_down, norm_gains, norm_shifts, cotangent):
    z, _, _, core, yh = place()

    def pick(values, axis, index):
        return lax.dynamic_index_in_dim(values, index, axis, keepdims=False)

    rows = jnp.concatenate(
        [norm_gains, norm_shifts, segments.astype(BF16).reshape(4, 512), jnp.zeros((8, 512), BF16)], axis=0
    )
    biases = b_qkv.reshape(3, 4, 2, 2, 16).transpose(4, 1, 2, 3, 0).reshape(16, 48)
    packed = jnp.concatenate([rows, jnp.pad(biases, ((0, 0), (0, 80)))], axis=1)
    cosine, sine = rotation_tables()
    f = forward(
        tokens[0], cotangent[0], packed, w_qkv.transpose(1, 0, 2), w_out, w_down, w_gate_up, cosine, sine
    )
    gains, shifts = f.norms[:2], f.norms[2:4]
    x_own, dy_own, middle = f.x_own.astype(F32), f.dy_own, f.middle
    h1, h2, dy, o_t, kept, o_wide, lse = f.h1, f.h2, f.dy, f.o_t, f.kept, f.wide, f.lse
    item_segments, segment_column = f.seg_row, f.seg_col
    m_qkv, m_out, m_down = f.m_qkv.reshape(768, WIDTH), f.m_out.reshape(256, WIDTH), f.m_down.reshape(704, WIDTH)
    m_gate, m_up = f.m_gate.reshape(704, WIDTH), f.m_up.reshape(704, WIDTH)
    _, normed_a, rstd_a = layer_norm(x_own, gains[:1], shifts[:1])
    _, normed_b, rstd_b = layer_norm(middle, gains[1:], shifts[1:])

    gate, up = dot(m_gate, h2, (1, 1)), dot(m_up, h2, (1, 1))
    sigmoid = jax.nn.sigmoid(gate)
    silu = gate * sigmoid
    act = (silu * up).astype(BF16)
    d_act = dot(m_down, dy, (1, 1))
    d_gate = (d_act * up * sigmoid * (1.0 + gate * (1.0 - sigmoid))).astype(BF16)
    d_up = (d_act * silu).astype(BF16)
    mlp_part = dot(act, m_down, (0, 0)).astype(BF16)
    back_part = (dot(d_gate, m_gate, (0, 0)) + dot(d_up, m_up, (0, 0))).astype(BF16)

    def weight_grad(a, b):
        return dot(a, b, (1, 0)).astype(BF16).reshape(4, a.shape[0] // 4, WIDTH)

    g_gate, g_up, g_down = weight_grad(d_gate, h2), weight_grad(d_up, h2), weight_grad(act, dy)
    (dh2_own,), (mlp_own,), first_gate, first_down = exchange(
        "sum_mlp",
        2,
        [token_scatter_op(back_part), token_scatter_op(mlp_part), grad_first_op(g_gate), grad_first_op(g_down)],
        48,
        24,
    )

    out_own = spread((middle + mlp_own).astype(BF16))
    back_b, gain_b, shift_b = norm_back(dh2_own, normed_b, rstd_b, gains[1:])
    d_middle = dy_own.astype(F32) + back_b
    (dz,), first_up, (z_down,) = exchange(
        "gather_dz",
        3,
        [token_gather_op(d_middle.astype(BF16)), grad_first_op(g_up), grad_rest_op(*first_down)],
        48,
        24,
    )
    d_o = dot(m_out, dz, (1, 1)).astype(BF16)
    g_out = weight_grad(o_t, dz)
    (d_qkv,), (z_gate,), (z_up,), (layer_out,) = exchange(
        "attention_back",
        4,
        [
            attention_back_op(d_o, kept, o_wide, lse, item_segments, segment_column, cosine, sine),
            grad_rest_op(*first_gate),
            grad_rest_op(*first_up),
            hand_back_op(out_own),
        ],
        96,
        24,
    )
    mlp_z = jnp.concatenate([z_gate, z_up, z_down], axis=1)
    mlp_all = lax.all_gather(mlp_z, ("x", "yl", "core"), axis=0)

    back_part = dot(d_qkv, m_qkv, (0, 0)).astype(BF16)
    g_qkv = weight_grad(d_qkv, h1)
    g_bias = jnp.sum(d_qkv.astype(F32), axis=1)
    (dh1_own,), first_qkv, first_out = exchange(
        "sum_dh1", 5, [token_scatter_op(back_part), grad_first_op(g_qkv), grad_first_op(g_out)], 48, 24
    )
    back_a, gain_a, shift_a = norm_back(dh1_own, normed_a, rstd_a, gains[:1])
    grad_own = spread((d_middle + back_a).astype(BF16))
    norms = spread(jnp.pad(jnp.stack([gain_a, gain_b, shift_a, shift_b]), ((0, 4), (0, 0))))
    first_attn = [jnp.concatenate([a, b], axis=-2) for a, b in zip(first_qkv, first_out)]
    (attn_all,), (norm_sum, bias_all), (grad_tokens,) = exchange(
        "finish",
        6,
        [
            grad_rest_op(*first_attn, gather=True),
            small_sum_op(norms, jnp.pad(g_bias, (0, 256)).reshape(8, 128)),
            hand_back_op(grad_own),
        ],
        80,
        24,
    )
    attn_all = attn_all.reshape(16, 4, 256, 128)
    bias_all = bias_all.reshape(8, 1024)[:, :768].reshape(4, 2, 2, 2, 3, 4, 16)
    bias_all = pick(pick(bias_all, 2, yh), 4, z)
    grad_bias = bias_all.transpose(3, 0, 1, 2, 4).reshape(3, 16, 16)
    out_gu, out_down, out_qkv, out_out = assemble(mlp_all, attn_all)
    return (
        layer_out[None],
        grad_tokens.astype(F32)[None],
        out_qkv.transpose(1, 0, 2),
        grad_bias,
        out_out,
        out_gu,
        out_down,
        norm_sum[:2],
        norm_sum[2:4],
    )


def solution(mesh):
    fine = Mesh(mesh.devices.reshape(4, 4, 2, 2, 2), ("z", "x", "yl", "core", "yh"))
    ctx = ("x", "yl", "core")
    return jax.shard_map(
        local,
        mesh=fine,
        in_specs=(
            P("z", ctx, None),
            P("z", None),
            P("z", None, "yh"),
            P(None, "yh", "z"),
            P("yh", "z"),
            P("z", None, "yh"),
            P("yh", "z"),
            P(None, "z"),
            P(None, "z"),
            P("z", ctx, None),
        ),
        out_specs=(
            P("z", ctx, None),
            P("z", ctx, None),
            P("z", None, "yh"),
            P(None, "yh", "z"),
            P("yh", "z"),
            P("z", None, "yh"),
            P("yh", "z"),
            P(None, "z"),
            P(None, "z"),
        ),
        check_vma=False,
    )
```

```python
import functools

import jax
import jax.numpy as jnp
from jax import lax
from jax.experimental import pallas as pl
from jax.experimental.pallas import tpu as pltpu
from jax.sharding import Mesh
from jax.sharding import PartitionSpec as P

EPS = 1e-05
NEG = -1e30
ROT = 16
HEAD = 64
SEQ = 2048
WIDTH = 2048
OWN = 64
ROWS = 512
QB = 256
F32 = jnp.float32
BF16 = jnp.bfloat16
MESH_ID = pl.DeviceIdType.MESH
ANY = pl.BlockSpec(memory_space=pl.ANY)
VMEM = pl.BlockSpec(memory_space=pltpu.VMEM)


def place():
    return tuple(lax.axis_index(a) for a in ("z", "x", "yl", "core", "yh"))


def lanes(index, size=128):
    return pl.ds(pl.multiple_of(index * size, size), size)


def rows_at(index, size):
    return pl.ds(pl.multiple_of(index * size, size), size)


def z_peer(d):
    z = lax.axis_index("z")
    return {"z": lax.rem(z + d, 4)}


def x_peer(d):
    x = lax.axis_index("x")
    return {"x": lax.rem(x + d, 4)}


def y_peer(d):
    y = lax.rem(lax.axis_index("yh") * 2 + lax.axis_index("yl") + d, 4)
    return {"yh": y // 2, "yl": lax.rem(y, 2)}


def xy_peer(dx, dy):
    return {**x_peer(dx), **y_peer(dy)}


def sibling():
    return {"core": 1 - lax.axis_index("core")}


Z_PEERS = [functools.partial(z_peer, d) for d in (1, 2, 3)]
X_PEERS = [functools.partial(x_peer, d) for d in (1, 2, 3)]
Y_PEERS = [functools.partial(y_peer, d) for d in (1, 2, 3)]
XY_ALL = [(dx, dy) for dx in range(4) for dy in range(4) if dx or dy]
XY_PEERS = [functools.partial(xy_peer, dx, dy) for dx, dy in XY_ALL]


class Engine:
    def __init__(self, send_sem, recv_sem, local_sem):
        self.sems = (send_sem, recv_sem, local_sem)
        self.remote = 0
        self.locals = 0

    def send(self, src, dst, device):
        i = self.remote
        self.remote += 1
        copy = pltpu.make_async_remote_copy(
            src, dst, self.sems[0].at[i], self.sems[1].at[i], device_id=device, device_id_type=MESH_ID
        )
        copy.start()
        return copy

    def local(self, src, dst):
        i = self.locals
        self.locals += 1
        copy = pltpu.make_async_copy(src, dst, self.sems[2].at[i])
        copy.start()
        return copy


def greet(peers):
    barrier = pltpu.get_barrier_semaphore()
    for peer in peers:
        pl.semaphore_signal(barrier, 1, device_id=peer(), device_id_type=MESH_ID)
    pl.semaphore_wait(barrier, len(peers))


def semaphores(n_remote, n_local):
    return [
        pltpu.SemaphoreType.DMA((n_remote,)),
        pltpu.SemaphoreType.DMA((n_remote,)),
        pltpu.SemaphoreType.DMA((n_local,)),
    ]


def spread(values):
    return jnp.concatenate(
        [values[:, (a * 4 + b) * 128 : (a * 4 + b + 1) * 128] for b in range(4) for a in range(4)], axis=1
    )


def finish(thread):
    for _ in thread:
        pass


def send_pieces(engine, pieces, slots):
    z = lax.axis_index("z")
    copies = [engine.local(pieces(z), slots(z))]
    for d in (1, 2, 3):
        to = z_peer(d)
        copies.append(engine.send(pieces(to["z"]), slots(z), to))
    return copies


def gather_tokens(engine, src, dst):
    z, core = lax.axis_index("z"), lax.axis_index("core")
    mine = dst.at[rows_at(z * 2 + core, OWN)]
    first = [engine.send(src, mine, z_peer(d)) for d in (1, 2, 3)]
    rest = [engine.send(src, mine, sibling()), engine.local(src, mine)]
    yield
    for d in (1, 2, 3):
        first[d - 1].wait_recv()
        here = dst.at[rows_at(lax.rem(z + 4 - d, 4) * 2 + core, OWN)]
        rest.append(engine.send(here, here, sibling()))
    yield
    for copy in first:
        copy.wait_send()
    for copy in rest:
        copy.wait()


def gather_weight(engine, src, dst):
    n = src.shape[0]
    top = first_part(n)
    head, tail = pl.ds(0, top), pl.ds(top, n - top)
    x = lax.axis_index("x")
    y = lax.axis_index("yh") * 2 + lax.axis_index("yl")
    left_y, left_x = lax.rem(y + 3, 4), lax.rem(x + 3, 4)
    right_y, right_x = lax.rem(y + 1, 4), lax.rem(x + 1, 4)
    mine = lanes(x, 512)
    local = engine.local(src, dst.at[y, :, mine])
    along_x = [engine.send(src.at[head], dst.at[y, head, mine], x_peer(d)) for d in (1, 2, 3)]
    along_y = [engine.send(src.at[tail], dst.at[y, tail, mine], y_peer(d)) for d in (1, 2, 3)]
    yield
    local.wait()
    for copy in along_x:
        copy.wait_recv()
    ring_y = [engine.send(dst.at[y, head], dst.at[y, head], y_peer(d)) for d in (1, 3)]
    for copy in along_y:
        copy.wait_recv()
    ring_x = [engine.send(dst.at[:, tail, mine], dst.at[:, tail, mine], x_peer(d)) for d in (1, 3)]
    yield
    rest = []
    half = first_part(top)
    early, late = pl.ds(0, half), pl.ds(half, top - half)
    ring_y[0].wait_recv()
    rest.append(engine.send(dst.at[left_y, early], dst.at[left_y, early], y_peer(1)))
    ring_y[1].wait_recv()
    rest.append(engine.send(dst.at[right_y, late], dst.at[right_y, late], y_peer(3)))
    ring_x[0].wait_recv()
    block = dst.at[:, tail, lanes(left_x * 2, 256)]
    rest.append(engine.send(block, block, x_peer(1)))
    ring_x[1].wait_recv()
    block = dst.at[:, tail, lanes(right_x * 2 + 1, 256)]
    rest.append(engine.send(block, block, x_peer(3)))
    yield
    for copy in along_x + along_y + ring_y + ring_x:
        copy.wait_send()
    for copy in rest:
        copy.wait()


def first_part(n):
    return (n // 2 + 15) // 16 * 16


def send_items(engine, src, dst, n):
    x, yl, yh = (lax.axis_index(a) for a in ("x", "yl", "yh"))
    y = yh * 2 + yl
    mine = dst.at[:, lanes(x * 4 + yl * 2 + yh)]
    copies = []
    for dx, dy in XY_ALL:
        tx, ty = lax.rem(x + dx, 4), lax.rem(y + dy, 4)
        copies.append(engine.send(src.at[rows_at(ty, n), lanes(tx)], mine, xy_peer(dx, dy)))
    copies.append(engine.local(src.at[rows_at(y, n), lanes(x)], mine))
    return copies


def return_items(engine, src, dst, n):
    x, yl, yh = (lax.axis_index(a) for a in ("x", "yl", "yh"))
    mine = dst.at[rows_at(yh * 2 + yl, n), lanes(x)]
    copies = []
    for dx, dy in XY_ALL:
        to = xy_peer(dx, dy)
        copies.append(engine.send(src.at[:, lanes(to["x"] * 4 + to["yl"] * 2 + to["yh"])], mine, to))
    copies.append(engine.local(src.at[:, lanes(x * 4 + yl * 2 + yh)], mine))
    return copies


def add_up(total, own, others, index, rows, width):
    def step(i, carry):
        here = (*index, rows_at(i, 16), slice(0, width))
        value = own[here].astype(F32)
        for k in range(3):
            value += others[(k, *here)].astype(F32)
        total[here] = value.astype(total.dtype)
        return carry

    lax.fori_loop(0, rows // 16, step, 0)


def scatter_tokens(engine, src, dst, own, other, arrived):
    z, core = lax.axis_index("z"), lax.axis_index("core")
    pairs = []
    for i in range(4):
        base = lax.rem(z + 1 + i, 4) * 2
        there = engine.send(src.at[rows_at(base + 1 - core, OWN)], other.at[i], sibling())
        here = engine.local(src.at[rows_at(base + core, OWN)], own.at[i])
        pairs.append((there, here))
    yield
    sent = []
    for i in range(3):
        pairs[i][0].wait_recv()
        pairs[i][1].wait()
        own[i] = (own[i].astype(F32) + other[i].astype(F32)).astype(BF16)
        sent.append(engine.send(own.at[i], arrived.at[i], z_peer(i + 1)))
    yield
    pairs[3][0].wait_recv()
    pairs[3][1].wait()
    dst[...] = own[3].astype(F32) + other[3].astype(F32)
    for i in range(3):
        sent[i].wait_recv()
        dst[...] += arrived[i].astype(F32)
    yield
    for copy in sent:
        copy.wait_send()
    for there, _ in pairs:
        there.wait_send()


def scatter_product(engine, rows, matrix, dst, give, own, other, total, arrived):
    z, core = lax.axis_index("z"), lax.axis_index("core")
    to_core = []
    for i in range(4):
        base = lax.rem(z + 1 + i, 4) * 2
        give[i] = dot(rows[rows_at(base + 1 - core, OWN), :], matrix, (1, 0)).astype(BF16)
        to_core.append(engine.send(give.at[i], other.at[i], sibling()))
        own[i] = dot(rows[rows_at(base + core, OWN), :], matrix, (1, 0))
    to_z = []
    for i in range(3):
        to_core[i].wait_recv()
        total[i] = (own[i] + other[i].astype(F32)).astype(BF16)
        to_z.append(engine.send(total.at[i], arrived.at[i], z_peer(i + 1)))
    yield
    to_core[3].wait_recv()
    dst[...] = own[3] + other[3].astype(F32)
    for i in range(3):
        to_z[i].wait_recv()
        dst[...] += arrived[i].astype(F32)
    yield
    for copy in to_core + to_z:
        copy.wait_send()


def sum_first(engine, src, sum_y, sum_x, by_y, by_x, own_y, own_x):
    n, cut = src.shape[1], sum_y.shape[0]
    rest = n - cut
    head, tail = pl.ds(0, cut), pl.ds(cut, rest)
    x = lax.axis_index("x")
    y = lax.axis_index("yh") * 2 + lax.axis_index("yl")
    copies = []
    for d in (2, 1, 3):
        ty, tx = y_peer(d), x_peer(d)
        copies.append(engine.send(src.at[ty["yh"] * 2 + ty["yl"], head], by_y.at[d - 1], ty))
        copies.append(engine.send(src.at[:, tail, lanes(tx["x"], 512)], by_x.at[d - 1], tx))
    yield
    own_y, own_x = own_y.at[head], own_x.at[:, pl.ds(0, rest)]
    local = [engine.local(src.at[y, head], own_y), engine.local(src.at[:, tail, lanes(x, 512)], own_x)]
    for copy in local:
        copy.wait()
    for copy in copies:
        copy.wait_recv()
    add_up(sum_y, own_y, by_y, (), cut, WIDTH)
    for q in range(4):
        add_up(sum_x, own_x, by_x, (q,), rest, 512)
    yield
    for copy in copies:
        copy.wait_send()


def sum_rest(engine, heads, tails, landing, by_x, by_y, own, total):
    cut, rest = heads.shape[0], tails.shape[1]
    x = lax.axis_index("x")
    y = lax.axis_index("yh") * 2 + lax.axis_index("yl")
    first, second = pl.ds(0, cut), pl.ds(cut, rest)
    copies = []
    for d in (2, 1, 3):
        ty, tx = y_peer(d), x_peer(d)
        copies.append(engine.send(heads.at[:, lanes(tx["x"], 512)], by_x.at[d - 1], tx))
        copies.append(engine.send(tails.at[ty["yh"] * 2 + ty["yl"]], by_y.at[d - 1], ty))
    local = [engine.local(tails.at[y], own.at[second]), engine.local(heads.at[:, lanes(x, 512)], own.at[first])]
    yield
    for copy in local:
        copy.wait()
    for copy in copies:
        copy.wait_recv()
    add_up(total.at[first], own.at[first], by_x, (), cut, 512)
    add_up(total.at[second], own.at[second], by_y, (), rest, 512)
    moved = send_pieces(engine, lambda z: total.at[:, lanes(z)], landing)
    yield
    moved[0].wait()
    for copy in moved[1:]:
        copy.wait_recv()
    yield
    for copy in copies + moved[1:]:
        copy.wait_send()


def gather_ctx(engine, landing, dst):
    x, yl, core = (lax.axis_index(a) for a in ("x", "yl", "core"))

    def slot(xx, ll):
        return (xx * 2 + ll) * 2 + core

    first, second = pl.ds(0, 2), pl.ds(2, 2)
    me, other = slot(x, yl), slot(x, 1 - yl)
    partner, there = {"yl": 1 - yl}, sibling()
    local = engine.local(landing, dst.at[me])
    done = [engine.send(landing, dst.at[me], there)]
    to_y = engine.send(landing.at[first], dst.at[me, first], partner)
    to_x = [engine.send(landing.at[second], dst.at[me, second], x_peer(d)) for d in (1, 2, 3)]
    final = []
    for d in (1, 2, 3):
        copy = engine.send(landing.at[first], dst.at[me, first], x_peer(d))
        final.append((slot(lax.rem(x + 4 - d, 4), yl), first, copy))
    final.append((other, second, engine.send(landing.at[second], dst.at[me, second], partner)))
    yield

    def pass_on(index, part):
        block = dst.at[index, part]
        done.append(engine.send(block, block, there))

    to_y.wait_recv()
    block = dst.at[other, first]
    for d in (1, 2, 3):
        final.append((slot(lax.rem(x + 4 - d, 4), 1 - yl), first, engine.send(block, block, x_peer(d))))
    pass_on(other, first)
    for d in (1, 2, 3):
        to_x[d - 1].wait_recv()
        source = lax.rem(x + 4 - d, 4)
        block = dst.at[slot(source, yl), second]
        final.append((slot(source, 1 - yl), second, engine.send(block, block, partner)))
        pass_on(slot(source, yl), second)
    yield
    for index, part, copy in final:
        copy.wait_recv()
        pass_on(index, part)
    yield
    local.wait()
    for copy in [to_y] + to_x + [c for _, _, c in final]:
        copy.wait_send()
    for copy in done:
        copy.wait()


def group_peer(dz, dc):
    return {
        "z": lax.rem(lax.axis_index("z") + dz, 4),
        "core": lax.rem(lax.axis_index("core") + dc, 2),
    }


GROUP_ALL = [(dz, dc) for dz in range(4) for dc in range(2) if dz or dc]


def sum_small(engine, norms, bias, norm_sum, bias_all, by_group, by_x, by_y):
    z, x, yl, core, yh = place()
    y = yh * 2 + yl
    me = z * 2 + core
    first = []
    for dz, dc in GROUP_ALL:
        to = group_peer(dz, dc)
        first.append(engine.send(norms.at[:, lanes(to["z"], 512)], by_group.at[me], to))
    mine = engine.local(norms.at[:, lanes(z, 512)], by_group.at[me])
    yield
    mine.wait()
    for copy in first:
        copy.wait_recv()
    by_x[x, :, :512] = sum(by_group[k] for k in range(8))
    by_x[x, :, 512:] = bias[...]
    second = [engine.send(by_x.at[x], by_x.at[x], x_peer(d)) for d in (1, 2, 3)]
    yield
    for copy in second:
        copy.wait_recv()
    by_y[y] = sum(by_x[k] for k in range(4))
    third = [engine.send(by_y.at[y], by_y.at[y], y_peer(d)) for d in (1, 2, 3)]
    yield
    for copy in third:
        copy.wait_recv()
    total = sum(by_y[k] for k in range(4))
    norm_sum[...] = total[:, :512]
    bias_all[me] = total[:, 512:]
    last = [engine.send(bias_all.at[me], bias_all.at[me], group_peer(dz, dc)) for dz, dc in GROUP_ALL]
    yield
    for copy in last:
        copy.wait()
    for copy in first + second + third:
        copy.wait_send()


def hand_back(engine, src, dst):
    core, yh = lax.axis_index("core"), lax.axis_index("yh")
    far = {"core": yh, "yh": 1 - yh}
    near = {"core": yh}
    stays = core == yh
    mine = dst.at[rows_at(core, OWN)]
    i, j = engine.remote, engine.locals
    engine.remote += 4
    engine.locals += 1
    send_sem, recv_sem, local_sem = engine.sems

    def make(to, slot):
        return pltpu.make_async_remote_copy(
            src,
            mine,
            send_sem.at[i + slot],
            recv_sem.at[i + 2 + core],
            device_id=to,
            device_id_type=MESH_ID,
        )

    def arrival(half):
        part = dst.at[rows_at(half, OWN)]
        return pltpu.make_async_remote_copy(
            part, part, send_sem.at[i], recv_sem.at[i + 2 + half], device_id=far, device_id_type=MESH_ID
        )

    make(far, 0).start()

    @pl.when(stays)
    def _():
        pltpu.make_async_copy(src, mine, local_sem.at[j]).start()

    @pl.when(jnp.logical_not(stays))
    def _():
        make(near, 1).start()

    yield
    make(far, 0).wait_send()

    @pl.when(stays)
    def _():
        pltpu.make_async_copy(src, mine, local_sem.at[j]).wait()
        arrival(1 - core).wait_recv()

    @pl.when(jnp.logical_not(stays))
    def _():
        make(near, 1).wait_send()
        arrival(core).wait_recv()
        arrival(1 - core).wait_recv()


def dot(a, b, dims):
    return lax.dot_general(a, b, ((dims[:1], dims[1:]), ((), ())), preferred_element_type=F32)


def rope(block, cosine, sine):
    front, back = block[:8], block[8:16]
    return jnp.concatenate(
        [front * cosine - back * sine, back * cosine + front * sine, block[16:]], axis=0
    )


def rope_back(block, cosine, sine):
    front, back = block[:8], block[8:16]
    return jnp.concatenate(
        [front * cosine + back * sine, back * cosine - front * sine, block[16:]], axis=0
    )


def masked_scores(scores, start, seg_row, seg_col):
    stop = start + QB

    def hide(first, last, by_segment, causal):
        part = scores[first:last]
        keep = None
        if by_segment:
            keep = seg_col[first:last] == seg_row[:, start:stop]
        if causal:
            key_at = first + lax.broadcasted_iota(jnp.int32, part.shape, 0)
            query_at = start + lax.broadcasted_iota(jnp.int32, part.shape, 1)
            order = key_at <= query_at
            keep = order if keep is None else keep & order
        return jnp.where(keep, part, NEG)

    if start == 0:
        return hide(0, stop, True, True)
    if stop + 127 <= SEQ:
        parts = [hide(0, 128, True, False)]
        if start > 128:
            parts.append(scores[128:start])
        parts.append(hide(start, stop, False, True))
        return jnp.concatenate(parts, axis=0)
    return jnp.concatenate([hide(0, start, True, False), hide(start, stop, True, True)], axis=0)


def attend(qkv_ref, row_ref, col_ref, cos_ref, sin_ref, o_ref, wide_ref, lse_ref, kept_ref):
    cosine, sine = cos_ref[...], sin_ref[...]
    q_t = rope(qkv_ref[:HEAD].astype(F32), cosine, sine).astype(BF16) * jnp.asarray(0.125, BF16)
    k_t = rope(qkv_ref[HEAD : 2 * HEAD].astype(F32), cosine, sine).astype(BF16)
    v_t = qkv_ref[2 * HEAD :]
    kept_ref[:HEAD] = q_t
    kept_ref[HEAD : 2 * HEAD] = k_t
    kept_ref[2 * HEAD :] = v_t
    keys = k_t.astype(F32).T.astype(BF16)
    seg_row, seg_col = row_ref[...], col_ref[...]
    for start in range(0, SEQ, QB):
        stop = start + QB
        scores = dot(keys[:stop], q_t[:, start:stop], (1, 0))
        scores = masked_scores(scores, start, seg_row, seg_col)
        top = jnp.max(scores, axis=0, keepdims=True)
        terms = jnp.exp(scores - top)
        total = jnp.sum(terms, axis=0, keepdims=True)
        out = dot(v_t[:, :stop], terms.astype(BF16), (1, 0)) / total
        wide_ref[:, start:stop] = out
        o_ref[:, start:stop] = out.astype(BF16)
        lse_ref[:, start:stop] = top + jnp.log(total)


def attend_back(kept_ref, do_ref, wide_ref, lse_ref, row_ref, col_ref, cos_ref, sin_ref, out_ref, dk_ref, dv_ref):
    cosine, sine = cos_ref[...], sin_ref[...]
    q_t, k_t, do_t = kept_ref[:HEAD], kept_ref[HEAD : 2 * HEAD], do_ref[...]
    queries = q_t.astype(F32).T.astype(BF16)
    keys = k_t.astype(F32).T.astype(BF16)
    values = kept_ref[2 * HEAD :].astype(F32).T.astype(BF16)
    grads = do_t.astype(F32).T.astype(BF16)
    centre = jnp.sum(do_t.astype(F32) * wide_ref[...], axis=0, keepdims=True)
    lse = lse_ref[...]
    seg_row, seg_col = row_ref[...], col_ref[...]
    dk_ref[...] = jnp.zeros_like(dk_ref)
    dv_ref[...] = jnp.zeros_like(dv_ref)
    dq_parts = []
    for start in range(0, SEQ, QB):
        stop = start + QB
        scores = dot(keys[:stop], q_t[:, start:stop], (1, 0))
        scores = masked_scores(scores, start, seg_row, seg_col)
        probs = jnp.exp(scores - lse[:, start:stop])
        d_probs = dot(values[:stop], do_t[:, start:stop], (1, 0))
        d_scores = (probs * (d_probs - centre[:, start:stop])).astype(BF16)
        dv_ref[:stop] += dot(probs.astype(BF16), grads[start:stop], (1, 0))
        dk_ref[:stop] += dot(d_scores, queries[start:stop], (1, 0))
        dq_parts.append(dot(k_t[:, :stop], d_scores, (1, 0)) * 0.125)
    out_ref[:HEAD] = rope_back(jnp.concatenate(dq_parts, axis=1), cosine, sine).astype(BF16)
    out_ref[HEAD : 2 * HEAD] = rope_back(dk_ref[...].T, cosine, sine).astype(BF16)
    out_ref[2 * HEAD :] = dv_ref[...].T.astype(BF16)


def small_peer(dz, dh):
    return {
        "z": lax.rem(lax.axis_index("z") + dz, 4),
        "yh": lax.rem(lax.axis_index("yh") + dh, 2),
    }


SMALL_ALL = [(dz, dh) for dz in range(4) for dh in range(2) if dz or dh]
FORWARD_PEERS = XY_PEERS + Z_PEERS + [sibling]
FORWARD_PEERS += [functools.partial(small_peer, dz, 1) for dz in (1, 2, 3)]

FORWARD_OUTS = [
    ("m_qkv", (4, 192, WIDTH), BF16, VMEM),
    ("m_out", (4, 64, WIDTH), BF16, VMEM),
    ("m_down", (4, 176, WIDTH), BF16, ANY),
    ("m_gate", (4, 176, WIDTH), BF16, ANY),
    ("m_up", (4, 176, WIDTH), BF16, ANY),
    ("x_own", (OWN, WIDTH), BF16, VMEM),
    ("dy_own", (OWN, WIDTH), BF16, VMEM),
    ("middle", (OWN, WIDTH), F32, VMEM),
    ("norms", (8, WIDTH), F32, VMEM),
    ("h1", (ROWS, WIDTH), BF16, VMEM),
    ("h2", (ROWS, WIDTH), BF16, VMEM),
    ("dy", (ROWS, WIDTH), BF16, ANY),
    ("o_t", (4 * HEAD, ROWS), BF16, VMEM),
    ("kept", (3 * HEAD, SEQ), BF16, VMEM),
    ("wide", (HEAD, SEQ), F32, VMEM),
    ("lse", (1, SEQ), F32, VMEM),
    ("seg_row", (1, SEQ), F32, VMEM),
    ("seg_col", (SEQ, 1), F32, VMEM),
]
FORWARD_SCRATCH = [
    ("small", (4, 2, 16, 640), BF16),
    ("near_x", (OWN, WIDTH), BF16),
    ("near_dy", (OWN, WIDTH), BF16),
    ("far_x", (OWN, WIDTH), BF16),
    ("far_dy", (OWN, WIDTH), BF16),
    ("h1_own", (OWN, WIDTH), BF16),
    ("h2_own", (OWN, WIDTH), BF16),
    ("held_qkv", (3, 128, 1024), BF16),
    ("held_gu", (128, 2, 2816), BF16),
    ("turned", (2816, 128), F32),
    ("cut_qkv", (4, 192, 128), BF16),
    ("cut_gate", (4, 176, 128), BF16),
    ("cut_up", (4, 176, 128), BF16),
    ("p_qkv", (192, 512), BF16),
    ("p_out", (64, 512), BF16),
    ("p_down", (176, 512), BF16),
    ("p_gate", (176, 512), BF16),
    ("p_up", (176, 512), BF16),
    ("bias", (4, 192, 1), F32),
    ("qkv_t", (12 * HEAD, ROWS), BF16),
    ("item", (3 * HEAD, SEQ), BF16),
    ("out", (HEAD, SEQ), BF16),
    ("o_rows", (ROWS, 4 * HEAD), BF16),
    ("give", (4, OWN, WIDTH), BF16),
    ("other", (4, OWN, WIDTH), BF16),
    ("own", (4, OWN, WIDTH), F32),
    ("total", (3, OWN, WIDTH), BF16),
    ("arrived", (3, OWN, WIDTH), BF16),
]


class Refs:
    pass


def forward_kernel(*refs):
    r = Refs()
    names = ["tokens", "cotangent", "packed", "w_qkv", "w_out", "w_down", "w_gate_up", "cos", "sin"]
    names += [o[0] for o in FORWARD_OUTS] + [o[0] for o in FORWARD_SCRATCH]
    for name, ref in zip(names, refs):
        setattr(r, name, ref)
    engine = Engine(*refs[len(names) :])
    z, x, yl, core, yh = place()
    y = yh * 2 + yl
    greet(FORWARD_PEERS)

    load_qkv = engine.local(r.w_qkv.at[:, rows_at(x, 128)], r.held_qkv)
    load_x = engine.local(r.tokens.at[rows_at(core, OWN)], r.near_x)
    load_dy = engine.local(r.cotangent.at[rows_at(core, OWN)], r.near_dy)
    swap_x = engine.send(r.tokens.at[rows_at(1 - core, OWN)], r.far_x, sibling())
    smalls = [engine.send(r.packed, r.small.at[z, yh], small_peer(dz, dh)) for dz, dh in SMALL_ALL]
    small_here = engine.local(r.packed, r.small.at[z, yh])
    load_gu = engine.local(r.w_gate_up.at[rows_at(x, 128)], r.held_gu)
    swap_dy = engine.send(r.cotangent.at[rows_at(1 - core, OWN)], r.far_dy, sibling())

    def rows_of(n):
        return lambda zz: rows_at((zz * 2 + core) * 2 + yl, n)

    def slots_of(piece):
        return lambda zz: piece.at[:, lanes(zz)]

    load_qkv.wait()
    for part in range(3):
        r.turned[:1024, :] = r.held_qkv[part].astype(F32).T
        for zz in range(4):
            r.cut_qkv[zz, part * HEAD : (part + 1) * HEAD] = r.turned[rows_of(HEAD)(zz), :].astype(BF16)
    pieces_qkv = send_pieces(engine, lambda zz: r.cut_qkv.at[zz], slots_of(r.p_qkv))

    stays = core == yh
    load_x.wait()
    swap_x.wait_recv()
    x_rows = spread(jnp.where(stays, r.near_x[...].astype(F32), r.far_x[...].astype(F32)))
    r.x_own[...] = x_rows.astype(BF16)
    small_here.wait()
    for copy in smalls:
        copy.wait_recv()
    parts = [r.small[zz, 0].astype(F32) for zz in range(4)]
    r.norms[...] = jnp.concatenate(
        [parts[zz][:8, xx * 128 : (xx + 1) * 128] for xx in range(4) for zz in range(4)], axis=1
    )
    h1_full, _, _ = layer_norm(x_rows, r.norms[0:1], r.norms[2:3])
    r.h1_own[...] = h1_full.astype(BF16)
    tokens_h1 = gather_tokens(engine, r.h1_own, r.h1)
    next(tokens_h1)

    for copy in pieces_qkv[1:]:
        copy.wait_recv()
    pieces_qkv[0].wait()
    weight_qkv = gather_weight(engine, r.p_qkv, r.m_qkv)
    next(weight_qkv)
    pieces_out = send_pieces(engine, lambda zz: r.w_out.at[rows_of(64)(zz), lanes(x)], slots_of(r.p_out))

    lane_at = lax.broadcasted_iota(jnp.int32, (64, 128), 1)
    for h in range(2):
        table = jnp.concatenate([r.small[zz, h, :, 512:].astype(F32) for zz in range(4)], axis=0)
        for j in range(2):
            for part in range(3):
                picked = jnp.where(lane_at == (z * 2 + core) * 6 + j * 3 + part, table, 0.0)
                r.bias[h * 2 + j, part * HEAD : (part + 1) * HEAD] = jnp.sum(picked, axis=1, keepdims=True)
    marks = r.small[x, 0, :, :512].astype(F32)
    marks = [marks[4 + i : 5 + i, k * 128 : (k + 1) * 128] for i in range(4) for k in range(4)]
    r.seg_row[...] = jnp.concatenate(marks, axis=1)
    marks = jnp.concatenate(marks, axis=0).T
    r.seg_col[...] = jnp.concatenate([marks[:, k : k + 1] for k in range(16)], axis=0)

    next(weight_qkv)
    load_gu.wait()
    r.turned[...] = r.held_gu[:, 0, :].astype(F32).T
    for zz in range(4):
        r.cut_gate[zz] = r.turned[rows_of(176)(zz), :].astype(BF16)
    next(tokens_h1)
    next(weight_qkv)
    pieces_gate = send_pieces(engine, lambda zz: r.cut_gate.at[zz], slots_of(r.p_gate))
    pieces_down = send_pieces(engine, lambda zz: r.w_down.at[rows_of(176)(zz), lanes(x)], slots_of(r.p_down))
    r.turned[...] = r.held_gu[:, 1, :].astype(F32).T
    for zz in range(4):
        r.cut_up[zz] = r.turned[rows_of(176)(zz), :].astype(BF16)
    pieces_up = send_pieces(engine, lambda zz: r.cut_up.at[zz], slots_of(r.p_up))

    def start_weight(pieces, piece, matrix):
        pieces[0].wait()
        for copy in pieces[1:]:
            copy.wait_recv()
        thread = gather_weight(engine, piece, matrix)
        next(thread)
        return thread

    weight_out = start_weight(pieces_out, r.p_out, r.m_out)
    load_dy.wait()
    swap_dy.wait_recv()
    dy_rows = jnp.where(stays, r.near_dy[...].astype(F32), r.far_dy[...].astype(F32))
    r.dy_own[...] = spread(dy_rows).astype(BF16)
    finish(tokens_h1)
    finish(weight_qkv)

    place_here = lanes(x * 4 + yl * 2 + yh)
    to_items, stay = [], None
    for dy in (2, 1, 3, 0):
        ty = lax.rem(y + dy, 4)
        rows = rows_at(ty, 3 * HEAD)
        r.qkv_t[rows, :] = (dot(r.m_qkv[ty], r.h1[...], (1, 1)) + r.bias[ty]).astype(BF16)
        for dx in (2, 1, 3, 0):
            block = r.qkv_t.at[rows, lanes(lax.rem(x + dx, 4))]
            if dx or dy:
                to_items.append(engine.send(block, r.item.at[:, place_here], xy_peer(dx, dy)))
            else:
                stay = engine.local(block, r.item.at[:, place_here])
    tokens_dy = gather_tokens(engine, r.dy_own, r.dy)
    next(tokens_dy)
    next(weight_out)
    stay.wait()
    for copy in to_items:
        copy.wait_recv()
    next(weight_out)
    weight_down = start_weight(pieces_down, r.p_down, r.m_down)
    weight_gate = start_weight(pieces_gate, r.p_gate, r.m_gate)
    attend(r.item, r.seg_row, r.seg_col, r.cos, r.sin, r.out, r.wide, r.lse, r.kept)
    back = return_items(engine, r.out, r.o_t, HEAD)
    next(weight_down)
    next(tokens_dy)
    finish(weight_out)
    back[-1].wait()
    for copy in back[:-1]:
        copy.wait_recv()

    r.o_rows[...] = r.o_t[...].astype(F32).T.astype(BF16)
    matrix = r.m_out[...].reshape(4 * HEAD, WIDTH)
    to_core = []
    for i in range(4):
        base = lax.rem(z + 1 + i, 4) * 2
        r.give[i] = dot(r.o_rows[rows_at(base + 1 - core, OWN), :], matrix, (1, 0)).astype(BF16)
        to_core.append(engine.send(r.give.at[i], r.other.at[i], sibling()))
        r.own[i] = dot(r.o_rows[rows_at(base + core, OWN), :], matrix, (1, 0))
    to_z = []
    for i in range(3):
        to_core[i].wait_recv()
        r.total[i] = (r.own[i] + r.other[i].astype(F32)).astype(BF16)
        to_z.append(engine.send(r.total.at[i], r.arrived.at[i], z_peer(i + 1)))
    next(weight_gate)
    next(weight_down)
    weight_up = start_weight(pieces_up, r.p_up, r.m_up)
    to_core[3].wait_recv()
    r.middle[...] = x_rows + r.own[3] + r.other[3].astype(F32)
    for copy, arrived in zip(to_z, range(3)):
        copy.wait_recv()
        r.middle[...] += r.arrived[arrived].astype(F32)

    h2_full, _, _ = layer_norm(r.middle[...], r.norms[1:2], r.norms[3:4])
    r.h2_own[...] = h2_full.astype(BF16)
    tokens_h2 = gather_tokens(engine, r.h2_own, r.h2)
    next(tokens_h2)
    next(weight_up)
    next(weight_gate)
    finish(weight_down)
    next(weight_up)
    next(tokens_h2)
    finish(weight_gate)
    finish(tokens_dy)
    finish(weight_up)
    finish(tokens_h2)
    sent = smalls + to_items + back[:-1] + to_core + to_z + [swap_x, swap_dy]
    for pieces in (pieces_qkv, pieces_out, pieces_gate, pieces_down, pieces_up):
        sent += pieces[1:]
    for copy in sent:
        copy.wait_send()


def forward(tokens, cotangent, packed, w_qkv, w_out, w_down, w_gate_up, cosine, sine):
    values = pl.pallas_call(
        forward_kernel,
        out_shape=[jax.ShapeDtypeStruct(o[1], o[2]) for o in FORWARD_OUTS],
        in_specs=[ANY] * 7 + [VMEM] * 2,
        out_specs=[o[3] for o in FORWARD_OUTS],
        scratch_shapes=[pltpu.VMEM(shape, dtype) for _, shape, dtype in FORWARD_SCRATCH] + semaphores(160, 24),
        compiler_params=pltpu.CompilerParams(
            collective_id=1, has_side_effects=True, vmem_limit_bytes=50 * 2**20
        ),
        name="forward",
    )(tokens, cotangent, packed, w_qkv, w_out, w_down, w_gate_up, cosine, sine)
    result = Refs()
    for (name, *_), value in zip(FORWARD_OUTS, values):
        setattr(result, name, value)
    return result


def back_peer(dc, dh):
    return {
        "core": lax.rem(lax.axis_index("core") + dc, 2),
        "yh": lax.rem(lax.axis_index("yh") + dh, 2),
    }


BACKWARD_PEERS = XY_PEERS + Z_PEERS + [sibling, functools.partial(back_peer, 1, 1)]
BACKWARD_PEERS += [functools.partial(group_peer, dz, 1) for dz in (1, 2, 3)]
BACKWARD_FAR = ["back_part", "mlp_part", "g_gate", "g_up", "g_down", "h1", "m_qkv"]
BACKWARD_NEAR = ["middle", "x_own", "dy_own", "norms", "m_out", "o_t", "kept", "wide", "lse"]
BACKWARD_NEAR += ["seg_row", "seg_col", "cos", "sin"]
BACKWARD_OUTS = [
    ("layer_out", (2 * OWN, WIDTH), BF16, ANY),
    ("grad_tokens", (2 * OWN, WIDTH), BF16, ANY),
    ("mlp_all", (16, 4, 528, 128), BF16, ANY),
    ("attn_all", (16, 4, 256, 128), BF16, ANY),
    ("norm_sum", (8, 512), F32, VMEM),
    ("bias_all", (8, 8, 768), F32, VMEM),
]
BACKWARD_SCRATCH = [
    ("v_h1", (ROWS, WIDTH), BF16),
    ("v_qkv", (4, 192, WIDTH), BF16),
    ("dz_own", (OWN, WIDTH), BF16),
    ("dz", (ROWS, WIDTH), BF16),
    ("d_middle", (OWN, WIDTH), F32),
    ("summed", (OWN, WIDTH), F32),
    ("out_own", (OWN, WIDTH), BF16),
    ("grad_own", (OWN, WIDTH), BF16),
    ("own_dh2", (4, OWN, WIDTH), BF16),
    ("other_dh2", (4, OWN, WIDTH), BF16),
    ("arrived_dh2", (3, OWN, WIDTH), BF16),
    ("own_mlp", (4, OWN, WIDTH), BF16),
    ("other_mlp", (4, OWN, WIDTH), BF16),
    ("arrived_mlp", (3, OWN, WIDTH), BF16),
    ("give", (4, OWN, WIDTH), BF16),
    ("own_dh1", (4, OWN, WIDTH), F32),
    ("other_dh1", (4, OWN, WIDTH), BF16),
    ("total_dh1", (3, OWN, WIDTH), BF16),
    ("arrived_dh1", (3, OWN, WIDTH), BF16),
    ("own_y", (128, WIDTH), BF16),
    ("own_x", (4, 128, 512), BF16),
    ("d_o", (4 * HEAD, ROWS), BF16),
    ("item", (HEAD, SEQ), BF16),
    ("item_out", (3 * HEAD, SEQ), BF16),
    ("dk", (SEQ, HEAD), F32),
    ("dv", (SEQ, HEAD), F32),
    ("d_qkv", (12 * HEAD, ROWS), BF16),
    ("d_rows", (ROWS, 12 * HEAD), BF16),
    ("g_attn", (4, 256, WIDTH), BF16),
    ("landing_mlp", (4, 528, 128), BF16),
    ("landing_attn", (4, 256, 128), BF16),
    ("small_norms", (8, WIDTH), F32),
    ("small_bias", (8, 768), F32),
    ("by_group", (8, 8, 512), F32),
    ("small_x", (4, 8, 1280), F32),
    ("small_y", (4, 8, 1280), F32),
]
for _name, _n in (("gate", 176), ("down", 176), ("up", 176), ("attn", 256)):
    _cut = first_part(_n)
    BACKWARD_SCRATCH += [
        ("sum_y_" + _name, (_cut, WIDTH), BF16),
        ("sum_x_" + _name, (4, _n - _cut, 512), BF16),
        ("by_y_" + _name, (3, _cut, WIDTH), BF16),
        ("by_x_" + _name, (3, 4, _n - _cut, 512), BF16),
        ("rest_x_" + _name, (3, _cut, 512), BF16),
        ("rest_y_" + _name, (3, _n - _cut, 512), BF16),
        ("rest_own_" + _name, (_n, 512), BF16),
        ("rest_total_" + _name, (_n, 512), BF16),
    ]


def backward_kernel(*refs):
    r = Refs()
    names = BACKWARD_FAR + BACKWARD_NEAR + [o[0] for o in BACKWARD_OUTS] + [o[0] for o in BACKWARD_SCRATCH]
    for name, ref in zip(names, refs):
        setattr(r, name, ref)
    engine = Engine(*refs[len(names) :])
    z, x, yl, core, yh = place()
    y = yh * 2 + yl
    greet(BACKWARD_PEERS)

    def first_of(name, grad):
        parts = [getattr(r, part + name) for part in ("sum_y_", "sum_x_", "by_y_", "by_x_")]
        thread = sum_first(engine, grad, *parts, r.own_y, r.own_x)
        next(thread)
        return thread

    def rest_of(name, landing):
        parts = [getattr(r, part + name) for part in ("rest_x_", "rest_y_", "rest_own_", "rest_total_")]
        thread = sum_rest(engine, getattr(r, "sum_y_" + name), getattr(r, "sum_x_" + name), landing, *parts)
        next(thread)
        return thread

    def mlp_landing(first):
        return lambda zz: r.landing_mlp.at[zz, pl.ds(first, 176)]

    dh2 = scatter_tokens(engine, r.back_part, r.summed, r.own_dh2, r.other_dh2, r.arrived_dh2)
    next(dh2)
    gate = first_of("gate", r.g_gate)
    down = first_of("down", r.g_down)
    load_h1 = engine.local(r.h1, r.v_h1)
    load_qkv = engine.local(r.m_qkv, r.v_qkv)
    next(dh2)
    mlp = scatter_tokens(engine, r.mlp_part, r.d_middle, r.own_mlp, r.other_mlp, r.arrived_mlp)
    next(mlp)
    _, normed_b, rstd_b = layer_norm(r.middle[...], r.norms[1:2], r.norms[3:4])
    next(dh2)
    back_b, gain_b, shift_b = norm_back(r.summed[...], normed_b, rstd_b, r.norms[1:2])
    d_middle = r.dy_own[...].astype(F32) + back_b
    r.dz_own[...] = d_middle.astype(BF16)
    tokens_dz = gather_tokens(engine, r.dz_own, r.dz)
    next(tokens_dz)
    r.small_norms[1:2] = gain_b[None]
    r.small_norms[3:4] = shift_b[None]
    next(mlp)
    next(gate)
    rest_gate = rest_of("gate", mlp_landing(0))
    next(tokens_dz)
    finish(tokens_dz)

    place_here = lanes(x * 4 + yl * 2 + yh)
    to_items, stay = [], None
    for dy in (2, 1, 3, 0):
        ty = lax.rem(y + dy, 4)
        rows = rows_at(ty, HEAD)
        r.d_o[rows, :] = dot(r.m_out[ty], r.dz[...], (1, 1)).astype(BF16)
        for dx in (2, 1, 3, 0):
            block = r.d_o.at[rows, lanes(lax.rem(x + dx, 4))]
            if dx or dy:
                to_items.append(engine.send(block, r.item.at[:, place_here], xy_peer(dx, dy)))
            else:
                stay = engine.local(block, r.item.at[:, place_here])
    up = first_of("up", r.g_up)
    next(mlp)
    r.out_own[...] = spread(r.middle[...] + r.d_middle[...]).astype(BF16)
    r.d_middle[...] = d_middle
    hand_out = hand_back(engine, r.out_own, r.layer_out)
    next(hand_out)
    for q in range(4):
        r.g_attn[q, 192:] = dot(r.o_t[q * HEAD : (q + 1) * HEAD, :], r.dz[...], (1, 0)).astype(BF16)
    stay.wait()
    for copy in to_items:
        copy.wait_recv()
    next(down)
    rest_down = rest_of("down", mlp_landing(352))
    attend_back(
        r.kept, r.item, r.wide, r.lse, r.seg_row, r.seg_col, r.cos, r.sin, r.item_out, r.dk, r.dv
    )
    back = return_items(engine, r.item_out, r.d_qkv, 3 * HEAD)
    next(rest_gate)
    next(rest_down)
    next(up)
    rest_up = rest_of("up", mlp_landing(176))
    back[-1].wait()
    for copy in back[:-1]:
        copy.wait_recv()

    load_h1.wait()
    load_qkv.wait()
    r.d_rows[...] = r.d_qkv[...].astype(F32).T.astype(BF16)
    matrix = r.v_qkv[...].reshape(12 * HEAD, WIDTH)
    dh1 = scatter_product(
        engine, r.d_rows, matrix, r.summed, r.give, r.own_dh1, r.other_dh1, r.total_dh1, r.arrived_dh1
    )
    next(dh1)
    for q in range(4):
        rows = slice(q * 3 * HEAD, (q + 1) * 3 * HEAD)
        r.g_attn[q, :192] = dot(r.d_qkv[rows, :], r.v_h1[...], (1, 0)).astype(BF16)
    attn = first_of("attn", r.g_attn)
    r.small_bias[...] = dot(jnp.ones((8, ROWS), BF16), r.d_qkv[...], (1, 1))
    next(rest_up)
    for thread in (rest_gate, rest_down, rest_up):
        next(thread)
    gather_mlp = gather_ctx(engine, r.landing_mlp, r.mlp_all)
    next(gather_mlp)
    _, normed_a, rstd_a = layer_norm(r.x_own[...].astype(F32), r.norms[0:1], r.norms[2:3])
    next(dh1)
    back_a, gain_a, shift_a = norm_back(r.summed[...], normed_a, rstd_a, r.norms[0:1])
    r.grad_own[...] = spread(r.d_middle[...] + back_a).astype(BF16)
    hand_grad = hand_back(engine, r.grad_own, r.grad_tokens)
    next(hand_grad)
    r.small_norms[0:1] = gain_a[None]
    r.small_norms[2:3] = shift_a[None]
    r.small_norms[4:] = jnp.zeros((4, WIDTH), F32)
    r.small_norms[...] = spread(r.small_norms[...])
    small = sum_small(
        engine, r.small_norms, r.small_bias, r.norm_sum, r.bias_all, r.by_group, r.small_x, r.small_y
    )
    next(small)
    next(attn)
    rest_attn = rest_of("attn", lambda zz: r.landing_attn.at[zz])
    next(small)
    next(rest_attn)
    next(small)
    next(rest_attn)
    gather_attn = gather_ctx(engine, r.landing_attn, r.attn_all)
    next(gather_attn)
    next(gather_mlp)
    next(small)
    next(gather_attn)
    next(gather_mlp)
    next(gather_attn)
    threads = (dh2, mlp, gate, down, up, attn, rest_gate, rest_down, rest_up, rest_attn)
    for thread in threads + (hand_out, dh1, hand_grad, small, gather_mlp, gather_attn):
        finish(thread)
    for copy in to_items + back[:-1]:
        copy.wait_send()


def backward(values):
    given = [values[name] for name in BACKWARD_FAR + BACKWARD_NEAR]
    return pl.pallas_call(
        backward_kernel,
        out_shape=[jax.ShapeDtypeStruct(o[1], o[2]) for o in BACKWARD_OUTS],
        in_specs=[ANY] * len(BACKWARD_FAR) + [VMEM] * len(BACKWARD_NEAR),
        out_specs=[o[3] for o in BACKWARD_OUTS],
        scratch_shapes=[pltpu.VMEM(shape, dtype) for _, shape, dtype in BACKWARD_SCRATCH] + semaphores(240, 48),
        compiler_params=pltpu.CompilerParams(
            collective_id=2, has_side_effects=True, vmem_limit_bytes=58 * 2**20
        ),
        name="backward",
    )(*given)


def assemble_kernel(mlp_ref, attn_ref, gu_ref, down_ref, qkv_ref, out_ref, turned):
    for g in range(2):
        for zz in range(4):
            for core in range(2):
                for yl in range(2):
                    row = zz * 704 + core * 352 + yl * 176
                    block = mlp_ref[0, yl * 2 + core, zz, g * 176 : (g + 1) * 176]
                    turned[row : row + 176, :] = block.astype(F32)
        for t in range(22):
            gu_ref[:, g, t * 128 : (t + 1) * 128] = turned[t * 128 : (t + 1) * 128, :].T
    for zz in range(4):
        for core in range(2):
            for yl in range(2):
                row = zz * 704 + core * 352 + yl * 176
                down_ref[row : row + 176, :] = mlp_ref[0, yl * 2 + core, zz, 352:].astype(F32)
                row = zz * 256 + core * 128 + yl * 64
                out_ref[row : row + 64, :] = attn_ref[0, yl * 2 + core, zz, 192:].astype(F32)
            for part in range(3):
                rows = slice(part * 64, (part + 1) * 64)
                block = jnp.concatenate([attn_ref[0, core, zz, rows], attn_ref[0, 2 + core, zz, rows]], axis=0)
                column = zz * 256 + core * 128
                qkv_ref[part, :, column : column + 128] = block.astype(F32).T


def assemble(mlp_all, attn_all):
    mlp_all = mlp_all.reshape(4, 4, 4, 528, 128)
    attn_all = attn_all.reshape(4, 4, 4, 256, 128)
    return pl.pallas_call(
        assemble_kernel,
        grid=(4,),
        in_specs=[
            pl.BlockSpec((1, 4, 4, 528, 128), lambda i: (i, 0, 0, 0, 0)),
            pl.BlockSpec((1, 4, 4, 256, 128), lambda i: (i, 0, 0, 0, 0)),
        ],
        out_specs=[
            pl.BlockSpec((128, 2, 2816), lambda i: (i, 0, 0)),
            pl.BlockSpec((2816, 128), lambda i: (0, i)),
            pl.BlockSpec((3, 128, 1024), lambda i: (0, i, 0)),
            pl.BlockSpec((1024, 128), lambda i: (0, i)),
        ],
        out_shape=[
            jax.ShapeDtypeStruct((512, 2, 2816), F32),
            jax.ShapeDtypeStruct((2816, 512), F32),
            jax.ShapeDtypeStruct((3, 512, 1024), F32),
            jax.ShapeDtypeStruct((1024, 512), F32),
        ],
        scratch_shapes=[pltpu.VMEM((2816, 128), F32)],
        compiler_params=pltpu.CompilerParams(vmem_limit_bytes=48 * 2**20),
        name="assemble",
    )(mlp_all, attn_all)


def rotation_tables():
    half = ROT // 2
    positions = jnp.arange(SEQ).astype(F32)
    inverse = 10000.0 ** (-(jnp.arange(half).astype(F32) * 2.0 / ROT))
    angles = inverse[:, None] * positions[None, :]
    return jnp.cos(angles), jnp.sin(angles)


def layer_norm(values, gain_row, shift_row):
    row_mean = jnp.mean(values, axis=-1, keepdims=True)
    centred = values - row_mean
    variance = jnp.mean(centred * centred, axis=-1, keepdims=True)
    rstd = lax.rsqrt(variance + EPS)
    normed = centred * rstd
    return normed * gain_row + shift_row, normed, rstd


def norm_back(gradient, normed, rstd, gain_row):
    shaped = gradient * gain_row
    centre = (
        shaped
        - jnp.mean(shaped, axis=-1, keepdims=True)
        - normed * jnp.mean(shaped * normed, axis=-1, keepdims=True)
    )
    return centre * rstd, jnp.sum(gradient * normed, axis=0), jnp.sum(gradient, axis=0)


def local(tokens, segments, w_qkv, b_qkv, w_out, w_gate_up, w_down, norm_gains, norm_shifts, cotangent):
    z, _, _, core, yh = place()

    def pick(values, axis, index):
        return lax.dynamic_index_in_dim(values, index, axis, keepdims=False)

    rows = jnp.concatenate(
        [norm_gains, norm_shifts, segments.astype(BF16).reshape(4, 512), jnp.zeros((8, 512), BF16)], axis=0
    )
    biases = b_qkv.reshape(3, 4, 2, 2, 16).transpose(4, 1, 2, 3, 0).reshape(16, 48)
    packed = jnp.concatenate([rows, jnp.pad(biases, ((0, 0), (0, 80)))], axis=1)
    cosine, sine = rotation_tables()
    f = forward(
        tokens[0], cotangent[0], packed, w_qkv.transpose(1, 0, 2), w_out, w_down, w_gate_up, cosine, sine
    )
    h2, dy = f.h2, f.dy
    m_down, m_gate, m_up = (m.reshape(704, WIDTH) for m in (f.m_down, f.m_gate, f.m_up))

    gate, up = dot(m_gate, h2, (1, 1)), dot(m_up, h2, (1, 1))
    sigmoid = jax.nn.sigmoid(gate)
    silu = gate * sigmoid
    act = (silu * up).astype(BF16)
    d_act = dot(m_down, dy, (1, 1))
    d_gate = (d_act * up * sigmoid * (1.0 + gate * (1.0 - sigmoid))).astype(BF16)
    d_up = (d_act * silu).astype(BF16)
    mlp_part = dot(act, m_down, (0, 0)).astype(BF16)
    back_part = (dot(d_gate, m_gate, (0, 0)) + dot(d_up, m_up, (0, 0))).astype(BF16)

    def weight_grad(a, b):
        return dot(a, b, (1, 0)).astype(BF16).reshape(4, a.shape[0] // 4, WIDTH)

    g_gate, g_up, g_down = weight_grad(d_gate, h2), weight_grad(d_up, h2), weight_grad(act, dy)
    values = dict(vars(f), cos=cosine, sin=sine, back_part=back_part, mlp_part=mlp_part)
    values.update(g_gate=g_gate, g_up=g_up, g_down=g_down)
    layer_out, grad_tokens, mlp_all, attn_all, norm_sum, bias_all = backward(values)

    bias_all = bias_all[:, 0].reshape(4, 2, 2, 2, 3, 4, 16)
    bias_all = pick(pick(bias_all, 2, yh), 4, z)
    grad_bias = bias_all.transpose(3, 0, 1, 2, 4).reshape(3, 16, 16)
    out_gu, out_down, out_qkv, out_out = assemble(mlp_all, attn_all)
    return (
        layer_out[None],
        grad_tokens.astype(F32)[None],
        out_qkv.transpose(1, 0, 2),
        grad_bias,
        out_out,
        out_gu,
        out_down,
        norm_sum[:2],
        norm_sum[2:4],
    )


def solution(mesh):
    fine = Mesh(mesh.devices.reshape(4, 4, 2, 2, 2), ("z", "x", "yl", "core", "yh"))
    ctx = ("x", "yl", "core")
    return jax.shard_map(
        local,
        mesh=fine,
        in_specs=(
            P("z", ctx, None),
            P("z", None),
            P("z", None, "yh"),
            P(None, "yh", "z"),
            P("yh", "z"),
            P("z", None, "yh"),
            P("yh", "z"),
            P(None, "z"),
            P(None, "z"),
            P("z", ctx, None),
        ),
        out_specs=(
            P("z", ctx, None),
            P("z", ctx, None),
            P("z", None, "yh"),
            P(None, "yh", "z"),
            P("yh", "z"),
            P("z", None, "yh"),
            P("yh", "z"),
            P(None, "z"),
            P(None, "z"),
        ),
        check_vma=False,
    )
```

```python
import functools

import jax
import jax.numpy as jnp
from jax import lax
from jax.experimental import pallas as pl
from jax.experimental.pallas import tpu as pltpu
from jax.sharding import Mesh
from jax.sharding import PartitionSpec as P

EPS = 1e-05
NEG = -1e30
ROT = 16
HEAD = 64
SEQ = 2048
WIDTH = 2048
OWN = 64
ROWS = 512
QB = 256
F32 = jnp.float32
BF16 = jnp.bfloat16
MESH_ID = pl.DeviceIdType.MESH
ANY = pl.BlockSpec(memory_space=pl.ANY)
VMEM = pl.BlockSpec(memory_space=pltpu.VMEM)


def place():
    return tuple(lax.axis_index(a) for a in ("z", "x", "yl", "core", "yh"))


def lanes(index, size=128):
    return pl.ds(pl.multiple_of(index * size, size), size)


def rows_at(index, size):
    return pl.ds(pl.multiple_of(index * size, size), size)


def z_peer(d):
    z = lax.axis_index("z")
    return {"z": lax.rem(z + d, 4)}


def x_peer(d):
    x = lax.axis_index("x")
    return {"x": lax.rem(x + d, 4)}


def y_peer(d):
    y = lax.rem(lax.axis_index("yh") * 2 + lax.axis_index("yl") + d, 4)
    return {"yh": y // 2, "yl": lax.rem(y, 2)}


def xy_peer(dx, dy):
    return {**x_peer(dx), **y_peer(dy)}


def sibling():
    return {"core": 1 - lax.axis_index("core")}


Z_PEERS = [functools.partial(z_peer, d) for d in (1, 2, 3)]
X_PEERS = [functools.partial(x_peer, d) for d in (1, 2, 3)]
Y_PEERS = [functools.partial(y_peer, d) for d in (1, 2, 3)]
XY_ALL = [(dx, dy) for dx in range(4) for dy in range(4) if dx or dy]
XY_PEERS = [functools.partial(xy_peer, dx, dy) for dx, dy in XY_ALL]


class Engine:
    def __init__(self, send_sem, recv_sem, local_sem):
        self.sems = (send_sem, recv_sem, local_sem)
        self.remote = 0
        self.locals = 0

    def send(self, src, dst, device):
        i = self.remote
        self.remote += 1
        copy = pltpu.make_async_remote_copy(
            src, dst, self.sems[0].at[i], self.sems[1].at[i], device_id=device, device_id_type=MESH_ID
        )
        copy.start()
        return copy

    def local(self, src, dst):
        i = self.locals
        self.locals += 1
        copy = pltpu.make_async_copy(src, dst, self.sems[2].at[i])
        copy.start()
        return copy


def greet(peers):
    barrier = pltpu.get_barrier_semaphore()
    for peer in peers:
        pl.semaphore_signal(barrier, 1, device_id=peer(), device_id_type=MESH_ID)
    pl.semaphore_wait(barrier, len(peers))


def semaphores(n_remote, n_local):
    return [
        pltpu.SemaphoreType.DMA((n_remote,)),
        pltpu.SemaphoreType.DMA((n_remote,)),
        pltpu.SemaphoreType.DMA((n_local,)),
    ]


def spread(values):
    return jnp.concatenate(
        [values[:, (a * 4 + b) * 128 : (a * 4 + b + 1) * 128] for b in range(4) for a in range(4)], axis=1
    )


def finish(thread):
    for _ in thread:
        pass


def send_pieces(engine, pieces, slots):
    z = lax.axis_index("z")
    copies = [engine.local(pieces(z), slots(z))]
    for d in (1, 2, 3):
        to = z_peer(d)
        copies.append(engine.send(pieces(to["z"]), slots(z), to))
    return copies


def gather_tokens(engine, src, dst):
    z, core = lax.axis_index("z"), lax.axis_index("core")
    mine = dst.at[rows_at(z * 2 + core, OWN)]
    first = [engine.send(src, mine, z_peer(d)) for d in (1, 2, 3)]
    rest = [engine.send(src, mine, sibling()), engine.local(src, mine)]
    yield
    for d in (1, 2, 3):
        first[d - 1].wait_recv()
        here = dst.at[rows_at(lax.rem(z + 4 - d, 4) * 2 + core, OWN)]
        rest.append(engine.send(here, here, sibling()))
    yield
    for copy in first:
        copy.wait_send()
    for copy in rest:
        copy.wait()


def gather_weight(engine, src, dst):
    n = src.shape[0]
    top = first_part(n)
    head, tail = pl.ds(0, top), pl.ds(top, n - top)
    x = lax.axis_index("x")
    y = lax.axis_index("yh") * 2 + lax.axis_index("yl")
    left_y, left_x = lax.rem(y + 3, 4), lax.rem(x + 3, 4)
    right_y, right_x = lax.rem(y + 1, 4), lax.rem(x + 1, 4)
    mine = lanes(x, 512)
    local = engine.local(src, dst.at[y, :, mine])
    along_x = [engine.send(src.at[head], dst.at[y, head, mine], x_peer(d)) for d in (1, 2, 3)]
    along_y = [engine.send(src.at[tail], dst.at[y, tail, mine], y_peer(d)) for d in (1, 2, 3)]
    yield
    local.wait()
    for copy in along_x:
        copy.wait_recv()
    ring_y = [engine.send(dst.at[y, head], dst.at[y, head], y_peer(d)) for d in (1, 3)]
    for copy in along_y:
        copy.wait_recv()
    ring_x = [engine.send(dst.at[:, tail, mine], dst.at[:, tail, mine], x_peer(d)) for d in (1, 3)]
    yield
    rest = []
    half = first_part(top)
    early, late = pl.ds(0, half), pl.ds(half, top - half)
    ring_y[0].wait_recv()
    rest.append(engine.send(dst.at[left_y, early], dst.at[left_y, early], y_peer(1)))
    ring_y[1].wait_recv()
    rest.append(engine.send(dst.at[right_y, late], dst.at[right_y, late], y_peer(3)))
    ring_x[0].wait_recv()
    block = dst.at[:, tail, lanes(left_x * 2, 256)]
    rest.append(engine.send(block, block, x_peer(1)))
    ring_x[1].wait_recv()
    block = dst.at[:, tail, lanes(right_x * 2 + 1, 256)]
    rest.append(engine.send(block, block, x_peer(3)))
    yield
    for copy in along_x + along_y + ring_y + ring_x:
        copy.wait_send()
    for copy in rest:
        copy.wait()


def first_part(n):
    return (n // 2 + 15) // 16 * 16


def send_items(engine, src, dst, n):
    x, yl, yh = (lax.axis_index(a) for a in ("x", "yl", "yh"))
    y = yh * 2 + yl
    mine = dst.at[:, lanes(x * 4 + yl * 2 + yh)]
    copies = []
    for dx, dy in XY_ALL:
        tx, ty = lax.rem(x + dx, 4), lax.rem(y + dy, 4)
        copies.append(engine.send(src.at[rows_at(ty, n), lanes(tx)], mine, xy_peer(dx, dy)))
    copies.append(engine.local(src.at[rows_at(y, n), lanes(x)], mine))
    return copies


def return_items(engine, src, dst, n):
    x, yl, yh = (lax.axis_index(a) for a in ("x", "yl", "yh"))
    mine = dst.at[rows_at(yh * 2 + yl, n), lanes(x)]
    copies = []
    for dx, dy in XY_ALL:
        to = xy_peer(dx, dy)
        copies.append(engine.send(src.at[:, lanes(to["x"] * 4 + to["yl"] * 2 + to["yh"])], mine, to))
    copies.append(engine.local(src.at[:, lanes(x * 4 + yl * 2 + yh)], mine))
    return copies


def add_up(total, terms, index, rows, width):
    def step(i, carry):
        here = (*index, rows_at(i, 16), slice(0, width))
        value = terms[0][here].astype(F32)
        for term in terms[1:]:
            value += term[here].astype(F32)
        total[here] = value.astype(total.dtype)
        return carry

    lax.fori_loop(0, rows // 16, step, 0)


def scatter_tokens(engine, src, dst, own, other, arrived):
    z, core = lax.axis_index("z"), lax.axis_index("core")
    pairs = []
    for i in range(4):
        base = lax.rem(z + 1 + i, 4) * 2
        there = engine.send(src.at[rows_at(base + 1 - core, OWN)], other.at[i], sibling())
        here = engine.local(src.at[rows_at(base + core, OWN)], own.at[i])
        pairs.append((there, here))
    yield
    sent = []
    for i in range(3):
        pairs[i][0].wait_recv()
        pairs[i][1].wait()
        own[i] = (own[i].astype(F32) + other[i].astype(F32)).astype(BF16)
        sent.append(engine.send(own.at[i], arrived.at[i], z_peer(i + 1)))
    yield
    pairs[3][0].wait_recv()
    pairs[3][1].wait()
    dst[...] = own[3].astype(F32) + other[3].astype(F32)
    for i in range(3):
        sent[i].wait_recv()
        dst[...] += arrived[i].astype(F32)
    yield
    for copy in sent:
        copy.wait_send()
    for there, _ in pairs:
        there.wait_send()


def scatter_product(engine, rows, matrix, dst, product, other, arrived):
    z, core = lax.axis_index("z"), lax.axis_index("core")
    for k in range(4):
        columns = slice(k * 512, (k + 1) * 512)
        product[:, columns] = dot(rows[...], matrix[:, columns], (1, 0)).astype(BF16)
    to_core = []
    for i in range(4):
        give = product.at[rows_at(lax.rem(z + 1 + i, 4) * 2 + 1 - core, OWN)]
        to_core.append(engine.send(give, other.at[i], sibling()))
    yield
    to_z = []
    for i in range(3):
        own = rows_at(lax.rem(z + 1 + i, 4) * 2 + core, OWN)
        to_core[i].wait_recv()
        product[own, :] = (product[own, :].astype(F32) + other[i].astype(F32)).astype(BF16)
        to_z.append(engine.send(product.at[own], arrived.at[i], z_peer(i + 1)))
    yield
    to_core[3].wait_recv()
    dst[...] = product[rows_at(z * 2 + core, OWN), :].astype(F32) + other[3].astype(F32)
    for i in range(3):
        to_z[i].wait_recv()
        dst[...] += arrived[i].astype(F32)
    yield
    for copy in to_core + to_z:
        copy.wait_send()


def sum_first(engine, src, sum_y, sum_x, by_y, by_x, relay_y, relay_x, own_y, own_x):
    n, cut = src.shape[1], sum_y.shape[0]
    rest, half = n - cut, first_part(cut)
    tail = pl.ds(cut, rest)
    early, late = pl.ds(0, half), pl.ds(half, cut - half)
    low, high = pl.ds(0, 2), pl.ds(2, 2)
    x = lax.axis_index("x")
    y = lax.axis_index("yh") * 2 + lax.axis_index("yl")
    up_y, down_y = lax.rem(y + 1, 4), lax.rem(y + 3, 4)
    up_x, down_x = lanes(lax.rem(x + 1, 4), 512), lanes(lax.rem(x + 3, 4), 512)
    far_y, far_x = lax.rem(y + 2, 4), lanes(lax.rem(x + 2, 4), 512)
    relays = [
        engine.send(src.at[far_y, early], relay_y.at[early], y_peer(1)),
        engine.send(src.at[low, tail, far_x], relay_x.at[low], x_peer(1)),
        engine.send(src.at[far_y, late], relay_y.at[late], y_peer(3)),
        engine.send(src.at[high, tail, far_x], relay_x.at[high], x_peer(3)),
    ]
    copies = [
        engine.send(src.at[up_y, late], by_y.at[0, late], y_peer(1)),
        engine.send(src.at[high, tail, up_x], by_x.at[0, high], x_peer(1)),
        engine.send(src.at[down_y, early], by_y.at[1, early], y_peer(3)),
        engine.send(src.at[low, tail, down_x], by_x.at[1, low], x_peer(3)),
    ]
    yield
    own_y, own_x = own_y.at[pl.ds(0, cut)], own_x.at[:, pl.ds(0, rest)]
    local = [
        engine.local(src.at[up_y, early], own_y.at[early]),
        engine.local(src.at[down_y, late], own_y.at[late]),
        engine.local(src.at[low, tail, up_x], own_x.at[low]),
        engine.local(src.at[high, tail, down_x], own_x.at[high]),
    ]
    for copy in local:
        copy.wait()
    relays[0].wait_recv()
    add_up(relay_y.at[early], [relay_y.at[early], own_y.at[early]], (), half, WIDTH)
    copies.append(engine.send(relay_y.at[early], by_y.at[0, early], y_peer(1)))
    relays[1].wait_recv()
    for q in range(2):
        add_up(relay_x, [relay_x, own_x], (q,), rest, 512)
    copies.append(engine.send(relay_x.at[low], by_x.at[0, low], x_peer(1)))
    relays[2].wait_recv()
    add_up(relay_y.at[late], [relay_y.at[late], own_y.at[late]], (), cut - half, WIDTH)
    copies.append(engine.send(relay_y.at[late], by_y.at[1, late], y_peer(3)))
    relays[3].wait_recv()
    for q in range(2, 4):
        add_up(relay_x, [relay_x, own_x], (q,), rest, 512)
    copies.append(engine.send(relay_x.at[high], by_x.at[1, high], x_peer(3)))
    yield
    local = [
        engine.local(src.at[y, pl.ds(0, cut)], own_y),
        engine.local(src.at[:, tail, lanes(x, 512)], own_x),
    ]
    for copy in local:
        copy.wait()
    for copy in copies:
        copy.wait_recv()
    add_up(sum_y, [own_y, by_y.at[0], by_y.at[1]], (), cut, WIDTH)
    for q in range(4):
        add_up(sum_x, [own_x, by_x.at[0], by_x.at[1]], (q,), rest, 512)
    yield
    for copy in relays + copies:
        copy.wait_send()


def sum_rest(engine, heads, tails, landing, by_x, by_y, own, total):
    cut, rest = heads.shape[0], tails.shape[1]
    x = lax.axis_index("x")
    y = lax.axis_index("yh") * 2 + lax.axis_index("yl")
    first, second = pl.ds(0, cut), pl.ds(cut, rest)
    copies = []
    for d in (2, 1, 3):
        ty, tx = y_peer(d), x_peer(d)
        copies.append(engine.send(heads.at[:, lanes(tx["x"], 512)], by_x.at[d - 1], tx))
        copies.append(engine.send(tails.at[ty["yh"] * 2 + ty["yl"]], by_y.at[d - 1], ty))
    local = [engine.local(tails.at[y], own.at[second]), engine.local(heads.at[:, lanes(x, 512)], own.at[first])]
    yield
    for copy in local:
        copy.wait()
    for copy in copies:
        copy.wait_recv()
    add_up(total.at[first], [own.at[first]] + [by_x.at[k] for k in range(3)], (), cut, 512)
    add_up(total.at[second], [own.at[second]] + [by_y.at[k] for k in range(3)], (), rest, 512)
    moved = send_pieces(engine, lambda z: total.at[:, lanes(z)], landing)
    yield
    moved[0].wait()
    for copy in moved[1:]:
        copy.wait_recv()
    yield
    for copy in copies + moved[1:]:
        copy.wait_send()


def gather_ctx(engine, landing, dst):
    x, yl, core = (lax.axis_index(a) for a in ("x", "yl", "core"))

    def slot(dx, ll):
        return (lax.rem(x + dx, 4) * 2 + ll) * 2 + core

    other = 1 - yl
    first, second = pl.ds(0, 2), pl.ds(2, 2)
    even, odd = (pl.ds(0, 1), pl.ds(1, 1)), (pl.ds(2, 1), pl.ds(3, 1))
    partner, there = {"yl": other}, sibling()
    sent = []

    def send(source, target, part, device):
        copy = engine.send(source, dst.at[target, part], device)
        sent.append(copy)
        return copy

    def hand(index, part):
        block = dst.at[index, part]
        return send(block, index, part, there)

    def on(index, part, device):
        return send(dst.at[index, part], index, part, device)

    me = slot(0, yl)
    local = engine.local(landing, dst.at[me])
    siblings = [engine.send(landing, dst.at[me], there)]
    to_y = send(landing.at[first], me, first, partner)
    round_b = [send(landing.at[second], me, second, x_peer(d)) for d in (1, 3)]
    round_a = [send(landing.at[first], me, first, x_peer(d)) for d in (1, 3)]
    over = [send(landing.at[second], me, second, partner)]
    yield
    to_y.wait_recv()
    round_c = [on(slot(0, other), first, x_peer(d)) for d in (1, 3)]
    siblings.append(hand(slot(0, other), first))
    onward = []
    for k, (d, to) in enumerate(((3, 1), (1, 3))):
        round_b[k].wait_recv()
        onward.append(on(slot(d, yl), odd[k], x_peer(to)))
        over.append(on(slot(d, yl), second, partner))
        siblings.append(hand(slot(d, yl), second))
    for k, (d, to) in enumerate(((3, 1), (1, 3))):
        round_a[k].wait_recv()
        onward.append(on(slot(d, yl), even[k], x_peer(to)))
        siblings.append(hand(slot(d, yl), first))
    yield
    for k in range(2):
        onward[k].wait_recv()
    over.append(on(slot(2, yl), second, partner))
    siblings.append(hand(slot(2, yl), second))
    for k, (d, to) in enumerate(((3, 1), (1, 3))):
        round_c[k].wait_recv()
        onward.append(on(slot(d, other), even[k], x_peer(to)))
        siblings.append(hand(slot(d, other), first))
    yield
    for k in (2, 3):
        onward[k].wait_recv()
    siblings.append(hand(slot(2, yl), first))
    for k, d in enumerate((0, 3, 1, 2)):
        over[k].wait_recv()
        siblings.append(hand(slot(d, other), second))
    for k in (4, 5):
        onward[k].wait_recv()
    siblings.append(hand(slot(2, other), first))
    yield
    local.wait()
    for copy in siblings:
        copy.wait_recv()
    siblings[0].wait_send()
    for copy in sent:
        copy.wait_send()


def group_peer(dz, dc):
    return {
        "z": lax.rem(lax.axis_index("z") + dz, 4),
        "core": lax.rem(lax.axis_index("core") + dc, 2),
    }


GROUP_ALL = [(dz, dc) for dz in range(4) for dc in range(2) if dz or dc]


def sum_small(engine, norms, bias, norm_sum, bias_all, by_group, by_x, by_y):
    z, x, yl, core, yh = place()
    y = yh * 2 + yl
    me = z * 2 + core
    first = []
    for dz, dc in GROUP_ALL:
        to = group_peer(dz, dc)
        first.append(engine.send(norms.at[:, lanes(to["z"], 512)], by_group.at[me], to))
    mine = engine.local(norms.at[:, lanes(z, 512)], by_group.at[me])
    yield
    mine.wait()
    for copy in first:
        copy.wait_recv()
    by_x[x, :, :512] = sum(by_group[k] for k in range(8))
    by_x[x, :, 512:] = bias[...]
    second = [engine.send(by_x.at[x], by_x.at[x], x_peer(d)) for d in (1, 2, 3)]
    yield
    for copy in second:
        copy.wait_recv()
    by_y[y] = sum(by_x[k] for k in range(4))
    third = [engine.send(by_y.at[y], by_y.at[y], y_peer(d)) for d in (1, 2, 3)]
    yield
    for copy in third:
        copy.wait_recv()
    total = sum(by_y[k] for k in range(4))
    norm_sum[...] = total[:, :512]
    bias_all[me] = total[:, 512:]
    last = [engine.send(bias_all.at[me], bias_all.at[me], group_peer(dz, dc)) for dz, dc in GROUP_ALL]
    yield
    for copy in last:
        copy.wait()
    for copy in first + second + third:
        copy.wait_send()


def hand_back(engine, src, dst):
    core, yh = lax.axis_index("core"), lax.axis_index("yh")
    far = {"core": yh, "yh": 1 - yh}
    near = {"core": yh}
    stays = core == yh
    mine = dst.at[rows_at(core, OWN)]
    i, j = engine.remote, engine.locals
    engine.remote += 4
    engine.locals += 1
    send_sem, recv_sem, local_sem = engine.sems

    def make(to, slot):
        return pltpu.make_async_remote_copy(
            src,
            mine,
            send_sem.at[i + slot],
            recv_sem.at[i + 2 + core],
            device_id=to,
            device_id_type=MESH_ID,
        )

    def arrival(half):
        part = dst.at[rows_at(half, OWN)]
        return pltpu.make_async_remote_copy(
            part, part, send_sem.at[i], recv_sem.at[i + 2 + half], device_id=far, device_id_type=MESH_ID
        )

    make(far, 0).start()

    @pl.when(stays)
    def _():
        pltpu.make_async_copy(src, mine, local_sem.at[j]).start()

    @pl.when(jnp.logical_not(stays))
    def _():
        make(near, 1).start()

    yield
    make(far, 0).wait_send()

    @pl.when(stays)
    def _():
        pltpu.make_async_copy(src, mine, local_sem.at[j]).wait()
        arrival(1 - core).wait_recv()

    @pl.when(jnp.logical_not(stays))
    def _():
        make(near, 1).wait_send()
        arrival(core).wait_recv()
        arrival(1 - core).wait_recv()


def dot(a, b, dims):
    return lax.dot_general(a, b, ((dims[:1], dims[1:]), ((), ())), preferred_element_type=F32)


def rope(block, cosine, sine):
    front, back = block[:8], block[8:16]
    return jnp.concatenate(
        [front * cosine - back * sine, back * cosine + front * sine, block[16:]], axis=0
    )


def rope_back(block, cosine, sine):
    front, back = block[:8], block[8:16]
    return jnp.concatenate(
        [front * cosine + back * sine, back * cosine - front * sine, block[16:]], axis=0
    )


def masked_scores(scores, start, seg_row, seg_col):
    stop = start + QB

    def hide(first, last, by_segment, causal):
        part = scores[first:last]
        keep = None
        if by_segment:
            keep = seg_col[first:last] == seg_row[:, start:stop]
        if causal:
            key_at = first + lax.broadcasted_iota(jnp.int32, part.shape, 0)
            query_at = start + lax.broadcasted_iota(jnp.int32, part.shape, 1)
            order = key_at <= query_at
            keep = order if keep is None else keep & order
        return jnp.where(keep, part, NEG)

    if start == 0:
        return hide(0, stop, True, True)
    if stop + 127 <= SEQ:
        parts = [hide(0, 128, True, False)]
        if start > 128:
            parts.append(scores[128:start])
        parts.append(hide(start, stop, False, True))
        return jnp.concatenate(parts, axis=0)
    return jnp.concatenate([hide(0, start, True, False), hide(start, stop, True, True)], axis=0)


def attend(qkv_ref, row_ref, col_ref, cos_ref, sin_ref, o_ref, wide_ref, lse_ref, kept_ref):
    cosine, sine = cos_ref[...], sin_ref[...]
    q_t = rope(qkv_ref[:HEAD].astype(F32), cosine, sine).astype(BF16) * jnp.asarray(0.125, BF16)
    k_t = rope(qkv_ref[HEAD : 2 * HEAD].astype(F32), cosine, sine).astype(BF16)
    v_t = qkv_ref[2 * HEAD :]
    kept_ref[:HEAD] = q_t
    kept_ref[HEAD : 2 * HEAD] = k_t
    kept_ref[2 * HEAD :] = v_t
    keys = k_t.astype(F32).T.astype(BF16)
    seg_row, seg_col = row_ref[...], col_ref[...]
    for start in range(0, SEQ, QB):
        stop = start + QB
        scores = dot(keys[:stop], q_t[:, start:stop], (1, 0))
        scores = masked_scores(scores, start, seg_row, seg_col)
        top = jnp.max(scores, axis=0, keepdims=True)
        terms = jnp.exp(scores - top)
        total = jnp.sum(terms, axis=0, keepdims=True)
        out = dot(v_t[:, :stop], terms.astype(BF16), (1, 0)) / total
        wide_ref[:, start:stop] = out
        o_ref[:, start:stop] = out.astype(BF16)
        lse_ref[:, start:stop] = top + jnp.log(total)


def attend_back(kept_ref, do_ref, wide_ref, lse_ref, row_ref, col_ref, cos_ref, sin_ref, out_ref, sum_ref):
    cosine, sine = cos_ref[...], sin_ref[...]
    q_t, k_t, do_t = kept_ref[:HEAD], kept_ref[HEAD : 2 * HEAD], do_ref[...]
    queries = q_t.astype(F32).T.astype(BF16)
    keys = k_t.astype(F32).T.astype(BF16)
    values = kept_ref[2 * HEAD :].astype(F32).T.astype(BF16)
    grads = do_t.astype(F32).T.astype(BF16)
    centre = jnp.sum(do_t.astype(F32) * wide_ref[...], axis=0, keepdims=True)
    lse = lse_ref[...]
    seg_row, seg_col = row_ref[...], col_ref[...]
    sum_ref[...] = jnp.zeros_like(sum_ref)
    dq_parts = []
    for start in range(0, SEQ, QB):
        stop = start + QB
        scores = dot(keys[:stop], q_t[:, start:stop], (1, 0))
        scores = masked_scores(scores, start, seg_row, seg_col)
        probs = jnp.exp(scores - lse[:, start:stop])
        d_probs = dot(values[:stop], do_t[:, start:stop], (1, 0))
        d_scores = (probs * (d_probs - centre[:, start:stop])).astype(BF16)
        d_keys = dot(d_scores, queries[start:stop], (1, 0))
        d_values = dot(probs.astype(BF16), grads[start:stop], (1, 0))
        sum_ref[:stop] += jnp.concatenate([d_keys, d_values], axis=1)
        dq_parts.append(dot(k_t[:, :stop], d_scores, (1, 0)) * 0.125)
    out_ref[:HEAD] = rope_back(jnp.concatenate(dq_parts, axis=1), cosine, sine).astype(BF16)
    turned = sum_ref[...].T
    out_ref[HEAD : 2 * HEAD] = rope_back(turned[:HEAD], cosine, sine).astype(BF16)
    out_ref[2 * HEAD :] = turned[HEAD:].astype(BF16)


def small_peer(dz, dh):
    return {
        "z": lax.rem(lax.axis_index("z") + dz, 4),
        "yh": lax.rem(lax.axis_index("yh") + dh, 2),
    }


SMALL_ALL = [(dz, dh) for dz in range(4) for dh in range(2) if dz or dh]
FORWARD_PEERS = XY_PEERS + Z_PEERS + [sibling]
FORWARD_PEERS += [functools.partial(small_peer, dz, 1) for dz in (1, 2, 3)]

FORWARD_OUTS = [
    ("m_qkv", (4, 192, WIDTH), BF16, VMEM),
    ("m_out", (4, 64, WIDTH), BF16, VMEM),
    ("m_down", (4, 176, WIDTH), BF16, ANY),
    ("m_gate", (4, 176, WIDTH), BF16, ANY),
    ("m_up", (4, 176, WIDTH), BF16, ANY),
    ("x_own", (OWN, WIDTH), BF16, VMEM),
    ("dy_own", (OWN, WIDTH), BF16, VMEM),
    ("middle", (OWN, WIDTH), F32, VMEM),
    ("norms", (8, WIDTH), F32, VMEM),
    ("h1", (ROWS, WIDTH), BF16, VMEM),
    ("h2", (ROWS, WIDTH), BF16, VMEM),
    ("dy", (ROWS, WIDTH), BF16, ANY),
    ("o_t", (4 * HEAD, ROWS), BF16, VMEM),
    ("kept", (3 * HEAD, SEQ), BF16, VMEM),
    ("wide", (HEAD, SEQ), F32, VMEM),
    ("lse", (1, SEQ), F32, VMEM),
    ("seg_row", (1, SEQ), F32, VMEM),
    ("seg_col", (SEQ, 1), F32, VMEM),
]
FORWARD_SCRATCH = [
    ("small", (4, 2, 16, 640), BF16),
    ("near_x", (OWN, WIDTH), BF16),
    ("near_dy", (OWN, WIDTH), BF16),
    ("far_x", (OWN, WIDTH), BF16),
    ("far_dy", (OWN, WIDTH), BF16),
    ("h1_own", (OWN, WIDTH), BF16),
    ("h2_own", (OWN, WIDTH), BF16),
    ("held_qkv", (3, 128, 1024), BF16),
    ("held_gu", (128, 2, 2816), BF16),
    ("turned", (2816, 128), F32),
    ("cut_qkv", (4, 192, 128), BF16),
    ("cut_gate", (4, 176, 128), BF16),
    ("cut_up", (4, 176, 128), BF16),
    ("p_qkv", (192, 512), BF16),
    ("p_out", (64, 512), BF16),
    ("p_down", (176, 512), BF16),
    ("p_gate", (176, 512), BF16),
    ("p_up", (176, 512), BF16),
    ("bias", (4, 192, 1), F32),
    ("qkv_t", (12 * HEAD, ROWS), BF16),
    ("item", (3 * HEAD, SEQ), BF16),
    ("out", (HEAD, SEQ), BF16),
    ("o_rows", (ROWS, 4 * HEAD), BF16),
    ("other", (4, OWN, WIDTH), BF16),
    ("product", (ROWS, WIDTH), BF16),
    ("arrived", (3, OWN, WIDTH), BF16),
]


FIRST_PARTS = ("sum_y_", "sum_x_", "by_y_", "by_x_", "relay_y_", "relay_x_")


class Refs:
    pass


def forward_kernel(*refs):
    r = Refs()
    names = ["tokens", "cotangent", "packed", "w_qkv", "w_out", "w_down", "w_gate_up", "cos", "sin"]
    names += [o[0] for o in FORWARD_OUTS] + [o[0] for o in FORWARD_SCRATCH]
    for name, ref in zip(names, refs):
        setattr(r, name, ref)
    engine = Engine(*refs[len(names) :])
    z, x, yl, core, yh = place()
    y = yh * 2 + yl

    load_qkv = engine.local(r.w_qkv.at[:, rows_at(x, 128)], r.held_qkv)
    load_gu = engine.local(r.w_gate_up.at[rows_at(x, 128)], r.held_gu)
    load_x = engine.local(r.tokens.at[rows_at(core, OWN)], r.near_x)
    load_dy = engine.local(r.cotangent.at[rows_at(core, OWN)], r.near_dy)
    small_here = engine.local(r.packed, r.small.at[z, yh])

    def rows_of(n):
        return lambda zz: rows_at((zz * 2 + core) * 2 + yl, n)

    def slots_of(piece):
        return lambda zz: piece.at[:, lanes(zz)]

    load_qkv.wait()
    for part in range(3):
        r.turned[:1024, :] = r.held_qkv[part].astype(F32).T
        for zz in range(4):
            r.cut_qkv[zz, part * HEAD : (part + 1) * HEAD] = r.turned[rows_of(HEAD)(zz), :].astype(BF16)
    greet(FORWARD_PEERS)
    pieces_qkv = send_pieces(engine, lambda zz: r.cut_qkv.at[zz], slots_of(r.p_qkv))
    swap_x = engine.send(r.tokens.at[rows_at(1 - core, OWN)], r.far_x, sibling())
    smalls = [engine.send(r.packed, r.small.at[z, yh], small_peer(dz, dh)) for dz, dh in SMALL_ALL]
    pieces_out = send_pieces(engine, lambda zz: r.w_out.at[rows_of(64)(zz), lanes(x)], slots_of(r.p_out))
    swap_dy = engine.send(r.cotangent.at[rows_at(1 - core, OWN)], r.far_dy, sibling())
    load_gu.wait()
    for g, cut in ((0, r.cut_gate), (1, r.cut_up)):
        r.turned[...] = r.held_gu[:, g, :].astype(F32).T
        for zz in range(4):
            cut[zz] = r.turned[rows_of(176)(zz), :].astype(BF16)

    stays = core == yh
    load_x.wait()
    swap_x.wait_recv()
    x_rows = spread(jnp.where(stays, r.near_x[...].astype(F32), r.far_x[...].astype(F32)))
    r.x_own[...] = x_rows.astype(BF16)
    small_here.wait()
    for copy in smalls:
        copy.wait_recv()
    parts = [r.small[zz, 0].astype(F32) for zz in range(4)]
    r.norms[...] = jnp.concatenate(
        [parts[zz][:8, xx * 128 : (xx + 1) * 128] for xx in range(4) for zz in range(4)], axis=1
    )
    h1_full, _, _ = layer_norm(x_rows, r.norms[0:1], r.norms[2:3])
    r.h1_own[...] = h1_full.astype(BF16)
    tokens_h1 = gather_tokens(engine, r.h1_own, r.h1)
    next(tokens_h1)

    for copy in pieces_qkv[1:]:
        copy.wait_recv()
    pieces_qkv[0].wait()
    weight_qkv = gather_weight(engine, r.p_qkv, r.m_qkv)
    next(weight_qkv)

    lane_at = lax.broadcasted_iota(jnp.int32, (64, 128), 1)
    for h in range(2):
        table = jnp.concatenate([r.small[zz, h, :, 512:].astype(F32) for zz in range(4)], axis=0)
        for j in range(2):
            for part in range(3):
                picked = jnp.where(lane_at == (z * 2 + core) * 6 + j * 3 + part, table, 0.0)
                r.bias[h * 2 + j, part * HEAD : (part + 1) * HEAD] = jnp.sum(picked, axis=1, keepdims=True)
    marks = r.small[x, 0, :, :512].astype(F32)
    marks = [marks[4 + i : 5 + i, k * 128 : (k + 1) * 128] for i in range(4) for k in range(4)]
    r.seg_row[...] = jnp.concatenate(marks, axis=1)
    marks = jnp.concatenate(marks, axis=0).T
    r.seg_col[...] = jnp.concatenate([marks[:, k : k + 1] for k in range(16)], axis=0)

    next(weight_qkv)
    next(tokens_h1)
    pieces_down = send_pieces(engine, lambda zz: r.w_down.at[rows_of(176)(zz), lanes(x)], slots_of(r.p_down))
    pieces_gate = send_pieces(engine, lambda zz: r.cut_gate.at[zz], slots_of(r.p_gate))
    pieces_up = send_pieces(engine, lambda zz: r.cut_up.at[zz], slots_of(r.p_up))
    next(weight_qkv)

    def start_weight(pieces, piece, matrix):
        pieces[0].wait()
        for copy in pieces[1:]:
            copy.wait_recv()
        thread = gather_weight(engine, piece, matrix)
        next(thread)
        return thread

    weight_out = start_weight(pieces_out, r.p_out, r.m_out)
    load_dy.wait()
    swap_dy.wait_recv()
    dy_rows = jnp.where(stays, r.near_dy[...].astype(F32), r.far_dy[...].astype(F32))
    r.dy_own[...] = spread(dy_rows).astype(BF16)
    finish(tokens_h1)
    next(weight_out)
    finish(weight_qkv)

    r.qkv_t[...] = (
        dot(r.m_qkv[...].reshape(12 * HEAD, WIDTH), r.h1[...], (1, 1)) + r.bias[...].reshape(12 * HEAD, 1)
    ).astype(BF16)
    to_items = send_items(engine, r.qkv_t, r.item, 3 * HEAD)
    tokens_dy = gather_tokens(engine, r.dy_own, r.dy)
    next(tokens_dy)
    weight_down = start_weight(pieces_down, r.p_down, r.m_down)
    weight_gate = start_weight(pieces_gate, r.p_gate, r.m_gate)
    weight_up = start_weight(pieces_up, r.p_up, r.m_up)
    to_items[-1].wait()
    for copy in to_items[:-1]:
        copy.wait_recv()
    next(weight_out)
    attend(r.item, r.seg_row, r.seg_col, r.cos, r.sin, r.out, r.wide, r.lse, r.kept)
    back = return_items(engine, r.out, r.o_t, HEAD)
    next(weight_down)
    next(tokens_dy)
    finish(weight_out)
    back[-1].wait()
    for copy in back[:-1]:
        copy.wait_recv()

    r.o_rows[...] = r.o_t[...].astype(F32).T.astype(BF16)
    matrix = r.m_out[...].reshape(4 * HEAD, WIDTH)
    out = scatter_product(engine, r.o_rows, matrix, r.middle, r.product, r.other, r.arrived)
    next(out)
    next(out)
    next(weight_gate)
    next(weight_up)
    next(weight_down)
    next(weight_gate)
    next(out)
    r.middle[...] += x_rows

    h2_full, _, _ = layer_norm(r.middle[...], r.norms[1:2], r.norms[3:4])
    r.h2_own[...] = h2_full.astype(BF16)
    tokens_h2 = gather_tokens(engine, r.h2_own, r.h2)
    next(tokens_h2)
    next(weight_up)
    next(tokens_h2)
    finish(weight_down)
    finish(weight_gate)
    finish(tokens_dy)
    finish(weight_up)
    finish(tokens_h2)
    finish(out)
    sent = smalls + to_items[:-1] + back[:-1] + [swap_x, swap_dy]
    for pieces in (pieces_qkv, pieces_out, pieces_gate, pieces_down, pieces_up):
        sent += pieces[1:]
    for copy in sent:
        copy.wait_send()


def forward(tokens, cotangent, packed, w_qkv, w_out, w_down, w_gate_up, cosine, sine):
    values = pl.pallas_call(
        forward_kernel,
        out_shape=[jax.ShapeDtypeStruct(o[1], o[2]) for o in FORWARD_OUTS],
        in_specs=[ANY] * 7 + [VMEM] * 2,
        out_specs=[o[3] for o in FORWARD_OUTS],
        scratch_shapes=[pltpu.VMEM(shape, dtype) for _, shape, dtype in FORWARD_SCRATCH] + semaphores(160, 24),
        compiler_params=pltpu.CompilerParams(
            collective_id=1, has_side_effects=True, vmem_limit_bytes=50 * 2**20
        ),
        name="forward",
    )(tokens, cotangent, packed, w_qkv, w_out, w_down, w_gate_up, cosine, sine)
    result = Refs()
    for (name, *_), value in zip(FORWARD_OUTS, values):
        setattr(result, name, value)
    return result


def back_peer(dc, dh):
    return {
        "core": lax.rem(lax.axis_index("core") + dc, 2),
        "yh": lax.rem(lax.axis_index("yh") + dh, 2),
    }


BACKWARD_PEERS = XY_PEERS + Z_PEERS + [sibling, functools.partial(back_peer, 1, 1)]
BACKWARD_PEERS += [functools.partial(group_peer, dz, 1) for dz in (1, 2, 3)]
BACKWARD_FAR = ["back_part", "mlp_part", "g_gate", "g_up", "g_down", "h1", "m_qkv"]
BACKWARD_NEAR = ["middle", "x_own", "dy_own", "norms", "m_out", "o_t", "kept", "wide", "lse"]
BACKWARD_NEAR += ["seg_row", "seg_col", "cos", "sin"]
BACKWARD_OUTS = [
    ("layer_out", (2 * OWN, WIDTH), BF16, ANY),
    ("grad_tokens", (2 * OWN, WIDTH), BF16, ANY),
    ("gd_all", (16, 4, 352, 128), BF16, ANY),
    ("up_all", (16, 4, 176, 128), BF16, ANY),
    ("attn_all", (16, 4, 256, 128), BF16, ANY),
    ("norm_sum", (8, 512), F32, VMEM),
    ("bias_all", (8, 8, 768), F32, VMEM),
]
BACKWARD_SCRATCH = [
    ("v_h1", (ROWS, WIDTH), BF16),
    ("v_qkv", (4, 192, WIDTH), BF16),
    ("dz_own", (OWN, WIDTH), BF16),
    ("dz", (ROWS, WIDTH), BF16),
    ("d_middle", (OWN, WIDTH), F32),
    ("summed", (OWN, WIDTH), F32),
    ("out_own", (OWN, WIDTH), BF16),
    ("grad_own", (OWN, WIDTH), BF16),
    ("own_dh2", (4, OWN, WIDTH), BF16),
    ("other_dh2", (4, OWN, WIDTH), BF16),
    ("arrived_dh2", (3, OWN, WIDTH), BF16),
    ("own_mlp", (4, OWN, WIDTH), BF16),
    ("other_mlp", (4, OWN, WIDTH), BF16),
    ("arrived_mlp", (3, OWN, WIDTH), BF16),
    ("product", (ROWS, WIDTH), BF16),
    ("other_dh1", (4, OWN, WIDTH), BF16),
    ("arrived_dh1", (3, OWN, WIDTH), BF16),
    ("own_y", (128, WIDTH), BF16),
    ("own_x", (4, 128, 512), BF16),
    ("d_o", (4 * HEAD, ROWS), BF16),
    ("item", (HEAD, SEQ), BF16),
    ("item_out", (3 * HEAD, SEQ), BF16),
    ("d_kv", (SEQ, 2 * HEAD), F32),
    ("d_qkv", (12 * HEAD, ROWS), BF16),
    ("d_rows", (ROWS, 12 * HEAD), BF16),
    ("g_attn", (4, 256, WIDTH), BF16),
    ("landing_gd", (4, 352, 128), BF16),
    ("landing_up", (4, 176, 128), BF16),
    ("landing_attn", (4, 256, 128), BF16),
    ("small_norms", (8, WIDTH), F32),
    ("small_bias", (8, 768), F32),
    ("by_group", (8, 8, 512), F32),
    ("small_x", (4, 8, 1280), F32),
    ("small_y", (4, 8, 1280), F32),
]
for _name, _n in (("gate", 176), ("down", 176), ("up", 176), ("attn", 256)):
    _cut = first_part(_n)
    BACKWARD_SCRATCH += [
        ("sum_y_" + _name, (_cut, WIDTH), BF16),
        ("sum_x_" + _name, (4, _n - _cut, 512), BF16),
        ("by_y_" + _name, (2, _cut, WIDTH), BF16),
        ("by_x_" + _name, (2, 4, _n - _cut, 512), BF16),
        ("relay_y_" + _name, (_cut, WIDTH), BF16),
        ("relay_x_" + _name, (4, _n - _cut, 512), BF16),
        ("rest_x_" + _name, (3, _cut, 512), BF16),
        ("rest_y_" + _name, (3, _n - _cut, 512), BF16),
        ("rest_own_" + _name, (_n, 512), BF16),
        ("rest_total_" + _name, (_n, 512), BF16),
    ]


def backward_kernel(*refs):
    r = Refs()
    names = BACKWARD_FAR + BACKWARD_NEAR + [o[0] for o in BACKWARD_OUTS] + [o[0] for o in BACKWARD_SCRATCH]
    for name, ref in zip(names, refs):
        setattr(r, name, ref)
    engine = Engine(*refs[len(names) :])
    z, x, yl, core, yh = place()
    y = yh * 2 + yl
    load_h1 = engine.local(r.h1, r.v_h1)
    load_qkv = engine.local(r.m_qkv, r.v_qkv)
    greet(BACKWARD_PEERS)

    def first_of(name, grad):
        parts = [getattr(r, part + name) for part in FIRST_PARTS]
        thread = sum_first(engine, grad, *parts, r.own_y, r.own_x)
        next(thread)
        return thread

    def rest_of(name, landing):
        parts = [getattr(r, part + name) for part in ("rest_x_", "rest_y_", "rest_own_", "rest_total_")]
        thread = sum_rest(engine, getattr(r, "sum_y_" + name), getattr(r, "sum_x_" + name), landing, *parts)
        next(thread)
        return thread

    def part_of(landing, first):
        return lambda zz: landing.at[zz, pl.ds(first, 176)]

    dh2 = scatter_tokens(engine, r.back_part, r.summed, r.own_dh2, r.other_dh2, r.arrived_dh2)
    next(dh2)
    gate = first_of("gate", r.g_gate)
    down = first_of("down", r.g_down)
    next(dh2)
    mlp = scatter_tokens(engine, r.mlp_part, r.d_middle, r.own_mlp, r.other_mlp, r.arrived_mlp)
    next(mlp)
    _, normed_b, rstd_b = layer_norm(r.middle[...], r.norms[1:2], r.norms[3:4])
    next(gate)
    next(down)
    next(dh2)
    back_b, gain_b, shift_b = norm_back(r.summed[...], normed_b, rstd_b, r.norms[1:2])
    d_middle = r.dy_own[...].astype(F32) + back_b
    r.dz_own[...] = d_middle.astype(BF16)
    tokens_dz = gather_tokens(engine, r.dz_own, r.dz)
    next(tokens_dz)
    r.small_norms[1:2] = gain_b[None]
    r.small_norms[3:4] = shift_b[None]
    next(gate)
    rest_gate = rest_of("gate", part_of(r.landing_gd, 0))
    next(down)
    rest_down = rest_of("down", part_of(r.landing_gd, 176))
    next(tokens_dz)
    finish(tokens_dz)
    next(mlp)

    r.d_o[...] = dot(r.m_out[...].reshape(4 * HEAD, WIDTH), r.dz[...], (1, 1)).astype(BF16)
    to_items = send_items(engine, r.d_o, r.item, HEAD)
    up = first_of("up", r.g_up)
    g_out = dot(r.o_t[...], r.dz[...], (1, 0)).astype(BF16)
    for q in range(4):
        r.g_attn[q, 192:] = g_out[q * HEAD : (q + 1) * HEAD]
    next(rest_gate)
    next(rest_down)
    to_items[-1].wait()
    for copy in to_items[:-1]:
        copy.wait_recv()
    attend_back(
        r.kept, r.item, r.wide, r.lse, r.seg_row, r.seg_col, r.cos, r.sin, r.item_out, r.d_kv
    )
    back = return_items(engine, r.item_out, r.d_qkv, 3 * HEAD)
    next(up)
    next(rest_gate)
    next(rest_down)
    gather_gd = gather_ctx(engine, r.landing_gd, r.gd_all)
    next(gather_gd)
    next(mlp)
    r.out_own[...] = spread(r.middle[...] + r.d_middle[...]).astype(BF16)
    r.d_middle[...] = d_middle
    hand_out = hand_back(engine, r.out_own, r.layer_out)
    next(hand_out)
    load_h1.wait()
    load_qkv.wait()
    back[-1].wait()
    for copy in back[:-1]:
        copy.wait_recv()

    r.d_rows[...] = r.d_qkv[...].astype(F32).T.astype(BF16)
    matrix = r.v_qkv[...].reshape(12 * HEAD, WIDTH)
    dh1 = scatter_product(engine, r.d_rows, matrix, r.summed, r.product, r.other_dh1, r.arrived_dh1)
    next(dh1)
    g_qkv = dot(r.d_qkv[...], r.v_h1[...], (1, 0)).astype(BF16)
    for q in range(4):
        r.g_attn[q, :192] = g_qkv[q * 3 * HEAD : (q + 1) * 3 * HEAD]
    attn = first_of("attn", r.g_attn)
    next(dh1)
    r.small_bias[...] = dot(jnp.ones((8, ROWS), BF16), r.d_qkv[...], (1, 1))
    _, normed_a, rstd_a = layer_norm(r.x_own[...].astype(F32), r.norms[0:1], r.norms[2:3])
    next(up)
    rest_up = rest_of("up", part_of(r.landing_up, 0))
    next(gather_gd)
    next(attn)
    next(dh1)
    back_a, gain_a, shift_a = norm_back(r.summed[...], normed_a, rstd_a, r.norms[0:1])
    r.grad_own[...] = spread(r.d_middle[...] + back_a).astype(BF16)
    hand_grad = hand_back(engine, r.grad_own, r.grad_tokens)
    next(hand_grad)
    r.small_norms[0:1] = gain_a[None]
    r.small_norms[2:3] = shift_a[None]
    r.small_norms[4:] = jnp.zeros((4, WIDTH), F32)
    r.small_norms[...] = spread(r.small_norms[...])
    small = sum_small(
        engine, r.small_norms, r.small_bias, r.norm_sum, r.bias_all, r.by_group, r.small_x, r.small_y
    )
    next(small)
    next(rest_up)
    next(attn)
    rest_attn = rest_of("attn", lambda zz: r.landing_attn.at[zz])
    next(rest_up)
    gather_up = gather_ctx(engine, r.landing_up, r.up_all)
    next(gather_up)
    next(small)
    next(gather_gd)
    next(rest_attn)
    next(small)
    next(rest_attn)
    gather_attn = gather_ctx(engine, r.landing_attn, r.attn_all)
    next(gather_attn)
    next(gather_up)
    next(small)
    next(gather_gd)
    next(gather_attn)
    next(gather_up)
    next(gather_attn)
    next(gather_up)
    next(gather_attn)
    threads = (dh2, mlp, gate, down, up, attn, rest_gate, rest_down, rest_up, rest_attn)
    for thread in threads + (hand_out, dh1, hand_grad, small, gather_gd, gather_up, gather_attn):
        finish(thread)
    for copy in to_items[:-1] + back[:-1]:
        copy.wait_send()


def backward(values):
    given = [values[name] for name in BACKWARD_FAR + BACKWARD_NEAR]
    return pl.pallas_call(
        backward_kernel,
        out_shape=[jax.ShapeDtypeStruct(o[1], o[2]) for o in BACKWARD_OUTS],
        in_specs=[ANY] * len(BACKWARD_FAR) + [VMEM] * len(BACKWARD_NEAR),
        out_specs=[o[3] for o in BACKWARD_OUTS],
        scratch_shapes=[pltpu.VMEM(shape, dtype) for _, shape, dtype in BACKWARD_SCRATCH] + semaphores(320, 64),
        compiler_params=pltpu.CompilerParams(
            collective_id=2, has_side_effects=True, vmem_limit_bytes=58 * 2**20
        ),
        name="backward",
    )(*given)


def assemble_kernel(gd_ref, up_ref, attn_ref, gu_ref, down_ref, qkv_ref, out_ref, turned):
    for g in range(2):
        for zz in range(4):
            for core in range(2):
                for yl in range(2):
                    row = zz * 704 + core * 352 + yl * 176
                    block = up_ref[0, yl * 2 + core, zz] if g else gd_ref[0, yl * 2 + core, zz, :176]
                    turned[row : row + 176, :] = block.astype(F32)
        for t in range(22):
            gu_ref[:, g, t * 128 : (t + 1) * 128] = turned[t * 128 : (t + 1) * 128, :].T
    for zz in range(4):
        for core in range(2):
            for yl in range(2):
                row = zz * 704 + core * 352 + yl * 176
                down_ref[row : row + 176, :] = gd_ref[0, yl * 2 + core, zz, 176:].astype(F32)
                row = zz * 256 + core * 128 + yl * 64
                out_ref[row : row + 64, :] = attn_ref[0, yl * 2 + core, zz, 192:].astype(F32)
            for part in range(3):
                rows = slice(part * 64, (part + 1) * 64)
                block = jnp.concatenate([attn_ref[0, core, zz, rows], attn_ref[0, 2 + core, zz, rows]], axis=0)
                column = zz * 256 + core * 128
                qkv_ref[part, :, column : column + 128] = block.astype(F32).T


def assemble(gd_all, up_all, attn_all):
    gd_all = gd_all.reshape(4, 4, 4, 352, 128)
    up_all = up_all.reshape(4, 4, 4, 176, 128)
    attn_all = attn_all.reshape(4, 4, 4, 256, 128)
    return pl.pallas_call(
        assemble_kernel,
        grid=(4,),
        in_specs=[
            pl.BlockSpec((1, 4, 4, 352, 128), lambda i: (i, 0, 0, 0, 0)),
            pl.BlockSpec((1, 4, 4, 176, 128), lambda i: (i, 0, 0, 0, 0)),
            pl.BlockSpec((1, 4, 4, 256, 128), lambda i: (i, 0, 0, 0, 0)),
        ],
        out_specs=[
            pl.BlockSpec((128, 2, 2816), lambda i: (i, 0, 0)),
            pl.BlockSpec((2816, 128), lambda i: (0, i)),
            pl.BlockSpec((3, 128, 1024), lambda i: (0, i, 0)),
            pl.BlockSpec((1024, 128), lambda i: (0, i)),
        ],
        out_shape=[
            jax.ShapeDtypeStruct((512, 2, 2816), F32),
            jax.ShapeDtypeStruct((2816, 512), F32),
            jax.ShapeDtypeStruct((3, 512, 1024), F32),
            jax.ShapeDtypeStruct((1024, 512), F32),
        ],
        scratch_shapes=[pltpu.VMEM((2816, 128), F32)],
        compiler_params=pltpu.CompilerParams(vmem_limit_bytes=48 * 2**20),
        name="assemble",
    )(gd_all, up_all, attn_all)


def rotation_tables():
    half = ROT // 2
    positions = jnp.arange(SEQ).astype(F32)
    inverse = 10000.0 ** (-(jnp.arange(half).astype(F32) * 2.0 / ROT))
    angles = inverse[:, None] * positions[None, :]
    return jnp.cos(angles), jnp.sin(angles)


def layer_norm(values, gain_row, shift_row):
    row_mean = jnp.mean(values, axis=-1, keepdims=True)
    centred = values - row_mean
    variance = jnp.mean(centred * centred, axis=-1, keepdims=True)
    rstd = lax.rsqrt(variance + EPS)
    normed = centred * rstd
    return normed * gain_row + shift_row, normed, rstd


def norm_back(gradient, normed, rstd, gain_row):
    shaped = gradient * gain_row
    centre = (
        shaped
        - jnp.mean(shaped, axis=-1, keepdims=True)
        - normed * jnp.mean(shaped * normed, axis=-1, keepdims=True)
    )
    return centre * rstd, jnp.sum(gradient * normed, axis=0), jnp.sum(gradient, axis=0)


def local(tokens, segments, w_qkv, b_qkv, w_out, w_gate_up, w_down, norm_gains, norm_shifts, cotangent):
    z, _, _, core, yh = place()

    def pick(values, axis, index):
        return lax.dynamic_index_in_dim(values, index, axis, keepdims=False)

    rows = jnp.concatenate(
        [norm_gains, norm_shifts, segments.astype(BF16).reshape(4, 512), jnp.zeros((8, 512), BF16)], axis=0
    )
    biases = b_qkv.reshape(3, 4, 2, 2, 16).transpose(4, 1, 2, 3, 0).reshape(16, 48)
    packed = jnp.concatenate([rows, jnp.pad(biases, ((0, 0), (0, 80)))], axis=1)
    cosine, sine = rotation_tables()
    f = forward(
        tokens[0], cotangent[0], packed, w_qkv.transpose(1, 0, 2), w_out, w_down, w_gate_up, cosine, sine
    )
    h2, dy = f.h2, f.dy
    m_down, m_gate, m_up = (m.reshape(704, WIDTH) for m in (f.m_down, f.m_gate, f.m_up))

    gate, up = dot(m_gate, h2, (1, 1)), dot(m_up, h2, (1, 1))
    sigmoid = jax.nn.sigmoid(gate)
    silu = gate * sigmoid
    act = (silu * up).astype(BF16)
    d_act = dot(m_down, dy, (1, 1))
    d_gate = (d_act * up * sigmoid * (1.0 + gate * (1.0 - sigmoid))).astype(BF16)
    d_up = (d_act * silu).astype(BF16)
    mlp_part = dot(act, m_down, (0, 0)).astype(BF16)
    back_part = (dot(d_gate, m_gate, (0, 0)) + dot(d_up, m_up, (0, 0))).astype(BF16)

    def weight_grad(a, b):
        return dot(a, b, (1, 0)).astype(BF16).reshape(4, a.shape[0] // 4, WIDTH)

    g_gate, g_up, g_down = weight_grad(d_gate, h2), weight_grad(d_up, h2), weight_grad(act, dy)
    values = dict(vars(f), cos=cosine, sin=sine, back_part=back_part, mlp_part=mlp_part)
    values.update(g_gate=g_gate, g_up=g_up, g_down=g_down)
    layer_out, grad_tokens, gd_all, up_all, attn_all, norm_sum, bias_all = backward(values)

    bias_all = bias_all[:, 0].reshape(4, 2, 2, 2, 3, 4, 16)
    bias_all = pick(pick(bias_all, 2, yh), 4, z)
    grad_bias = bias_all.transpose(3, 0, 1, 2, 4).reshape(3, 16, 16)
    out_gu, out_down, out_qkv, out_out = assemble(gd_all, up_all, attn_all)
    return (
        layer_out[None],
        grad_tokens.astype(F32)[None],
        out_qkv.transpose(1, 0, 2),
        grad_bias,
        out_out,
        out_gu,
        out_down,
        norm_sum[:2],
        norm_sum[2:4],
    )


def solution(mesh):
    fine = Mesh(mesh.devices.reshape(4, 4, 2, 2, 2), ("z", "x", "yl", "core", "yh"))
    ctx = ("x", "yl", "core")
    return jax.shard_map(
        local,
        mesh=fine,
        in_specs=(
            P("z", ctx, None),
            P("z", None),
            P("z", None, "yh"),
            P(None, "yh", "z"),
            P("yh", "z"),
            P("z", None, "yh"),
            P("yh", "z"),
            P(None, "z"),
            P(None, "z"),
            P("z", ctx, None),
        ),
        out_specs=(
            P("z", ctx, None),
            P("z", ctx, None),
            P("z", None, "yh"),
            P(None, "yh", "z"),
            P("yh", "z"),
            P("z", None, "yh"),
            P("yh", "z"),
            P(None, "z"),
            P(None, "z"),
        ),
        check_vma=False,
    )
```

```python
import functools

import jax
import jax.numpy as jnp
import numpy as np
from jax import lax
from jax.experimental import pallas as pl
from jax.experimental.pallas import tpu as pltpu
from jax.sharding import Mesh
from jax.sharding import PartitionSpec as P

EPS = 1e-05
NEG = -1e30
ROT = 16
HEAD = 64
SEQ = 2048
WIDTH = 2048
OWN = 64
ROWS = 512
QB = 256
VMEM_BYTES = 63 * 2**20
F32 = jnp.float32
BF16 = jnp.bfloat16
MESH_ID = pl.DeviceIdType.MESH
HBM = pl.BlockSpec(memory_space=pltpu.HBM)
VMEM = pl.BlockSpec(memory_space=pltpu.VMEM)


def place():
    return tuple(lax.axis_index(a) for a in ("z", "x", "yl", "core", "yh"))


def lanes(index, size=128):
    return pl.ds(pl.multiple_of(index * size, size), size)


def rows_at(index, size):
    return pl.ds(pl.multiple_of(index * size, size), size)


def z_peer(d):
    z = lax.axis_index("z")
    return {"z": lax.rem(z + d, 4)}


def x_peer(d):
    x = lax.axis_index("x")
    return {"x": lax.rem(x + d, 4)}


def y_peer(d):
    y = lax.rem(lax.axis_index("yh") * 2 + lax.axis_index("yl") + d, 4)
    return {"yh": y // 2, "yl": lax.rem(y, 2)}


def xy_peer(dx, dy):
    return {**x_peer(dx), **y_peer(dy)}


def sibling():
    return {"core": 1 - lax.axis_index("core")}


Z_PEERS = [functools.partial(z_peer, d) for d in (1, 2, 3)]
X_PEERS = [functools.partial(x_peer, d) for d in (1, 2, 3)]
Y_PEERS = [functools.partial(y_peer, d) for d in (1, 2, 3)]
XY_ALL = [(dx, dy) for dx in range(4) for dy in range(4) if dx or dy]
XY_PEERS = [functools.partial(xy_peer, dx, dy) for dx, dy in XY_ALL]


class Remote:
    def __init__(self, engine, index, copy):
        self.engine, self.index, self.copy = engine, index, copy

    def wait_recv(self):
        self.copy.wait_recv()

    def wait_send(self):
        self.copy.wait_send()
        self.engine.free_send.append(self.index)

    def wait(self):
        self.wait_recv()
        self.wait_send()


class Local:
    def __init__(self, engine, index, copy):
        self.engine, self.index, self.copy = engine, index, copy

    def wait(self):
        self.copy.wait()
        self.engine.free_local.append(self.index)


class Engine:
    def __init__(self, send_sem, recv_sem, local_sem):
        self.send_sem, self.recv_sem, self.local_sem = send_sem, recv_sem, local_sem
        self.free_send = list(range(send_sem.shape[0]))[::-1]
        self.free_recv = list(range(recv_sem.shape[0]))[::-1]
        self.free_local = list(range(local_sem.shape[0]))[::-1]

    def send(self, src, dst, device):
        i, k = self.free_send.pop(), self.free_recv.pop()
        copy = pltpu.make_async_remote_copy(
            src, dst, self.send_sem.at[i], self.recv_sem.at[k], device_id=device, device_id_type=MESH_ID
        )
        copy.start()
        return Remote(self, i, copy)

    def local(self, src, dst):
        i = self.free_local.pop()
        copy = pltpu.make_async_copy(src, dst, self.local_sem.at[i])
        copy.start()
        return Local(self, i, copy)


def greet(peers):
    barrier = pltpu.get_barrier_semaphore()
    for peer in peers:
        pl.semaphore_signal(barrier, 1, device_id=peer(), device_id_type=MESH_ID)
    pl.semaphore_wait(barrier, len(peers))


def semaphores(n_send, n_recv, n_local):
    return [pltpu.SemaphoreType.DMA((n,)) for n in (n_send, n_recv, n_local)]


def spread(values):
    return jnp.concatenate(
        [values[:, (a * 4 + b) * 128 : (a * 4 + b + 1) * 128] for b in range(4) for a in range(4)], axis=1
    )


def finish(thread):
    for _ in thread:
        pass


def send_pieces(engine, pieces, slots):
    z = lax.axis_index("z")
    copies = [engine.local(pieces(z), slots(z))]
    for d in (1, 2, 3):
        to = z_peer(d)
        copies.append(engine.send(pieces(to["z"]), slots(z), to))
    return copies


def gather_tokens(engine, src, dst):
    z, core = lax.axis_index("z"), lax.axis_index("core")
    mine = dst.at[rows_at(z * 2 + core, OWN)]
    first = [engine.send(src, mine, z_peer(d)) for d in (1, 2, 3)]
    rest = [engine.send(src, mine, sibling()), engine.local(src, mine)]
    yield
    for d in (1, 2, 3):
        first[d - 1].wait_recv()
        here = dst.at[rows_at(lax.rem(z + 4 - d, 4) * 2 + core, OWN)]
        rest.append(engine.send(here, here, sibling()))
    yield
    for copy in first:
        copy.wait_send()
    for copy in rest:
        copy.wait()


def gather_weight(engine, src, dst):
    n = src.shape[0]
    top = first_part(n)
    head, tail = pl.ds(0, top), pl.ds(top, n - top)
    x = lax.axis_index("x")
    y = lax.axis_index("yh") * 2 + lax.axis_index("yl")
    left_y, left_x = lax.rem(y + 3, 4), lax.rem(x + 3, 4)
    right_y, right_x = lax.rem(y + 1, 4), lax.rem(x + 1, 4)
    mine = lanes(x, 512)
    local = engine.local(src, dst.at[y, :, mine])
    along_x = [engine.send(src.at[head], dst.at[y, head, mine], x_peer(d)) for d in (1, 2, 3)]
    along_y = [engine.send(src.at[tail], dst.at[y, tail, mine], y_peer(d)) for d in (1, 2, 3)]
    yield
    local.wait()
    for copy in along_x:
        copy.wait_recv()
    ring_y = [engine.send(dst.at[y, head], dst.at[y, head], y_peer(d)) for d in (1, 3)]
    for copy in along_y:
        copy.wait_recv()
    ring_x = [engine.send(dst.at[:, tail, mine], dst.at[:, tail, mine], x_peer(d)) for d in (1, 3)]
    yield
    rest = []
    half = first_part(top)
    early, late = pl.ds(0, half), pl.ds(half, top - half)
    ring_y[0].wait_recv()
    rest.append(engine.send(dst.at[left_y, early], dst.at[left_y, early], y_peer(1)))
    ring_y[1].wait_recv()
    rest.append(engine.send(dst.at[right_y, late], dst.at[right_y, late], y_peer(3)))
    ring_x[0].wait_recv()
    block = dst.at[:, tail, lanes(left_x * 2, 256)]
    rest.append(engine.send(block, block, x_peer(1)))
    ring_x[1].wait_recv()
    block = dst.at[:, tail, lanes(right_x * 2 + 1, 256)]
    rest.append(engine.send(block, block, x_peer(3)))
    yield
    for copy in along_x + along_y + ring_y + ring_x:
        copy.wait_send()
    for copy in rest:
        copy.wait()


def first_part(n):
    return (n // 2 + 15) // 16 * 16


def send_items(engine, src, dst, n):
    x, yl, yh = (lax.axis_index(a) for a in ("x", "yl", "yh"))
    y = yh * 2 + yl
    mine = dst.at[:, lanes(x * 4 + yl * 2 + yh)]
    copies = []
    for dx, dy in XY_ALL:
        tx, ty = lax.rem(x + dx, 4), lax.rem(y + dy, 4)
        copies.append(engine.send(src.at[rows_at(ty, n), lanes(tx)], mine, xy_peer(dx, dy)))
    copies.append(engine.local(src.at[rows_at(y, n), lanes(x)], mine))
    return copies


def return_items(engine, src, dst, n):
    x, yl, yh = (lax.axis_index(a) for a in ("x", "yl", "yh"))
    mine = dst.at[rows_at(yh * 2 + yl, n), lanes(x)]
    copies = []
    for dx, dy in XY_ALL:
        to = xy_peer(dx, dy)
        copies.append(engine.send(src.at[:, lanes(to["x"] * 4 + to["yl"] * 2 + to["yh"])], mine, to))
    copies.append(engine.local(src.at[:, lanes(x * 4 + yl * 2 + yh)], mine))
    return copies


def add_up(total, terms, index, rows, width):
    def step(i, carry):
        here = (*index, rows_at(i, 16), slice(0, width))
        value = terms[0][here].astype(F32)
        for term in terms[1:]:
            value += term[here].astype(F32)
        total[here] = value.astype(total.dtype)
        return carry

    lax.fori_loop(0, rows // 16, step, 0)


def exact_dot(a, b):
    return jnp.dot(a, b, precision=lax.Precision.HIGHEST, preferred_element_type=F32)


def by_columns(dst, value_of):
    for k in range(4):
        columns = slice(k * 512, (k + 1) * 512)
        value = value_of(columns).astype(dst.dtype)
        dst[..., columns] = value.reshape(dst.shape[:-1] + (512,))


def scatter_tokens(engine, product, dst, other, arrived):
    z, core = lax.axis_index("z"), lax.axis_index("core")
    to_core = []
    for i in range(4):
        give = product.at[rows_at(lax.rem(z + 1 + i, 4) * 2 + 1 - core, OWN)]
        to_core.append(engine.send(give, other.at[i], sibling()))
    yield
    to_z = []
    for i in range(3):
        own = rows_at(lax.rem(z + 1 + i, 4) * 2 + core, OWN)
        to_core[i].wait_recv()
        product[own, :] = (product[own, :].astype(F32) + other[i].astype(F32)).astype(BF16)
        to_z.append(engine.send(product.at[own], arrived.at[i], z_peer(i + 1)))
    yield
    to_core[3].wait_recv()
    dst[...] = product[rows_at(z * 2 + core, OWN), :].astype(F32) + other[3].astype(F32)
    for i in range(3):
        to_z[i].wait_recv()
        dst[...] += arrived[i].astype(F32)
    yield
    for copy in to_core + to_z:
        copy.wait_send()


def sum_first(engine, src, sum_y, sum_x, by_y, by_x, relay_y, relay_x, own_y, own_x):
    n, cut = src.shape[1], sum_y.shape[0]
    rest, half = n - cut, first_part(cut)
    tail = pl.ds(cut, rest)
    early, late = pl.ds(0, half), pl.ds(half, cut - half)
    low, high = pl.ds(0, 2), pl.ds(2, 2)
    x = lax.axis_index("x")
    y = lax.axis_index("yh") * 2 + lax.axis_index("yl")
    up_y, down_y = lax.rem(y + 1, 4), lax.rem(y + 3, 4)
    up_x, down_x = lanes(lax.rem(x + 1, 4), 512), lanes(lax.rem(x + 3, 4), 512)
    far_y, far_x = lax.rem(y + 2, 4), lanes(lax.rem(x + 2, 4), 512)
    relays = [
        engine.send(src.at[far_y, early], relay_y.at[early], y_peer(1)),
        engine.send(src.at[low, tail, far_x], relay_x.at[low], x_peer(1)),
        engine.send(src.at[far_y, late], relay_y.at[late], y_peer(3)),
        engine.send(src.at[high, tail, far_x], relay_x.at[high], x_peer(3)),
    ]
    copies = [
        engine.send(src.at[up_y, late], by_y.at[0, late], y_peer(1)),
        engine.send(src.at[high, tail, up_x], by_x.at[0, high], x_peer(1)),
        engine.send(src.at[down_y, early], by_y.at[1, early], y_peer(3)),
        engine.send(src.at[low, tail, down_x], by_x.at[1, low], x_peer(3)),
    ]
    yield
    own_y, own_x = own_y.at[pl.ds(0, cut)], own_x.at[:, pl.ds(0, rest)]
    local = [
        engine.local(src.at[up_y, early], own_y.at[early]),
        engine.local(src.at[down_y, late], own_y.at[late]),
        engine.local(src.at[low, tail, up_x], own_x.at[low]),
        engine.local(src.at[high, tail, down_x], own_x.at[high]),
    ]
    for copy in local:
        copy.wait()
    passed = []
    relays[0].wait_recv()
    add_up(relay_y.at[early], [relay_y.at[early], own_y.at[early]], (), half, WIDTH)
    passed.append(engine.send(relay_y.at[early], by_y.at[0, early], y_peer(1)))
    relays[1].wait_recv()
    for q in range(2):
        add_up(relay_x, [relay_x, own_x], (q,), rest, 512)
    passed.append(engine.send(relay_x.at[low], by_x.at[0, low], x_peer(1)))
    relays[2].wait_recv()
    add_up(relay_y.at[late], [relay_y.at[late], own_y.at[late]], (), cut - half, WIDTH)
    passed.append(engine.send(relay_y.at[late], by_y.at[1, late], y_peer(3)))
    relays[3].wait_recv()
    for q in range(2, 4):
        add_up(relay_x, [relay_x, own_x], (q,), rest, 512)
    passed.append(engine.send(relay_x.at[high], by_x.at[1, high], x_peer(3)))
    yield
    local = [
        engine.local(src.at[y, pl.ds(0, cut)], own_y),
        engine.local(src.at[:, tail, lanes(x, 512)], own_x),
    ]
    for copy in local:
        copy.wait()
    for copy in copies + passed:
        copy.wait_recv()
    add_up(sum_y, [own_y, by_y.at[0], by_y.at[1]], (), cut, WIDTH)
    for q in range(4):
        add_up(sum_x, [own_x, by_x.at[0], by_x.at[1]], (q,), rest, 512)
    for copy in passed:
        copy.wait_send()
    yield
    for copy in relays + copies:
        copy.wait_send()


def sum_rest(engine, heads, tails, landing, by_x, by_y, own, total):
    cut, rest = heads.shape[0], tails.shape[1]
    x = lax.axis_index("x")
    y = lax.axis_index("yh") * 2 + lax.axis_index("yl")
    first, second = pl.ds(0, cut), pl.ds(cut, rest)
    copies = []
    for d in (2, 1, 3):
        ty, tx = y_peer(d), x_peer(d)
        copies.append(engine.send(heads.at[:, lanes(tx["x"], 512)], by_x.at[d - 1], tx))
        copies.append(engine.send(tails.at[ty["yh"] * 2 + ty["yl"]], by_y.at[d - 1], ty))
    local = [engine.local(tails.at[y], own.at[second]), engine.local(heads.at[:, lanes(x, 512)], own.at[first])]
    yield
    for copy in local:
        copy.wait()
    for copy in copies:
        copy.wait_recv()
    add_up(total.at[first], [own.at[first]] + [by_x.at[k] for k in range(3)], (), cut, 512)
    add_up(total.at[second], [own.at[second]] + [by_y.at[k] for k in range(3)], (), rest, 512)
    moved = send_pieces(engine, lambda z: total.at[:, lanes(z)], landing)
    yield
    moved[0].wait()
    for copy in moved[1:]:
        copy.wait_recv()
    yield
    for copy in copies + moved[1:]:
        copy.wait_send()


def gather_ctx(engine, landing, dst):
    x, yl, core = (lax.axis_index(a) for a in ("x", "yl", "core"))

    def slot(dx, ll):
        return (lax.rem(x + dx, 4) * 2 + ll) * 2 + core

    other, n = 1 - yl, landing.shape[1]
    half = first_part(n)
    first, second = (pl.ds(0, 3),), (pl.ds(3, 1),)
    even, even_other = ((pl.ds(0, 2),), (pl.ds(2, 1),)), ((pl.ds(0, 1),), (pl.ds(1, 2),))
    odd = ((pl.ds(3, 1), pl.ds(0, half)), (pl.ds(3, 1), pl.ds(half, n - half)))
    partner, there = {"yl": other}, sibling()
    sent = []

    def send(source, target, part, device):
        copy = engine.send(source, dst.at[(target, *part)], device)
        sent.append(copy)
        return copy

    def hand(index, part):
        return send(dst.at[(index, *part)], index, part, there)

    def on(index, part, device):
        return send(dst.at[(index, *part)], index, part, device)

    me = slot(0, yl)
    local = engine.local(landing, dst.at[me])
    siblings = [engine.send(landing, dst.at[me], there)]
    to_y = send(landing.at[*first], me, first, partner)
    round_b = [send(landing.at[*second], me, second, x_peer(d)) for d in (1, 3)]
    round_a = [send(landing.at[*first], me, first, x_peer(d)) for d in (1, 3)]
    over = [send(landing.at[*second], me, second, partner)]
    yield
    to_y.wait_recv()
    round_c = [on(slot(0, other), first, x_peer(d)) for d in (1, 3)]
    siblings.append(hand(slot(0, other), first))
    onward = []
    for k, (d, to) in enumerate(((3, 1), (1, 3))):
        round_b[k].wait_recv()
        onward.append(on(slot(d, yl), odd[k], x_peer(to)))
        over.append(on(slot(d, yl), second, partner))
        siblings.append(hand(slot(d, yl), second))
    for k, (d, to) in enumerate(((3, 1), (1, 3))):
        round_a[k].wait_recv()
        onward.append(on(slot(d, yl), even[k], x_peer(to)))
        siblings.append(hand(slot(d, yl), first))
    yield
    for k in range(2):
        onward[k].wait_recv()
    over.append(on(slot(2, yl), second, partner))
    siblings.append(hand(slot(2, yl), second))
    for k, (d, to) in enumerate(((3, 1), (1, 3))):
        round_c[k].wait_recv()
        onward.append(on(slot(d, other), even_other[k], x_peer(to)))
        siblings.append(hand(slot(d, other), first))
    yield
    for k in (2, 3):
        onward[k].wait_recv()
    siblings.append(hand(slot(2, yl), first))
    for k, d in enumerate((0, 3, 1, 2)):
        over[k].wait_recv()
        siblings.append(hand(slot(d, other), second))
    for k in (4, 5):
        onward[k].wait_recv()
    siblings.append(hand(slot(2, other), first))
    yield
    local.wait()
    for copy in siblings:
        copy.wait_recv()
    siblings[0].wait_send()
    for copy in sent:
        copy.wait_send()


def group_peer(dz, dc):
    return {
        "z": lax.rem(lax.axis_index("z") + dz, 4),
        "core": lax.rem(lax.axis_index("core") + dc, 2),
    }


GROUP_ALL = [(dz, dc) for dz in range(4) for dc in range(2) if dz or dc]


def sum_small(engine, norms, bias, norm_sum, bias_all, by_group, by_x, by_y):
    z, x, yl, core, yh = place()
    y = yh * 2 + yl
    me = z * 2 + core
    first = []
    for dz, dc in GROUP_ALL:
        to = group_peer(dz, dc)
        first.append(engine.send(norms.at[:, lanes(to["z"], 512)], by_group.at[me], to))
    mine = engine.local(norms.at[:, lanes(z, 512)], by_group.at[me])
    yield
    mine.wait()
    for copy in first:
        copy.wait_recv()
    by_x[x, :, :512] = sum(by_group[k] for k in range(8))
    by_x[x, :, 512:] = bias[...]
    second = [engine.send(by_x.at[x], by_x.at[x], x_peer(d)) for d in (1, 2, 3)]
    yield
    for copy in second:
        copy.wait_recv()
    by_y[y] = sum(by_x[k] for k in range(4))
    third = [engine.send(by_y.at[y], by_y.at[y], y_peer(d)) for d in (1, 2, 3)]
    yield
    for copy in third:
        copy.wait_recv()
    total = sum(by_y[k] for k in range(4))
    norm_sum[...] = total[:, :512]
    bias_all[me] = total[:, 512:]
    last = [engine.send(bias_all.at[me], bias_all.at[me], group_peer(dz, dc)) for dz, dc in GROUP_ALL]
    yield
    for copy in last:
        copy.wait()
    for copy in first + second + third:
        copy.wait_send()


def hand_back(engine, src, dst):
    core, yh = lax.axis_index("core"), lax.axis_index("yh")
    far = {"core": yh, "yh": 1 - yh}
    near = {"core": yh}
    stays = core == yh
    mine = dst.at[rows_at(core, OWN)]
    sends = [engine.free_send.pop() for _ in range(2)]
    arrivals = [engine.free_recv.pop() for _ in range(2)]
    j = engine.free_local.pop()
    send_sem, recv_sem, local_sem = engine.send_sem, engine.recv_sem, engine.local_sem

    def make(to, slot):
        return pltpu.make_async_remote_copy(
            src,
            mine,
            send_sem.at[sends[slot]],
            recv_sem.at[arrivals[0] + (arrivals[1] - arrivals[0]) * core],
            device_id=to,
            device_id_type=MESH_ID,
        )

    def arrival(half):
        part = dst.at[rows_at(half, OWN)]
        return pltpu.make_async_remote_copy(
            part, part, send_sem.at[sends[0]], recv_sem.at[arrivals[0] + (arrivals[1] - arrivals[0]) * half], device_id=far, device_id_type=MESH_ID
        )

    make(far, 0).start()

    @pl.when(stays)
    def _():
        pltpu.make_async_copy(src, mine, local_sem.at[j]).start()

    @pl.when(jnp.logical_not(stays))
    def _():
        make(near, 1).start()

    yield
    make(far, 0).wait_send()

    @pl.when(stays)
    def _():
        pltpu.make_async_copy(src, mine, local_sem.at[j]).wait()
        arrival(1 - core).wait_recv()

    @pl.when(jnp.logical_not(stays))
    def _():
        make(near, 1).wait_send()
        arrival(core).wait_recv()
        arrival(1 - core).wait_recv()

    engine.free_send.extend(sends)
    engine.free_local.append(j)


def dot(a, b, dims):
    return lax.dot_general(a, b, ((dims[:1], dims[1:]), ((), ())), preferred_element_type=F32)


def rope(block, cosine, sine):
    front, back = block[:8], block[8:16]
    return jnp.concatenate(
        [front * cosine - back * sine, back * cosine + front * sine, block[16:]], axis=0
    )


def rope_back(block, cosine, sine):
    front, back = block[:8], block[8:16]
    return jnp.concatenate(
        [front * cosine + back * sine, back * cosine - front * sine, block[16:]], axis=0
    )


def masked_scores(scores, start, seg_row, seg_col):
    stop = start + QB

    def hide(first, last, by_segment, causal):
        part = scores[first:last]
        keep = None
        if by_segment:
            keep = seg_col[first:last] == seg_row[:, start:stop]
        if causal:
            key_at = first + lax.broadcasted_iota(jnp.int32, part.shape, 0)
            query_at = start + lax.broadcasted_iota(jnp.int32, part.shape, 1)
            order = key_at <= query_at
            keep = order if keep is None else keep & order
        return jnp.where(keep, part, NEG)

    if start == 0:
        return hide(0, stop, True, True)
    if stop + 127 <= SEQ:
        parts = [hide(0, 128, True, False)]
        if start > 128:
            parts.append(scores[128:start])
        parts.append(hide(start, stop, False, True))
        return jnp.concatenate(parts, axis=0)
    return jnp.concatenate([hide(0, start, True, False), hide(start, stop, True, True)], axis=0)


def attend(qkv_ref, row_ref, col_ref, cos_ref, sin_ref, o_ref, wide_ref, lse_ref, kept_ref):
    cosine, sine = cos_ref[...], sin_ref[...]
    q_t = rope(qkv_ref[:HEAD].astype(F32), cosine, sine).astype(BF16) * jnp.asarray(0.125, BF16)
    k_t = rope(qkv_ref[HEAD : 2 * HEAD].astype(F32), cosine, sine).astype(BF16)
    v_t = qkv_ref[2 * HEAD :]
    kept_ref[:HEAD] = q_t
    kept_ref[HEAD : 2 * HEAD] = k_t
    kept_ref[2 * HEAD :] = v_t
    keys = k_t.astype(F32).T.astype(BF16)
    seg_row, seg_col = row_ref[...], col_ref[...]
    for start in range(0, SEQ, QB):
        stop = start + QB
        scores = dot(keys[:stop], q_t[:, start:stop], (1, 0))
        scores = masked_scores(scores, start, seg_row, seg_col)
        top = jnp.max(scores, axis=0, keepdims=True)
        terms = jnp.exp(scores - top)
        total = jnp.sum(terms, axis=0, keepdims=True)
        out = dot(v_t[:, :stop], terms.astype(BF16), (1, 0)) / total
        wide_ref[:, start:stop] = out
        o_ref[:, start:stop] = out.astype(BF16)
        lse_ref[:, start:stop] = top + jnp.log(total)


def attend_back(kept_ref, do_ref, wide_ref, lse_ref, row_ref, col_ref, cos_ref, sin_ref, out_ref, sum_ref):
    cosine, sine = cos_ref[...], sin_ref[...]
    q_t, k_t, do_t = kept_ref[:HEAD], kept_ref[HEAD : 2 * HEAD], do_ref[...]
    queries = q_t.astype(F32).T.astype(BF16)
    keys = k_t.astype(F32).T.astype(BF16)
    values = kept_ref[2 * HEAD :].astype(F32).T.astype(BF16)
    grads = do_t.astype(F32).T.astype(BF16)
    centre = jnp.sum(do_t.astype(F32) * wide_ref[...], axis=0, keepdims=True)
    lse = lse_ref[...]
    seg_row, seg_col = row_ref[...], col_ref[...]
    sum_ref[...] = jnp.zeros_like(sum_ref)
    dq_parts = []
    for start in range(0, SEQ, QB):
        stop = start + QB
        scores = dot(keys[:stop], q_t[:, start:stop], (1, 0))
        scores = masked_scores(scores, start, seg_row, seg_col)
        probs = jnp.exp(scores - lse[:, start:stop])
        d_probs = dot(values[:stop], do_t[:, start:stop], (1, 0))
        d_scores = (probs * (d_probs - centre[:, start:stop])).astype(BF16)
        d_keys = dot(d_scores, queries[start:stop], (1, 0))
        d_values = dot(probs.astype(BF16), grads[start:stop], (1, 0))
        sum_ref[:stop] += jnp.concatenate([d_keys, d_values], axis=1)
        dq_parts.append(dot(k_t[:, :stop], d_scores, (1, 0)) * 0.125)
    out_ref[:HEAD] = rope_back(jnp.concatenate(dq_parts, axis=1), cosine, sine).astype(BF16)
    turned = sum_ref[...].T
    out_ref[HEAD : 2 * HEAD] = rope_back(turned[:HEAD], cosine, sine).astype(BF16)
    out_ref[2 * HEAD :] = turned[HEAD:].astype(BF16)


def small_peer(dz, dh):
    return {
        "z": lax.rem(lax.axis_index("z") + dz, 4),
        "yh": lax.rem(lax.axis_index("yh") + dh, 2),
    }


SMALL_ALL = [(dz, dh) for dz in range(4) for dh in range(2) if dz or dh]
FORWARD_PEERS = XY_PEERS + Z_PEERS + [sibling]
FORWARD_PEERS += [functools.partial(small_peer, dz, 1) for dz in (1, 2, 3)]

FORWARD_KEPT = [
    ("m_qkv", (4, 192, WIDTH), BF16),
    ("m_out", (4, 64, WIDTH), BF16),
    ("x_own", (OWN, WIDTH), BF16),
    ("dy_own", (OWN, WIDTH), BF16),
    ("middle", (OWN, WIDTH), F32),
    ("norms", (8, WIDTH), F32),
    ("h1", (ROWS, WIDTH), BF16),
    ("o_t", (4 * HEAD, ROWS), BF16),
    ("kept", (3 * HEAD, SEQ), BF16),
    ("wide", (HEAD, SEQ), F32),
    ("lse", (1, SEQ), F32),
    ("seg_row", (1, SEQ), F32),
]
FORWARD_OUTS = [
    ("m_down", (4, 176, WIDTH), BF16),
    ("m_gate", (4, 176, WIDTH), BF16),
    ("m_up", (4, 176, WIDTH), BF16),
    ("h2", (ROWS, WIDTH), BF16),
    ("dy", (ROWS, WIDTH), BF16),
]
FORWARD_OUTS += [("to_" + name, shape, dtype) for name, shape, dtype in FORWARD_KEPT]
FORWARD_SCRATCH = FORWARD_KEPT + [
    ("seg_col", (SEQ, 1), F32),
    ("packed", (16, 640), BF16),
    ("small", (4, 2, 16, 640), BF16),
    ("near_x", (OWN, WIDTH), BF16),
    ("near_dy", (OWN, WIDTH), BF16),
    ("far_x", (OWN, WIDTH), BF16),
    ("far_dy", (OWN, WIDTH), BF16),
    ("h1_own", (OWN, WIDTH), BF16),
    ("h2_own", (OWN, WIDTH), BF16),
    ("held_qkv", (3, 128, 1024), BF16),
    ("held_gu", (128, 2, 2816), BF16),
    ("turned", (2816, 128), F32),
    ("cut_qkv", (4, 192, 128), BF16),
    ("cut_gate", (4, 176, 128), BF16),
    ("cut_up", (4, 176, 128), BF16),
    ("p_qkv", (192, 512), BF16),
    ("p_out", (64, 512), BF16),
    ("p_down", (176, 512), BF16),
    ("p_gate", (176, 512), BF16),
    ("p_up", (176, 512), BF16),
    ("bias", (4, 192, 1), F32),
    ("qkv_t", (12 * HEAD, ROWS), BF16),
    ("item", (3 * HEAD, SEQ), BF16),
    ("out", (HEAD, SEQ), BF16),
    ("o_rows", (ROWS, 4 * HEAD), BF16),
    ("other", (4, OWN, WIDTH), BF16),
    ("product", (ROWS, WIDTH), BF16),
    ("arrived", (3, OWN, WIDTH), BF16),
]


class Refs:
    pass


def column_of(row):
    blocks = jnp.concatenate([row[:, k * 128 : (k + 1) * 128] for k in range(16)], axis=0).T
    return jnp.concatenate([blocks[:, k : k + 1] for k in range(16)], axis=0)


def forward_kernel(*refs):
    r = Refs()
    names = ["tokens", "cotangent", "gains", "shifts", "biases", "segments"]
    names += ["w_qkv", "w_out", "w_down", "w_gate_up", "cos", "sin"]
    names += [o[0] for o in FORWARD_OUTS] + [o[0] for o in FORWARD_SCRATCH]
    for name, ref in zip(names, refs):
        setattr(r, name, ref)
    engine = Engine(*refs[len(names) :])
    z, x, yl, core, yh = place()
    y = yh * 2 + yl

    load_qkv = engine.local(r.w_qkv.at[:, rows_at(x, 128)], r.held_qkv)
    load_gu = engine.local(r.w_gate_up.at[rows_at(x, 128)], r.held_gu)
    load_x = engine.local(r.tokens.at[rows_at(core, OWN)], r.near_x)
    load_dy = engine.local(r.cotangent.at[rows_at(core, OWN)], r.near_dy)
    marks = r.segments[...].astype(F32)
    rows = [r.gains[...].astype(F32), r.shifts[...].astype(F32)]
    rows += [marks[:, k * 512 : (k + 1) * 512] for k in range(4)] + [jnp.zeros((8, 512), F32)]
    r.packed[:, :512] = jnp.concatenate(rows, axis=0).astype(BF16)
    unit = (
        lax.broadcasted_iota(jnp.int32, (16, 16), 0) == lax.broadcasted_iota(jnp.int32, (16, 16), 1)
    ).astype(BF16)
    columns = [dot(r.biases[part], unit, (0, 0)) for part in range(3)] + [jnp.zeros((16, 80), F32)]
    r.packed[:, 512:] = jnp.concatenate(columns, axis=1).astype(BF16)
    small_here = engine.local(r.packed, r.small.at[z, yh])

    def rows_of(n):
        return lambda zz: rows_at((zz * 2 + core) * 2 + yl, n)

    def slots_of(piece):
        return lambda zz: piece.at[:, lanes(zz)]

    load_qkv.wait()
    for part in range(3):
        r.turned[:1024, :] = r.held_qkv[part].astype(F32).T
        for zz in range(4):
            r.cut_qkv[zz, part * HEAD : (part + 1) * HEAD] = r.turned[rows_of(HEAD)(zz), :].astype(BF16)
    greet(FORWARD_PEERS)
    stores = []

    def store(*names):
        for name in names:
            stores.append(engine.local(getattr(r, name), getattr(r, "to_" + name)))

    pieces_qkv = send_pieces(engine, lambda zz: r.cut_qkv.at[zz], slots_of(r.p_qkv))
    swap_x = engine.send(r.tokens.at[rows_at(1 - core, OWN)], r.far_x, sibling())
    smalls = [engine.send(r.packed, r.small.at[z, yh], small_peer(dz, dh)) for dz, dh in SMALL_ALL]
    pieces_out = send_pieces(engine, lambda zz: r.w_out.at[rows_of(64)(zz), lanes(x)], slots_of(r.p_out))
    swap_dy = engine.send(r.cotangent.at[rows_at(1 - core, OWN)], r.far_dy, sibling())
    load_gu.wait()
    for g, cut in ((0, r.cut_gate), (1, r.cut_up)):
        r.turned[...] = r.held_gu[:, g, :].astype(F32).T
        for zz in range(4):
            cut[zz] = r.turned[rows_of(176)(zz), :].astype(BF16)

    stays = core == yh
    load_x.wait()
    swap_x.wait_recv()
    x_rows = spread(jnp.where(stays, r.near_x[...].astype(F32), r.far_x[...].astype(F32)))
    r.x_own[...] = x_rows.astype(BF16)
    small_here.wait()
    for copy in smalls:
        copy.wait_recv()
    parts = [r.small[zz, 0].astype(F32) for zz in range(4)]
    r.norms[...] = jnp.concatenate(
        [parts[zz][:8, xx * 128 : (xx + 1) * 128] for xx in range(4) for zz in range(4)], axis=1
    )
    h1_full, _, _ = layer_norm(x_rows, r.norms[0:1], r.norms[2:3])
    r.h1_own[...] = h1_full.astype(BF16)
    tokens_h1 = gather_tokens(engine, r.h1_own, r.h1)
    next(tokens_h1)

    for copy in pieces_qkv[1:]:
        copy.wait_recv()
    pieces_qkv[0].wait()
    weight_qkv = gather_weight(engine, r.p_qkv, r.m_qkv)
    next(weight_qkv)

    lane_at = lax.broadcasted_iota(jnp.int32, (64, 128), 1)
    for h in range(2):
        table = jnp.concatenate([r.small[zz, h, :, 512:].astype(F32) for zz in range(4)], axis=0)
        for j in range(2):
            for part in range(3):
                picked = jnp.where(lane_at == part * 16 + (z * 2 + core) * 2 + j, table, 0.0)
                r.bias[h * 2 + j, part * HEAD : (part + 1) * HEAD] = jnp.sum(picked, axis=1, keepdims=True)
    marks = r.small[x, 0, :, :512].astype(F32)
    r.seg_row[...] = jnp.concatenate([marks[4 + i : 5 + i] for i in range(4)], axis=1)
    r.seg_col[...] = column_of(r.seg_row[...])

    next(weight_qkv)
    next(tokens_h1)
    pieces_down = send_pieces(engine, lambda zz: r.w_down.at[rows_of(176)(zz), lanes(x)], slots_of(r.p_down))
    pieces_gate = send_pieces(engine, lambda zz: r.cut_gate.at[zz], slots_of(r.p_gate))
    pieces_up = send_pieces(engine, lambda zz: r.cut_up.at[zz], slots_of(r.p_up))
    next(weight_qkv)

    def start_weight(pieces, piece, matrix):
        pieces[0].wait()
        for copy in pieces[1:]:
            copy.wait_recv()
        thread = gather_weight(engine, piece, matrix)
        next(thread)
        return thread

    load_dy.wait()
    swap_dy.wait_recv()
    dy_rows = jnp.where(stays, r.near_dy[...].astype(F32), r.far_dy[...].astype(F32))
    r.dy_own[...] = spread(dy_rows).astype(BF16)
    finish(tokens_h1)
    finish(weight_qkv)

    r.qkv_t[...] = (
        dot(r.m_qkv[...].reshape(12 * HEAD, WIDTH), r.h1[...], (1, 1)) + r.bias[...].reshape(12 * HEAD, 1)
    ).astype(BF16)
    to_items = send_items(engine, r.qkv_t, r.item, 3 * HEAD)
    tokens_dy = gather_tokens(engine, r.dy_own, r.dy)
    weight_out = start_weight(pieces_out, r.p_out, r.m_out)
    next(tokens_dy)
    weight_down = start_weight(pieces_down, r.p_down, r.m_down)
    to_items[-1].wait()
    for copy in to_items[:-1]:
        copy.wait_recv()
    next(weight_out)
    weight_gate = start_weight(pieces_gate, r.p_gate, r.m_gate)
    store("m_qkv", "h1", "x_own", "dy_own", "norms", "seg_row")
    attend(r.item, r.seg_row, r.seg_col, r.cos, r.sin, r.out, r.wide, r.lse, r.kept)
    next(weight_out)
    back = return_items(engine, r.out, r.o_t, HEAD)
    next(weight_down)
    weight_up = start_weight(pieces_up, r.p_up, r.m_up)
    next(tokens_dy)
    finish(weight_out)
    back[-1].wait()
    for copy in back[:-1]:
        copy.wait_recv()

    r.o_rows[...] = r.o_t[...].astype(F32).T.astype(BF16)
    matrix = r.m_out[...].reshape(4 * HEAD, WIDTH)
    by_columns(r.product, lambda columns: dot(r.o_rows[...], matrix[:, columns], (1, 0)))
    out = scatter_tokens(engine, r.product, r.middle, r.other, r.arrived)
    next(out)
    next(out)
    next(weight_gate)
    next(weight_up)
    next(weight_down)
    next(weight_gate)
    next(out)
    r.middle[...] += x_rows

    store("kept", "wide", "lse", "o_t", "m_out")

    h2_full, _, _ = layer_norm(r.middle[...], r.norms[1:2], r.norms[3:4])
    r.h2_own[...] = h2_full.astype(BF16)
    tokens_h2 = gather_tokens(engine, r.h2_own, r.h2)
    next(tokens_h2)
    store("middle")
    next(weight_up)
    next(tokens_h2)
    finish(weight_down)
    finish(weight_gate)
    finish(tokens_dy)
    finish(weight_up)
    finish(tokens_h2)
    finish(out)
    for copy in stores:
        copy.wait()
    sent = smalls + to_items[:-1] + back[:-1] + [swap_x, swap_dy]
    for pieces in (pieces_qkv, pieces_out, pieces_gate, pieces_down, pieces_up):
        sent += pieces[1:]
    for copy in sent:
        copy.wait_send()


def forward(tokens, cotangent, gains, shifts, biases, segments, w_qkv, w_out, w_down, w_gate_up, cosine, sine):
    values = pl.pallas_call(
        forward_kernel,
        out_shape=[jax.ShapeDtypeStruct(o[1], o[2]) for o in FORWARD_OUTS],
        in_specs=[HBM] * 2 + [VMEM] * 4 + [HBM] * 4 + [VMEM] * 2,
        out_specs=[HBM] * len(FORWARD_OUTS),
        scratch_shapes=[pltpu.VMEM(shape, dtype) for _, shape, dtype in FORWARD_SCRATCH] + semaphores(117, 152, 20),
        compiler_params=pltpu.CompilerParams(
            collective_id=1, has_side_effects=True, vmem_limit_bytes=VMEM_BYTES
        ),
        name="forward",
    )(tokens, cotangent, gains, shifts, biases, segments, w_qkv, w_out, w_down, w_gate_up, cosine, sine)
    result = Refs()
    for (name, *_), value in zip(FORWARD_OUTS, values):
        setattr(result, name.removeprefix("to_"), value)
    return result


def back_peer(dc, dh):
    return {
        "core": lax.rem(lax.axis_index("core") + dc, 2),
        "yh": lax.rem(lax.axis_index("yh") + dh, 2),
    }


BACKWARD_PEERS = XY_PEERS + Z_PEERS + [sibling, functools.partial(back_peer, 1, 1)]
BACKWARD_PEERS += [functools.partial(group_peer, dz, 1) for dz in (1, 2, 3)]
BACKWARD_FAR = ["m_gate", "m_up", "m_down", "h2", "dy", "h1", "m_qkv"]
BACKWARD_NEAR = [
    ("middle", (OWN, WIDTH), F32),
    ("norms", (8, WIDTH), F32),
    ("dy_own", (OWN, WIDTH), BF16),
    ("m_out", (4, 64, WIDTH), BF16),
    ("kept", (3 * HEAD, SEQ), BF16),
    ("wide", (HEAD, SEQ), F32),
    ("lse", (1, SEQ), F32),
    ("seg_row", (1, SEQ), F32),
    ("cos", (8, SEQ), F32),
    ("sin", (8, SEQ), F32),
    ("o_t", (4 * HEAD, ROWS), BF16),
    ("x_own", (OWN, WIDTH), BF16),
]
BACKWARD_OUTS = [
    ("layer_out", (2 * OWN, WIDTH), BF16, HBM),
    ("grad_tokens", (2 * OWN, WIDTH), BF16, HBM),
    ("gd_all", (16, 4, 352, 128), BF16, HBM),
    ("up_all", (16, 4, 176, 128), BF16, HBM),
    ("attn_all", (16, 4, 256, 128), BF16, HBM),
    ("norm_sum", (8, 512), F32, VMEM),
    ("grad_bias", (3, 16, 16), F32, VMEM),
]
BACKWARD_SCRATCH = BACKWARD_NEAR + [
    ("seg_col", (SEQ, 1), F32),
    ("gate_qkv", (4, 192, WIDTH), BF16),
    ("up_attn", (4, 256, WIDTH), BF16),
    ("down", (4, 176, WIDTH), BF16),
    ("normed", (ROWS, WIDTH), BF16),
    ("dy_all", (ROWS, WIDTH), BF16),
    ("product", (ROWS, WIDTH), BF16),
    ("product_mlp", (ROWS, WIDTH), BF16),
    ("act", (704, ROWS), BF16),
    ("d_gate", (704, ROWS), BF16),
    ("d_up", (704, ROWS), BF16),
    ("dz_own", (OWN, WIDTH), BF16),
    ("dz", (ROWS, WIDTH), BF16),
    ("d_middle", (OWN, WIDTH), F32),
    ("summed", (OWN, WIDTH), F32),
    ("out_own", (OWN, WIDTH), BF16),
    ("grad_own", (OWN, WIDTH), BF16),
    ("other_dh2", (4, OWN, WIDTH), BF16),
    ("arrived_dh2", (3, OWN, WIDTH), BF16),
    ("other_mlp", (4, OWN, WIDTH), BF16),
    ("arrived_mlp", (3, OWN, WIDTH), BF16),
    ("other_dh1", (4, OWN, WIDTH), BF16),
    ("arrived_dh1", (3, OWN, WIDTH), BF16),
    ("own_y", (128, WIDTH), BF16),
    ("own_x", (4, 128, 512), BF16),
    ("d_o", (4 * HEAD, ROWS), BF16),
    ("item", (HEAD, SEQ), BF16),
    ("item_out", (3 * HEAD, SEQ), BF16),
    ("d_kv", (SEQ, 2 * HEAD), F32),
    ("d_qkv", (12 * HEAD, ROWS), BF16),
    ("d_rows", (ROWS, 12 * HEAD), BF16),
    ("landing_gd", (4, 352, 128), BF16),
    ("landing_up", (4, 176, 128), BF16),
    ("landing_attn", (4, 256, 128), BF16),
    ("small_norms", (8, WIDTH), F32),
    ("small_bias", (8, 768), F32),
    ("bias_all", (8, 8, 768), F32),
    ("by_group", (8, 8, 512), F32),
    ("small_x", (4, 8, 1280), F32),
    ("small_y", (4, 8, 1280), F32),
]
for _name, _n in (("gate", 176), ("down", 176), ("up", 176), ("attn", 256)):
    _cut = first_part(_n)
    BACKWARD_SCRATCH += [
        ("sum_y_" + _name, (_cut, WIDTH), BF16),
        ("sum_x_" + _name, (4, _n - _cut, 512), BF16),
        ("rest_x_" + _name, (3, _cut, 512), BF16),
        ("rest_y_" + _name, (3, _n - _cut, 512), BF16),
        ("rest_own_" + _name, (_n, 512), BF16),
        ("rest_total_" + _name, (_n, 512), BF16),
    ]
for _name, _cut, _rest in (("a", 96, 80), ("b", 128, 128)):
    BACKWARD_SCRATCH += [
        ("by_y_" + _name, (2, _cut, WIDTH), BF16),
        ("by_x_" + _name, (2, 4, _rest, 512), BF16),
        ("relay_y_" + _name, (_cut, WIDTH), BF16),
        ("relay_x_" + _name, (4, _rest, 512), BF16),
    ]


def backward_kernel(*refs):
    r = Refs()
    names = BACKWARD_FAR + ["in_" + n[0] for n in BACKWARD_NEAR] + [o[0] for o in BACKWARD_OUTS] + [o[0] for o in BACKWARD_SCRATCH]
    for name, ref in zip(names, refs):
        setattr(r, name, ref)
    engine = Engine(*refs[len(names) :])
    z, x, yl, core, yh = place()
    y = yh * 2 + yl
    m_gate, m_up = r.gate_qkv.at[:, pl.ds(0, 176)], r.up_attn.at[:, pl.ds(0, 176)]
    loads = [
        engine.local(source, target)
        for source, target in (
            (r.m_gate, m_gate),
            (r.h2, r.normed),
            (r.m_up, m_up),
            (r.m_down, r.down),
            (r.dy, r.dy_all),
        )
    ]
    near = [engine.local(getattr(r, "in_" + n[0]), getattr(r, n[0])) for n in BACKWARD_NEAR]
    greet(BACKWARD_PEERS)

    def first_of(name, grad, places):
        cut, rest = getattr(r, "sum_y_" + name).shape[0], getattr(r, "sum_x_" + name).shape[1]
        head, tail = pl.ds(0, cut), pl.ds(0, rest)
        thread = sum_first(
            engine,
            grad,
            getattr(r, "sum_y_" + name),
            getattr(r, "sum_x_" + name),
            getattr(r, "by_y_" + places).at[:, head],
            getattr(r, "by_x_" + places).at[:, :, tail],
            getattr(r, "relay_y_" + places).at[head],
            getattr(r, "relay_x_" + places).at[:, tail],
            r.own_y,
            r.own_x,
        )
        next(thread)
        return thread

    def rest_of(name, landing):
        parts = [getattr(r, part + name) for part in ("rest_x_", "rest_y_", "rest_own_", "rest_total_")]
        thread = sum_rest(engine, getattr(r, "sum_y_" + name), getattr(r, "sum_x_" + name), landing, *parts)
        next(thread)
        return thread

    def part_of(landing, first):
        return lambda zz: landing.at[zz, pl.ds(first, 176)]

    for load in loads:
        load.wait()
    for half in range(2):
        two, rows = slice(2 * half, 2 * half + 2), slice(352 * half, 352 * half + 352)
        gate = dot(r.gate_qkv[two, :176].reshape(352, WIDTH), r.normed[...], (1, 1))
        up = dot(r.up_attn[two, :176].reshape(352, WIDTH), r.normed[...], (1, 1))
        d_act = dot(r.down[two].reshape(352, WIDTH), r.dy_all[...], (1, 1))
        sigmoid = jax.nn.sigmoid(gate)
        silu = gate * sigmoid
        r.act[rows] = (silu * up).astype(BF16)
        r.d_gate[rows] = (d_act * up * sigmoid * (1.0 + gate * (1.0 - sigmoid))).astype(BF16)
        r.d_up[rows] = (d_act * silu).astype(BF16)

    def turned(ref):
        return ref[...].astype(F32).T.astype(BF16)

    def columns_of(ref, columns):
        return ref[:, :176, columns].reshape(704, 512)

    gate_rows, up_rows = turned(r.d_gate), turned(r.d_up)
    by_columns(
        r.product,
        lambda columns: dot(gate_rows, columns_of(r.gate_qkv, columns), (1, 0))
        + dot(up_rows, columns_of(r.up_attn, columns), (1, 0)),
    )
    dh2 = scatter_tokens(engine, r.product, r.summed, r.other_dh2, r.arrived_dh2)
    next(dh2)
    by_columns(m_gate, lambda columns: dot(r.d_gate[...], r.normed[:, columns], (1, 0)))
    gate = first_of("gate", m_gate, "a")
    next(dh2)
    act_rows = turned(r.act)
    by_columns(r.product_mlp, lambda columns: dot(act_rows, columns_of(r.down, columns), (1, 0)))
    by_columns(r.down, lambda columns: dot(r.act[...], r.dy_all[:, columns], (1, 0)))
    down = first_of("down", r.down, "b")
    by_columns(m_up, lambda columns: dot(r.d_up[...], r.normed[:, columns], (1, 0)))
    load_h1 = engine.local(r.h1, r.normed)
    mlp = scatter_tokens(engine, r.product_mlp, r.d_middle, r.other_mlp, r.arrived_mlp)
    next(mlp)
    for load in near:
        load.wait()
    r.seg_col[...] = column_of(r.seg_row[...])
    _, normed_b, rstd_b = layer_norm(r.middle[...], r.norms[1:2], r.norms[3:4])
    next(gate)
    next(down)
    next(dh2)
    back_b, gain_b, shift_b = norm_back(r.summed[...], normed_b, rstd_b, r.norms[1:2])
    d_middle = r.dy_own[...].astype(F32) + back_b
    r.dz_own[...] = d_middle.astype(BF16)
    tokens_dz = gather_tokens(engine, r.dz_own, r.dz)
    next(tokens_dz)
    r.small_norms[1:2] = gain_b[None]
    r.small_norms[3:4] = shift_b[None]
    next(gate)
    rest_gate = rest_of("gate", part_of(r.landing_gd, 0))
    next(down)
    rest_down = rest_of("down", part_of(r.landing_gd, 176))
    next(tokens_dz)
    finish(tokens_dz)

    r.d_o[...] = dot(r.m_out[...].reshape(4 * HEAD, WIDTH), r.dz[...], (1, 1)).astype(BF16)
    to_items = send_items(engine, r.d_o, r.item, HEAD)
    next(rest_gate)
    up = first_of("up", m_up, "a")
    next(rest_down)
    next(mlp)
    finish(gate)
    load_qkv = engine.local(r.m_qkv, r.gate_qkv)
    to_items[-1].wait()
    for copy in to_items[:-1]:
        copy.wait_recv()
    next(rest_gate)
    next(rest_down)
    gather_gd = gather_ctx(engine, r.landing_gd, r.gd_all)
    next(gather_gd)
    finish(down)
    finish(rest_gate)
    finish(rest_down)
    attend_back(
        r.kept, r.item, r.wide, r.lse, r.seg_row, r.seg_col, r.cos, r.sin, r.item_out, r.d_kv
    )
    back = return_items(engine, r.item_out, r.d_qkv, 3 * HEAD)
    for copy in to_items[:-1]:
        copy.wait_send()
    next(up)
    next(gather_gd)
    next(mlp)
    r.out_own[...] = spread(r.middle[...] + r.d_middle[...]).astype(BF16)
    r.d_middle[...] = d_middle
    hand_out = hand_back(engine, r.out_own, r.layer_out)
    next(hand_out)
    load_h1.wait()
    load_qkv.wait()
    back[-1].wait()
    for copy in back[:-1]:
        copy.wait_recv()
    finish(mlp)

    r.d_rows[...] = r.d_qkv[...].astype(F32).T.astype(BF16)
    matrix = r.gate_qkv[...].reshape(12 * HEAD, WIDTH)
    finish(dh2)
    by_columns(r.product, lambda columns: dot(r.d_rows[...], matrix[:, columns], (1, 0)))
    dh1 = scatter_tokens(engine, r.product, r.summed, r.other_dh1, r.arrived_dh1)
    next(dh1)
    next(up)
    rest_up = rest_of("up", part_of(r.landing_up, 0))
    finish(up)
    by_columns(
        r.up_attn.at[:, pl.ds(0, 192)], lambda columns: dot(r.d_qkv[...], r.normed[:, columns], (1, 0))
    )
    by_columns(r.up_attn.at[:, pl.ds(192, 64)], lambda columns: dot(r.o_t[...], r.dz[:, columns], (1, 0)))
    attn = first_of("attn", r.up_attn, "b")
    next(dh1)
    r.small_bias[...] = dot(jnp.ones((8, ROWS), BF16), r.d_qkv[...], (1, 1))
    _, normed_a, rstd_a = layer_norm(r.x_own[...].astype(F32), r.norms[0:1], r.norms[2:3])
    next(gather_gd)
    next(attn)
    next(rest_up)
    next(dh1)
    back_a, gain_a, shift_a = norm_back(r.summed[...], normed_a, rstd_a, r.norms[0:1])
    r.grad_own[...] = spread(r.d_middle[...] + back_a).astype(BF16)
    hand_grad = hand_back(engine, r.grad_own, r.grad_tokens)
    next(hand_grad)
    r.small_norms[0:1] = gain_a[None]
    r.small_norms[2:3] = shift_a[None]
    r.small_norms[4:] = jnp.zeros((4, WIDTH), F32)
    r.small_norms[...] = spread(r.small_norms[...])
    small = sum_small(
        engine, r.small_norms, r.small_bias, r.norm_sum, r.bias_all, r.by_group, r.small_x, r.small_y
    )
    next(small)
    next(rest_up)
    finish(rest_up)
    gather_up = gather_ctx(engine, r.landing_up, r.up_all)
    next(gather_up)
    next(gather_gd)
    next(small)
    next(attn)
    rest_attn = rest_of("attn", lambda zz: r.landing_attn.at[zz])
    next(gather_up)
    next(small)
    next(rest_attn)
    next(gather_up)
    next(rest_attn)
    gather_attn = gather_ctx(engine, r.landing_attn, r.attn_all)
    next(gather_attn)
    next(small)
    next(gather_up)
    next(gather_attn)
    finish(small)
    table = jnp.concatenate([r.bias_all[k, 0:1] for k in range(8)], axis=0)
    from_at = lax.broadcasted_iota(jnp.int32, (768, 16), 0)
    to_at = lax.broadcasted_iota(jnp.int32, (768, 16), 1)
    row_at = lax.broadcasted_iota(jnp.int32, (16, 8), 0)
    group_at = lax.broadcasted_iota(jnp.int32, (16, 8), 1)
    for part in range(3):
        total = jnp.zeros((16, 16), F32)
        for j in range(2):
            chosen = (from_at == to_at + ((yh * 2 + j) * 3 + part) * HEAD + z * 16).astype(F32)
            spread_rows = (row_at == group_at * 2 + j).astype(F32)
            total += exact_dot(spread_rows, exact_dot(table, chosen))
        r.grad_bias[part] = total
    next(gather_attn)
    finish(gather_gd)
    finish(gather_up)
    next(gather_attn)
    threads = (dh2, mlp, gate, down, up, attn, rest_gate, rest_down, rest_up, rest_attn)
    for thread in threads + (hand_out, dh1, hand_grad, small, gather_gd, gather_up, gather_attn):
        finish(thread)
    for copy in back[:-1]:
        copy.wait_send()


def backward(values):
    given = [values[name] for name in BACKWARD_FAR + [n[0] for n in BACKWARD_NEAR]]
    return pl.pallas_call(
        backward_kernel,
        out_shape=[jax.ShapeDtypeStruct(o[1], o[2]) for o in BACKWARD_OUTS],
        in_specs=[HBM] * len(given),
        out_specs=[o[3] for o in BACKWARD_OUTS],
        scratch_shapes=[pltpu.VMEM(shape, dtype) for _, shape, dtype in BACKWARD_SCRATCH] + semaphores(157, 262, 20),
        compiler_params=pltpu.CompilerParams(
            collective_id=2, has_side_effects=True, vmem_limit_bytes=VMEM_BYTES
        ),
        name="backward",
    )(*given)


def assemble_kernel(
    gd_ref,
    up_ref,
    attn_ref,
    layer_ref,
    tokens_ref,
    norms_ref,
    gu_ref,
    down_ref,
    qkv_ref,
    out_ref,
    layer_out_ref,
    tokens_out_ref,
    gains_ref,
    shifts_ref,
    turned,
):
    layer_out_ref[...] = layer_ref[...]
    tokens_out_ref[...] = tokens_ref[...].astype(F32)
    gains_ref[...] = norms_ref[0:2]
    shifts_ref[...] = norms_ref[2:4]
    for g in range(2):
        for zz in range(4):
            for core in range(2):
                for yl in range(2):
                    row = zz * 704 + core * 352 + yl * 176
                    block = up_ref[0, yl * 2 + core, zz] if g else gd_ref[0, yl * 2 + core, zz, :176]
                    turned[row : row + 176, :] = block.astype(F32)
        for t in range(22):
            gu_ref[:, g, t * 128 : (t + 1) * 128] = turned[t * 128 : (t + 1) * 128, :].T
    for zz in range(4):
        for core in range(2):
            for yl in range(2):
                row = zz * 704 + core * 352 + yl * 176
                down_ref[row : row + 176, :] = gd_ref[0, yl * 2 + core, zz, 176:].astype(F32)
                row = zz * 256 + core * 128 + yl * 64
                out_ref[row : row + 64, :] = attn_ref[0, yl * 2 + core, zz, 192:].astype(F32)
            for part in range(3):
                rows = slice(part * 64, (part + 1) * 64)
                block = jnp.concatenate([attn_ref[0, core, zz, rows], attn_ref[0, 2 + core, zz, rows]], axis=0)
                column = zz * 256 + core * 128
                qkv_ref[part, :, column : column + 128] = block.astype(F32).T


def assemble(gd_all, up_all, attn_all, layer_out, grad_tokens, norm_sum):
    gd_all = gd_all.reshape(4, 4, 4, 352, 128)
    up_all = up_all.reshape(4, 4, 4, 176, 128)
    attn_all = attn_all.reshape(4, 4, 4, 256, 128)
    return pl.pallas_call(
        assemble_kernel,
        grid=(4,),
        in_specs=[
            pl.BlockSpec((1, 4, 4, 352, 128), lambda i: (i, 0, 0, 0, 0)),
            pl.BlockSpec((1, 4, 4, 176, 128), lambda i: (i, 0, 0, 0, 0)),
            pl.BlockSpec((1, 4, 4, 256, 128), lambda i: (i, 0, 0, 0, 0)),
            pl.BlockSpec((32, WIDTH), lambda i: (i, 0)),
            pl.BlockSpec((32, WIDTH), lambda i: (i, 0)),
            pl.BlockSpec((8, 512), lambda i: (0, 0)),
        ],
        out_specs=[
            pl.BlockSpec((128, 2, 2816), lambda i: (i, 0, 0)),
            pl.BlockSpec((2816, 128), lambda i: (0, i)),
            pl.BlockSpec((3, 128, 1024), lambda i: (0, i, 0)),
            pl.BlockSpec((1024, 128), lambda i: (0, i)),
            pl.BlockSpec((32, WIDTH), lambda i: (i, 0)),
            pl.BlockSpec((32, WIDTH), lambda i: (i, 0)),
            pl.BlockSpec((2, 512), lambda i: (0, 0)),
            pl.BlockSpec((2, 512), lambda i: (0, 0)),
        ],
        out_shape=[
            jax.ShapeDtypeStruct((512, 2, 2816), F32),
            jax.ShapeDtypeStruct((2816, 512), F32),
            jax.ShapeDtypeStruct((3, 512, 1024), F32),
            jax.ShapeDtypeStruct((1024, 512), F32),
            jax.ShapeDtypeStruct((2 * OWN, WIDTH), BF16),
            jax.ShapeDtypeStruct((2 * OWN, WIDTH), F32),
            jax.ShapeDtypeStruct((2, 512), F32),
            jax.ShapeDtypeStruct((2, 512), F32),
        ],
        scratch_shapes=[pltpu.VMEM((2816, 128), F32)],
        compiler_params=pltpu.CompilerParams(vmem_limit_bytes=VMEM_BYTES),
        name="assemble",
    )(gd_all, up_all, attn_all, layer_out, grad_tokens, norm_sum)


def rotation_tables():
    half = ROT // 2
    positions = np.arange(SEQ, dtype=np.float32)
    inverse = (10000.0 ** (-(np.arange(half) * 2.0 / ROT))).astype(np.float32)
    angles = (inverse[:, None] * positions[None, :]).astype(np.float64)
    return jnp.asarray(np.cos(angles).astype(np.float32)), jnp.asarray(np.sin(angles).astype(np.float32))


def layer_norm(values, gain_row, shift_row):
    row_mean = jnp.mean(values, axis=-1, keepdims=True)
    centred = values - row_mean
    variance = jnp.mean(centred * centred, axis=-1, keepdims=True)
    rstd = lax.rsqrt(variance + EPS)
    normed = centred * rstd
    return normed * gain_row + shift_row, normed, rstd


def norm_back(gradient, normed, rstd, gain_row):
    shaped = gradient * gain_row
    centre = (
        shaped
        - jnp.mean(shaped, axis=-1, keepdims=True)
        - normed * jnp.mean(shaped * normed, axis=-1, keepdims=True)
    )
    return centre * rstd, jnp.sum(gradient * normed, axis=0), jnp.sum(gradient, axis=0)


def local(tokens, segments, w_qkv, b_qkv, w_out, w_gate_up, w_down, norm_gains, norm_shifts, cotangent):
    cosine, sine = rotation_tables()
    f = forward(
        tokens[0], cotangent[0], norm_gains, norm_shifts, b_qkv, segments, w_qkv.transpose(1, 0, 2), w_out, w_down, w_gate_up, cosine, sine
    )
    values = dict(vars(f), cos=cosine, sin=sine)
    layer_out, grad_tokens, gd_all, up_all, attn_all, norm_sum, grad_bias = backward(values)
    out_gu, out_down, out_qkv, out_out, layer_out, grad_tokens, gains, shifts = assemble(
        gd_all, up_all, attn_all, layer_out, grad_tokens, norm_sum
    )
    return (
        layer_out[None],
        grad_tokens[None],
        out_qkv.transpose(1, 0, 2),
        grad_bias,
        out_out,
        out_gu,
        out_down,
        gains,
        shifts,
    )


def solution(mesh):
    fine = Mesh(mesh.devices.reshape(4, 4, 2, 2, 2), ("z", "x", "yl", "core", "yh"))
    ctx = ("x", "yl", "core")
    return jax.shard_map(
        local,
        mesh=fine,
        in_specs=(
            P("z", ctx, None),
            P("z", None),
            P("z", None, "yh"),
            P(None, "yh", "z"),
            P("yh", "z"),
            P("z", None, "yh"),
            P("yh", "z"),
            P(None, "z"),
            P(None, "z"),
            P("z", ctx, None),
        ),
        out_specs=(
            P("z", ctx, None),
            P("z", ctx, None),
            P("z", None, "yh"),
            P(None, "yh", "z"),
            P("yh", "z"),
            P("z", None, "yh"),
            P("yh", "z"),
            P(None, "z"),
            P(None, "z"),
        ),
        check_vma=False,
    )
```

```python
import functools

import jax
import jax.numpy as jnp
import numpy as np
from jax import lax
from jax.experimental import pallas as pl
from jax.experimental.pallas import tpu as pltpu
from jax.sharding import Mesh
from jax.sharding import PartitionSpec as P

EPS = 1e-05
NEG = -1e30
ROT = 16
HEAD = 64
SEQ = 2048
WIDTH = 2048
OWN = 64
ROWS = 512
QB = 256
VMEM_BYTES = 63 * 2**20
F32 = jnp.float32
BF16 = jnp.bfloat16
MESH_ID = pl.DeviceIdType.MESH
HBM = pl.BlockSpec(memory_space=pltpu.HBM)
VMEM = pl.BlockSpec(memory_space=pltpu.VMEM)


def place():
    return tuple(lax.axis_index(a) for a in ("z", "x", "yl", "core", "yh"))


def lanes(index, size=128):
    return pl.ds(pl.multiple_of(index * size, size), size)


def rows_at(index, size):
    return pl.ds(pl.multiple_of(index * size, size), size)


def z_peer(d):
    z = lax.axis_index("z")
    return {"z": lax.rem(z + d, 4)}


def x_peer(d):
    x = lax.axis_index("x")
    return {"x": lax.rem(x + d, 4)}


def y_peer(d):
    y = lax.rem(lax.axis_index("yh") * 2 + lax.axis_index("yl") + d, 4)
    return {"yh": y // 2, "yl": lax.rem(y, 2)}


def xy_peer(dx, dy):
    return {**x_peer(dx), **y_peer(dy)}


def sibling():
    return {"core": 1 - lax.axis_index("core")}


Z_PEERS = [functools.partial(z_peer, d) for d in (1, 2, 3)]
X_PEERS = [functools.partial(x_peer, d) for d in (1, 2, 3)]
Y_PEERS = [functools.partial(y_peer, d) for d in (1, 2, 3)]
XY_ALL = [(dx, dy) for dx in range(4) for dy in range(4) if dx or dy]
XY_PEERS = [functools.partial(xy_peer, dx, dy) for dx, dy in XY_ALL]


class Remote:
    def __init__(self, engine, index, copy):
        self.engine, self.index, self.copy = engine, index, copy

    def wait_recv(self):
        self.copy.wait_recv()

    def wait_send(self):
        self.copy.wait_send()
        self.engine.free_send.append(self.index)

    def wait(self):
        self.wait_recv()
        self.wait_send()


class Local:
    def __init__(self, engine, index, copy):
        self.engine, self.index, self.copy = engine, index, copy

    def wait(self):
        self.copy.wait()
        self.engine.free_local.append(self.index)


class Engine:
    def __init__(self, send_sem, recv_sem, local_sem):
        self.send_sem, self.recv_sem, self.local_sem = send_sem, recv_sem, local_sem
        self.free_send = list(range(send_sem.shape[0]))[::-1]
        self.free_recv = list(range(recv_sem.shape[0]))[::-1]
        self.free_local = list(range(local_sem.shape[0]))[::-1]

    def send(self, src, dst, device):
        i, k = self.free_send.pop(), self.free_recv.pop()
        copy = pltpu.make_async_remote_copy(
            src, dst, self.send_sem.at[i], self.recv_sem.at[k], device_id=device, device_id_type=MESH_ID
        )
        copy.start()
        return Remote(self, i, copy)

    def local(self, src, dst):
        i = self.free_local.pop()
        copy = pltpu.make_async_copy(src, dst, self.local_sem.at[i])
        copy.start()
        return Local(self, i, copy)


def greet(peers):
    barrier = pltpu.get_barrier_semaphore()
    for peer in peers:
        pl.semaphore_signal(barrier, 1, device_id=peer(), device_id_type=MESH_ID)
    pl.semaphore_wait(barrier, len(peers))


def semaphores(n_send, n_recv, n_local):
    return [pltpu.SemaphoreType.DMA((n,)) for n in (n_send, n_recv, n_local)]


def spread(values):
    return jnp.concatenate(
        [values[:, (a * 4 + b) * 128 : (a * 4 + b + 1) * 128] for b in range(4) for a in range(4)], axis=1
    )


def finish(thread):
    for _ in thread:
        pass


def send_pieces(engine, pieces, slots):
    z = lax.axis_index("z")
    copies = [engine.local(pieces(z), slots(z))]
    for d in (1, 2, 3):
        to = z_peer(d)
        copies.append(engine.send(pieces(to["z"]), slots(z), to))
    return copies


def gather_tokens(engine, src, dst):
    z, core = lax.axis_index("z"), lax.axis_index("core")
    mine = dst.at[rows_at(z * 2 + core, OWN)]
    first = [engine.send(src, mine, z_peer(d)) for d in (1, 2, 3)]
    rest = [engine.send(src, mine, sibling()), engine.local(src, mine)]
    yield
    for d in (1, 2, 3):
        first[d - 1].wait_recv()
        here = dst.at[rows_at(lax.rem(z + 4 - d, 4) * 2 + core, OWN)]
        rest.append(engine.send(here, here, sibling()))
    yield
    for copy in first:
        copy.wait_send()
    for copy in rest:
        copy.wait()


def gather_weight(engine, src, dst):
    n = src.shape[0]
    top = first_part(n)
    head, tail = pl.ds(0, top), pl.ds(top, n - top)
    x = lax.axis_index("x")
    y = lax.axis_index("yh") * 2 + lax.axis_index("yl")
    left_y, left_x = lax.rem(y + 3, 4), lax.rem(x + 3, 4)
    right_y, right_x = lax.rem(y + 1, 4), lax.rem(x + 1, 4)
    mine = lanes(x, 512)
    local = engine.local(src, dst.at[y, :, mine])
    along_x = [engine.send(src.at[head], dst.at[y, head, mine], x_peer(d)) for d in (1, 2, 3)]
    along_y = [engine.send(src.at[tail], dst.at[y, tail, mine], y_peer(d)) for d in (1, 2, 3)]
    yield
    local.wait()
    for copy in along_x:
        copy.wait_recv()
    ring_y = [engine.send(dst.at[y, head], dst.at[y, head], y_peer(d)) for d in (1, 3)]
    for copy in along_y:
        copy.wait_recv()
    ring_x = [engine.send(dst.at[:, tail, mine], dst.at[:, tail, mine], x_peer(d)) for d in (1, 3)]
    yield
    rest = []
    half = first_part(top)
    early, late = pl.ds(0, half), pl.ds(half, top - half)
    ring_y[0].wait_recv()
    rest.append(engine.send(dst.at[left_y, early], dst.at[left_y, early], y_peer(1)))
    ring_y[1].wait_recv()
    rest.append(engine.send(dst.at[right_y, late], dst.at[right_y, late], y_peer(3)))
    ring_x[0].wait_recv()
    block = dst.at[:, tail, lanes(left_x * 2, 256)]
    rest.append(engine.send(block, block, x_peer(1)))
    ring_x[1].wait_recv()
    block = dst.at[:, tail, lanes(right_x * 2 + 1, 256)]
    rest.append(engine.send(block, block, x_peer(3)))
    yield
    for copy in along_x + along_y + ring_y + ring_x:
        copy.wait_send()
    for copy in rest:
        copy.wait()


def first_part(n):
    return (n // 2 + 15) // 16 * 16


def send_items(engine, src, dst, n):
    x, yl, yh = (lax.axis_index(a) for a in ("x", "yl", "yh"))
    y = yh * 2 + yl
    mine = dst.at[:, lanes(x * 4 + yl * 2 + yh)]
    copies = []
    for dx, dy in XY_ALL:
        tx, ty = lax.rem(x + dx, 4), lax.rem(y + dy, 4)
        copies.append(engine.send(src.at[rows_at(ty, n), lanes(tx)], mine, xy_peer(dx, dy)))
    copies.append(engine.local(src.at[rows_at(y, n), lanes(x)], mine))
    return copies


def return_items(engine, src, dst, n):
    x, yl, yh = (lax.axis_index(a) for a in ("x", "yl", "yh"))
    mine = dst.at[rows_at(yh * 2 + yl, n), lanes(x)]
    copies = []
    for dx, dy in XY_ALL:
        to = xy_peer(dx, dy)
        copies.append(engine.send(src.at[:, lanes(to["x"] * 4 + to["yl"] * 2 + to["yh"])], mine, to))
    copies.append(engine.local(src.at[:, lanes(x * 4 + yl * 2 + yh)], mine))
    return copies


def add_up(total, terms, index, rows, width):
    def step(i, carry):
        here = (*index, rows_at(i, 16), slice(0, width))
        value = terms[0][here].astype(F32)
        for term in terms[1:]:
            value += term[here].astype(F32)
        total[here] = value.astype(total.dtype)
        return carry

    lax.fori_loop(0, rows // 16, step, 0)


def exact_dot(a, b):
    return jnp.dot(a, b, precision=lax.Precision.HIGHEST, preferred_element_type=F32)


def by_columns(dst, value_of):
    for k in range(4):
        columns = slice(k * 512, (k + 1) * 512)
        value = value_of(columns).astype(dst.dtype)
        dst[..., columns] = value.reshape(dst.shape[:-1] + (512,))


def scatter_tokens(engine, product, dst, other, arrived):
    z, core = lax.axis_index("z"), lax.axis_index("core")
    to_core = []
    for i in range(4):
        give = product.at[rows_at(lax.rem(z + 1 + i, 4) * 2 + 1 - core, OWN)]
        to_core.append(engine.send(give, other.at[i], sibling()))
    yield
    to_z = []
    for i in range(3):
        own = rows_at(lax.rem(z + 1 + i, 4) * 2 + core, OWN)
        to_core[i].wait_recv()
        product[own, :] = (product[own, :].astype(F32) + other[i].astype(F32)).astype(BF16)
        to_z.append(engine.send(product.at[own], arrived.at[i], z_peer(i + 1)))
    yield
    to_core[3].wait_recv()
    dst[...] = product[rows_at(z * 2 + core, OWN), :].astype(F32) + other[3].astype(F32)
    for i in range(3):
        to_z[i].wait_recv()
        dst[...] += arrived[i].astype(F32)
    yield
    for copy in to_core + to_z:
        copy.wait_send()


def sum_first(engine, src, sum_y, sum_x, by_y, by_x, relay_y, relay_x, own_y, own_x):
    n, cut = src.shape[1], sum_y.shape[0]
    rest, half = n - cut, first_part(cut)
    tail = pl.ds(cut, rest)
    early, late = pl.ds(0, half), pl.ds(half, cut - half)
    low, high = pl.ds(0, 2), pl.ds(2, 2)
    x = lax.axis_index("x")
    y = lax.axis_index("yh") * 2 + lax.axis_index("yl")
    up_y, down_y = lax.rem(y + 1, 4), lax.rem(y + 3, 4)
    up_x, down_x = lanes(lax.rem(x + 1, 4), 512), lanes(lax.rem(x + 3, 4), 512)
    far_y, far_x = lax.rem(y + 2, 4), lanes(lax.rem(x + 2, 4), 512)
    relays = [
        engine.send(src.at[far_y, early], relay_y.at[early], y_peer(1)),
        engine.send(src.at[low, tail, far_x], relay_x.at[low], x_peer(1)),
        engine.send(src.at[far_y, late], relay_y.at[late], y_peer(3)),
        engine.send(src.at[high, tail, far_x], relay_x.at[high], x_peer(3)),
    ]
    copies = [
        engine.send(src.at[up_y, late], by_y.at[0, late], y_peer(1)),
        engine.send(src.at[high, tail, up_x], by_x.at[0, high], x_peer(1)),
        engine.send(src.at[down_y, early], by_y.at[1, early], y_peer(3)),
        engine.send(src.at[low, tail, down_x], by_x.at[1, low], x_peer(3)),
    ]
    yield
    own_y, own_x = own_y.at[pl.ds(0, cut)], own_x.at[:, pl.ds(0, rest)]
    local = [
        engine.local(src.at[up_y, early], own_y.at[early]),
        engine.local(src.at[down_y, late], own_y.at[late]),
        engine.local(src.at[low, tail, up_x], own_x.at[low]),
        engine.local(src.at[high, tail, down_x], own_x.at[high]),
    ]
    for copy in local:
        copy.wait()
    passed = []
    relays[0].wait_recv()
    add_up(relay_y.at[early], [relay_y.at[early], own_y.at[early]], (), half, WIDTH)
    passed.append(engine.send(relay_y.at[early], by_y.at[0, early], y_peer(1)))
    relays[1].wait_recv()
    for q in range(2):
        add_up(relay_x, [relay_x, own_x], (q,), rest, 512)
    passed.append(engine.send(relay_x.at[low], by_x.at[0, low], x_peer(1)))
    relays[2].wait_recv()
    add_up(relay_y.at[late], [relay_y.at[late], own_y.at[late]], (), cut - half, WIDTH)
    passed.append(engine.send(relay_y.at[late], by_y.at[1, late], y_peer(3)))
    relays[3].wait_recv()
    for q in range(2, 4):
        add_up(relay_x, [relay_x, own_x], (q,), rest, 512)
    passed.append(engine.send(relay_x.at[high], by_x.at[1, high], x_peer(3)))
    yield
    local = [
        engine.local(src.at[y, pl.ds(0, cut)], own_y),
        engine.local(src.at[:, tail, lanes(x, 512)], own_x),
    ]
    for copy in local:
        copy.wait()
    for copy in copies + passed:
        copy.wait_recv()
    add_up(sum_y, [own_y, by_y.at[0], by_y.at[1]], (), cut, WIDTH)
    for q in range(4):
        add_up(sum_x, [own_x, by_x.at[0], by_x.at[1]], (q,), rest, 512)
    for copy in passed:
        copy.wait_send()
    yield
    for copy in relays + copies:
        copy.wait_send()


def sum_rest(engine, heads, tails, landing, by_x, by_y, own, total):
    cut, rest = heads.shape[0], tails.shape[1]
    x = lax.axis_index("x")
    y = lax.axis_index("yh") * 2 + lax.axis_index("yl")
    first, second = pl.ds(0, cut), pl.ds(cut, rest)
    copies = []
    for d in (2, 1, 3):
        ty, tx = y_peer(d), x_peer(d)
        copies.append(engine.send(heads.at[:, lanes(tx["x"], 512)], by_x.at[d - 1], tx))
        copies.append(engine.send(tails.at[ty["yh"] * 2 + ty["yl"]], by_y.at[d - 1], ty))
    local = [engine.local(tails.at[y], own.at[second]), engine.local(heads.at[:, lanes(x, 512)], own.at[first])]
    yield
    for copy in local:
        copy.wait()
    for copy in copies:
        copy.wait_recv()
    add_up(total.at[first], [own.at[first]] + [by_x.at[k] for k in range(3)], (), cut, 512)
    add_up(total.at[second], [own.at[second]] + [by_y.at[k] for k in range(3)], (), rest, 512)
    moved = send_pieces(engine, lambda z: total.at[:, lanes(z)], landing)
    yield
    moved[0].wait()
    for copy in moved[1:]:
        copy.wait_recv()
    yield
    for copy in copies + moved[1:]:
        copy.wait_send()


def gather_ctx(engine, landing, dst):
    x, yl, core = (lax.axis_index(a) for a in ("x", "yl", "core"))

    def slot(dx, ll):
        return (lax.rem(x + dx, 4) * 2 + ll) * 2 + core

    other, n = 1 - yl, landing.shape[1]
    half = first_part(n)
    first, second = (pl.ds(0, 3),), (pl.ds(3, 1),)
    even, even_other = ((pl.ds(0, 2),), (pl.ds(2, 1),)), ((pl.ds(0, 1),), (pl.ds(1, 2),))
    odd = ((pl.ds(3, 1), pl.ds(0, half)), (pl.ds(3, 1), pl.ds(half, n - half)))
    partner, there = {"yl": other}, sibling()
    sent = []

    def send(source, target, part, device):
        copy = engine.send(source, dst.at[(target, *part)], device)
        sent.append(copy)
        return copy

    def hand(index, part):
        return send(dst.at[(index, *part)], index, part, there)

    def on(index, part, device):
        return send(dst.at[(index, *part)], index, part, device)

    me = slot(0, yl)
    local = engine.local(landing, dst.at[me])
    siblings = [engine.send(landing, dst.at[me], there)]
    to_y = send(landing.at[*first], me, first, partner)
    round_b = [send(landing.at[*second], me, second, x_peer(d)) for d in (1, 3)]
    round_a = [send(landing.at[*first], me, first, x_peer(d)) for d in (1, 3)]
    over = [send(landing.at[*second], me, second, partner)]
    yield
    to_y.wait_recv()
    round_c = [on(slot(0, other), first, x_peer(d)) for d in (1, 3)]
    siblings.append(hand(slot(0, other), first))
    onward = []
    for k, (d, to) in enumerate(((3, 1), (1, 3))):
        round_b[k].wait_recv()
        onward.append(on(slot(d, yl), odd[k], x_peer(to)))
        over.append(on(slot(d, yl), second, partner))
        siblings.append(hand(slot(d, yl), second))
    for k, (d, to) in enumerate(((3, 1), (1, 3))):
        round_a[k].wait_recv()
        onward.append(on(slot(d, yl), even[k], x_peer(to)))
        siblings.append(hand(slot(d, yl), first))
    yield
    for k in range(2):
        onward[k].wait_recv()
    over.append(on(slot(2, yl), second, partner))
    siblings.append(hand(slot(2, yl), second))
    for k, (d, to) in enumerate(((3, 1), (1, 3))):
        round_c[k].wait_recv()
        onward.append(on(slot(d, other), even_other[k], x_peer(to)))
        siblings.append(hand(slot(d, other), first))
    yield
    for k in (2, 3):
        onward[k].wait_recv()
    siblings.append(hand(slot(2, yl), first))
    for k, d in enumerate((0, 3, 1, 2)):
        over[k].wait_recv()
        siblings.append(hand(slot(d, other), second))
    for k in (4, 5):
        onward[k].wait_recv()
    siblings.append(hand(slot(2, other), first))
    yield
    local.wait()
    for copy in siblings:
        copy.wait_recv()
    siblings[0].wait_send()
    for copy in sent:
        copy.wait_send()


def group_peer(dz, dc):
    return {
        "z": lax.rem(lax.axis_index("z") + dz, 4),
        "core": lax.rem(lax.axis_index("core") + dc, 2),
    }


GROUP_ALL = [(dz, dc) for dz in range(4) for dc in range(2) if dz or dc]


def sum_small(engine, norms, bias, norm_sum, bias_all, by_group, by_x, by_y):
    z, x, yl, core, yh = place()
    y = yh * 2 + yl
    me = z * 2 + core
    first = []
    for dz, dc in GROUP_ALL:
        to = group_peer(dz, dc)
        first.append(engine.send(norms.at[:, lanes(to["z"], 512)], by_group.at[me], to))
    mine = engine.local(norms.at[:, lanes(z, 512)], by_group.at[me])
    yield
    mine.wait()
    for copy in first:
        copy.wait_recv()
    by_x[x, :, :512] = sum(by_group[k] for k in range(8))
    by_x[x, :, 512:] = bias[...]
    second = [engine.send(by_x.at[x], by_x.at[x], x_peer(d)) for d in (1, 2, 3)]
    yield
    for copy in second:
        copy.wait_recv()
    by_y[y] = sum(by_x[k] for k in range(4))
    third = [engine.send(by_y.at[y], by_y.at[y], y_peer(d)) for d in (1, 2, 3)]
    yield
    for copy in third:
        copy.wait_recv()
    total = sum(by_y[k] for k in range(4))
    norm_sum[...] = total[:, :512]
    bias_all[me] = total[:, 512:]
    last = [engine.send(bias_all.at[me], bias_all.at[me], group_peer(dz, dc)) for dz, dc in GROUP_ALL]
    yield
    for copy in last:
        copy.wait()
    for copy in first + second + third:
        copy.wait_send()


def hand_back(engine, src, dst):
    core, yh = lax.axis_index("core"), lax.axis_index("yh")
    far = {"core": yh, "yh": 1 - yh}
    near = {"core": yh}
    stays = core == yh
    mine = dst.at[rows_at(core, OWN)]
    sends = [engine.free_send.pop() for _ in range(2)]
    arrivals = [engine.free_recv.pop() for _ in range(2)]
    j = engine.free_local.pop()
    send_sem, recv_sem, local_sem = engine.send_sem, engine.recv_sem, engine.local_sem

    def make(to, slot):
        return pltpu.make_async_remote_copy(
            src,
            mine,
            send_sem.at[sends[slot]],
            recv_sem.at[arrivals[0] + (arrivals[1] - arrivals[0]) * core],
            device_id=to,
            device_id_type=MESH_ID,
        )

    def arrival(half):
        part = dst.at[rows_at(half, OWN)]
        return pltpu.make_async_remote_copy(
            part, part, send_sem.at[sends[0]], recv_sem.at[arrivals[0] + (arrivals[1] - arrivals[0]) * half], device_id=far, device_id_type=MESH_ID
        )

    make(far, 0).start()

    @pl.when(stays)
    def _():
        pltpu.make_async_copy(src, mine, local_sem.at[j]).start()

    @pl.when(jnp.logical_not(stays))
    def _():
        make(near, 1).start()

    yield
    make(far, 0).wait_send()

    @pl.when(stays)
    def _():
        pltpu.make_async_copy(src, mine, local_sem.at[j]).wait()
        arrival(1 - core).wait_recv()

    @pl.when(jnp.logical_not(stays))
    def _():
        make(near, 1).wait_send()
        arrival(core).wait_recv()
        arrival(1 - core).wait_recv()

    engine.free_send.extend(sends)
    engine.free_local.append(j)


def dot(a, b, dims):
    return lax.dot_general(a, b, ((dims[:1], dims[1:]), ((), ())), preferred_element_type=F32)


def rope(block, cosine, sine):
    front, back = block[:8], block[8:16]
    return jnp.concatenate(
        [front * cosine - back * sine, back * cosine + front * sine, block[16:]], axis=0
    )


def rope_back(block, cosine, sine):
    front, back = block[:8], block[8:16]
    return jnp.concatenate(
        [front * cosine + back * sine, back * cosine - front * sine, block[16:]], axis=0
    )


def masked_scores(scores, start, seg_row, seg_col):
    stop = start + QB

    def hide(first, last, by_segment, causal):
        part = scores[first:last]
        keep = None
        if by_segment:
            keep = seg_col[first:last] == seg_row[:, start:stop]
        if causal:
            key_at = first + lax.broadcasted_iota(jnp.int32, part.shape, 0)
            query_at = start + lax.broadcasted_iota(jnp.int32, part.shape, 1)
            order = key_at <= query_at
            keep = order if keep is None else keep & order
        return jnp.where(keep, part, NEG)

    if start == 0:
        return hide(0, stop, True, True)
    if stop + 127 <= SEQ:
        parts = [hide(0, 128, True, False)]
        if start > 128:
            parts.append(scores[128:start])
        parts.append(hide(start, stop, False, True))
        return jnp.concatenate(parts, axis=0)
    return jnp.concatenate([hide(0, start, True, False), hide(start, stop, True, True)], axis=0)


def attend(qkv_ref, row_ref, col_ref, cos_ref, sin_ref, o_ref, wide_ref, lse_ref, kept_ref):
    cosine, sine = cos_ref[...], sin_ref[...]
    q_t = rope(qkv_ref[:HEAD].astype(F32), cosine, sine).astype(BF16) * jnp.asarray(0.125, BF16)
    k_t = rope(qkv_ref[HEAD : 2 * HEAD].astype(F32), cosine, sine).astype(BF16)
    v_t = qkv_ref[2 * HEAD :]
    kept_ref[:HEAD] = q_t
    kept_ref[HEAD : 2 * HEAD] = k_t
    kept_ref[2 * HEAD :] = v_t
    keys = k_t.astype(F32).T.astype(BF16)
    seg_row, seg_col = row_ref[...], col_ref[...]
    for start in range(0, SEQ, QB):
        stop = start + QB
        scores = dot(keys[:stop], q_t[:, start:stop], (1, 0))
        scores = masked_scores(scores, start, seg_row, seg_col)
        top = jnp.max(scores, axis=0, keepdims=True)
        terms = jnp.exp(scores - top)
        total = jnp.sum(terms, axis=0, keepdims=True)
        out = dot(v_t[:, :stop], terms.astype(BF16), (1, 0)) / total
        wide_ref[:, start:stop] = out
        o_ref[:, start:stop] = out.astype(BF16)
        lse_ref[:, start:stop] = top + jnp.log(total)


def attend_back(kept_ref, do_ref, wide_ref, lse_ref, row_ref, col_ref, cos_ref, sin_ref, out_ref, sum_ref):
    cosine, sine = cos_ref[...], sin_ref[...]
    q_t, k_t, do_t = kept_ref[:HEAD], kept_ref[HEAD : 2 * HEAD], do_ref[...]
    queries = q_t.astype(F32).T.astype(BF16)
    keys = k_t.astype(F32).T.astype(BF16)
    values = kept_ref[2 * HEAD :].astype(F32).T.astype(BF16)
    grads = do_t.astype(F32).T.astype(BF16)
    centre = jnp.sum(do_t.astype(F32) * wide_ref[...], axis=0, keepdims=True)
    lse = lse_ref[...]
    seg_row, seg_col = row_ref[...], col_ref[...]
    sum_ref[...] = jnp.zeros_like(sum_ref)
    dq_parts = []
    for start in range(0, SEQ, QB):
        stop = start + QB
        scores = dot(keys[:stop], q_t[:, start:stop], (1, 0))
        scores = masked_scores(scores, start, seg_row, seg_col)
        probs = jnp.exp(scores - lse[:, start:stop])
        d_probs = dot(values[:stop], do_t[:, start:stop], (1, 0))
        d_scores = (probs * (d_probs - centre[:, start:stop])).astype(BF16)
        d_keys = dot(d_scores, queries[start:stop], (1, 0))
        d_values = dot(probs.astype(BF16), grads[start:stop], (1, 0))
        sum_ref[:stop] += jnp.concatenate([d_keys, d_values], axis=1)
        dq_parts.append(dot(k_t[:, :stop], d_scores, (1, 0)) * 0.125)
    out_ref[:HEAD] = rope_back(jnp.concatenate(dq_parts, axis=1), cosine, sine).astype(BF16)
    turned = sum_ref[...].T
    out_ref[HEAD : 2 * HEAD] = rope_back(turned[:HEAD], cosine, sine).astype(BF16)
    out_ref[2 * HEAD :] = turned[HEAD:].astype(BF16)


def small_peer(dz, dh):
    return {
        "z": lax.rem(lax.axis_index("z") + dz, 4),
        "yh": lax.rem(lax.axis_index("yh") + dh, 2),
    }


SMALL_ALL = [(dz, dh) for dz in range(4) for dh in range(2) if dz or dh]
SCRATCH = [
    ("m_qkv", (4, 192, WIDTH), BF16),
    ("m_out", (4, 64, WIDTH), BF16),
    ("x_own", (OWN, WIDTH), BF16),
    ("dy_own", (OWN, WIDTH), BF16),
    ("middle", (OWN, WIDTH), F32),
    ("norms", (8, WIDTH), F32),
    ("h1", (ROWS, WIDTH), BF16),
    ("o_t", (4 * HEAD, ROWS), BF16),
    ("kept", (3 * HEAD, SEQ), BF16),
    ("wide", (HEAD, SEQ), F32),
    ("lse", (1, SEQ), F32),
    ("seg_row", (1, SEQ), F32),
    ("seg_col", (SEQ, 1), F32),
    ("packed", (16, 640), BF16),
    ("small", (4, 2, 16, 640), BF16),
    ("near_x", (OWN, WIDTH), BF16),
    ("near_dy", (OWN, WIDTH), BF16),
    ("far_x", (OWN, WIDTH), BF16),
    ("far_dy", (OWN, WIDTH), BF16),
    ("h1_own", (OWN, WIDTH), BF16),
    ("h2_own", (OWN, WIDTH), BF16),
    ("held_qkv", (3, 128, 1024), BF16),
    ("held_gu", (128, 2, 2816), BF16),
    ("turned", (2816, 128), F32),
    ("cut_qkv", (4, 192, 128), BF16),
    ("cut_gate", (4, 176, 128), BF16),
    ("cut_up", (4, 176, 128), BF16),
    ("p_qkv", (192, 512), BF16),
    ("p_out", (64, 512), BF16),
    ("p_down", (176, 512), BF16),
    ("p_gate", (176, 512), BF16),
    ("p_up", (176, 512), BF16),
    ("bias", (4, 192, 1), F32),
    ("out", (HEAD, SEQ), BF16),
    ("o_rows", (ROWS, 4 * HEAD), BF16),
    ("product", (ROWS, WIDTH), BF16),
]


class Refs:
    pass


def column_of(row):
    blocks = jnp.concatenate([row[:, k * 128 : (k + 1) * 128] for k in range(16)], axis=0).T
    return jnp.concatenate([blocks[:, k : k + 1] for k in range(16)], axis=0)


def back_peer(dc, dh):
    return {
        "core": lax.rem(lax.axis_index("core") + dc, 2),
        "yh": lax.rem(lax.axis_index("yh") + dh, 2),
    }


LAYER_PEERS = XY_PEERS + Z_PEERS + [sibling, functools.partial(back_peer, 1, 1)]
LAYER_PEERS += [functools.partial(small_peer, dz, 1) for dz in (1, 2, 3)]
LAYER_PEERS += [functools.partial(group_peer, dz, 1) for dz in (1, 2, 3)]
PLACES = [
    ("m_gate", (4, 176, WIDTH), BF16, HBM),
    ("far_m_qkv", (4, 192, WIDTH), BF16, HBM),
    ("far_h1", (ROWS, WIDTH), BF16, HBM),
]
RESULTS = [
    ("layer_out", (2 * OWN, WIDTH), BF16, HBM),
    ("grad_tokens", (2 * OWN, WIDTH), BF16, HBM),
    ("gd_all", (16, 4, 352, 128), BF16, HBM),
    ("up_all", (16, 4, 176, 128), BF16, HBM),
    ("attn_all", (16, 4, 256, 128), BF16, HBM),
    ("norm_sum", (8, 512), F32, VMEM),
    ("grad_bias", (3, 16, 16), F32, VMEM),
]
SCRATCH += [
    ("up_attn", (4, 256, WIDTH), BF16),
    ("down", (4, 176, WIDTH), BF16),
    ("dy_all", (ROWS, WIDTH), BF16),
    ("product_mlp", (ROWS, WIDTH), BF16),
    ("gate", (704, ROWS), F32),
    ("act", (704, ROWS), BF16),
    ("d_gate", (704, ROWS), BF16),
    ("d_up", (704, ROWS), BF16),
    ("dz_own", (OWN, WIDTH), BF16),
    ("dz", (ROWS, WIDTH), BF16),
    ("d_middle", (OWN, WIDTH), F32),
    ("summed", (OWN, WIDTH), F32),
    ("out_own", (OWN, WIDTH), BF16),
    ("grad_own", (OWN, WIDTH), BF16),
    ("other_dh2", (4, OWN, WIDTH), BF16),
    ("arrived_dh2", (3, OWN, WIDTH), BF16),
    ("other_mlp", (4, OWN, WIDTH), BF16),
    ("arrived_mlp", (3, OWN, WIDTH), BF16),
    ("other_dh1", (4, OWN, WIDTH), BF16),
    ("arrived_dh1", (3, OWN, WIDTH), BF16),
    ("own_y", (128, WIDTH), BF16),
    ("own_x", (4, 128, 512), BF16),
    ("d_o", (4 * HEAD, ROWS), BF16),
    ("item_do", (HEAD, SEQ), BF16),
    ("item_out", (3 * HEAD, SEQ), BF16),
    ("d_kv", (SEQ, 2 * HEAD), F32),
    ("d_qkv", (12 * HEAD, ROWS), BF16),
    ("d_rows", (ROWS, 12 * HEAD), BF16),
    ("landing_gd", (4, 352, 128), BF16),
    ("landing_up", (4, 176, 128), BF16),
    ("landing_attn", (4, 256, 128), BF16),
    ("small_norms", (8, WIDTH), F32),
    ("small_bias", (8, 768), F32),
    ("bias_all", (8, 8, 768), F32),
    ("by_group", (8, 8, 512), F32),
    ("small_x", (4, 8, 1280), F32),
    ("small_y", (4, 8, 1280), F32),
]
for _name, _n in (("gate", 176), ("down", 176), ("up", 176), ("attn", 256)):
    _cut = first_part(_n)
    SCRATCH += [
        ("sum_y_" + _name, (_cut, WIDTH), BF16),
        ("sum_x_" + _name, (4, _n - _cut, 512), BF16),
        ("rest_x_" + _name, (3, _cut, 512), BF16),
        ("rest_y_" + _name, (3, _n - _cut, 512), BF16),
        ("rest_own_" + _name, (_n, 512), BF16),
        ("rest_total_" + _name, (_n, 512), BF16),
    ]
for _name, _cut, _rest in (("a", 96, 80), ("b", 128, 128)):
    SCRATCH += [
        ("by_y_" + _name, (2, _cut, WIDTH), BF16),
        ("by_x_" + _name, (2, 4, _rest, 512), BF16),
        ("relay_y_" + _name, (_cut, WIDTH), BF16),
        ("relay_x_" + _name, (4, _rest, 512), BF16),
    ]


LAYER_INPUTS = ["tokens", "cotangent", "gains", "shifts", "biases", "segments"]
LAYER_INPUTS += ["w_qkv", "w_out", "w_down", "w_gate_up", "cos", "sin"]


def layer_kernel(*refs):
    r = Refs()
    names = LAYER_INPUTS + [o[0] for o in PLACES + RESULTS] + [o[0] for o in SCRATCH]
    for name, ref in zip(names, refs):
        setattr(r, name, ref)
    r.gate_qkv, r.normed, r.qkv_t, r.item = r.m_qkv, r.h1, r.d_qkv, r.item_out
    r.other, r.arrived = r.other_dh2, r.arrived_dh2
    m_gate, m_up = r.gate_qkv.at[:, pl.ds(0, 176)], r.up_attn.at[:, pl.ds(0, 176)]
    engine = Engine(*refs[len(names) :])
    z, x, yl, core, yh = place()
    y = yh * 2 + yl

    load_qkv = engine.local(r.w_qkv.at[:, rows_at(x, 128)], r.held_qkv)
    load_gu = engine.local(r.w_gate_up.at[rows_at(x, 128)], r.held_gu)
    load_x = engine.local(r.tokens.at[rows_at(core, OWN)], r.near_x)
    load_dy = engine.local(r.cotangent.at[rows_at(core, OWN)], r.near_dy)
    marks = r.segments[...].astype(F32)
    rows = [r.gains[...].astype(F32), r.shifts[...].astype(F32)]
    rows += [marks[:, k * 512 : (k + 1) * 512] for k in range(4)] + [jnp.zeros((8, 512), F32)]
    r.packed[:, :512] = jnp.concatenate(rows, axis=0).astype(BF16)
    unit = (
        lax.broadcasted_iota(jnp.int32, (16, 16), 0) == lax.broadcasted_iota(jnp.int32, (16, 16), 1)
    ).astype(BF16)
    columns = [dot(r.biases[part], unit, (0, 0)) for part in range(3)] + [jnp.zeros((16, 80), F32)]
    r.packed[:, 512:] = jnp.concatenate(columns, axis=1).astype(BF16)
    small_here = engine.local(r.packed, r.small.at[z, yh])

    def rows_of(n):
        return lambda zz: rows_at((zz * 2 + core) * 2 + yl, n)

    def slots_of(piece):
        return lambda zz: piece.at[:, lanes(zz)]

    load_qkv.wait()
    for part in range(3):
        r.turned[:1024, :] = r.held_qkv[part].astype(F32).T
        for zz in range(4):
            r.cut_qkv[zz, part * HEAD : (part + 1) * HEAD] = r.turned[rows_of(HEAD)(zz), :].astype(BF16)
    greet(LAYER_PEERS)
    pieces_qkv = send_pieces(engine, lambda zz: r.cut_qkv.at[zz], slots_of(r.p_qkv))
    swap_x = engine.send(r.tokens.at[rows_at(1 - core, OWN)], r.far_x, sibling())
    smalls = [engine.send(r.packed, r.small.at[z, yh], small_peer(dz, dh)) for dz, dh in SMALL_ALL]
    pieces_out = send_pieces(engine, lambda zz: r.w_out.at[rows_of(64)(zz), lanes(x)], slots_of(r.p_out))
    swap_dy = engine.send(r.cotangent.at[rows_at(1 - core, OWN)], r.far_dy, sibling())
    load_gu.wait()
    for g, cut in ((0, r.cut_gate), (1, r.cut_up)):
        r.turned[...] = r.held_gu[:, g, :].astype(F32).T
        for zz in range(4):
            cut[zz] = r.turned[rows_of(176)(zz), :].astype(BF16)

    stays = core == yh
    load_x.wait()
    swap_x.wait_recv()
    x_rows = spread(jnp.where(stays, r.near_x[...].astype(F32), r.far_x[...].astype(F32)))
    r.x_own[...] = x_rows.astype(BF16)
    small_here.wait()
    for copy in smalls:
        copy.wait_recv()
    parts = [r.small[zz, 0].astype(F32) for zz in range(4)]
    r.norms[...] = jnp.concatenate(
        [parts[zz][:8, xx * 128 : (xx + 1) * 128] for xx in range(4) for zz in range(4)], axis=1
    )
    h1_full, _, _ = layer_norm(x_rows, r.norms[0:1], r.norms[2:3])
    r.h1_own[...] = h1_full.astype(BF16)
    tokens_h1 = gather_tokens(engine, r.h1_own, r.h1)
    next(tokens_h1)

    for copy in pieces_qkv[1:]:
        copy.wait_recv()
    pieces_qkv[0].wait()
    weight_qkv = gather_weight(engine, r.p_qkv, r.m_qkv)
    next(weight_qkv)

    lane_at = lax.broadcasted_iota(jnp.int32, (64, 128), 1)
    for h in range(2):
        table = jnp.concatenate([r.small[zz, h, :, 512:].astype(F32) for zz in range(4)], axis=0)
        for j in range(2):
            for part in range(3):
                picked = jnp.where(lane_at == part * 16 + (z * 2 + core) * 2 + j, table, 0.0)
                r.bias[h * 2 + j, part * HEAD : (part + 1) * HEAD] = jnp.sum(picked, axis=1, keepdims=True)
    marks = r.small[x, 0, :, :512].astype(F32)
    r.seg_row[...] = jnp.concatenate([marks[4 + i : 5 + i] for i in range(4)], axis=1)
    r.seg_col[...] = column_of(r.seg_row[...])

    next(weight_qkv)
    next(tokens_h1)
    pieces_down = send_pieces(engine, lambda zz: r.w_down.at[rows_of(176)(zz), lanes(x)], slots_of(r.p_down))
    pieces_gate = send_pieces(engine, lambda zz: r.cut_gate.at[zz], slots_of(r.p_gate))
    pieces_up = send_pieces(engine, lambda zz: r.cut_up.at[zz], slots_of(r.p_up))
    next(weight_qkv)

    def start_weight(pieces, piece, matrix):
        pieces[0].wait()
        for copy in pieces[1:]:
            copy.wait_recv()
        thread = gather_weight(engine, piece, matrix)
        next(thread)
        return thread

    load_dy.wait()
    swap_dy.wait_recv()
    dy_rows = jnp.where(stays, r.near_dy[...].astype(F32), r.far_dy[...].astype(F32))
    r.dy_own[...] = spread(dy_rows).astype(BF16)
    finish(tokens_h1)
    finish(weight_qkv)

    r.qkv_t[...] = (
        dot(r.m_qkv[...].reshape(12 * HEAD, WIDTH), r.h1[...], (1, 1)) + r.bias[...].reshape(12 * HEAD, 1)
    ).astype(BF16)
    to_items = send_items(engine, r.qkv_t, r.item, 3 * HEAD)
    tokens_dy = gather_tokens(engine, r.dy_own, r.dy_all)
    weight_out = start_weight(pieces_out, r.p_out, r.m_out)
    next(tokens_dy)
    weight_down = start_weight(pieces_down, r.p_down, r.down)
    to_items[-1].wait()
    for copy in to_items[:-1]:
        copy.wait_recv()
    next(weight_out)
    weight_gate = start_weight(pieces_gate, r.p_gate, r.m_gate)
    stores = [engine.local(r.m_qkv, r.far_m_qkv), engine.local(r.h1, r.far_h1)]
    attend(r.item, r.seg_row, r.seg_col, r.cos, r.sin, r.out, r.wide, r.lse, r.kept)
    next(weight_out)
    back = return_items(engine, r.out, r.o_t, HEAD)
    next(weight_down)
    weight_up = start_weight(pieces_up, r.p_up, m_up)
    next(tokens_dy)
    finish(weight_out)
    back[-1].wait()
    for copy in back[:-1]:
        copy.wait_recv()

    for copy in stores:
        copy.wait()

    r.o_rows[...] = r.o_t[...].astype(F32).T.astype(BF16)
    matrix = r.m_out[...].reshape(4 * HEAD, WIDTH)
    by_columns(r.product, lambda columns: dot(r.o_rows[...], matrix[:, columns], (1, 0)))
    out = scatter_tokens(engine, r.product, r.middle, r.other, r.arrived)
    next(out)
    next(out)
    next(weight_gate)
    next(weight_up)
    next(weight_down)
    next(weight_gate)
    next(out)
    r.middle[...] += x_rows

    h2_full, _, _ = layer_norm(r.middle[...], r.norms[1:2], r.norms[3:4])
    r.h2_own[...] = h2_full.astype(BF16)
    tokens_h2 = gather_tokens(engine, r.h2_own, r.normed)
    next(tokens_h2)
    next(weight_up)

    halves = [(slice(2 * k, 2 * k + 2), slice(352 * k, 352 * k + 352)) for k in range(2)]
    finish(tokens_dy)
    finish(weight_down)
    for two, rows in halves:
        d_act = dot(r.down[two].reshape(352, WIDTH), r.dy_all[...], (1, 1))
        for k in range(4):
            r.turned[704 * k + rows.start : 704 * k + rows.stop] = d_act[:, k * 128 : (k + 1) * 128]
    next(tokens_h2)
    finish(weight_gate)
    load_gate = engine.local(r.m_gate, m_gate)
    finish(tokens_h2)
    load_gate.wait()
    for two, rows in halves:
        r.gate[rows] = dot(r.gate_qkv[two, :176].reshape(352, WIDTH), r.normed[...], (1, 1))
    finish(out)
    sent = smalls + to_items[:-1] + back[:-1] + [swap_x, swap_dy]
    for pieces in (pieces_qkv, pieces_out, pieces_gate, pieces_down, pieces_up):
        sent += pieces[1:]
    for copy in sent:
        copy.wait_send()
    finish(weight_up)
    for two, rows in halves:
        up = dot(r.up_attn[two, :176].reshape(352, WIDTH), r.normed[...], (1, 1))
        gate = r.gate[rows]
        d_act = [r.turned[704 * k + rows.start : 704 * k + rows.stop] for k in range(4)]
        d_act = jnp.concatenate(d_act, axis=1)
        sigmoid = jax.nn.sigmoid(gate)
        silu = gate * sigmoid
        r.act[rows] = (silu * up).astype(BF16)
        r.d_gate[rows] = (d_act * up * sigmoid * (1.0 + gate * (1.0 - sigmoid))).astype(BF16)
        r.d_up[rows] = (d_act * silu).astype(BF16)

    def first_of(name, grad, places):
        cut, rest = getattr(r, "sum_y_" + name).shape[0], getattr(r, "sum_x_" + name).shape[1]
        head, tail = pl.ds(0, cut), pl.ds(0, rest)
        thread = sum_first(
            engine,
            grad,
            getattr(r, "sum_y_" + name),
            getattr(r, "sum_x_" + name),
            getattr(r, "by_y_" + places).at[:, head],
            getattr(r, "by_x_" + places).at[:, :, tail],
            getattr(r, "relay_y_" + places).at[head],
            getattr(r, "relay_x_" + places).at[:, tail],
            r.own_y,
            r.own_x,
        )
        next(thread)
        return thread

    def rest_of(name, landing):
        parts = [getattr(r, part + name) for part in ("rest_x_", "rest_y_", "rest_own_", "rest_total_")]
        thread = sum_rest(engine, getattr(r, "sum_y_" + name), getattr(r, "sum_x_" + name), landing, *parts)
        next(thread)
        return thread

    def part_of(landing, first):
        return lambda zz: landing.at[zz, pl.ds(first, 176)]

    def turned(ref):
        return ref[...].astype(F32).T.astype(BF16)

    def columns_of(ref, columns):
        return ref[:, :176, columns].reshape(704, 512)

    gate_rows, up_rows = turned(r.d_gate), turned(r.d_up)
    by_columns(
        r.product,
        lambda columns: dot(gate_rows, columns_of(r.gate_qkv, columns), (1, 0))
        + dot(up_rows, columns_of(r.up_attn, columns), (1, 0)),
    )
    dh2 = scatter_tokens(engine, r.product, r.summed, r.other_dh2, r.arrived_dh2)
    next(dh2)
    by_columns(m_gate, lambda columns: dot(r.d_gate[...], r.normed[:, columns], (1, 0)))
    gate = first_of("gate", m_gate, "a")
    next(dh2)
    act_rows = turned(r.act)
    by_columns(r.product_mlp, lambda columns: dot(act_rows, columns_of(r.down, columns), (1, 0)))
    by_columns(r.down, lambda columns: dot(r.act[...], r.dy_all[:, columns], (1, 0)))
    down = first_of("down", r.down, "b")
    by_columns(m_up, lambda columns: dot(r.d_up[...], r.normed[:, columns], (1, 0)))
    load_h1 = engine.local(r.far_h1, r.normed)
    mlp = scatter_tokens(engine, r.product_mlp, r.d_middle, r.other_mlp, r.arrived_mlp)
    next(mlp)
    _, normed_b, rstd_b = layer_norm(r.middle[...], r.norms[1:2], r.norms[3:4])
    next(gate)
    next(down)
    next(dh2)
    back_b, gain_b, shift_b = norm_back(r.summed[...], normed_b, rstd_b, r.norms[1:2])
    d_middle = r.dy_own[...].astype(F32) + back_b
    r.dz_own[...] = d_middle.astype(BF16)
    tokens_dz = gather_tokens(engine, r.dz_own, r.dz)
    next(tokens_dz)
    r.small_norms[1:2] = gain_b[None]
    r.small_norms[3:4] = shift_b[None]
    next(gate)
    rest_gate = rest_of("gate", part_of(r.landing_gd, 0))
    next(down)
    rest_down = rest_of("down", part_of(r.landing_gd, 176))
    next(tokens_dz)
    finish(tokens_dz)

    r.d_o[...] = dot(r.m_out[...].reshape(4 * HEAD, WIDTH), r.dz[...], (1, 1)).astype(BF16)
    to_items = send_items(engine, r.d_o, r.item_do, HEAD)
    next(rest_gate)
    up = first_of("up", m_up, "a")
    next(rest_down)
    next(mlp)
    finish(gate)
    load_qkv = engine.local(r.far_m_qkv, r.gate_qkv)
    to_items[-1].wait()
    for copy in to_items[:-1]:
        copy.wait_recv()
    next(rest_gate)
    next(rest_down)
    gather_gd = gather_ctx(engine, r.landing_gd, r.gd_all)
    next(gather_gd)
    finish(down)
    finish(rest_gate)
    finish(rest_down)
    attend_back(
        r.kept, r.item_do, r.wide, r.lse, r.seg_row, r.seg_col, r.cos, r.sin, r.item_out, r.d_kv
    )
    back = return_items(engine, r.item_out, r.d_qkv, 3 * HEAD)
    for copy in to_items[:-1]:
        copy.wait_send()
    next(up)
    next(gather_gd)
    next(mlp)
    r.out_own[...] = spread(r.middle[...] + r.d_middle[...]).astype(BF16)
    r.d_middle[...] = d_middle
    hand_out = hand_back(engine, r.out_own, r.layer_out)
    next(hand_out)
    load_h1.wait()
    load_qkv.wait()
    back[-1].wait()
    for copy in back[:-1]:
        copy.wait_recv()
    finish(mlp)

    r.d_rows[...] = r.d_qkv[...].astype(F32).T.astype(BF16)
    matrix = r.gate_qkv[...].reshape(12 * HEAD, WIDTH)
    finish(dh2)
    by_columns(r.product, lambda columns: dot(r.d_rows[...], matrix[:, columns], (1, 0)))
    dh1 = scatter_tokens(engine, r.product, r.summed, r.other_dh1, r.arrived_dh1)
    next(dh1)
    next(up)
    rest_up = rest_of("up", part_of(r.landing_up, 0))
    finish(up)
    by_columns(
        r.up_attn.at[:, pl.ds(0, 192)], lambda columns: dot(r.d_qkv[...], r.normed[:, columns], (1, 0))
    )
    by_columns(r.up_attn.at[:, pl.ds(192, 64)], lambda columns: dot(r.o_t[...], r.dz[:, columns], (1, 0)))
    attn = first_of("attn", r.up_attn, "b")
    next(dh1)
    r.small_bias[...] = dot(jnp.ones((8, ROWS), BF16), r.d_qkv[...], (1, 1))
    _, normed_a, rstd_a = layer_norm(r.x_own[...].astype(F32), r.norms[0:1], r.norms[2:3])
    next(rest_up)
    next(attn)
    next(gather_gd)
    next(rest_up)
    finish(rest_up)
    gather_up = gather_ctx(engine, r.landing_up, r.up_all)
    next(gather_up)
    next(dh1)
    back_a, gain_a, shift_a = norm_back(r.summed[...], normed_a, rstd_a, r.norms[0:1])
    r.grad_own[...] = spread(r.d_middle[...] + back_a).astype(BF16)
    r.small_norms[0:1] = gain_a[None]
    r.small_norms[2:3] = shift_a[None]
    r.small_norms[4:] = jnp.zeros((4, WIDTH), F32)
    r.small_norms[...] = spread(r.small_norms[...])
    small = sum_small(
        engine, r.small_norms, r.small_bias, r.norm_sum, r.bias_all, r.by_group, r.small_x, r.small_y
    )
    next(small)
    next(attn)
    rest_attn = rest_of("attn", lambda zz: r.landing_attn.at[zz])
    next(small)
    next(gather_gd)
    next(gather_up)
    hand_grad = hand_back(engine, r.grad_own, r.grad_tokens)
    next(hand_grad)
    next(rest_attn)
    next(small)
    next(gather_up)
    next(small)
    next(rest_attn)
    gather_attn = gather_ctx(engine, r.landing_attn, r.attn_all)
    next(gather_attn)
    next(gather_up)
    next(gather_attn)
    finish(small)
    table = jnp.concatenate([r.bias_all[k, 0:1] for k in range(8)], axis=0)
    from_at = lax.broadcasted_iota(jnp.int32, (768, 16), 0)
    to_at = lax.broadcasted_iota(jnp.int32, (768, 16), 1)
    row_at = lax.broadcasted_iota(jnp.int32, (16, 8), 0)
    group_at = lax.broadcasted_iota(jnp.int32, (16, 8), 1)
    for part in range(3):
        total = jnp.zeros((16, 16), F32)
        for j in range(2):
            chosen = (from_at == to_at + ((yh * 2 + j) * 3 + part) * HEAD + z * 16).astype(F32)
            spread_rows = (row_at == group_at * 2 + j).astype(F32)
            total += exact_dot(spread_rows, exact_dot(table, chosen))
        r.grad_bias[part] = total
    next(gather_attn)
    finish(gather_gd)
    finish(gather_up)
    next(gather_attn)
    threads = (dh2, mlp, gate, down, up, attn, rest_gate, rest_down, rest_up, rest_attn)
    for thread in threads + (hand_out, dh1, hand_grad, small, gather_gd, gather_up, gather_attn):
        finish(thread)
    for copy in back[:-1]:
        copy.wait_send()


def layer(*inputs):
    outs = PLACES + RESULTS
    values = pl.pallas_call(
        layer_kernel,
        out_shape=[jax.ShapeDtypeStruct(o[1], o[2]) for o in outs],
        in_specs=[HBM] * 2 + [VMEM] * 4 + [HBM] * 4 + [VMEM] * 2,
        out_specs=[o[3] for o in outs],
        scratch_shapes=[pltpu.VMEM(shape, dtype) for _, shape, dtype in SCRATCH] + semaphores(147, 414, 20),
        compiler_params=pltpu.CompilerParams(
            collective_id=1, has_side_effects=True, vmem_limit_bytes=VMEM_BYTES
        ),
        name="layer",
    )(*inputs)
    return values[len(PLACES) :]


def assemble_kernel(
    gd_ref,
    up_ref,
    attn_ref,
    layer_ref,
    tokens_ref,
    norms_ref,
    gu_ref,
    down_ref,
    qkv_ref,
    out_ref,
    layer_out_ref,
    tokens_out_ref,
    gains_ref,
    shifts_ref,
    turned,
):
    layer_out_ref[...] = layer_ref[...]
    tokens_out_ref[...] = tokens_ref[...].astype(F32)
    gains_ref[...] = norms_ref[0:2]
    shifts_ref[...] = norms_ref[2:4]
    for g in range(2):
        for zz in range(4):
            for core in range(2):
                for yl in range(2):
                    row = zz * 704 + core * 352 + yl * 176
                    block = up_ref[0, yl * 2 + core, zz] if g else gd_ref[0, yl * 2 + core, zz, :176]
                    turned[row : row + 176, :] = block.astype(F32)
        for t in range(22):
            gu_ref[:, g, t * 128 : (t + 1) * 128] = turned[t * 128 : (t + 1) * 128, :].T
    for zz in range(4):
        for core in range(2):
            for yl in range(2):
                row = zz * 704 + core * 352 + yl * 176
                down_ref[row : row + 176, :] = gd_ref[0, yl * 2 + core, zz, 176:].astype(F32)
                row = zz * 256 + core * 128 + yl * 64
                out_ref[row : row + 64, :] = attn_ref[0, yl * 2 + core, zz, 192:].astype(F32)
            for part in range(3):
                rows = slice(part * 64, (part + 1) * 64)
                block = jnp.concatenate([attn_ref[0, core, zz, rows], attn_ref[0, 2 + core, zz, rows]], axis=0)
                column = zz * 256 + core * 128
                qkv_ref[part, :, column : column + 128] = block.astype(F32).T


def assemble(gd_all, up_all, attn_all, layer_out, grad_tokens, norm_sum):
    gd_all = gd_all.reshape(4, 4, 4, 352, 128)
    up_all = up_all.reshape(4, 4, 4, 176, 128)
    attn_all = attn_all.reshape(4, 4, 4, 256, 128)
    return pl.pallas_call(
        assemble_kernel,
        grid=(4,),
        in_specs=[
            pl.BlockSpec((1, 4, 4, 352, 128), lambda i: (i, 0, 0, 0, 0)),
            pl.BlockSpec((1, 4, 4, 176, 128), lambda i: (i, 0, 0, 0, 0)),
            pl.BlockSpec((1, 4, 4, 256, 128), lambda i: (i, 0, 0, 0, 0)),
            pl.BlockSpec((32, WIDTH), lambda i: (i, 0)),
            pl.BlockSpec((32, WIDTH), lambda i: (i, 0)),
            pl.BlockSpec((8, 512), lambda i: (0, 0)),
        ],
        out_specs=[
            pl.BlockSpec((128, 2, 2816), lambda i: (i, 0, 0)),
            pl.BlockSpec((2816, 128), lambda i: (0, i)),
            pl.BlockSpec((3, 128, 1024), lambda i: (0, i, 0)),
            pl.BlockSpec((1024, 128), lambda i: (0, i)),
            pl.BlockSpec((32, WIDTH), lambda i: (i, 0)),
            pl.BlockSpec((32, WIDTH), lambda i: (i, 0)),
            pl.BlockSpec((2, 512), lambda i: (0, 0)),
            pl.BlockSpec((2, 512), lambda i: (0, 0)),
        ],
        out_shape=[
            jax.ShapeDtypeStruct((512, 2, 2816), F32),
            jax.ShapeDtypeStruct((2816, 512), F32),
            jax.ShapeDtypeStruct((3, 512, 1024), F32),
            jax.ShapeDtypeStruct((1024, 512), F32),
            jax.ShapeDtypeStruct((2 * OWN, WIDTH), BF16),
            jax.ShapeDtypeStruct((2 * OWN, WIDTH), F32),
            jax.ShapeDtypeStruct((2, 512), F32),
            jax.ShapeDtypeStruct((2, 512), F32),
        ],
        scratch_shapes=[pltpu.VMEM((2816, 128), F32)],
        compiler_params=pltpu.CompilerParams(vmem_limit_bytes=VMEM_BYTES),
        name="assemble",
    )(gd_all, up_all, attn_all, layer_out, grad_tokens, norm_sum)


def rotation_tables():
    half = ROT // 2
    positions = np.arange(SEQ, dtype=np.float32)
    inverse = (10000.0 ** (-(np.arange(half) * 2.0 / ROT))).astype(np.float32)
    angles = (inverse[:, None] * positions[None, :]).astype(np.float64)
    return jnp.asarray(np.cos(angles).astype(np.float32)), jnp.asarray(np.sin(angles).astype(np.float32))


def layer_norm(values, gain_row, shift_row):
    row_mean = jnp.mean(values, axis=-1, keepdims=True)
    centred = values - row_mean
    variance = jnp.mean(centred * centred, axis=-1, keepdims=True)
    rstd = lax.rsqrt(variance + EPS)
    normed = centred * rstd
    return normed * gain_row + shift_row, normed, rstd


def norm_back(gradient, normed, rstd, gain_row):
    shaped = gradient * gain_row
    centre = (
        shaped
        - jnp.mean(shaped, axis=-1, keepdims=True)
        - normed * jnp.mean(shaped * normed, axis=-1, keepdims=True)
    )
    return centre * rstd, jnp.sum(gradient * normed, axis=0), jnp.sum(gradient, axis=0)


def local(tokens, segments, w_qkv, b_qkv, w_out, w_gate_up, w_down, norm_gains, norm_shifts, cotangent):
    cosine, sine = rotation_tables()
    layer_out, grad_tokens, gd_all, up_all, attn_all, norm_sum, grad_bias = layer(
        tokens[0],
        cotangent[0],
        norm_gains,
        norm_shifts,
        b_qkv,
        segments,
        w_qkv.transpose(1, 0, 2),
        w_out,
        w_down,
        w_gate_up,
        cosine,
        sine,
    )
    out_gu, out_down, out_qkv, out_out, layer_out, grad_tokens, gains, shifts = assemble(
        gd_all, up_all, attn_all, layer_out, grad_tokens, norm_sum
    )
    return (
        layer_out[None],
        grad_tokens[None],
        out_qkv.transpose(1, 0, 2),
        grad_bias,
        out_out,
        out_gu,
        out_down,
        gains,
        shifts,
    )


def solution(mesh):
    fine = Mesh(mesh.devices.reshape(4, 4, 2, 2, 2), ("z", "x", "yl", "core", "yh"))
    ctx = ("x", "yl", "core")
    return jax.shard_map(
        local,
        mesh=fine,
        in_specs=(
            P("z", ctx, None),
            P("z", None),
            P("z", None, "yh"),
            P(None, "yh", "z"),
            P("yh", "z"),
            P("z", None, "yh"),
            P("yh", "z"),
            P(None, "z"),
            P(None, "z"),
            P("z", ctx, None),
        ),
        out_specs=(
            P("z", ctx, None),
            P("z", ctx, None),
            P("z", None, "yh"),
            P(None, "yh", "z"),
            P("yh", "z"),
            P("z", None, "yh"),
            P("yh", "z"),
            P(None, "z"),
            P(None, "z"),
        ),
        check_vma=False,
    )
```

```python
import functools

import jax
import jax.numpy as jnp
import numpy as np
from jax import lax
from jax.experimental import pallas as pl
from jax.experimental.pallas import tpu as pltpu
from jax.sharding import Mesh
from jax.sharding import PartitionSpec as P

EPS = 1e-05
NEG = -1e30
ROT = 16
HEAD = 64
SEQ = 2048
WIDTH = 2048
OWN = 64
ROWS = 512
QB = 256
VMEM_BYTES = 63 * 2**20
F32 = jnp.float32
BF16 = jnp.bfloat16
MESH_ID = pl.DeviceIdType.MESH
HBM = pl.BlockSpec(memory_space=pltpu.HBM)
VMEM = pl.BlockSpec(memory_space=pltpu.VMEM)


def place():
    return tuple(lax.axis_index(a) for a in ("z", "x", "yl", "core", "yh"))


def lanes(index, size=128):
    return pl.ds(pl.multiple_of(index * size, size), size)


def rows_at(index, size):
    return pl.ds(pl.multiple_of(index * size, size), size)


def z_peer(d):
    z = lax.axis_index("z")
    return {"z": lax.rem(z + d, 4)}


def x_peer(d):
    x = lax.axis_index("x")
    return {"x": lax.rem(x + d, 4)}


def y_peer(d):
    y = lax.rem(lax.axis_index("yh") * 2 + lax.axis_index("yl") + d, 4)
    return {"yh": y // 2, "yl": lax.rem(y, 2)}


def xy_peer(dx, dy):
    return {**x_peer(dx), **y_peer(dy)}


def sibling():
    return {"core": 1 - lax.axis_index("core")}


Z_PEERS = [functools.partial(z_peer, d) for d in (1, 2, 3)]
X_PEERS = [functools.partial(x_peer, d) for d in (1, 2, 3)]
Y_PEERS = [functools.partial(y_peer, d) for d in (1, 2, 3)]
XY_ALL = [(dx, dy) for dx in range(4) for dy in range(4) if dx or dy]
XY_PEERS = [functools.partial(xy_peer, dx, dy) for dx, dy in XY_ALL]


class Remote:
    def __init__(self, engine, index, copy):
        self.engine, self.index, self.copy = engine, index, copy

    def wait_recv(self):
        self.copy.wait_recv()

    def wait_send(self):
        self.copy.wait_send()
        self.engine.free_send.append(self.index)

    def wait(self):
        self.wait_recv()
        self.wait_send()


class Local:
    def __init__(self, engine, index, copy):
        self.engine, self.index, self.copy = engine, index, copy

    def wait(self):
        self.copy.wait()
        self.engine.free_local.append(self.index)


class Group:
    def __init__(self, engine, view, device):
        self.engine, self.view, self.device = engine, view, device
        self.index, self.place = engine.free_send.pop(), engine.free_recv.pop()

    def copy(self, src, dst, device):
        return pltpu.make_async_remote_copy(
            src,
            dst,
            self.engine.send_sem.at[self.index],
            self.engine.recv_sem.at[self.place],
            device_id=device,
            device_id_type=MESH_ID,
        )

    def send(self, src, dst, device):
        self.copy(src, dst, device).start()

    def wait_recv(self):
        self.copy(self.view, self.view, self.device).wait_recv()

    def wait_send(self):
        self.copy(self.view, self.view, self.device).wait_send()
        self.engine.free_send.append(self.index)


class Engine:
    def __init__(self, send_sem, recv_sem, local_sem):
        self.send_sem, self.recv_sem, self.local_sem = send_sem, recv_sem, local_sem
        self.free_send = list(range(send_sem.shape[0]))[::-1]
        self.free_recv = list(range(recv_sem.shape[0]))[::-1]
        self.free_local = list(range(local_sem.shape[0]))[::-1]

    def send(self, src, dst, device):
        i, k = self.free_send.pop(), self.free_recv.pop()
        copy = pltpu.make_async_remote_copy(
            src, dst, self.send_sem.at[i], self.recv_sem.at[k], device_id=device, device_id_type=MESH_ID
        )
        copy.start()
        return Remote(self, i, copy)

    def local(self, src, dst):
        i = self.free_local.pop()
        copy = pltpu.make_async_copy(src, dst, self.local_sem.at[i])
        copy.start()
        return Local(self, i, copy)


def greet(peers):
    barrier = pltpu.get_barrier_semaphore()
    for peer in peers:
        pl.semaphore_signal(barrier, 1, device_id=peer(), device_id_type=MESH_ID)
    pl.semaphore_wait(barrier, len(peers))


def semaphores(n_send, n_recv, n_local):
    return [pltpu.SemaphoreType.DMA((n,)) for n in (n_send, n_recv, n_local)]


def spread(values):
    return jnp.concatenate(
        [values[:, (a * 4 + b) * 128 : (a * 4 + b + 1) * 128] for b in range(4) for a in range(4)], axis=1
    )


def finish(thread):
    for _ in thread:
        pass


def send_pieces(engine, pieces, slots):
    z = lax.axis_index("z")
    copies = [engine.local(pieces(z), slots(z))]
    for d in (1, 2, 3):
        to = z_peer(d)
        copies.append(engine.send(pieces(to["z"]), slots(z), to))
    return copies


def gather_tokens(engine, src, dst):
    z, core = lax.axis_index("z"), lax.axis_index("core")
    mine = dst.at[rows_at(z * 2 + core, OWN)]
    first = [engine.send(src, mine, z_peer(d)) for d in (1, 2, 3)]
    rest = [engine.send(src, mine, sibling()), engine.local(src, mine)]
    yield
    for d in (1, 2, 3):
        first[d - 1].wait_recv()
        here = dst.at[rows_at(lax.rem(z + 4 - d, 4) * 2 + core, OWN)]
        rest.append(engine.send(here, here, sibling()))
    yield
    for copy in first:
        copy.wait_send()
    for copy in rest:
        copy.wait()


def gather_weight(engine, src, dst):
    n = src.shape[0]
    top = first_part(n)
    head, tail = pl.ds(0, top), pl.ds(top, n - top)
    x = lax.axis_index("x")
    y = lax.axis_index("yh") * 2 + lax.axis_index("yl")
    left_y, left_x = lax.rem(y + 3, 4), lax.rem(x + 3, 4)
    right_y, right_x = lax.rem(y + 1, 4), lax.rem(x + 1, 4)
    mine = lanes(x, 512)
    local = engine.local(src, dst.at[y, :, mine])
    along_x = [engine.send(src.at[head], dst.at[y, head, mine], x_peer(d)) for d in (1, 2, 3)]
    along_y = [engine.send(src.at[tail], dst.at[y, tail, mine], y_peer(d)) for d in (1, 2, 3)]
    yield
    local.wait()
    for copy in along_x:
        copy.wait_recv()
    ring_y = [engine.send(dst.at[y, head], dst.at[y, head], y_peer(d)) for d in (1, 3)]
    for copy in along_y:
        copy.wait_recv()
    ring_x = [engine.send(dst.at[:, tail, mine], dst.at[:, tail, mine], x_peer(d)) for d in (1, 3)]
    yield
    rest = []
    half = first_part(top)
    early, late = pl.ds(0, half), pl.ds(half, top - half)
    ring_y[0].wait_recv()
    rest.append(engine.send(dst.at[left_y, early], dst.at[left_y, early], y_peer(1)))
    ring_y[1].wait_recv()
    rest.append(engine.send(dst.at[right_y, late], dst.at[right_y, late], y_peer(3)))
    ring_x[0].wait_recv()
    block = dst.at[:, tail, lanes(left_x * 2, 256)]
    rest.append(engine.send(block, block, x_peer(1)))
    ring_x[1].wait_recv()
    block = dst.at[:, tail, lanes(right_x * 2 + 1, 256)]
    rest.append(engine.send(block, block, x_peer(3)))
    yield
    for copy in along_x + along_y + ring_y + ring_x:
        copy.wait_send()
    for copy in rest:
        copy.wait()


def first_part(n):
    return (n // 2 + 15) // 16 * 16


class Items:
    def __init__(self, group, local):
        self.group, self.local = group, local

    def wait_recv(self):
        self.local.wait()
        self.group.wait_recv()

    def wait_send(self):
        self.group.wait_send()


def send_items(engine, src, dst, n):
    x, yl, yh = (lax.axis_index(a) for a in ("x", "yl", "yh"))
    y = yh * 2 + yl
    mine = dst.at[:, lanes(x * 4 + yl * 2 + yh)]
    group = Group(engine, dst.at[:, pl.ds(0, 15 * 128)], xy_peer(*XY_ALL[0]))
    for dx, dy in XY_ALL:
        tx, ty = lax.rem(x + dx, 4), lax.rem(y + dy, 4)
        group.send(src.at[rows_at(ty, n), lanes(tx)], mine, xy_peer(dx, dy))
    return Items(group, engine.local(src.at[rows_at(y, n), lanes(x)], mine))


def return_items(engine, src, dst, n):
    x, yl, yh = (lax.axis_index(a) for a in ("x", "yl", "yh"))
    mine = dst.at[rows_at(yh * 2 + yl, n), lanes(x)]
    group = Group(engine, dst.at[pl.ds(0, 15 * n // 4)], xy_peer(*XY_ALL[0]))
    for dx, dy in XY_ALL:
        to = xy_peer(dx, dy)
        group.send(src.at[:, lanes(to["x"] * 4 + to["yl"] * 2 + to["yh"])], mine, to)
    return Items(group, engine.local(src.at[:, lanes(x * 4 + yl * 2 + yh)], mine))


def add_up(total, terms, index, rows, width):
    def step(i, carry):
        here = (*index, rows_at(i, 16), slice(0, width))
        value = terms[0][here].astype(F32)
        for term in terms[1:]:
            value += term[here].astype(F32)
        total[here] = value.astype(total.dtype)
        return carry

    lax.fori_loop(0, rows // 16, step, 0)


def exact_dot(a, b):
    return jnp.dot(a, b, precision=lax.Precision.HIGHEST, preferred_element_type=F32)


def by_columns(dst, value_of):
    for k in range(4):
        columns = slice(k * 512, (k + 1) * 512)
        value = value_of(columns).astype(dst.dtype)
        dst[..., columns] = value.reshape(dst.shape[:-1] + (512,))


def scatter_tokens(engine, product, dst, other, arrived):
    z, core = lax.axis_index("z"), lax.axis_index("core")
    to_core = []
    for i in range(4):
        give = product.at[rows_at(lax.rem(z + 1 + i, 4) * 2 + 1 - core, OWN)]
        to_core.append(engine.send(give, other.at[i], sibling()))
    yield
    to_z = []
    for i in range(3):
        own = rows_at(lax.rem(z + 1 + i, 4) * 2 + core, OWN)
        to_core[i].wait_recv()
        product[own, :] = (product[own, :].astype(F32) + other[i].astype(F32)).astype(BF16)
        to_z.append(engine.send(product.at[own], arrived.at[i], z_peer(i + 1)))
    yield
    to_core[3].wait_recv()
    dst[...] = product[rows_at(z * 2 + core, OWN), :].astype(F32) + other[3].astype(F32)
    for i in range(3):
        to_z[i].wait_recv()
        dst[...] += arrived[i].astype(F32)
    yield
    for copy in to_core + to_z:
        copy.wait_send()


def sum_first(engine, src, sum_y, sum_x, by_y, by_x, relay_y, relay_x, own_y, own_x):
    n, cut = src.shape[1], sum_y.shape[0]
    rest, half = n - cut, first_part(cut)
    tail = pl.ds(cut, rest)
    early, late = pl.ds(0, half), pl.ds(half, cut - half)
    low, high = pl.ds(0, 2), pl.ds(2, 2)
    x = lax.axis_index("x")
    y = lax.axis_index("yh") * 2 + lax.axis_index("yl")
    up_y, down_y = lax.rem(y + 1, 4), lax.rem(y + 3, 4)
    up_x, down_x = lanes(lax.rem(x + 1, 4), 512), lanes(lax.rem(x + 3, 4), 512)
    far_y, far_x = lax.rem(y + 2, 4), lanes(lax.rem(x + 2, 4), 512)
    relays = [
        engine.send(src.at[far_y, early], relay_y.at[early], y_peer(1)),
        engine.send(src.at[low, tail, far_x], relay_x.at[low], x_peer(1)),
        engine.send(src.at[far_y, late], relay_y.at[late], y_peer(3)),
        engine.send(src.at[high, tail, far_x], relay_x.at[high], x_peer(3)),
    ]
    copies = [
        engine.send(src.at[up_y, late], by_y.at[0, late], y_peer(1)),
        engine.send(src.at[high, tail, up_x], by_x.at[0, high], x_peer(1)),
        engine.send(src.at[down_y, early], by_y.at[1, early], y_peer(3)),
        engine.send(src.at[low, tail, down_x], by_x.at[1, low], x_peer(3)),
    ]
    yield
    own_y, own_x = own_y.at[pl.ds(0, cut)], own_x.at[:, pl.ds(0, rest)]
    local = [
        engine.local(src.at[up_y, early], own_y.at[early]),
        engine.local(src.at[down_y, late], own_y.at[late]),
        engine.local(src.at[low, tail, up_x], own_x.at[low]),
        engine.local(src.at[high, tail, down_x], own_x.at[high]),
    ]
    for copy in local:
        copy.wait()
    passed = []
    relays[0].wait_recv()
    add_up(relay_y.at[early], [relay_y.at[early], own_y.at[early]], (), half, WIDTH)
    passed.append(engine.send(relay_y.at[early], by_y.at[0, early], y_peer(1)))
    relays[1].wait_recv()
    for q in range(2):
        add_up(relay_x, [relay_x, own_x], (q,), rest, 512)
    passed.append(engine.send(relay_x.at[low], by_x.at[0, low], x_peer(1)))
    relays[2].wait_recv()
    add_up(relay_y.at[late], [relay_y.at[late], own_y.at[late]], (), cut - half, WIDTH)
    passed.append(engine.send(relay_y.at[late], by_y.at[1, late], y_peer(3)))
    relays[3].wait_recv()
    for q in range(2, 4):
        add_up(relay_x, [relay_x, own_x], (q,), rest, 512)
    passed.append(engine.send(relay_x.at[high], by_x.at[1, high], x_peer(3)))
    yield
    local = [
        engine.local(src.at[y, pl.ds(0, cut)], own_y),
        engine.local(src.at[:, tail, lanes(x, 512)], own_x),
    ]
    for copy in local:
        copy.wait()
    for copy in copies + passed:
        copy.wait_recv()
    add_up(sum_y, [own_y, by_y.at[0], by_y.at[1]], (), cut, WIDTH)
    for q in range(4):
        add_up(sum_x, [own_x, by_x.at[0], by_x.at[1]], (q,), rest, 512)
    for copy in passed:
        copy.wait_send()
    yield
    for copy in relays + copies:
        copy.wait_send()


def sum_rest(engine, heads, tails, landing, by_x, by_y, own, total):
    cut, rest = heads.shape[0], tails.shape[1]
    x = lax.axis_index("x")
    y = lax.axis_index("yh") * 2 + lax.axis_index("yl")
    first, second = pl.ds(0, cut), pl.ds(cut, rest)
    copies = []
    for d in (2, 1, 3):
        ty, tx = y_peer(d), x_peer(d)
        copies.append(engine.send(heads.at[:, lanes(tx["x"], 512)], by_x.at[d - 1], tx))
        copies.append(engine.send(tails.at[ty["yh"] * 2 + ty["yl"]], by_y.at[d - 1], ty))
    local = [engine.local(tails.at[y], own.at[second]), engine.local(heads.at[:, lanes(x, 512)], own.at[first])]
    yield
    for copy in local:
        copy.wait()
    for copy in copies:
        copy.wait_recv()
    add_up(total.at[first], [own.at[first]] + [by_x.at[k] for k in range(3)], (), cut, 512)
    add_up(total.at[second], [own.at[second]] + [by_y.at[k] for k in range(3)], (), rest, 512)
    moved = send_pieces(engine, lambda z: total.at[:, lanes(z)], landing)
    yield
    moved[0].wait()
    for copy in moved[1:]:
        copy.wait_recv()
    yield
    for copy in copies + moved[1:]:
        copy.wait_send()


def gather_ctx(engine, landing, dst):
    x, yl, core = (lax.axis_index(a) for a in ("x", "yl", "core"))

    def slot(dx, ll):
        return (lax.rem(x + dx, 4) * 2 + ll) * 2 + core

    other, n = 1 - yl, landing.shape[1]
    half = first_part(n)
    first, second = (pl.ds(0, 3),), (pl.ds(3, 1),)
    even, even_other = ((pl.ds(0, 2),), (pl.ds(2, 1),)), ((pl.ds(0, 1),), (pl.ds(1, 2),))
    odd = ((pl.ds(3, 1), pl.ds(0, half)), (pl.ds(3, 1), pl.ds(half, n - half)))
    partner, there = {"yl": other}, sibling()
    sent = []

    def send(source, target, part, device):
        copy = engine.send(source, dst.at[(target, *part)], device)
        sent.append(copy)
        return copy

    siblings = Group(engine, dst.at[pl.ds(0, 8)], there)

    def hand(index, part):
        block = dst.at[(index, *part)]
        siblings.send(block, block, there)

    def on(index, part, device):
        return send(dst.at[(index, *part)], index, part, device)

    me = slot(0, yl)
    local = engine.local(landing, dst.at[me])
    siblings.send(landing, dst.at[me], there)
    to_y = send(landing.at[*first], me, first, partner)
    round_b = [send(landing.at[*second], me, second, x_peer(d)) for d in (1, 3)]
    round_a = [send(landing.at[*first], me, first, x_peer(d)) for d in (1, 3)]
    over = [send(landing.at[*second], me, second, partner)]
    yield
    to_y.wait_recv()
    round_c = [on(slot(0, other), first, x_peer(d)) for d in (1, 3)]
    hand(slot(0, other), first)
    onward = []
    for k, (d, to) in enumerate(((3, 1), (1, 3))):
        round_b[k].wait_recv()
        onward.append(on(slot(d, yl), odd[k], x_peer(to)))
        over.append(on(slot(d, yl), second, partner))
        hand(slot(d, yl), second)
    for k, (d, to) in enumerate(((3, 1), (1, 3))):
        round_a[k].wait_recv()
        onward.append(on(slot(d, yl), even[k], x_peer(to)))
        hand(slot(d, yl), first)
    yield
    for k in range(2):
        onward[k].wait_recv()
    over.append(on(slot(2, yl), second, partner))
    hand(slot(2, yl), second)
    for k, (d, to) in enumerate(((3, 1), (1, 3))):
        round_c[k].wait_recv()
        onward.append(on(slot(d, other), even_other[k], x_peer(to)))
        hand(slot(d, other), first)
    yield
    for k in (2, 3):
        onward[k].wait_recv()
    hand(slot(2, yl), first)
    for k, d in enumerate((0, 3, 1, 2)):
        over[k].wait_recv()
        hand(slot(d, other), second)
    for k in (4, 5):
        onward[k].wait_recv()
    hand(slot(2, other), first)
    yield
    local.wait()
    siblings.wait_recv()
    siblings.wait_send()
    for copy in sent:
        copy.wait_send()


def group_peer(dz, dc):
    return {
        "z": lax.rem(lax.axis_index("z") + dz, 4),
        "core": lax.rem(lax.axis_index("core") + dc, 2),
    }


GROUP_ALL = [(dz, dc) for dz in range(4) for dc in range(2) if dz or dc]


def sum_small(engine, norms, bias, norm_sum, bias_all, by_group, by_x, by_y):
    z, x, yl, core, yh = place()
    y = yh * 2 + yl
    me = z * 2 + core
    first = []
    for dz, dc in GROUP_ALL:
        to = group_peer(dz, dc)
        first.append(engine.send(norms.at[:, lanes(to["z"], 512)], by_group.at[me], to))
    mine = engine.local(norms.at[:, lanes(z, 512)], by_group.at[me])
    yield
    mine.wait()
    for copy in first:
        copy.wait_recv()
    by_x[x, :, :512] = sum(by_group[k] for k in range(8))
    by_x[x, :, 512:] = bias[...]
    second = [engine.send(by_x.at[x], by_x.at[x], x_peer(d)) for d in (1, 2, 3)]
    yield
    for copy in second:
        copy.wait_recv()
    by_y[y] = sum(by_x[k] for k in range(4))
    third = [engine.send(by_y.at[y], by_y.at[y], y_peer(d)) for d in (1, 2, 3)]
    yield
    for copy in third:
        copy.wait_recv()
    total = sum(by_y[k] for k in range(4))
    norm_sum[...] = total[:, :512]
    bias_all[me] = total[:, 512:]
    last = [engine.send(bias_all.at[me], bias_all.at[me], group_peer(dz, dc)) for dz, dc in GROUP_ALL]
    yield
    for copy in last:
        copy.wait()
    for copy in first + second + third:
        copy.wait_send()


def hand_back(engine, src, dst):
    core, yh = lax.axis_index("core"), lax.axis_index("yh")
    far = {"core": yh, "yh": 1 - yh}
    near = {"core": yh}
    stays = core == yh
    mine = dst.at[rows_at(core, OWN)]
    sends = [engine.free_send.pop() for _ in range(2)]
    arrivals = [engine.free_recv.pop() for _ in range(2)]
    j = engine.free_local.pop()
    send_sem, recv_sem, local_sem = engine.send_sem, engine.recv_sem, engine.local_sem

    def make(to, slot):
        return pltpu.make_async_remote_copy(
            src,
            mine,
            send_sem.at[sends[slot]],
            recv_sem.at[arrivals[0] + (arrivals[1] - arrivals[0]) * core],
            device_id=to,
            device_id_type=MESH_ID,
        )

    def arrival(half):
        part = dst.at[rows_at(half, OWN)]
        return pltpu.make_async_remote_copy(
            part, part, send_sem.at[sends[0]], recv_sem.at[arrivals[0] + (arrivals[1] - arrivals[0]) * half], device_id=far, device_id_type=MESH_ID
        )

    make(far, 0).start()

    @pl.when(stays)
    def _():
        pltpu.make_async_copy(src, mine, local_sem.at[j]).start()

    @pl.when(jnp.logical_not(stays))
    def _():
        make(near, 1).start()

    yield
    make(far, 0).wait_send()

    @pl.when(stays)
    def _():
        pltpu.make_async_copy(src, mine, local_sem.at[j]).wait()
        arrival(1 - core).wait_recv()

    @pl.when(jnp.logical_not(stays))
    def _():
        make(near, 1).wait_send()
        arrival(core).wait_recv()
        arrival(1 - core).wait_recv()

    engine.free_send.extend(sends)
    engine.free_local.append(j)


def dot(a, b, dims):
    return lax.dot_general(a, b, ((dims[:1], dims[1:]), ((), ())), preferred_element_type=F32)


def rope(block, cosine, sine):
    front, back = block[:8], block[8:16]
    return jnp.concatenate(
        [front * cosine - back * sine, back * cosine + front * sine, block[16:]], axis=0
    )


def rope_back(block, cosine, sine):
    front, back = block[:8], block[8:16]
    return jnp.concatenate(
        [front * cosine + back * sine, back * cosine - front * sine, block[16:]], axis=0
    )


def masked_scores(scores, start, seg_row, seg_col):
    stop = start + QB

    def hide(first, last, by_segment, causal):
        part = scores[first:last]
        keep = None
        if by_segment:
            keep = seg_col[first:last] == seg_row[:, start:stop]
        if causal:
            key_at = first + lax.broadcasted_iota(jnp.int32, part.shape, 0)
            query_at = start + lax.broadcasted_iota(jnp.int32, part.shape, 1)
            order = key_at <= query_at
            keep = order if keep is None else keep & order
        return jnp.where(keep, part, NEG)

    if start == 0:
        return hide(0, stop, True, True)
    if stop + 127 <= SEQ:
        parts = [hide(0, 128, True, False)]
        if start > 128:
            parts.append(scores[128:start])
        parts.append(hide(start, stop, False, True))
        return jnp.concatenate(parts, axis=0)
    return jnp.concatenate([hide(0, start, True, False), hide(start, stop, True, True)], axis=0)


def attend(qkv_ref, row_ref, col_ref, cos_ref, sin_ref, o_ref, wide_ref, lse_ref, kept_ref):
    cosine, sine = cos_ref[...], sin_ref[...]
    q_t = rope(qkv_ref[:HEAD].astype(F32), cosine, sine).astype(BF16) * jnp.asarray(0.125, BF16)
    k_t = rope(qkv_ref[HEAD : 2 * HEAD].astype(F32), cosine, sine).astype(BF16)
    v_t = qkv_ref[2 * HEAD :]
    kept_ref[:HEAD] = q_t
    kept_ref[HEAD : 2 * HEAD] = k_t
    kept_ref[2 * HEAD :] = v_t
    keys = k_t.astype(F32).T.astype(BF16)
    seg_row, seg_col = row_ref[...], col_ref[...]
    for start in range(0, SEQ, QB):
        stop = start + QB
        scores = dot(keys[:stop], q_t[:, start:stop], (1, 0))
        scores = masked_scores(scores, start, seg_row, seg_col)
        top = jnp.max(scores, axis=0, keepdims=True)
        terms = jnp.exp(scores - top)
        total = jnp.sum(terms, axis=0, keepdims=True)
        out = dot(v_t[:, :stop], terms.astype(BF16), (1, 0)) / total
        wide_ref[:, start:stop] = out
        o_ref[:, start:stop] = out.astype(BF16)
        lse_ref[:, start:stop] = top + jnp.log(total)


def attend_back(kept_ref, do_ref, wide_ref, lse_ref, row_ref, col_ref, cos_ref, sin_ref, out_ref, sum_ref):
    cosine, sine = cos_ref[...], sin_ref[...]
    q_t, k_t, do_t = kept_ref[:HEAD], kept_ref[HEAD : 2 * HEAD], do_ref[...]
    queries = q_t.astype(F32).T.astype(BF16)
    keys = k_t.astype(F32).T.astype(BF16)
    values = kept_ref[2 * HEAD :].astype(F32).T.astype(BF16)
    grads = do_t.astype(F32).T.astype(BF16)
    centre = jnp.sum(do_t.astype(F32) * wide_ref[...], axis=0, keepdims=True)
    lse = lse_ref[...]
    seg_row, seg_col = row_ref[...], col_ref[...]
    sum_ref[...] = jnp.zeros_like(sum_ref)
    dq_parts = []
    for start in range(0, SEQ, QB):
        stop = start + QB
        scores = dot(keys[:stop], q_t[:, start:stop], (1, 0))
        scores = masked_scores(scores, start, seg_row, seg_col)
        probs = jnp.exp(scores - lse[:, start:stop])
        d_probs = dot(values[:stop], do_t[:, start:stop], (1, 0))
        d_scores = (probs * (d_probs - centre[:, start:stop])).astype(BF16)
        d_keys = dot(d_scores, queries[start:stop], (1, 0))
        d_values = dot(probs.astype(BF16), grads[start:stop], (1, 0))
        sum_ref[:stop] += jnp.concatenate([d_keys, d_values], axis=1)
        dq_parts.append(dot(k_t[:, :stop], d_scores, (1, 0)) * 0.125)
    out_ref[:HEAD] = rope_back(jnp.concatenate(dq_parts, axis=1), cosine, sine).astype(BF16)
    turned = sum_ref[...].T
    out_ref[HEAD : 2 * HEAD] = rope_back(turned[:HEAD], cosine, sine).astype(BF16)
    out_ref[2 * HEAD :] = turned[HEAD:].astype(BF16)


def small_peer(dz, dh):
    return {
        "z": lax.rem(lax.axis_index("z") + dz, 4),
        "yh": lax.rem(lax.axis_index("yh") + dh, 2),
    }


SMALL_ALL = [(dz, dh) for dz in range(4) for dh in range(2) if dz or dh]
SCRATCH = [
    ("m_qkv", (4, 192, WIDTH), BF16),
    ("m_out", (4, 64, WIDTH), BF16),
    ("x_own", (OWN, WIDTH), BF16),
    ("dy_own", (OWN, WIDTH), BF16),
    ("middle", (OWN, WIDTH), F32),
    ("norms", (8, WIDTH), F32),
    ("h1", (ROWS, WIDTH), BF16),
    ("o_t", (4 * HEAD, ROWS), BF16),
    ("kept", (3 * HEAD, SEQ), BF16),
    ("wide", (HEAD, SEQ), F32),
    ("lse", (1, SEQ), F32),
    ("seg_row", (1, SEQ), F32),
    ("seg_col", (SEQ, 1), F32),
    ("packed", (16, 640), BF16),
    ("small", (4, 2, 16, 640), BF16),
    ("near_x", (OWN, WIDTH), BF16),
    ("near_dy", (OWN, WIDTH), BF16),
    ("far_x", (OWN, WIDTH), BF16),
    ("far_dy", (OWN, WIDTH), BF16),
    ("h1_own", (OWN, WIDTH), BF16),
    ("h2_own", (OWN, WIDTH), BF16),
    ("held_qkv", (3, 128, 1024), BF16),
    ("held_gu", (128, 2, 2816), BF16),
    ("turned", (2816, 128), F32),
    ("cut_qkv", (4, 192, 128), BF16),
    ("cut_gate", (4, 176, 128), BF16),
    ("cut_up", (4, 176, 128), BF16),
    ("p_qkv", (192, 512), BF16),
    ("p_out", (64, 512), BF16),
    ("p_down", (176, 512), BF16),
    ("p_gate", (176, 512), BF16),
    ("p_up", (176, 512), BF16),
    ("bias", (4, 192, 1), F32),
    ("out", (HEAD, SEQ), BF16),
    ("o_rows", (ROWS, 4 * HEAD), BF16),
    ("product", (ROWS, WIDTH), BF16),
]


class Refs:
    pass


def column_of(row):
    blocks = jnp.concatenate([row[:, k * 128 : (k + 1) * 128] for k in range(16)], axis=0).T
    return jnp.concatenate([blocks[:, k : k + 1] for k in range(16)], axis=0)


def back_peer(dc, dh):
    return {
        "core": lax.rem(lax.axis_index("core") + dc, 2),
        "yh": lax.rem(lax.axis_index("yh") + dh, 2),
    }


LAYER_PEERS = XY_PEERS + Z_PEERS + [sibling, functools.partial(back_peer, 1, 1)]
LAYER_PEERS += [functools.partial(small_peer, dz, 1) for dz in (1, 2, 3)]
LAYER_PEERS += [functools.partial(group_peer, dz, 1) for dz in (1, 2, 3)]
PLACES = [
    ("m_gate", (4, 176, WIDTH), BF16, HBM),
    ("far_m_qkv", (4, 192, WIDTH), BF16, HBM),
    ("far_h1", (ROWS, WIDTH), BF16, HBM),
]
RESULTS = [
    ("layer_out", (2 * OWN, WIDTH), BF16, HBM),
    ("grad_tokens", (2 * OWN, WIDTH), BF16, HBM),
    ("gd_all", (16, 4, 352, 128), BF16, HBM),
    ("up_all", (16, 4, 176, 128), BF16, HBM),
    ("attn_all", (16, 4, 256, 128), BF16, HBM),
    ("norm_sum", (8, 512), F32, VMEM),
    ("grad_bias", (3, 16, 16), F32, VMEM),
]
SCRATCH += [
    ("up_attn", (4, 256, WIDTH), BF16),
    ("down", (4, 176, WIDTH), BF16),
    ("dy_all", (ROWS, WIDTH), BF16),
    ("product_mlp", (ROWS, WIDTH), BF16),
    ("gate", (704, ROWS), F32),
    ("act", (704, ROWS), BF16),
    ("d_gate", (704, ROWS), BF16),
    ("d_up", (704, ROWS), BF16),
    ("dz_own", (OWN, WIDTH), BF16),
    ("dz", (ROWS, WIDTH), BF16),
    ("d_middle", (OWN, WIDTH), F32),
    ("summed", (OWN, WIDTH), F32),
    ("out_own", (OWN, WIDTH), BF16),
    ("grad_own", (OWN, WIDTH), BF16),
    ("other_dh2", (4, OWN, WIDTH), BF16),
    ("arrived_dh2", (3, OWN, WIDTH), BF16),
    ("other_mlp", (4, OWN, WIDTH), BF16),
    ("arrived_mlp", (3, OWN, WIDTH), BF16),
    ("other_dh1", (4, OWN, WIDTH), BF16),
    ("arrived_dh1", (3, OWN, WIDTH), BF16),
    ("own_y", (128, WIDTH), BF16),
    ("own_x", (4, 128, 512), BF16),
    ("d_o", (4 * HEAD, ROWS), BF16),
    ("item_do", (HEAD, SEQ), BF16),
    ("item_out", (3 * HEAD, SEQ), BF16),
    ("d_kv", (SEQ, 2 * HEAD), F32),
    ("d_qkv", (12 * HEAD, ROWS), BF16),
    ("d_rows", (ROWS, 12 * HEAD), BF16),
    ("landing_gd", (4, 352, 128), BF16),
    ("landing_up", (4, 176, 128), BF16),
    ("landing_attn", (4, 256, 128), BF16),
    ("small_norms", (8, WIDTH), F32),
    ("small_bias", (8, 768), F32),
    ("bias_all", (8, 8, 768), F32),
    ("by_group", (8, 8, 512), F32),
    ("small_x", (4, 8, 1280), F32),
    ("small_y", (4, 8, 1280), F32),
]
for _name, _n in (("gate", 176), ("down", 176), ("up", 176), ("attn", 256)):
    _cut = first_part(_n)
    SCRATCH += [
        ("sum_y_" + _name, (_cut, WIDTH), BF16),
        ("sum_x_" + _name, (4, _n - _cut, 512), BF16),
        ("rest_x_" + _name, (3, _cut, 512), BF16),
        ("rest_y_" + _name, (3, _n - _cut, 512), BF16),
        ("rest_own_" + _name, (_n, 512), BF16),
        ("rest_total_" + _name, (_n, 512), BF16),
    ]
for _name, _cut, _rest in (("a", 96, 80), ("b", 128, 128)):
    SCRATCH += [
        ("by_y_" + _name, (2, _cut, WIDTH), BF16),
        ("by_x_" + _name, (2, 4, _rest, 512), BF16),
        ("relay_y_" + _name, (_cut, WIDTH), BF16),
        ("relay_x_" + _name, (4, _rest, 512), BF16),
    ]


LAYER_INPUTS = ["tokens", "cotangent", "gains", "shifts", "biases", "segments"]
LAYER_INPUTS += ["w_qkv", "w_out", "w_down", "w_gate_up", "cos", "sin"]


def layer_kernel(*refs):
    r = Refs()
    names = LAYER_INPUTS + [o[0] for o in PLACES + RESULTS] + [o[0] for o in SCRATCH]
    for name, ref in zip(names, refs):
        setattr(r, name, ref)
    r.gate_qkv, r.normed, r.qkv_t, r.item = r.m_qkv, r.h1, r.d_qkv, r.item_out
    r.other, r.arrived = r.other_dh2, r.arrived_dh2
    m_gate, m_up = r.gate_qkv.at[:, pl.ds(0, 176)], r.up_attn.at[:, pl.ds(0, 176)]
    engine = Engine(*refs[len(names) :])
    z, x, yl, core, yh = place()
    y = yh * 2 + yl

    load_qkv = engine.local(r.w_qkv.at[:, rows_at(x, 128)], r.held_qkv)
    load_gu = engine.local(r.w_gate_up.at[rows_at(x, 128)], r.held_gu)
    load_x = engine.local(r.tokens.at[rows_at(core, OWN)], r.near_x)
    load_dy = engine.local(r.cotangent.at[rows_at(core, OWN)], r.near_dy)
    marks = r.segments[...].astype(F32)
    rows = [r.gains[...].astype(F32), r.shifts[...].astype(F32)]
    rows += [marks[:, k * 512 : (k + 1) * 512] for k in range(4)] + [jnp.zeros((8, 512), F32)]
    r.packed[:, :512] = jnp.concatenate(rows, axis=0).astype(BF16)
    unit = (
        lax.broadcasted_iota(jnp.int32, (16, 16), 0) == lax.broadcasted_iota(jnp.int32, (16, 16), 1)
    ).astype(BF16)
    columns = [dot(r.biases[part], unit, (0, 0)) for part in range(3)] + [jnp.zeros((16, 80), F32)]
    r.packed[:, 512:] = jnp.concatenate(columns, axis=1).astype(BF16)
    small_here = engine.local(r.packed, r.small.at[z, yh])

    def rows_of(n):
        return lambda zz: rows_at((zz * 2 + core) * 2 + yl, n)

    def slots_of(piece):
        return lambda zz: piece.at[:, lanes(zz)]

    load_qkv.wait()
    for part in range(3):
        r.turned[:1024, :] = r.held_qkv[part].astype(F32).T
        for zz in range(4):
            r.cut_qkv[zz, part * HEAD : (part + 1) * HEAD] = r.turned[rows_of(HEAD)(zz), :].astype(BF16)
    greet(LAYER_PEERS)
    pieces_qkv = send_pieces(engine, lambda zz: r.cut_qkv.at[zz], slots_of(r.p_qkv))
    swap_x = engine.send(r.tokens.at[rows_at(1 - core, OWN)], r.far_x, sibling())
    smalls = [engine.send(r.packed, r.small.at[z, yh], small_peer(dz, dh)) for dz, dh in SMALL_ALL]
    pieces_out = send_pieces(engine, lambda zz: r.w_out.at[rows_of(64)(zz), lanes(x)], slots_of(r.p_out))
    swap_dy = engine.send(r.cotangent.at[rows_at(1 - core, OWN)], r.far_dy, sibling())
    load_gu.wait()
    for g, cut in ((0, r.cut_gate), (1, r.cut_up)):
        r.turned[...] = r.held_gu[:, g, :].astype(F32).T
        for zz in range(4):
            cut[zz] = r.turned[rows_of(176)(zz), :].astype(BF16)

    stays = core == yh
    load_x.wait()
    swap_x.wait_recv()
    x_rows = spread(jnp.where(stays, r.near_x[...].astype(F32), r.far_x[...].astype(F32)))
    r.x_own[...] = x_rows.astype(BF16)
    small_here.wait()
    for copy in smalls:
        copy.wait_recv()
    parts = [r.small[zz, 0].astype(F32) for zz in range(4)]
    r.norms[...] = jnp.concatenate(
        [parts[zz][:8, xx * 128 : (xx + 1) * 128] for xx in range(4) for zz in range(4)], axis=1
    )
    h1_full, _, _ = layer_norm(x_rows, r.norms[0:1], r.norms[2:3])
    r.h1_own[...] = h1_full.astype(BF16)
    tokens_h1 = gather_tokens(engine, r.h1_own, r.h1)
    next(tokens_h1)

    for copy in pieces_qkv[1:]:
        copy.wait_recv()
    pieces_qkv[0].wait()
    weight_qkv = gather_weight(engine, r.p_qkv, r.m_qkv)
    next(weight_qkv)

    lane_at = lax.broadcasted_iota(jnp.int32, (64, 128), 1)
    for h in range(2):
        table = jnp.concatenate([r.small[zz, h, :, 512:].astype(F32) for zz in range(4)], axis=0)
        for j in range(2):
            for part in range(3):
                picked = jnp.where(lane_at == part * 16 + (z * 2 + core) * 2 + j, table, 0.0)
                r.bias[h * 2 + j, part * HEAD : (part + 1) * HEAD] = jnp.sum(picked, axis=1, keepdims=True)
    marks = r.small[x, 0, :, :512].astype(F32)
    r.seg_row[...] = jnp.concatenate([marks[4 + i : 5 + i] for i in range(4)], axis=1)
    r.seg_col[...] = column_of(r.seg_row[...])

    next(weight_qkv)
    next(tokens_h1)
    pieces_down = send_pieces(engine, lambda zz: r.w_down.at[rows_of(176)(zz), lanes(x)], slots_of(r.p_down))
    pieces_gate = send_pieces(engine, lambda zz: r.cut_gate.at[zz], slots_of(r.p_gate))
    pieces_up = send_pieces(engine, lambda zz: r.cut_up.at[zz], slots_of(r.p_up))
    next(weight_qkv)

    def start_weight(pieces, piece, matrix):
        pieces[0].wait()
        for copy in pieces[1:]:
            copy.wait_recv()
        thread = gather_weight(engine, piece, matrix)
        next(thread)
        return thread

    load_dy.wait()
    swap_dy.wait_recv()
    dy_rows = jnp.where(stays, r.near_dy[...].astype(F32), r.far_dy[...].astype(F32))
    r.dy_own[...] = spread(dy_rows).astype(BF16)
    finish(tokens_h1)
    finish(weight_qkv)

    r.qkv_t[...] = (
        dot(r.m_qkv[...].reshape(12 * HEAD, WIDTH), r.h1[...], (1, 1)) + r.bias[...].reshape(12 * HEAD, 1)
    ).astype(BF16)
    to_items = send_items(engine, r.qkv_t, r.item, 3 * HEAD)
    tokens_dy = gather_tokens(engine, r.dy_own, r.dy_all)
    weight_out = start_weight(pieces_out, r.p_out, r.m_out)
    next(tokens_dy)
    weight_down = start_weight(pieces_down, r.p_down, r.down)
    to_items.wait_recv()
    next(weight_out)
    weight_gate = start_weight(pieces_gate, r.p_gate, r.m_gate)
    stores = [engine.local(r.m_qkv, r.far_m_qkv), engine.local(r.h1, r.far_h1)]
    attend(r.item, r.seg_row, r.seg_col, r.cos, r.sin, r.out, r.wide, r.lse, r.kept)
    next(weight_out)
    back = return_items(engine, r.out, r.o_t, HEAD)
    next(weight_down)
    weight_up = start_weight(pieces_up, r.p_up, m_up)
    next(tokens_dy)
    finish(weight_out)
    back.wait_recv()

    for copy in stores:
        copy.wait()

    r.o_rows[...] = r.o_t[...].astype(F32).T.astype(BF16)
    matrix = r.m_out[...].reshape(4 * HEAD, WIDTH)
    by_columns(r.product, lambda columns: dot(r.o_rows[...], matrix[:, columns], (1, 0)))
    out = scatter_tokens(engine, r.product, r.middle, r.other, r.arrived)
    next(out)
    next(out)
    next(weight_gate)
    next(weight_up)
    next(weight_down)
    next(weight_gate)
    next(out)
    r.middle[...] += x_rows

    h2_full, _, _ = layer_norm(r.middle[...], r.norms[1:2], r.norms[3:4])
    r.h2_own[...] = h2_full.astype(BF16)
    tokens_h2 = gather_tokens(engine, r.h2_own, r.normed)
    next(tokens_h2)
    next(weight_up)

    halves = [(slice(2 * k, 2 * k + 2), slice(352 * k, 352 * k + 352)) for k in range(2)]
    finish(tokens_dy)
    finish(weight_down)
    for two, rows in halves:
        d_act = dot(r.down[two].reshape(352, WIDTH), r.dy_all[...], (1, 1))
        for k in range(4):
            r.turned[704 * k + rows.start : 704 * k + rows.stop] = d_act[:, k * 128 : (k + 1) * 128]
    next(tokens_h2)
    finish(weight_gate)
    load_gate = engine.local(r.m_gate, m_gate)
    finish(tokens_h2)
    load_gate.wait()
    for two, rows in halves:
        r.gate[rows] = dot(r.gate_qkv[two, :176].reshape(352, WIDTH), r.normed[...], (1, 1))
    finish(out)
    sent = smalls + [to_items, back, swap_x, swap_dy]
    for pieces in (pieces_qkv, pieces_out, pieces_gate, pieces_down, pieces_up):
        sent += pieces[1:]
    for copy in sent:
        copy.wait_send()
    finish(weight_up)
    for two, rows in halves:
        up = dot(r.up_attn[two, :176].reshape(352, WIDTH), r.normed[...], (1, 1))
        gate = r.gate[rows]
        d_act = [r.turned[704 * k + rows.start : 704 * k + rows.stop] for k in range(4)]
        d_act = jnp.concatenate(d_act, axis=1)
        sigmoid = jax.nn.sigmoid(gate)
        silu = gate * sigmoid
        r.act[rows] = (silu * up).astype(BF16)
        r.d_gate[rows] = (d_act * up * sigmoid * (1.0 + gate * (1.0 - sigmoid))).astype(BF16)
        r.d_up[rows] = (d_act * silu).astype(BF16)

    def first_of(name, grad, places):
        cut, rest = getattr(r, "sum_y_" + name).shape[0], getattr(r, "sum_x_" + name).shape[1]
        head, tail = pl.ds(0, cut), pl.ds(0, rest)
        thread = sum_first(
            engine,
            grad,
            getattr(r, "sum_y_" + name),
            getattr(r, "sum_x_" + name),
            getattr(r, "by_y_" + places).at[:, head],
            getattr(r, "by_x_" + places).at[:, :, tail],
            getattr(r, "relay_y_" + places).at[head],
            getattr(r, "relay_x_" + places).at[:, tail],
            r.own_y,
            r.own_x,
        )
        next(thread)
        return thread

    def rest_of(name, landing):
        parts = [getattr(r, part + name) for part in ("rest_x_", "rest_y_", "rest_own_", "rest_total_")]
        thread = sum_rest(engine, getattr(r, "sum_y_" + name), getattr(r, "sum_x_" + name), landing, *parts)
        next(thread)
        return thread

    def part_of(landing, first):
        return lambda zz: landing.at[zz, pl.ds(first, 176)]

    def turned(ref):
        return ref[...].astype(F32).T.astype(BF16)

    def columns_of(ref, columns):
        return ref[:, :176, columns].reshape(704, 512)

    gate_rows, up_rows = turned(r.d_gate), turned(r.d_up)
    by_columns(
        r.product,
        lambda columns: dot(gate_rows, columns_of(r.gate_qkv, columns), (1, 0))
        + dot(up_rows, columns_of(r.up_attn, columns), (1, 0)),
    )
    dh2 = scatter_tokens(engine, r.product, r.summed, r.other_dh2, r.arrived_dh2)
    next(dh2)
    by_columns(m_gate, lambda columns: dot(r.d_gate[...], r.normed[:, columns], (1, 0)))
    gate = first_of("gate", m_gate, "a")
    next(dh2)
    act_rows = turned(r.act)
    by_columns(r.product_mlp, lambda columns: dot(act_rows, columns_of(r.down, columns), (1, 0)))
    by_columns(r.down, lambda columns: dot(r.act[...], r.dy_all[:, columns], (1, 0)))
    down = first_of("down", r.down, "b")
    by_columns(m_up, lambda columns: dot(r.d_up[...], r.normed[:, columns], (1, 0)))
    load_h1 = engine.local(r.far_h1, r.normed)
    mlp = scatter_tokens(engine, r.product_mlp, r.d_middle, r.other_mlp, r.arrived_mlp)
    next(mlp)
    _, normed_b, rstd_b = layer_norm(r.middle[...], r.norms[1:2], r.norms[3:4])
    next(gate)
    next(down)
    next(dh2)
    back_b, gain_b, shift_b = norm_back(r.summed[...], normed_b, rstd_b, r.norms[1:2])
    d_middle = r.dy_own[...].astype(F32) + back_b
    r.dz_own[...] = d_middle.astype(BF16)
    tokens_dz = gather_tokens(engine, r.dz_own, r.dz)
    next(tokens_dz)
    r.small_norms[1:2] = gain_b[None]
    r.small_norms[3:4] = shift_b[None]
    next(gate)
    rest_gate = rest_of("gate", part_of(r.landing_gd, 0))
    next(down)
    rest_down = rest_of("down", part_of(r.landing_gd, 176))
    next(tokens_dz)
    finish(tokens_dz)

    r.d_o[...] = dot(r.m_out[...].reshape(4 * HEAD, WIDTH), r.dz[...], (1, 1)).astype(BF16)
    to_items = send_items(engine, r.d_o, r.item_do, HEAD)
    next(rest_gate)
    up = first_of("up", m_up, "a")
    next(rest_down)
    next(mlp)
    finish(gate)
    load_qkv = engine.local(r.far_m_qkv, r.gate_qkv)
    to_items.wait_recv()
    next(rest_gate)
    next(rest_down)
    gather_gd = gather_ctx(engine, r.landing_gd, r.gd_all)
    next(gather_gd)
    finish(down)
    finish(rest_gate)
    finish(rest_down)
    attend_back(
        r.kept, r.item_do, r.wide, r.lse, r.seg_row, r.seg_col, r.cos, r.sin, r.item_out, r.d_kv
    )
    back = return_items(engine, r.item_out, r.d_qkv, 3 * HEAD)
    to_items.wait_send()
    next(up)
    next(gather_gd)
    next(mlp)
    r.out_own[...] = spread(r.middle[...] + r.d_middle[...]).astype(BF16)
    r.d_middle[...] = d_middle
    hand_out = hand_back(engine, r.out_own, r.layer_out)
    next(hand_out)
    load_h1.wait()
    load_qkv.wait()
    back.wait_recv()
    finish(mlp)

    r.d_rows[...] = r.d_qkv[...].astype(F32).T.astype(BF16)
    matrix = r.gate_qkv[...].reshape(12 * HEAD, WIDTH)
    finish(dh2)
    by_columns(r.product, lambda columns: dot(r.d_rows[...], matrix[:, columns], (1, 0)))
    dh1 = scatter_tokens(engine, r.product, r.summed, r.other_dh1, r.arrived_dh1)
    next(dh1)
    next(up)
    rest_up = rest_of("up", part_of(r.landing_up, 0))
    finish(up)
    by_columns(
        r.up_attn.at[:, pl.ds(0, 192)], lambda columns: dot(r.d_qkv[...], r.normed[:, columns], (1, 0))
    )
    by_columns(r.up_attn.at[:, pl.ds(192, 64)], lambda columns: dot(r.o_t[...], r.dz[:, columns], (1, 0)))
    attn = first_of("attn", r.up_attn, "b")
    next(dh1)
    r.small_bias[...] = dot(jnp.ones((8, ROWS), BF16), r.d_qkv[...], (1, 1))
    _, normed_a, rstd_a = layer_norm(r.x_own[...].astype(F32), r.norms[0:1], r.norms[2:3])
    next(rest_up)
    next(attn)
    next(gather_gd)
    next(rest_up)
    finish(rest_up)
    gather_up = gather_ctx(engine, r.landing_up, r.up_all)
    next(gather_up)
    next(dh1)
    back_a, gain_a, shift_a = norm_back(r.summed[...], normed_a, rstd_a, r.norms[0:1])
    r.grad_own[...] = spread(r.d_middle[...] + back_a).astype(BF16)
    r.small_norms[0:1] = gain_a[None]
    r.small_norms[2:3] = shift_a[None]
    r.small_norms[4:] = jnp.zeros((4, WIDTH), F32)
    r.small_norms[...] = spread(r.small_norms[...])
    small = sum_small(
        engine, r.small_norms, r.small_bias, r.norm_sum, r.bias_all, r.by_group, r.small_x, r.small_y
    )
    next(small)
    next(attn)
    rest_attn = rest_of("attn", lambda zz: r.landing_attn.at[zz])
    next(small)
    next(gather_gd)
    next(gather_up)
    hand_grad = hand_back(engine, r.grad_own, r.grad_tokens)
    next(hand_grad)
    next(rest_attn)
    next(small)
    next(gather_up)
    next(small)
    next(rest_attn)
    gather_attn = gather_ctx(engine, r.landing_attn, r.attn_all)
    next(gather_attn)
    next(gather_up)
    next(gather_attn)
    finish(small)
    table = jnp.concatenate([r.bias_all[k, 0:1] for k in range(8)], axis=0)
    from_at = lax.broadcasted_iota(jnp.int32, (768, 16), 0)
    to_at = lax.broadcasted_iota(jnp.int32, (768, 16), 1)
    row_at = lax.broadcasted_iota(jnp.int32, (16, 8), 0)
    group_at = lax.broadcasted_iota(jnp.int32, (16, 8), 1)
    for part in range(3):
        total = jnp.zeros((16, 16), F32)
        for j in range(2):
            chosen = (from_at == to_at + ((yh * 2 + j) * 3 + part) * HEAD + z * 16).astype(F32)
            spread_rows = (row_at == group_at * 2 + j).astype(F32)
            total += exact_dot(spread_rows, exact_dot(table, chosen))
        r.grad_bias[part] = total
    next(gather_attn)
    finish(gather_gd)
    finish(gather_up)
    next(gather_attn)
    threads = (dh2, mlp, gate, down, up, attn, rest_gate, rest_down, rest_up, rest_attn)
    for thread in threads + (hand_out, dh1, hand_grad, small, gather_gd, gather_up, gather_attn):
        finish(thread)
    back.wait_send()


def layer(*inputs):
    outs = PLACES + RESULTS
    values = pl.pallas_call(
        layer_kernel,
        out_shape=[jax.ShapeDtypeStruct(o[1], o[2]) for o in outs],
        in_specs=[HBM] * 2 + [VMEM] * 4 + [HBM] * 4 + [VMEM] * 2,
        out_specs=[o[3] for o in outs],
        scratch_shapes=[pltpu.VMEM(shape, dtype) for _, shape, dtype in SCRATCH] + semaphores(100, 316, 20),
        compiler_params=pltpu.CompilerParams(
            collective_id=1, has_side_effects=True, vmem_limit_bytes=VMEM_BYTES
        ),
        name="layer",
    )(*inputs)
    return values[len(PLACES) :]


def assemble_kernel(
    gd_ref,
    up_ref,
    attn_ref,
    layer_ref,
    tokens_ref,
    norms_ref,
    gu_ref,
    down_ref,
    qkv_ref,
    out_ref,
    layer_out_ref,
    tokens_out_ref,
    gains_ref,
    shifts_ref,
    turned,
):
    layer_out_ref[...] = layer_ref[...]
    tokens_out_ref[...] = tokens_ref[...].astype(F32)
    gains_ref[...] = norms_ref[0:2]
    shifts_ref[...] = norms_ref[2:4]
    for g in range(2):
        for zz in range(2):
            for core in range(2):
                for yl in range(2):
                    row = zz * 704 + core * 352 + yl * 176
                    block = (up_ref[0, yl * 2 + core, zz] if g else gd_ref[0, yl * 2 + core, zz, :176]).astype(F32)
                    turned[row : row + 176, :] = block
        for t in range(11):
            gu_ref[:, g, t * 128 : (t + 1) * 128] = turned[t * 128 : (t + 1) * 128, :].T
    for zz in range(2):
        for core in range(2):
            for yl in range(2):
                row = zz * 704 + core * 352 + yl * 176
                down_ref[row : row + 176, :] = gd_ref[0, yl * 2 + core, zz, 176:].astype(F32)
                row = zz * 256 + core * 128 + yl * 64
                out_ref[row : row + 64, :] = attn_ref[0, yl * 2 + core, zz, 192:].astype(F32)
            for part in range(3):
                rows = slice(part * 64, (part + 1) * 64)
                block = jnp.concatenate([attn_ref[0, core, zz, rows], attn_ref[0, 2 + core, zz, rows]], axis=0)
                column = zz * 256 + core * 128
                qkv_ref[part, :, column : column + 128] = block.astype(F32).T


def assemble(gd_all, up_all, attn_all, layer_out, grad_tokens, norm_sum):
    gd_all = gd_all.reshape(4, 4, 4, 352, 128)
    up_all = up_all.reshape(4, 4, 4, 176, 128)
    attn_all = attn_all.reshape(4, 4, 4, 256, 128)
    return pl.pallas_call(
        assemble_kernel,
        grid=(4, 2),
        in_specs=[
            pl.BlockSpec((1, 4, 2, 352, 128), lambda i, j: (i, 0, j, 0, 0)),
            pl.BlockSpec((1, 4, 2, 176, 128), lambda i, j: (i, 0, j, 0, 0)),
            pl.BlockSpec((1, 4, 2, 256, 128), lambda i, j: (i, 0, j, 0, 0)),
            pl.BlockSpec((16, WIDTH), lambda i, j: (i * 2 + j, 0)),
            pl.BlockSpec((16, WIDTH), lambda i, j: (i * 2 + j, 0)),
            pl.BlockSpec((8, 512), lambda i, j: (0, 0)),
        ],
        out_specs=[
            pl.BlockSpec((128, 2, 1408), lambda i, j: (i, 0, j)),
            pl.BlockSpec((1408, 128), lambda i, j: (j, i)),
            pl.BlockSpec((3, 128, 512), lambda i, j: (0, i, j)),
            pl.BlockSpec((512, 128), lambda i, j: (j, i)),
            pl.BlockSpec((16, WIDTH), lambda i, j: (i * 2 + j, 0)),
            pl.BlockSpec((16, WIDTH), lambda i, j: (i * 2 + j, 0)),
            pl.BlockSpec((2, 512), lambda i, j: (0, 0)),
            pl.BlockSpec((2, 512), lambda i, j: (0, 0)),
        ],
        out_shape=[
            jax.ShapeDtypeStruct((512, 2, 2816), F32),
            jax.ShapeDtypeStruct((2816, 512), F32),
            jax.ShapeDtypeStruct((3, 512, 1024), F32),
            jax.ShapeDtypeStruct((1024, 512), F32),
            jax.ShapeDtypeStruct((2 * OWN, WIDTH), BF16),
            jax.ShapeDtypeStruct((2 * OWN, WIDTH), F32),
            jax.ShapeDtypeStruct((2, 512), F32),
            jax.ShapeDtypeStruct((2, 512), F32),
        ],
        scratch_shapes=[pltpu.VMEM((1408, 128), F32)],
        compiler_params=pltpu.CompilerParams(vmem_limit_bytes=VMEM_BYTES),
        name="assemble",
    )(gd_all, up_all, attn_all, layer_out, grad_tokens, norm_sum)


def rotation_tables():
    half = ROT // 2
    positions = np.arange(SEQ, dtype=np.float32)
    inverse = (10000.0 ** (-(np.arange(half) * 2.0 / ROT))).astype(np.float32)
    angles = (inverse[:, None] * positions[None, :]).astype(np.float64)
    return jnp.asarray(np.cos(angles).astype(np.float32)), jnp.asarray(np.sin(angles).astype(np.float32))


def layer_norm(values, gain_row, shift_row):
    row_mean = jnp.mean(values, axis=-1, keepdims=True)
    centred = values - row_mean
    variance = jnp.mean(centred * centred, axis=-1, keepdims=True)
    rstd = lax.rsqrt(variance + EPS)
    normed = centred * rstd
    return normed * gain_row + shift_row, normed, rstd


def norm_back(gradient, normed, rstd, gain_row):
    shaped = gradient * gain_row
    centre = (
        shaped
        - jnp.mean(shaped, axis=-1, keepdims=True)
        - normed * jnp.mean(shaped * normed, axis=-1, keepdims=True)
    )
    return centre * rstd, jnp.sum(gradient * normed, axis=0), jnp.sum(gradient, axis=0)


def local(tokens, segments, w_qkv, b_qkv, w_out, w_gate_up, w_down, norm_gains, norm_shifts, cotangent):
    cosine, sine = rotation_tables()
    layer_out, grad_tokens, gd_all, up_all, attn_all, norm_sum, grad_bias = layer(
        tokens[0],
        cotangent[0],
        norm_gains,
        norm_shifts,
        b_qkv,
        segments,
        w_qkv.transpose(1, 0, 2),
        w_out,
        w_down,
        w_gate_up,
        cosine,
        sine,
    )
    out_gu, out_down, out_qkv, out_out, layer_out, grad_tokens, gains, shifts = assemble(
        gd_all, up_all, attn_all, layer_out, grad_tokens, norm_sum
    )
    return (
        layer_out[None],
        grad_tokens[None],
        out_qkv.transpose(1, 0, 2),
        grad_bias,
        out_out,
        out_gu,
        out_down,
        gains,
        shifts,
    )


def solution(mesh):
    fine = Mesh(mesh.devices.reshape(4, 4, 2, 2, 2), ("z", "x", "yl", "core", "yh"))
    ctx = ("x", "yl", "core")
    return jax.shard_map(
        local,
        mesh=fine,
        in_specs=(
            P("z", ctx, None),
            P("z", None),
            P("z", None, "yh"),
            P(None, "yh", "z"),
            P("yh", "z"),
            P("z", None, "yh"),
            P("yh", "z"),
            P(None, "z"),
            P(None, "z"),
            P("z", ctx, None),
        ),
        out_specs=(
            P("z", ctx, None),
            P("z", ctx, None),
            P("z", None, "yh"),
            P(None, "yh", "z"),
            P("yh", "z"),
            P("z", None, "yh"),
            P("yh", "z"),
            P(None, "z"),
            P(None, "z"),
        ),
        check_vma=False,
    )
```

```python
import functools

import jax
import jax.numpy as jnp
import numpy as np
from jax import lax
from jax.experimental import pallas as pl
from jax.experimental.pallas import tpu as pltpu
from jax.sharding import Mesh
from jax.sharding import PartitionSpec as P

EPS = 1e-05
NEG = -1e30
ROT = 16
HEAD = 64
SEQ = 2048
WIDTH = 2048
OWN = 64
ROWS = 512
QB = 256
VMEM_BYTES = 63 * 2**20
F32 = jnp.float32
BF16 = jnp.bfloat16
MESH_ID = pl.DeviceIdType.MESH
HBM = pl.BlockSpec(memory_space=pltpu.HBM)
VMEM = pl.BlockSpec(memory_space=pltpu.VMEM)


def place():
    return tuple(lax.axis_index(a) for a in ("z", "x", "yl", "core", "yh"))


def lanes(index, size=128):
    return pl.ds(pl.multiple_of(index * size, size), size)


def rows_at(index, size):
    return pl.ds(pl.multiple_of(index * size, size), size)


def z_peer(d):
    z = lax.axis_index("z")
    return {"z": lax.rem(z + d, 4)}


def x_peer(d):
    x = lax.axis_index("x")
    return {"x": lax.rem(x + d, 4)}


def y_peer(d):
    y = lax.rem(lax.axis_index("yh") * 2 + lax.axis_index("yl") + d, 4)
    return {"yh": y // 2, "yl": lax.rem(y, 2)}


def xy_peer(dx, dy):
    return {**x_peer(dx), **y_peer(dy)}


def sibling():
    return {"core": 1 - lax.axis_index("core")}


Z_PEERS = [functools.partial(z_peer, d) for d in (1, 2, 3)]
X_PEERS = [functools.partial(x_peer, d) for d in (1, 2, 3)]
Y_PEERS = [functools.partial(y_peer, d) for d in (1, 2, 3)]
XY_ALL = [(dx, dy) for dx in range(4) for dy in range(4) if dx or dy]
XY_PEERS = [functools.partial(xy_peer, dx, dy) for dx, dy in XY_ALL]


class Remote:
    def __init__(self, engine, index, copy):
        self.engine, self.index, self.copy = engine, index, copy

    def wait_recv(self):
        self.copy.wait_recv()

    def wait_send(self):
        self.copy.wait_send()
        self.engine.free_send.append(self.index)

    def wait(self):
        self.wait_recv()
        self.wait_send()


class Local:
    def __init__(self, engine, index, copy):
        self.engine, self.index, self.copy = engine, index, copy

    def wait(self):
        self.copy.wait()
        self.engine.free_local.append(self.index)


class Group:
    def __init__(self, engine, view, device):
        self.engine, self.view, self.device = engine, view, device
        self.index, self.place = engine.free_send.pop(), engine.free_recv.pop()

    def copy(self, src, dst, device):
        return pltpu.make_async_remote_copy(
            src,
            dst,
            self.engine.send_sem.at[self.index],
            self.engine.recv_sem.at[self.place],
            device_id=device,
            device_id_type=MESH_ID,
        )

    def send(self, src, dst, device):
        self.copy(src, dst, device).start()

    def wait_recv(self):
        self.copy(self.view, self.view, self.device).wait_recv()

    def wait_send(self):
        self.copy(self.view, self.view, self.device).wait_send()
        self.engine.free_send.append(self.index)


class Engine:
    def __init__(self, send_sem, recv_sem, local_sem):
        self.send_sem, self.recv_sem, self.local_sem = send_sem, recv_sem, local_sem
        self.free_send = list(range(send_sem.shape[0]))[::-1]
        self.free_recv = list(range(recv_sem.shape[0]))[::-1]
        self.free_local = list(range(local_sem.shape[0]))[::-1]

    def send(self, src, dst, device):
        i, k = self.free_send.pop(), self.free_recv.pop()
        copy = pltpu.make_async_remote_copy(
            src, dst, self.send_sem.at[i], self.recv_sem.at[k], device_id=device, device_id_type=MESH_ID
        )
        copy.start()
        return Remote(self, i, copy)

    def local(self, src, dst):
        i = self.free_local.pop()
        copy = pltpu.make_async_copy(src, dst, self.local_sem.at[i])
        copy.start()
        return Local(self, i, copy)


def greet(peers):
    barrier = pltpu.get_barrier_semaphore()
    for peer in peers:
        pl.semaphore_signal(barrier, 1, device_id=peer(), device_id_type=MESH_ID)
    pl.semaphore_wait(barrier, len(peers))


def semaphores(n_send, n_recv, n_local):
    return [pltpu.SemaphoreType.DMA((n,)) for n in (n_send, n_recv, n_local)]


def spread(values):
    return jnp.concatenate(
        [values[:, (a * 4 + b) * 128 : (a * 4 + b + 1) * 128] for b in range(4) for a in range(4)], axis=1
    )


def finish(thread):
    for _ in thread:
        pass


def send_pieces(engine, pieces, slots):
    z = lax.axis_index("z")
    copies = [engine.local(pieces(z), slots(z))]
    for d in (1, 2, 3):
        to = z_peer(d)
        copies.append(engine.send(pieces(to["z"]), slots(z), to))
    return copies


def gather_tokens(engine, src, dst):
    z, core = lax.axis_index("z"), lax.axis_index("core")
    mine = dst.at[rows_at(z * 2 + core, OWN)]
    first = [engine.send(src, mine, z_peer(d)) for d in (1, 2, 3)]
    rest = [engine.send(src, mine, sibling()), engine.local(src, mine)]
    yield
    for d in (1, 2, 3):
        first[d - 1].wait_recv()
        here = dst.at[rows_at(lax.rem(z + 4 - d, 4) * 2 + core, OWN)]
        rest.append(engine.send(here, here, sibling()))
    yield
    for copy in first:
        copy.wait_send()
    for copy in rest:
        copy.wait()


def gather_weight(engine, src, dst):
    n = src.shape[0]
    top = first_part(n)
    head, tail = pl.ds(0, top), pl.ds(top, n - top)
    x = lax.axis_index("x")
    y = lax.axis_index("yh") * 2 + lax.axis_index("yl")
    left_y, left_x = lax.rem(y + 3, 4), lax.rem(x + 3, 4)
    right_y, right_x = lax.rem(y + 1, 4), lax.rem(x + 1, 4)
    mine = lanes(x, 512)
    local = engine.local(src, dst.at[y, :, mine])
    along_x = [engine.send(src.at[head], dst.at[y, head, mine], x_peer(d)) for d in (1, 2, 3)]
    along_y = [engine.send(src.at[tail], dst.at[y, tail, mine], y_peer(d)) for d in (1, 2, 3)]
    yield
    local.wait()
    for copy in along_x:
        copy.wait_recv()
    ring_y = [engine.send(dst.at[y, head], dst.at[y, head], y_peer(d)) for d in (1, 3)]
    for copy in along_y:
        copy.wait_recv()
    ring_x = [engine.send(dst.at[:, tail, mine], dst.at[:, tail, mine], x_peer(d)) for d in (1, 3)]
    yield
    rest = []
    half = first_part(top)
    early, late = pl.ds(0, half), pl.ds(half, top - half)
    ring_y[0].wait_recv()
    rest.append(engine.send(dst.at[left_y, early], dst.at[left_y, early], y_peer(1)))
    ring_y[1].wait_recv()
    rest.append(engine.send(dst.at[right_y, late], dst.at[right_y, late], y_peer(3)))
    ring_x[0].wait_recv()
    block = dst.at[:, tail, lanes(left_x * 2, 256)]
    rest.append(engine.send(block, block, x_peer(1)))
    ring_x[1].wait_recv()
    block = dst.at[:, tail, lanes(right_x * 2 + 1, 256)]
    rest.append(engine.send(block, block, x_peer(3)))
    yield
    for copy in along_x + along_y + ring_y + ring_x:
        copy.wait_send()
    for copy in rest:
        copy.wait()


def first_part(n):
    return (n // 2 + 15) // 16 * 16


class Items:
    def __init__(self, group, local):
        self.group, self.local = group, local

    def wait_recv(self):
        self.local.wait()
        self.group.wait_recv()

    def wait_send(self):
        self.group.wait_send()


def send_items(engine, src, dst, n):
    x, yl, yh = (lax.axis_index(a) for a in ("x", "yl", "yh"))
    y = yh * 2 + yl
    mine = dst.at[:, lanes(x * 4 + yl * 2 + yh)]
    group = Group(engine, dst.at[:, pl.ds(0, 15 * 128)], xy_peer(*XY_ALL[0]))
    for dx, dy in XY_ALL:
        tx, ty = lax.rem(x + dx, 4), lax.rem(y + dy, 4)
        group.send(src.at[rows_at(ty, n), lanes(tx)], mine, xy_peer(dx, dy))
    return Items(group, engine.local(src.at[rows_at(y, n), lanes(x)], mine))


def return_items(engine, src, dst, n):
    x, yl, yh = (lax.axis_index(a) for a in ("x", "yl", "yh"))
    mine = dst.at[rows_at(yh * 2 + yl, n), lanes(x)]
    group = Group(engine, dst.at[pl.ds(0, 15 * n // 4)], xy_peer(*XY_ALL[0]))
    for dx, dy in XY_ALL:
        to = xy_peer(dx, dy)
        group.send(src.at[:, lanes(to["x"] * 4 + to["yl"] * 2 + to["yh"])], mine, to)
    return Items(group, engine.local(src.at[:, lanes(x * 4 + yl * 2 + yh)], mine))


def add_up(total, terms, index, rows, width):
    def step(i, carry):
        here = (*index, rows_at(i, 16), slice(0, width))
        value = terms[0][here].astype(F32)
        for term in terms[1:]:
            value += term[here].astype(F32)
        total[here] = value.astype(total.dtype)
        return carry

    lax.fori_loop(0, rows // 16, step, 0)


def exact_dot(a, b):
    return jnp.dot(a, b, precision=lax.Precision.HIGHEST, preferred_element_type=F32)


def by_columns(dst, value_of):
    for k in range(4):
        columns = slice(k * 512, (k + 1) * 512)
        value = value_of(columns).astype(dst.dtype)
        dst[..., columns] = value.reshape(dst.shape[:-1] + (512,))


def scatter_tokens(engine, product, dst, other, arrived):
    z, core = lax.axis_index("z"), lax.axis_index("core")
    to_core = []
    for i in range(4):
        give = product.at[rows_at(lax.rem(z + 1 + i, 4) * 2 + 1 - core, OWN)]
        to_core.append(engine.send(give, other.at[i], sibling()))
    yield
    to_z = []
    for i in range(3):
        own = rows_at(lax.rem(z + 1 + i, 4) * 2 + core, OWN)
        to_core[i].wait_recv()
        product[own, :] = (product[own, :].astype(F32) + other[i].astype(F32)).astype(BF16)
        to_z.append(engine.send(product.at[own], arrived.at[i], z_peer(i + 1)))
    yield
    to_core[3].wait_recv()
    dst[...] = product[rows_at(z * 2 + core, OWN), :].astype(F32) + other[3].astype(F32)
    for i in range(3):
        to_z[i].wait_recv()
        dst[...] += arrived[i].astype(F32)
    yield
    for copy in to_core + to_z:
        copy.wait_send()


def sum_first(engine, src, sum_y, sum_x, by_y, by_x, relay_y, relay_x, own_y, own_x):
    n, cut = src.shape[1], sum_y.shape[0]
    rest, half = n - cut, first_part(cut)
    tail = pl.ds(cut, rest)
    early, late = pl.ds(0, half), pl.ds(half, cut - half)
    low, high = pl.ds(0, 2), pl.ds(2, 2)
    x = lax.axis_index("x")
    y = lax.axis_index("yh") * 2 + lax.axis_index("yl")
    up_y, down_y = lax.rem(y + 1, 4), lax.rem(y + 3, 4)
    up_x, down_x = lanes(lax.rem(x + 1, 4), 512), lanes(lax.rem(x + 3, 4), 512)
    far_y, far_x = lax.rem(y + 2, 4), lanes(lax.rem(x + 2, 4), 512)
    relays = [
        engine.send(src.at[far_y, early], relay_y.at[early], y_peer(1)),
        engine.send(src.at[low, tail, far_x], relay_x.at[low], x_peer(1)),
        engine.send(src.at[far_y, late], relay_y.at[late], y_peer(3)),
        engine.send(src.at[high, tail, far_x], relay_x.at[high], x_peer(3)),
    ]
    copies = [
        engine.send(src.at[up_y, late], by_y.at[0, late], y_peer(1)),
        engine.send(src.at[high, tail, up_x], by_x.at[0, high], x_peer(1)),
        engine.send(src.at[down_y, early], by_y.at[1, early], y_peer(3)),
        engine.send(src.at[low, tail, down_x], by_x.at[1, low], x_peer(3)),
    ]
    yield
    own_y, own_x = own_y.at[pl.ds(0, cut)], own_x.at[:, pl.ds(0, rest)]
    local = [
        engine.local(src.at[up_y, early], own_y.at[early]),
        engine.local(src.at[down_y, late], own_y.at[late]),
        engine.local(src.at[low, tail, up_x], own_x.at[low]),
        engine.local(src.at[high, tail, down_x], own_x.at[high]),
    ]
    for copy in local:
        copy.wait()
    passed = []
    relays[0].wait_recv()
    add_up(relay_y.at[early], [relay_y.at[early], own_y.at[early]], (), half, WIDTH)
    passed.append(engine.send(relay_y.at[early], by_y.at[0, early], y_peer(1)))
    relays[1].wait_recv()
    for q in range(2):
        add_up(relay_x, [relay_x, own_x], (q,), rest, 512)
    passed.append(engine.send(relay_x.at[low], by_x.at[0, low], x_peer(1)))
    relays[2].wait_recv()
    add_up(relay_y.at[late], [relay_y.at[late], own_y.at[late]], (), cut - half, WIDTH)
    passed.append(engine.send(relay_y.at[late], by_y.at[1, late], y_peer(3)))
    relays[3].wait_recv()
    for q in range(2, 4):
        add_up(relay_x, [relay_x, own_x], (q,), rest, 512)
    passed.append(engine.send(relay_x.at[high], by_x.at[1, high], x_peer(3)))
    yield
    local = [
        engine.local(src.at[y, pl.ds(0, cut)], own_y),
        engine.local(src.at[:, tail, lanes(x, 512)], own_x),
    ]
    for copy in local:
        copy.wait()
    for copy in copies + passed:
        copy.wait_recv()
    add_up(sum_y, [own_y, by_y.at[0], by_y.at[1]], (), cut, WIDTH)
    for q in range(4):
        add_up(sum_x, [own_x, by_x.at[0], by_x.at[1]], (q,), rest, 512)
    for copy in passed:
        copy.wait_send()
    yield
    for copy in relays + copies:
        copy.wait_send()


def sum_rest(engine, heads, tails, landing, by_x, by_y, own, total):
    cut, rest = heads.shape[0], tails.shape[1]
    x = lax.axis_index("x")
    y = lax.axis_index("yh") * 2 + lax.axis_index("yl")
    first, second = pl.ds(0, cut), pl.ds(cut, rest)
    copies = []
    for d in (2, 1, 3):
        ty, tx = y_peer(d), x_peer(d)
        copies.append(engine.send(heads.at[:, lanes(tx["x"], 512)], by_x.at[d - 1], tx))
        copies.append(engine.send(tails.at[ty["yh"] * 2 + ty["yl"]], by_y.at[d - 1], ty))
    local = [engine.local(tails.at[y], own.at[second]), engine.local(heads.at[:, lanes(x, 512)], own.at[first])]
    yield
    for copy in local:
        copy.wait()
    for copy in copies:
        copy.wait_recv()
    add_up(total.at[first], [own.at[first]] + [by_x.at[k] for k in range(3)], (), cut, 512)
    add_up(total.at[second], [own.at[second]] + [by_y.at[k] for k in range(3)], (), rest, 512)
    moved = send_pieces(engine, lambda z: total.at[:, lanes(z)], landing)
    yield
    moved[0].wait()
    for copy in moved[1:]:
        copy.wait_recv()
    yield
    for copy in copies + moved[1:]:
        copy.wait_send()


def gather_ctx(engine, landing, dst):
    x, yl, core = (lax.axis_index(a) for a in ("x", "yl", "core"))

    def slot(dx, ll):
        return (lax.rem(x + dx, 4) * 2 + ll) * 2 + core

    other, n = 1 - yl, landing.shape[1]
    half = first_part(n)
    first, second = (pl.ds(0, 3),), (pl.ds(3, 1),)
    even, even_other = ((pl.ds(0, 2),), (pl.ds(2, 1),)), ((pl.ds(0, 1),), (pl.ds(1, 2),))
    odd = ((pl.ds(3, 1), pl.ds(0, half)), (pl.ds(3, 1), pl.ds(half, n - half)))
    partner, there = {"yl": other}, sibling()
    sent = []

    def send(source, target, part, device):
        copy = engine.send(source, dst.at[(target, *part)], device)
        sent.append(copy)
        return copy

    siblings = Group(engine, dst.at[pl.ds(0, 8)], there)

    def hand(index, part):
        block = dst.at[(index, *part)]
        siblings.send(block, block, there)

    def on(index, part, device):
        return send(dst.at[(index, *part)], index, part, device)

    me = slot(0, yl)
    local = engine.local(landing, dst.at[me])
    siblings.send(landing, dst.at[me], there)
    to_y = send(landing.at[*first], me, first, partner)
    round_b = [send(landing.at[*second], me, second, x_peer(d)) for d in (1, 3)]
    round_a = [send(landing.at[*first], me, first, x_peer(d)) for d in (1, 3)]
    over = [send(landing.at[*second], me, second, partner)]
    yield
    to_y.wait_recv()
    round_c = [on(slot(0, other), first, x_peer(d)) for d in (1, 3)]
    hand(slot(0, other), first)
    onward = []
    for k, (d, to) in enumerate(((3, 1), (1, 3))):
        round_b[k].wait_recv()
        onward.append(on(slot(d, yl), odd[k], x_peer(to)))
        over.append(on(slot(d, yl), second, partner))
        hand(slot(d, yl), second)
    for k, (d, to) in enumerate(((3, 1), (1, 3))):
        round_a[k].wait_recv()
        onward.append(on(slot(d, yl), even[k], x_peer(to)))
        hand(slot(d, yl), first)
    yield
    for k in range(2):
        onward[k].wait_recv()
    over.append(on(slot(2, yl), second, partner))
    hand(slot(2, yl), second)
    for k, (d, to) in enumerate(((3, 1), (1, 3))):
        round_c[k].wait_recv()
        onward.append(on(slot(d, other), even_other[k], x_peer(to)))
        hand(slot(d, other), first)
    yield
    for k in (2, 3):
        onward[k].wait_recv()
    hand(slot(2, yl), first)
    for k, d in enumerate((0, 3, 1, 2)):
        over[k].wait_recv()
        hand(slot(d, other), second)
    for k in (4, 5):
        onward[k].wait_recv()
    hand(slot(2, other), first)
    yield
    local.wait()
    siblings.wait_recv()
    siblings.wait_send()
    for copy in sent:
        copy.wait_send()


def group_peer(dz, dc):
    return {
        "z": lax.rem(lax.axis_index("z") + dz, 4),
        "core": lax.rem(lax.axis_index("core") + dc, 2),
    }


GROUP_ALL = [(dz, dc) for dz in range(4) for dc in range(2) if dz or dc]


def sum_small(engine, norms, bias, norm_sum, bias_all, by_group, by_x, by_y):
    z, x, yl, core, yh = place()
    y = yh * 2 + yl
    me = z * 2 + core
    first = []
    for dz, dc in GROUP_ALL:
        to = group_peer(dz, dc)
        first.append(engine.send(norms.at[:, lanes(to["z"], 512)], by_group.at[me], to))
    mine = engine.local(norms.at[:, lanes(z, 512)], by_group.at[me])
    yield
    mine.wait()
    for copy in first:
        copy.wait_recv()
    by_x[x, :, :512] = sum(by_group[k] for k in range(8))
    by_x[x, :, 512:] = bias[...]
    second = [engine.send(by_x.at[x], by_x.at[x], x_peer(d)) for d in (1, 2, 3)]
    yield
    for copy in second:
        copy.wait_recv()
    by_y[y] = sum(by_x[k] for k in range(4))
    third = [engine.send(by_y.at[y], by_y.at[y], y_peer(d)) for d in (1, 2, 3)]
    yield
    for copy in third:
        copy.wait_recv()
    total = sum(by_y[k] for k in range(4))
    norm_sum[...] = total[:, :512]
    bias_all[me] = total[:, 512:]
    last = [engine.send(bias_all.at[me], bias_all.at[me], group_peer(dz, dc)) for dz, dc in GROUP_ALL]
    yield
    for copy in last:
        copy.wait()
    for copy in first + second + third:
        copy.wait_send()


def hand_back(engine, src, dst):
    core, yh = lax.axis_index("core"), lax.axis_index("yh")
    far = {"core": yh, "yh": 1 - yh}
    near = {"core": yh}
    stays = core == yh
    mine = dst.at[rows_at(core, OWN)]
    sends = [engine.free_send.pop() for _ in range(2)]
    arrivals = [engine.free_recv.pop() for _ in range(2)]
    j = engine.free_local.pop()
    send_sem, recv_sem, local_sem = engine.send_sem, engine.recv_sem, engine.local_sem

    def make(to, slot):
        return pltpu.make_async_remote_copy(
            src,
            mine,
            send_sem.at[sends[slot]],
            recv_sem.at[arrivals[0] + (arrivals[1] - arrivals[0]) * core],
            device_id=to,
            device_id_type=MESH_ID,
        )

    def arrival(half):
        part = dst.at[rows_at(half, OWN)]
        return pltpu.make_async_remote_copy(
            part, part, send_sem.at[sends[0]], recv_sem.at[arrivals[0] + (arrivals[1] - arrivals[0]) * half], device_id=far, device_id_type=MESH_ID
        )

    make(far, 0).start()

    @pl.when(stays)
    def _():
        pltpu.make_async_copy(src, mine, local_sem.at[j]).start()

    @pl.when(jnp.logical_not(stays))
    def _():
        make(near, 1).start()

    yield
    make(far, 0).wait_send()

    @pl.when(stays)
    def _():
        pltpu.make_async_copy(src, mine, local_sem.at[j]).wait()
        arrival(1 - core).wait_recv()

    @pl.when(jnp.logical_not(stays))
    def _():
        make(near, 1).wait_send()
        arrival(core).wait_recv()
        arrival(1 - core).wait_recv()

    engine.free_send.extend(sends)
    engine.free_local.append(j)


def dot(a, b, dims):
    return lax.dot_general(a, b, ((dims[:1], dims[1:]), ((), ())), preferred_element_type=F32)


def rope(block, cosine, sine):
    front, back = block[:8], block[8:16]
    return jnp.concatenate(
        [front * cosine - back * sine, back * cosine + front * sine, block[16:]], axis=0
    )


def rope_back(block, cosine, sine):
    front, back = block[:8], block[8:16]
    return jnp.concatenate(
        [front * cosine + back * sine, back * cosine - front * sine, block[16:]], axis=0
    )


def masked_scores(scores, start, seg_row, seg_col):
    stop = start + QB

    def hide(first, last, by_segment, causal):
        part = scores[first:last]
        keep = None
        if by_segment:
            keep = seg_col[first:last] == seg_row[:, start:stop]
        if causal:
            key_at = first + lax.broadcasted_iota(jnp.int32, part.shape, 0)
            query_at = start + lax.broadcasted_iota(jnp.int32, part.shape, 1)
            order = key_at <= query_at
            keep = order if keep is None else keep & order
        return jnp.where(keep, part, NEG)

    if start == 0:
        return hide(0, stop, True, True)
    if stop + 127 <= SEQ:
        parts = [hide(0, 128, True, False)]
        if start > 128:
            parts.append(scores[128:start])
        parts.append(hide(start, stop, False, True))
        return jnp.concatenate(parts, axis=0)
    return jnp.concatenate([hide(0, start, True, False), hide(start, stop, True, True)], axis=0)


def attend(qkv_ref, row_ref, col_ref, cos_ref, sin_ref, o_ref, wide_ref, lse_ref, kept_ref):
    cosine, sine = cos_ref[...], sin_ref[...]
    q_t = rope(qkv_ref[:HEAD].astype(F32), cosine, sine).astype(BF16) * jnp.asarray(0.125, BF16)
    k_t = rope(qkv_ref[HEAD : 2 * HEAD].astype(F32), cosine, sine).astype(BF16)
    v_t = qkv_ref[2 * HEAD :]
    kept_ref[:HEAD] = q_t
    kept_ref[HEAD : 2 * HEAD] = k_t
    kept_ref[2 * HEAD :] = v_t
    keys = k_t.astype(F32).T.astype(BF16)
    seg_row, seg_col = row_ref[...], col_ref[...]
    for start in range(0, SEQ, QB):
        stop = start + QB
        scores = dot(keys[:stop], q_t[:, start:stop], (1, 0))
        scores = masked_scores(scores, start, seg_row, seg_col)
        top = jnp.max(scores, axis=0, keepdims=True)
        terms = jnp.exp(scores - top)
        total = jnp.sum(terms, axis=0, keepdims=True)
        out = dot(v_t[:, :stop], terms.astype(BF16), (1, 0)) / total
        wide_ref[:, start:stop] = out
        o_ref[:, start:stop] = out.astype(BF16)
        lse_ref[:, start:stop] = top + jnp.log(total)


def attend_back(kept_ref, do_ref, wide_ref, lse_ref, row_ref, col_ref, cos_ref, sin_ref, out_ref, sum_ref):
    cosine, sine = cos_ref[...], sin_ref[...]
    q_t, k_t, do_t = kept_ref[:HEAD], kept_ref[HEAD : 2 * HEAD], do_ref[...]
    queries = q_t.astype(F32).T.astype(BF16)
    keys = k_t.astype(F32).T.astype(BF16)
    values = kept_ref[2 * HEAD :].astype(F32).T.astype(BF16)
    grads = do_t.astype(F32).T.astype(BF16)
    centre = jnp.sum(do_t.astype(F32) * wide_ref[...], axis=0, keepdims=True)
    lse = lse_ref[...]
    seg_row, seg_col = row_ref[...], col_ref[...]
    sum_ref[...] = jnp.zeros_like(sum_ref)
    dq_parts = []
    for start in range(0, SEQ, QB):
        stop = start + QB
        scores = dot(keys[:stop], q_t[:, start:stop], (1, 0))
        scores = masked_scores(scores, start, seg_row, seg_col)
        probs = jnp.exp(scores - lse[:, start:stop])
        d_probs = dot(values[:stop], do_t[:, start:stop], (1, 0))
        d_scores = (probs * (d_probs - centre[:, start:stop])).astype(BF16)
        d_keys = dot(d_scores, queries[start:stop], (1, 0))
        d_values = dot(probs.astype(BF16), grads[start:stop], (1, 0))
        sum_ref[:stop] += jnp.concatenate([d_keys, d_values], axis=1)
        dq_parts.append(dot(k_t[:, :stop], d_scores, (1, 0)) * 0.125)
    out_ref[:HEAD] = rope_back(jnp.concatenate(dq_parts, axis=1), cosine, sine).astype(BF16)
    turned = sum_ref[...].T
    out_ref[HEAD : 2 * HEAD] = rope_back(turned[:HEAD], cosine, sine).astype(BF16)
    out_ref[2 * HEAD :] = turned[HEAD:].astype(BF16)


def small_peer(dz, dh):
    return {
        "z": lax.rem(lax.axis_index("z") + dz, 4),
        "yh": lax.rem(lax.axis_index("yh") + dh, 2),
    }


SMALL_ALL = [(dz, dh) for dz in range(4) for dh in range(2) if dz or dh]
SCRATCH = [
    ("m_qkv", (4, 192, WIDTH), BF16),
    ("m_out", (4, 64, WIDTH), BF16),
    ("x_own", (OWN, WIDTH), BF16),
    ("dy_own", (OWN, WIDTH), BF16),
    ("middle", (OWN, WIDTH), F32),
    ("norms", (8, WIDTH), F32),
    ("h1", (ROWS, WIDTH), BF16),
    ("o_t", (4 * HEAD, ROWS), BF16),
    ("kept", (3 * HEAD, SEQ), BF16),
    ("wide", (HEAD, SEQ), F32),
    ("lse", (1, SEQ), F32),
    ("seg_row", (1, SEQ), F32),
    ("seg_col", (SEQ, 1), F32),
    ("packed", (16, 640), BF16),
    ("small", (4, 2, 16, 640), BF16),
    ("near_x", (OWN, WIDTH), BF16),
    ("near_dy", (OWN, WIDTH), BF16),
    ("far_x", (OWN, WIDTH), BF16),
    ("far_dy", (OWN, WIDTH), BF16),
    ("h1_own", (OWN, WIDTH), BF16),
    ("h2_own", (OWN, WIDTH), BF16),
    ("held_qkv", (3, 128, 1024), BF16),
    ("held_gu", (128, 2, 2816), BF16),
    ("turned", (2816, 128), F32),
    ("cut_qkv", (4, 192, 128), BF16),
    ("cut_gate", (4, 176, 128), BF16),
    ("cut_up", (4, 176, 128), BF16),
    ("p_qkv", (192, 512), BF16),
    ("p_out", (64, 512), BF16),
    ("p_down", (176, 512), BF16),
    ("p_gate", (176, 512), BF16),
    ("p_up", (176, 512), BF16),
    ("bias", (4, 192, 1), F32),
    ("out", (HEAD, SEQ), BF16),
    ("o_rows", (ROWS, 4 * HEAD), BF16),
    ("product", (ROWS, WIDTH), BF16),
]


class Refs:
    pass


def column_of(row):
    blocks = jnp.concatenate([row[:, k * 128 : (k + 1) * 128] for k in range(16)], axis=0).T
    return jnp.concatenate([blocks[:, k : k + 1] for k in range(16)], axis=0)


def back_peer(dc, dh):
    return {
        "core": lax.rem(lax.axis_index("core") + dc, 2),
        "yh": lax.rem(lax.axis_index("yh") + dh, 2),
    }


LAYER_PEERS = XY_PEERS + Z_PEERS + [sibling, functools.partial(back_peer, 1, 1)]
LAYER_PEERS += [functools.partial(small_peer, dz, 1) for dz in (1, 2, 3)]
LAYER_PEERS += [functools.partial(group_peer, dz, 1) for dz in (1, 2, 3)]
PLACES = [
    ("m_gate", (4, 176, WIDTH), BF16, HBM),
    ("far_m_qkv", (4, 192, WIDTH), BF16, HBM),
    ("far_h1", (ROWS, WIDTH), BF16, HBM),
]
RESULTS = [
    ("layer_out", (2 * OWN, WIDTH), BF16, HBM),
    ("grad_tokens", (2 * OWN, WIDTH), BF16, HBM),
    ("gd_all", (16, 4, 352, 128), BF16, HBM),
    ("up_all", (16, 4, 176, 128), BF16, HBM),
    ("attn_all", (16, 4, 256, 128), BF16, HBM),
    ("norm_sum", (8, 512), F32, VMEM),
    ("grad_bias", (3, 16, 16), F32, VMEM),
]
SCRATCH += [
    ("up_attn", (4, 256, WIDTH), BF16),
    ("down", (4, 176, WIDTH), BF16),
    ("dy_all", (ROWS, WIDTH), BF16),
    ("product_mlp", (ROWS, WIDTH), BF16),
    ("gate", (704, ROWS), F32),
    ("act", (704, ROWS), BF16),
    ("d_gate", (704, ROWS), BF16),
    ("d_up", (704, ROWS), BF16),
    ("dz_own", (OWN, WIDTH), BF16),
    ("dz", (ROWS, WIDTH), BF16),
    ("d_middle", (OWN, WIDTH), F32),
    ("summed", (OWN, WIDTH), F32),
    ("out_own", (OWN, WIDTH), BF16),
    ("grad_own", (OWN, WIDTH), BF16),
    ("other_dh2", (4, OWN, WIDTH), BF16),
    ("arrived_dh2", (3, OWN, WIDTH), BF16),
    ("other_mlp", (4, OWN, WIDTH), BF16),
    ("arrived_mlp", (3, OWN, WIDTH), BF16),
    ("other_dh1", (4, OWN, WIDTH), BF16),
    ("arrived_dh1", (3, OWN, WIDTH), BF16),
    ("own_y", (128, WIDTH), BF16),
    ("own_x", (4, 128, 512), BF16),
    ("d_o", (4 * HEAD, ROWS), BF16),
    ("item_do", (HEAD, SEQ), BF16),
    ("item_out", (3 * HEAD, SEQ), BF16),
    ("d_kv", (SEQ, 2 * HEAD), F32),
    ("d_qkv", (12 * HEAD, ROWS), BF16),
    ("d_rows", (ROWS, 12 * HEAD), BF16),
    ("landing_gd", (4, 352, 128), BF16),
    ("landing_up", (4, 176, 128), BF16),
    ("landing_attn", (4, 256, 128), BF16),
    ("small_norms", (8, WIDTH), F32),
    ("small_bias", (8, 768), F32),
    ("bias_all", (8, 8, 768), F32),
    ("by_group", (8, 8, 512), F32),
    ("small_x", (4, 8, 1280), F32),
    ("small_y", (4, 8, 1280), F32),
]
for _name, _n in (("gate", 176), ("down", 176), ("up", 176), ("attn", 256)):
    _cut = first_part(_n)
    SCRATCH += [
        ("sum_y_" + _name, (_cut, WIDTH), BF16),
        ("sum_x_" + _name, (4, _n - _cut, 512), BF16),
        ("rest_x_" + _name, (3, _cut, 512), BF16),
        ("rest_y_" + _name, (3, _n - _cut, 512), BF16),
        ("rest_own_" + _name, (_n, 512), BF16),
        ("rest_total_" + _name, (_n, 512), BF16),
    ]
for _name, _cut, _rest in (("a", 96, 80), ("b", 128, 128)):
    SCRATCH += [
        ("by_y_" + _name, (2, _cut, WIDTH), BF16),
        ("by_x_" + _name, (2, 4, _rest, 512), BF16),
        ("relay_y_" + _name, (_cut, WIDTH), BF16),
        ("relay_x_" + _name, (4, _rest, 512), BF16),
    ]


LAYER_INPUTS = ["tokens", "cotangent", "gains", "shifts", "biases", "segments"]
LAYER_INPUTS += ["w_qkv", "w_out", "w_down", "w_gate_up", "cos", "sin"]


def layer_kernel(*refs):
    r = Refs()
    names = LAYER_INPUTS + [o[0] for o in PLACES + RESULTS] + [o[0] for o in SCRATCH]
    for name, ref in zip(names, refs):
        setattr(r, name, ref)
    r.gate_qkv, r.normed, r.qkv_t, r.item = r.m_qkv, r.h1, r.d_qkv, r.item_out
    r.other, r.arrived = r.other_dh2, r.arrived_dh2
    m_gate, m_up = r.gate_qkv.at[:, pl.ds(0, 176)], r.up_attn.at[:, pl.ds(0, 176)]
    engine = Engine(*refs[len(names) :])
    z, x, yl, core, yh = place()
    y = yh * 2 + yl

    load_qkv = engine.local(r.w_qkv.at[:, rows_at(x, 128)], r.held_qkv)
    load_gu = engine.local(r.w_gate_up.at[rows_at(x, 128)], r.held_gu)
    load_x = engine.local(r.tokens.at[rows_at(core, OWN)], r.near_x)
    load_dy = engine.local(r.cotangent.at[rows_at(core, OWN)], r.near_dy)
    marks = r.segments[...].astype(F32)
    rows = [r.gains[...].astype(F32), r.shifts[...].astype(F32)]
    rows += [marks[:, k * 512 : (k + 1) * 512] for k in range(4)] + [jnp.zeros((8, 512), F32)]
    r.packed[:, :512] = jnp.concatenate(rows, axis=0).astype(BF16)
    unit = (
        lax.broadcasted_iota(jnp.int32, (16, 16), 0) == lax.broadcasted_iota(jnp.int32, (16, 16), 1)
    ).astype(BF16)
    columns = [dot(r.biases[part], unit, (0, 0)) for part in range(3)] + [jnp.zeros((16, 80), F32)]
    r.packed[:, 512:] = jnp.concatenate(columns, axis=1).astype(BF16)
    small_here = engine.local(r.packed, r.small.at[z, yh])

    def rows_of(n):
        return lambda zz: rows_at((zz * 2 + core) * 2 + yl, n)

    def slots_of(piece):
        return lambda zz: piece.at[:, lanes(zz)]

    load_qkv.wait()
    for part in range(3):
        r.turned[:1024, :] = r.held_qkv[part].astype(F32).T
        for zz in range(4):
            r.cut_qkv[zz, part * HEAD : (part + 1) * HEAD] = r.turned[rows_of(HEAD)(zz), :].astype(BF16)
    greet(LAYER_PEERS)
    pieces_qkv = send_pieces(engine, lambda zz: r.cut_qkv.at[zz], slots_of(r.p_qkv))
    swap_x = engine.send(r.tokens.at[rows_at(1 - core, OWN)], r.far_x, sibling())
    smalls = [engine.send(r.packed, r.small.at[z, yh], small_peer(dz, dh)) for dz, dh in SMALL_ALL]
    pieces_out = send_pieces(engine, lambda zz: r.w_out.at[rows_of(64)(zz), lanes(x)], slots_of(r.p_out))
    swap_dy = engine.send(r.cotangent.at[rows_at(1 - core, OWN)], r.far_dy, sibling())
    load_gu.wait()
    for g, cut in ((0, r.cut_gate), (1, r.cut_up)):
        r.turned[...] = r.held_gu[:, g, :].astype(F32).T
        for zz in range(4):
            cut[zz] = r.turned[rows_of(176)(zz), :].astype(BF16)

    stays = core == yh
    load_x.wait()
    swap_x.wait_recv()
    x_rows = spread(jnp.where(stays, r.near_x[...].astype(F32), r.far_x[...].astype(F32)))
    r.x_own[...] = x_rows.astype(BF16)
    small_here.wait()
    for copy in smalls:
        copy.wait_recv()
    parts = [r.small[zz, 0].astype(F32) for zz in range(4)]
    r.norms[...] = jnp.concatenate(
        [parts[zz][:8, xx * 128 : (xx + 1) * 128] for xx in range(4) for zz in range(4)], axis=1
    )
    h1_full, _, _ = layer_norm(x_rows, r.norms[0:1], r.norms[2:3])
    r.h1_own[...] = h1_full.astype(BF16)
    tokens_h1 = gather_tokens(engine, r.h1_own, r.h1)
    next(tokens_h1)

    for copy in pieces_qkv[1:]:
        copy.wait_recv()
    pieces_qkv[0].wait()
    weight_qkv = gather_weight(engine, r.p_qkv, r.m_qkv)
    next(weight_qkv)

    lane_at = lax.broadcasted_iota(jnp.int32, (64, 128), 1)
    for h in range(2):
        table = jnp.concatenate([r.small[zz, h, :, 512:].astype(F32) for zz in range(4)], axis=0)
        for j in range(2):
            for part in range(3):
                picked = jnp.where(lane_at == part * 16 + (z * 2 + core) * 2 + j, table, 0.0)
                r.bias[h * 2 + j, part * HEAD : (part + 1) * HEAD] = jnp.sum(picked, axis=1, keepdims=True)
    marks = r.small[x, 0, :, :512].astype(F32)
    r.seg_row[...] = jnp.concatenate([marks[4 + i : 5 + i] for i in range(4)], axis=1)
    r.seg_col[...] = column_of(r.seg_row[...])

    next(weight_qkv)
    next(tokens_h1)
    pieces_down = send_pieces(engine, lambda zz: r.w_down.at[rows_of(176)(zz), lanes(x)], slots_of(r.p_down))
    pieces_gate = send_pieces(engine, lambda zz: r.cut_gate.at[zz], slots_of(r.p_gate))
    pieces_up = send_pieces(engine, lambda zz: r.cut_up.at[zz], slots_of(r.p_up))
    next(weight_qkv)

    def start_weight(pieces, piece, matrix):
        pieces[0].wait()
        for copy in pieces[1:]:
            copy.wait_recv()
        thread = gather_weight(engine, piece, matrix)
        next(thread)
        return thread

    load_dy.wait()
    swap_dy.wait_recv()
    dy_rows = jnp.where(stays, r.near_dy[...].astype(F32), r.far_dy[...].astype(F32))
    r.dy_own[...] = spread(dy_rows).astype(BF16)
    finish(tokens_h1)
    finish(weight_qkv)

    r.qkv_t[...] = (
        dot(r.m_qkv[...].reshape(12 * HEAD, WIDTH), r.h1[...], (1, 1)) + r.bias[...].reshape(12 * HEAD, 1)
    ).astype(BF16)
    to_items = send_items(engine, r.qkv_t, r.item, 3 * HEAD)
    tokens_dy = gather_tokens(engine, r.dy_own, r.dy_all)
    weight_out = start_weight(pieces_out, r.p_out, r.m_out)
    next(tokens_dy)
    weight_down = start_weight(pieces_down, r.p_down, r.down)
    to_items.wait_recv()
    next(weight_out)
    weight_gate = start_weight(pieces_gate, r.p_gate, r.m_gate)
    stores = [engine.local(r.m_qkv, r.far_m_qkv), engine.local(r.h1, r.far_h1)]
    attend(r.item, r.seg_row, r.seg_col, r.cos, r.sin, r.out, r.wide, r.lse, r.kept)
    next(weight_out)
    back = return_items(engine, r.out, r.o_t, HEAD)
    next(weight_down)
    weight_up = start_weight(pieces_up, r.p_up, m_up)
    next(tokens_dy)
    finish(weight_out)
    back.wait_recv()

    for copy in stores:
        copy.wait()

    r.o_rows[...] = r.o_t[...].astype(F32).T.astype(BF16)
    matrix = r.m_out[...].reshape(4 * HEAD, WIDTH)
    by_columns(r.product, lambda columns: dot(r.o_rows[...], matrix[:, columns], (1, 0)))
    out = scatter_tokens(engine, r.product, r.middle, r.other, r.arrived)
    next(out)
    next(out)
    next(weight_gate)
    next(weight_up)
    next(weight_down)
    next(weight_gate)
    next(out)
    r.middle[...] += x_rows

    h2_full, _, _ = layer_norm(r.middle[...], r.norms[1:2], r.norms[3:4])
    r.h2_own[...] = h2_full.astype(BF16)
    tokens_h2 = gather_tokens(engine, r.h2_own, r.normed)
    next(tokens_h2)
    next(weight_up)

    halves = [(slice(2 * k, 2 * k + 2), slice(352 * k, 352 * k + 352)) for k in range(2)]
    finish(tokens_dy)
    finish(weight_down)
    for two, rows in halves:
        d_act = dot(r.down[two].reshape(352, WIDTH), r.dy_all[...], (1, 1))
        for k in range(4):
            r.turned[704 * k + rows.start : 704 * k + rows.stop] = d_act[:, k * 128 : (k + 1) * 128]
    next(tokens_h2)
    finish(weight_gate)
    load_gate = engine.local(r.m_gate, m_gate)
    finish(tokens_h2)
    load_gate.wait()
    for two, rows in halves:
        r.gate[rows] = dot(r.gate_qkv[two, :176].reshape(352, WIDTH), r.normed[...], (1, 1))
    finish(out)
    sent = smalls + [to_items, back, swap_x, swap_dy]
    for pieces in (pieces_qkv, pieces_out, pieces_gate, pieces_down, pieces_up):
        sent += pieces[1:]
    for copy in sent:
        copy.wait_send()
    finish(weight_up)
    for two, rows in halves:
        up = dot(r.up_attn[two, :176].reshape(352, WIDTH), r.normed[...], (1, 1))
        gate = r.gate[rows]
        d_act = [r.turned[704 * k + rows.start : 704 * k + rows.stop] for k in range(4)]
        d_act = jnp.concatenate(d_act, axis=1)
        sigmoid = jax.nn.sigmoid(gate)
        silu = gate * sigmoid
        r.act[rows] = (silu * up).astype(BF16)
        r.d_gate[rows] = (d_act * up * sigmoid * (1.0 + gate * (1.0 - sigmoid))).astype(BF16)
        r.d_up[rows] = (d_act * silu).astype(BF16)

    def first_of(name, grad, places):
        cut, rest = getattr(r, "sum_y_" + name).shape[0], getattr(r, "sum_x_" + name).shape[1]
        head, tail = pl.ds(0, cut), pl.ds(0, rest)
        thread = sum_first(
            engine,
            grad,
            getattr(r, "sum_y_" + name),
            getattr(r, "sum_x_" + name),
            getattr(r, "by_y_" + places).at[:, head],
            getattr(r, "by_x_" + places).at[:, :, tail],
            getattr(r, "relay_y_" + places).at[head],
            getattr(r, "relay_x_" + places).at[:, tail],
            r.own_y,
            r.own_x,
        )
        next(thread)
        return thread

    def rest_of(name, landing):
        parts = [getattr(r, part + name) for part in ("rest_x_", "rest_y_", "rest_own_", "rest_total_")]
        thread = sum_rest(engine, getattr(r, "sum_y_" + name), getattr(r, "sum_x_" + name), landing, *parts)
        next(thread)
        return thread

    def part_of(landing, first):
        return lambda zz: landing.at[zz, pl.ds(first, 176)]

    def turned(ref):
        return ref[...].astype(F32).T.astype(BF16)

    def columns_of(ref, columns):
        return ref[:, :176, columns].reshape(704, 512)

    gate_rows, up_rows = turned(r.d_gate), turned(r.d_up)
    by_columns(
        r.product,
        lambda columns: dot(gate_rows, columns_of(r.gate_qkv, columns), (1, 0))
        + dot(up_rows, columns_of(r.up_attn, columns), (1, 0)),
    )
    dh2 = scatter_tokens(engine, r.product, r.summed, r.other_dh2, r.arrived_dh2)
    next(dh2)
    by_columns(m_gate, lambda columns: dot(r.d_gate[...], r.normed[:, columns], (1, 0)))
    gate = first_of("gate", m_gate, "a")
    next(dh2)
    act_rows = turned(r.act)
    by_columns(r.product_mlp, lambda columns: dot(act_rows, columns_of(r.down, columns), (1, 0)))
    by_columns(r.down, lambda columns: dot(r.act[...], r.dy_all[:, columns], (1, 0)))
    down = first_of("down", r.down, "b")
    by_columns(m_up, lambda columns: dot(r.d_up[...], r.normed[:, columns], (1, 0)))
    load_h1 = engine.local(r.far_h1, r.normed)
    mlp = scatter_tokens(engine, r.product_mlp, r.d_middle, r.other_mlp, r.arrived_mlp)
    next(mlp)
    _, normed_b, rstd_b = layer_norm(r.middle[...], r.norms[1:2], r.norms[3:4])
    next(gate)
    next(down)
    next(dh2)
    back_b, gain_b, shift_b = norm_back(r.summed[...], normed_b, rstd_b, r.norms[1:2])
    d_middle = r.dy_own[...].astype(F32) + back_b
    r.dz_own[...] = d_middle.astype(BF16)
    tokens_dz = gather_tokens(engine, r.dz_own, r.dz)
    next(tokens_dz)
    r.small_norms[1:2] = gain_b[None]
    r.small_norms[3:4] = shift_b[None]
    next(gate)
    rest_gate = rest_of("gate", part_of(r.landing_gd, 0))
    next(down)
    rest_down = rest_of("down", part_of(r.landing_gd, 176))
    next(tokens_dz)
    finish(tokens_dz)

    r.d_o[...] = dot(r.m_out[...].reshape(4 * HEAD, WIDTH), r.dz[...], (1, 1)).astype(BF16)
    to_items = send_items(engine, r.d_o, r.item_do, HEAD)
    next(rest_gate)
    up = first_of("up", m_up, "a")
    next(rest_down)
    next(mlp)
    finish(gate)
    load_qkv = engine.local(r.far_m_qkv, r.gate_qkv)
    to_items.wait_recv()
    next(rest_gate)
    next(rest_down)
    gather_gd = gather_ctx(engine, r.landing_gd, r.gd_all)
    next(gather_gd)
    finish(down)
    finish(rest_gate)
    finish(rest_down)
    attend_back(
        r.kept, r.item_do, r.wide, r.lse, r.seg_row, r.seg_col, r.cos, r.sin, r.item_out, r.d_kv
    )
    back = return_items(engine, r.item_out, r.d_qkv, 3 * HEAD)
    to_items.wait_send()
    next(up)
    next(gather_gd)
    next(mlp)
    r.out_own[...] = spread(r.middle[...] + r.d_middle[...]).astype(BF16)
    r.d_middle[...] = d_middle
    hand_out = hand_back(engine, r.out_own, r.layer_out)
    next(hand_out)
    load_h1.wait()
    load_qkv.wait()
    back.wait_recv()
    finish(mlp)

    r.d_rows[...] = r.d_qkv[...].astype(F32).T.astype(BF16)
    matrix = r.gate_qkv[...].reshape(12 * HEAD, WIDTH)
    finish(dh2)
    by_columns(r.product, lambda columns: dot(r.d_rows[...], matrix[:, columns], (1, 0)))
    dh1 = scatter_tokens(engine, r.product, r.summed, r.other_dh1, r.arrived_dh1)
    next(dh1)
    next(up)
    rest_up = rest_of("up", part_of(r.landing_up, 0))
    finish(up)
    by_columns(
        r.up_attn.at[:, pl.ds(0, 192)], lambda columns: dot(r.d_qkv[...], r.normed[:, columns], (1, 0))
    )
    by_columns(r.up_attn.at[:, pl.ds(192, 64)], lambda columns: dot(r.o_t[...], r.dz[:, columns], (1, 0)))
    attn = first_of("attn", r.up_attn, "b")
    next(dh1)
    r.small_bias[...] = dot(jnp.ones((8, ROWS), BF16), r.d_qkv[...], (1, 1))
    _, normed_a, rstd_a = layer_norm(r.x_own[...].astype(F32), r.norms[0:1], r.norms[2:3])
    next(rest_up)
    next(attn)
    next(gather_gd)
    next(rest_up)
    finish(rest_up)
    gather_up = gather_ctx(engine, r.landing_up, r.up_all)
    next(gather_up)
    next(dh1)
    back_a, gain_a, shift_a = norm_back(r.summed[...], normed_a, rstd_a, r.norms[0:1])
    r.grad_own[...] = spread(r.d_middle[...] + back_a).astype(BF16)
    r.small_norms[0:1] = gain_a[None]
    r.small_norms[2:3] = shift_a[None]
    r.small_norms[4:] = jnp.zeros((4, WIDTH), F32)
    r.small_norms[...] = spread(r.small_norms[...])
    small = sum_small(
        engine, r.small_norms, r.small_bias, r.norm_sum, r.bias_all, r.by_group, r.small_x, r.small_y
    )
    next(small)
    next(attn)
    rest_attn = rest_of("attn", lambda zz: r.landing_attn.at[zz])
    next(small)
    next(gather_gd)
    next(gather_up)
    next(rest_attn)
    hand_grad = hand_back(engine, r.grad_own, r.grad_tokens)
    next(hand_grad)
    next(small)
    next(rest_attn)
    gather_attn = gather_ctx(engine, r.landing_attn, r.attn_all)
    next(gather_attn)
    next(gather_up)
    next(small)
    next(gather_attn)
    next(gather_up)
    next(gather_attn)
    finish(small)
    table = jnp.concatenate([r.bias_all[k, 0:1] for k in range(8)], axis=0)
    from_at = lax.broadcasted_iota(jnp.int32, (768, 16), 0)
    to_at = lax.broadcasted_iota(jnp.int32, (768, 16), 1)
    row_at = lax.broadcasted_iota(jnp.int32, (16, 8), 0)
    group_at = lax.broadcasted_iota(jnp.int32, (16, 8), 1)
    for part in range(3):
        total = jnp.zeros((16, 16), F32)
        for j in range(2):
            chosen = (from_at == to_at + ((yh * 2 + j) * 3 + part) * HEAD + z * 16).astype(F32)
            spread_rows = (row_at == group_at * 2 + j).astype(F32)
            total += exact_dot(spread_rows, exact_dot(table, chosen))
        r.grad_bias[part] = total
    next(gather_attn)
    threads = (dh2, mlp, gate, down, up, attn, rest_gate, rest_down, rest_up, rest_attn)
    for thread in threads + (hand_out, dh1, hand_grad, small, gather_gd, gather_up, gather_attn):
        finish(thread)
    back.wait_send()


def layer(*inputs):
    outs = PLACES + RESULTS
    values = pl.pallas_call(
        layer_kernel,
        out_shape=[jax.ShapeDtypeStruct(o[1], o[2]) for o in outs],
        in_specs=[HBM] * 2 + [VMEM] * 4 + [HBM] * 4 + [VMEM] * 2,
        out_specs=[o[3] for o in outs],
        scratch_shapes=[pltpu.VMEM(shape, dtype) for _, shape, dtype in SCRATCH] + semaphores(104, 316, 20),
        compiler_params=pltpu.CompilerParams(
            collective_id=1, has_side_effects=True, vmem_limit_bytes=VMEM_BYTES
        ),
        name="layer",
    )(*inputs)
    return values[len(PLACES) :]


def assemble_kernel(
    gd_ref,
    up_ref,
    attn_ref,
    layer_ref,
    tokens_ref,
    norms_ref,
    gu_ref,
    down_ref,
    qkv_ref,
    out_ref,
    layer_out_ref,
    tokens_out_ref,
    gains_ref,
    shifts_ref,
    turned,
):
    layer_out_ref[...] = layer_ref[...]
    tokens_out_ref[...] = tokens_ref[...].astype(F32)
    gains_ref[...] = norms_ref[0:2]
    shifts_ref[...] = norms_ref[2:4]
    for g in range(2):
        for zz in range(2):
            for core in range(2):
                for yl in range(2):
                    row = zz * 704 + core * 352 + yl * 176
                    block = (up_ref[0, yl * 2 + core, zz] if g else gd_ref[0, yl * 2 + core, zz, :176]).astype(F32)
                    turned[row : row + 176, :] = block
        for t in range(11):
            gu_ref[:, g, t * 128 : (t + 1) * 128] = turned[t * 128 : (t + 1) * 128, :].T
    for zz in range(2):
        for core in range(2):
            for yl in range(2):
                row = zz * 704 + core * 352 + yl * 176
                down_ref[row : row + 176, :] = gd_ref[0, yl * 2 + core, zz, 176:].astype(F32)
                row = zz * 256 + core * 128 + yl * 64
                out_ref[row : row + 64, :] = attn_ref[0, yl * 2 + core, zz, 192:].astype(F32)
            for part in range(3):
                rows = slice(part * 64, (part + 1) * 64)
                block = jnp.concatenate([attn_ref[0, core, zz, rows], attn_ref[0, 2 + core, zz, rows]], axis=0)
                column = zz * 256 + core * 128
                qkv_ref[part, :, column : column + 128] = block.astype(F32).T


def assemble(gd_all, up_all, attn_all, layer_out, grad_tokens, norm_sum):
    gd_all = gd_all.reshape(4, 4, 4, 352, 128)
    up_all = up_all.reshape(4, 4, 4, 176, 128)
    attn_all = attn_all.reshape(4, 4, 4, 256, 128)
    return pl.pallas_call(
        assemble_kernel,
        grid=(4, 2),
        in_specs=[
            pl.BlockSpec((1, 4, 2, 352, 128), lambda i, j: (i, 0, j, 0, 0)),
            pl.BlockSpec((1, 4, 2, 176, 128), lambda i, j: (i, 0, j, 0, 0)),
            pl.BlockSpec((1, 4, 2, 256, 128), lambda i, j: (i, 0, j, 0, 0)),
            pl.BlockSpec((16, WIDTH), lambda i, j: (i * 2 + j, 0)),
            pl.BlockSpec((16, WIDTH), lambda i, j: (i * 2 + j, 0)),
            pl.BlockSpec((8, 512), lambda i, j: (0, 0)),
        ],
        out_specs=[
            pl.BlockSpec((128, 2, 1408), lambda i, j: (i, 0, j)),
            pl.BlockSpec((1408, 128), lambda i, j: (j, i)),
            pl.BlockSpec((3, 128, 512), lambda i, j: (0, i, j)),
            pl.BlockSpec((512, 128), lambda i, j: (j, i)),
            pl.BlockSpec((16, WIDTH), lambda i, j: (i * 2 + j, 0)),
            pl.BlockSpec((16, WIDTH), lambda i, j: (i * 2 + j, 0)),
            pl.BlockSpec((2, 512), lambda i, j: (0, 0)),
            pl.BlockSpec((2, 512), lambda i, j: (0, 0)),
        ],
        out_shape=[
            jax.ShapeDtypeStruct((512, 2, 2816), F32),
            jax.ShapeDtypeStruct((2816, 512), F32),
            jax.ShapeDtypeStruct((3, 512, 1024), F32),
            jax.ShapeDtypeStruct((1024, 512), F32),
            jax.ShapeDtypeStruct((2 * OWN, WIDTH), BF16),
            jax.ShapeDtypeStruct((2 * OWN, WIDTH), F32),
            jax.ShapeDtypeStruct((2, 512), F32),
            jax.ShapeDtypeStruct((2, 512), F32),
        ],
        scratch_shapes=[pltpu.VMEM((1408, 128), F32)],
        compiler_params=pltpu.CompilerParams(vmem_limit_bytes=VMEM_BYTES),
        name="assemble",
    )(gd_all, up_all, attn_all, layer_out, grad_tokens, norm_sum)


def rotation_tables():
    half = ROT // 2
    positions = np.arange(SEQ, dtype=np.float32)
    inverse = (10000.0 ** (-(np.arange(half) * 2.0 / ROT))).astype(np.float32)
    angles = (inverse[:, None] * positions[None, :]).astype(np.float64)
    return jnp.asarray(np.cos(angles).astype(np.float32)), jnp.asarray(np.sin(angles).astype(np.float32))


def layer_norm(values, gain_row, shift_row):
    row_mean = jnp.mean(values, axis=-1, keepdims=True)
    centred = values - row_mean
    variance = jnp.mean(centred * centred, axis=-1, keepdims=True)
    rstd = lax.rsqrt(variance + EPS)
    normed = centred * rstd
    return normed * gain_row + shift_row, normed, rstd


def norm_back(gradient, normed, rstd, gain_row):
    shaped = gradient * gain_row
    centre = (
        shaped
        - jnp.mean(shaped, axis=-1, keepdims=True)
        - normed * jnp.mean(shaped * normed, axis=-1, keepdims=True)
    )
    return centre * rstd, jnp.sum(gradient * normed, axis=0), jnp.sum(gradient, axis=0)


def local(tokens, segments, w_qkv, b_qkv, w_out, w_gate_up, w_down, norm_gains, norm_shifts, cotangent):
    cosine, sine = rotation_tables()
    layer_out, grad_tokens, gd_all, up_all, attn_all, norm_sum, grad_bias = layer(
        tokens[0],
        cotangent[0],
        norm_gains,
        norm_shifts,
        b_qkv,
        segments,
        w_qkv.transpose(1, 0, 2),
        w_out,
        w_down,
        w_gate_up,
        cosine,
        sine,
    )
    out_gu, out_down, out_qkv, out_out, layer_out, grad_tokens, gains, shifts = assemble(
        gd_all, up_all, attn_all, layer_out, grad_tokens, norm_sum
    )
    return (
        layer_out[None],
        grad_tokens[None],
        out_qkv.transpose(1, 0, 2),
        grad_bias,
        out_out,
        out_gu,
        out_down,
        gains,
        shifts,
    )


def solution(mesh):
    fine = Mesh(mesh.devices.reshape(4, 4, 2, 2, 2), ("z", "x", "yl", "core", "yh"))
    ctx = ("x", "yl", "core")
    return jax.shard_map(
        local,
        mesh=fine,
        in_specs=(
            P("z", ctx, None),
            P("z", None),
            P("z", None, "yh"),
            P(None, "yh", "z"),
            P("yh", "z"),
            P("z", None, "yh"),
            P("yh", "z"),
            P(None, "z"),
            P(None, "z"),
            P("z", ctx, None),
        ),
        out_specs=(
            P("z", ctx, None),
            P("z", ctx, None),
            P("z", None, "yh"),
            P(None, "yh", "z"),
            P("yh", "z"),
            P("z", None, "yh"),
            P("yh", "z"),
            P(None, "z"),
            P(None, "z"),
        ),
        check_vma=False,
    )
```
